128 devices in a mesh: grp: 2 (over core), blk: 32 (over z_lo, y, x), head: 2 (over z_hi).
Axes of the slice: x: 4, y: 4, z: 4 (z_hi: 2, z_lo: 2; z = z_hi * 2 + z_lo), core: 2. Of those that a mesh axis runs over, the one named last changes fastest.
Arguments:
- tokens: bfloat16 [16384, 768], P(('grp', 'blk', 'head')), parts along dimension 0, may hold values from -16 to 16
- gain_one: bfloat16 [768], P(('blk', 'head')), may hold values from 0.25 to 1.75
- w_query: bfloat16 [768, 768], P(('blk', 'head')), may hold values from -0.3125 to 0.3125
- w_key: bfloat16 [768, 768], P(('blk', 'head')), may hold values from -0.3125 to 0.3125
- w_value: bfloat16 [768, 768], P(('blk', 'head')), may hold values from -0.21875 to 0.21875
- w_out: bfloat16 [768, 768], P(('blk', 'head')), may hold values from -0.875 to 0.875
- gain_two: bfloat16 [768], P(('blk', 'head')), may hold values from 0.25 to 1.75
- w_gate: bfloat16 [768, 3072], P(('blk', 'head')), may hold values from -0.21875 to 0.21875
- w_up: bfloat16 [768, 3072], P(('blk', 'head')), may hold values from -0.21875 to 0.21875
- w_down: bfloat16 [3072, 768], P(('blk', 'head')), may hold values from -0.109375 to 0.109375
- cotangent: bfloat16 [16384, 768], P(('grp', 'blk', 'head')), parts along dimension 0, may hold values from -6 to 6
- segment_ids: int32 [16384], P(('grp', 'blk')), parts along dimension 0, may hold values from 0 to 17, as said below
- positions: int32 [16384], P(('grp', 'blk')), parts along dimension 0, may hold values from 0 to 2303, as said below
Outputs:
- output: bfloat16 [16384, 768], P(('grp', 'blk', 'head')), parts along dimension 0
- input_grad: float32 [16384, 768], P(('grp', 'blk', 'head')), parts along dimension 0
- gain_one_grad: float32 [1536], P(('grp', 'blk', 'head')), parts along dimension 0
- w_query_grad: float32 [1536, 768], P(('grp', 'blk', 'head')), parts along dimension 0
- w_key_grad: float32 [1536, 768], P(('grp', 'blk', 'head')), parts along dimension 0
- w_value_grad: float32 [1536, 768], P(('grp', 'blk', 'head')), parts along dimension 0
- w_out_grad: float32 [1536, 768], P(('grp', 'blk', 'head')), parts along dimension 0
- gain_two_grad: float32 [1536], P(('grp', 'blk', 'head')), parts along dimension 0
- w_gate_grad: float32 [1536, 3072], P(('grp', 'blk', 'head')), parts along dimension 0
- w_up_grad: float32 [1536, 3072], P(('grp', 'blk', 'head')), parts along dimension 0
- w_down_grad: float32 [6144, 768], P(('grp', 'blk', 'head')), parts along dimension 0
The draws below stay inside these ranges and needn't reach their ends.
There are 2 independent parts, one for each index of `grp`. The reference program is written for one: setup_inputs(seed, part) draws one part's arguments, and reference() takes and returns one part's arrays. A program takes and returns all parts, laid end to end along the dimension named above; an argument that names none is the same for every part. Nothing has to cross between parts.
Inputs may be any that keep to these rules, and one draw needn't show every extreme that they name: `segment_ids`: tokens come in aligned slabs of 128 consecutive positions of one sequence, slabs in any order; every group g has a prompt with segment g * (9) and positions 0 to 2047 and continuations c = 1 to 8 with segment g * 9 + c and positions 2048 to 2303, each position of each sequence once. `positions`: positions of the sequences described for segment_ids.
All inputs are finite; a program needn't handle non-finite values.
Results may differ from the reference program's by a relative error of at most 0.035.
Values may be sent and summed in bfloat16 or wider, within the bound.
A program may use at most 192 MiB of HBM per device.

```python
import math
import jax
import jax.numpy as jnp
from jax import lax

D = 768
HEADS = 12
KV_HEADS = 12
HD = 64
FF = 3072
PROMPT = 2048
CONTS = 8
CLEN = 256
SLAB = 128
GROUPS = 2
TOKENS = 8192
KVD = 768


def slab_layout(key):
    per_group = (PROMPT + CONTS * CLEN) // SLAB
    slab_count = GROUPS * per_group
    prompt_slabs = PROMPT // SLAB
    cont_slabs = CLEN // SLAB
    order = jax.random.permutation(jax.random.fold_in(key, 11), slab_count).astype(jnp.int32)
    chosen = jax.random.randint(jax.random.fold_in(key, 12), (), 0, GROUPS).astype(jnp.int32)
    opening = chosen * per_group
    closing = opening + prompt_slabs - 1
    where_open = jnp.argmax(order == opening)
    order = order.at[where_open].set(order[0]).at[0].set(opening)
    where_close = jnp.argmax(order == closing)
    order = order.at[where_close].set(order[slab_count - 1]).at[slab_count - 1].set(closing)
    group_of = order // per_group
    within = order % per_group
    is_cont = within >= prompt_slabs
    beyond = jnp.maximum(within - prompt_slabs, 0)
    piece_of = jnp.where(is_cont, 1 + beyond // cont_slabs, 0)
    base_pos = jnp.where(is_cont, PROMPT + beyond % cont_slabs * SLAB, within * SLAB)
    segment = (group_of * (CONTS + 1) + piece_of).astype(jnp.int32)
    offsets = jnp.arange(SLAB, dtype=jnp.int32)
    position = (base_pos[:, None] + offsets[None, :]).reshape(-1).astype(jnp.int32)
    return (jnp.repeat(segment, SLAB).astype(jnp.int32), position)


def draw_segment_ids(key, part):
    return slab_layout(key)[0]


def draw_positions(key, part):
    return slab_layout(key)[1]


def strengthened(entries, rng, source, target, shards_of, factor):
    owner, partner = [(jnp.arange(entries.shape[axis_at]) // (entries.shape[axis_at] // shards_of)).reshape([-1 if axis == axis_at else 1 for axis in range(entries.ndim)]) for axis_at in (source, target)]
    chosen = jax.random.permutation(rng, shards_of)[partner]
    strong = (owner == chosen) | (owner == (partner + shards_of // 2) % shards_of)
    return jnp.where(strong, factor * entries, entries)


def steps_of(own_key, extent, cuts, smallest, high):
    level, own = 1.0, jax.random.fold_in(own_key, 6)
    for axis_at, parts in cuts:
        draws = jnp.exp(jax.random.uniform(jax.random.fold_in(own, axis_at), (parts,), jnp.float32, smallest / len(cuts), high / len(cuts)))
        level = level * jnp.repeat(draws, extent[axis_at] // parts).reshape([-1 if axis == axis_at else 1 for axis in range(len(extent))])
    return level


def bell_draw(rng, extent, spread, reach, cuts=(), held_as=jnp.bfloat16):
    array = spread * jax.random.normal(rng, extent, jnp.float32)
    if cuts:
        array = array * steps_of(rng, extent, cuts, -0.22, 0.18)
    return jnp.clip(array, -reach, reach).astype(held_as)


def heavy_noise(own_key, dims, scale, limit, split, heavy, kind=jnp.bfloat16):
    array = scale * jax.random.normal(own_key, dims, jnp.float32)
    if split:
        array = array * steps_of(own_key, dims, split, -0.22, 0.18)
    return jnp.clip(strengthened(array, jax.random.fold_in(own_key, 3), *heavy), -limit, limit).astype(kind)


def setup_inputs(seed: int = 0, part: int = 0) -> dict:
    keys = jax.random.split(jax.random.key(seed), 14)
    own_keys = jax.random.split(jax.random.fold_in(keys[13], part), 14)
    tokens = heavy_noise(own_keys[0], (TOKENS, D), 1.0, 16.0, ((0, 64),), (0, 1, 64, 4.0))
    gain_one = jnp.clip(1.0 + 0.15 * jax.random.normal(keys[1], (D,), jnp.float32), 0.25, 1.75).astype(jnp.bfloat16)
    w_query = bell_draw(keys[2], (D, D), (D // 2) ** -0.5, 0.3125, ((0, 64),))
    w_key = bell_draw(keys[3], (D, KVD), (D // 2) ** -0.5, 0.3125, ((0, 64),))
    w_value = bell_draw(keys[4], (D, KVD), D ** -0.5, 0.21875, ((0, 64),))
    w_out = bell_draw(keys[5], (D, D), (D // 16) ** -0.5, 0.875, ((0, 64),))
    gain_two = jnp.clip(1.0 + 0.15 * jax.random.normal(keys[6], (D,), jnp.float32), 0.25, 1.75).astype(jnp.bfloat16)
    w_gate = bell_draw(keys[7], (D, FF), D ** -0.5, 0.21875, ((0, 64),))
    w_up = bell_draw(keys[8], (D, FF), D ** -0.5, 0.21875, ((0, 64),))
    w_down = bell_draw(keys[9], (FF, D), FF ** -0.5, 0.109375, ((0, 64),))
    cotangent = bell_draw(own_keys[10], (TOKENS, D), 1.0, 6.0, ((0, 64),))
    segment_ids = draw_segment_ids(jax.random.fold_in(jax.random.fold_in(keys[13], part), 71), part)
    positions = draw_positions(jax.random.fold_in(jax.random.fold_in(keys[13], part), 71), part)
    return dict(tokens=tokens, gain_one=gain_one, w_query=w_query, w_key=w_key, w_value=w_value, w_out=w_out, gain_two=gain_two, w_gate=w_gate, w_up=w_up, w_down=w_down, cotangent=cotangent, segment_ids=segment_ids, positions=positions)


epsilon = 1e-05
rope_base = 10000.0

@jax.custom_vjp
def low(v):
    return lax.optimization_barrier(v.astype(jnp.bfloat16)).astype(jnp.float32)

@jax.custom_vjp
def low_back(v):
    return v

def low_keep(v):
    return (low(v), None)

def low_pass(kept, grad):
    return (grad,)

def back_keep(v):
    return (v, None)

def back_low(kept, grad):
    return (low(grad),)
low.defvjp(low_keep, low_pass)
low_back.defvjp(back_keep, back_low)

def product(left, right):
    return jnp.dot(left, right, precision=lax.Precision.HIGHEST)

def rms_scaled(values, gain):
    return values * lax.rsqrt(lax.optimization_barrier(jnp.mean(values * values, axis=-1, keepdims=True)) + epsilon) * gain

def rotate(field, positions):
    row_count = field.shape[0]
    pieces = field.reshape(row_count, -1, HD)
    half_dim = HD // 2
    frequency = rope_base ** (-jnp.arange(half_dim, dtype=jnp.float32) * 2.0 / HD)
    angles = positions.astype(jnp.float32)[:, None] * frequency[None, :]
    cosine = jnp.cos(angles)[:, None, :]
    sine_part = jnp.sin(angles)[:, None, :]
    leading = pieces[..., :half_dim]
    trailing = pieces[..., half_dim:]
    turned = jnp.concatenate([leading * cosine - trailing * sine_part, trailing * cosine + leading * sine_part], -1)
    return turned.reshape(row_count, -1)

def visible_pairs(seg_query, pos_query, seg_key, pos_key):
    same_group = (seg_query // (CONTS + 1))[:, None] == (seg_key // (CONTS + 1))[None, :]
    readable = (seg_key % (CONTS + 1) == 0)[None, :] | (seg_query[:, None] == seg_key[None, :])
    return same_group & readable & (pos_key[None, :] <= pos_query[:, None])

def attend(queries, key_field, value_field, segment_ids, positions):
    row_count = queries.shape[0]
    block_rows = math.gcd(row_count, 512)
    per_group = HEADS // KV_HEADS
    scale_factor = 1.0 / math.sqrt(HD)
    query_blocks = queries.reshape(row_count // block_rows, block_rows, KV_HEADS, per_group, HD)
    key_heads = key_field.reshape(row_count, KV_HEADS, HD).transpose(1, 0, 2)
    value_heads = value_field.reshape(row_count, KV_HEADS, HD).transpose(1, 0, 2)
    seg_blocks = segment_ids.reshape(row_count // block_rows, block_rows)
    pos_blocks = positions.reshape(row_count // block_rows, block_rows)

    def one_block(operands):
        query_block, seg_block, pos_block = operands
        allowed = visible_pairs(seg_block, pos_block, segment_ids, positions)

        def one_head(head_operands):
            query_head, key_head, value_head = head_operands
            scores = jnp.einsum('rgd,nd->grn', query_head, key_head, precision=lax.Precision.HIGHEST) * scale_factor
            scores = jnp.where(allowed[None], low_back(scores), -1e+30)
            weights = jax.nn.softmax(scores, axis=-1)
            return jnp.einsum('grn,nd->rgd', weights, value_head, precision=lax.Precision.HIGHEST)
        heads_out = lax.map(jax.checkpoint(one_head), (query_block.transpose(1, 0, 2, 3), key_heads, value_heads))
        return heads_out.transpose(1, 0, 2, 3).reshape(block_rows, KV_HEADS * per_group * HD)
    attended = lax.map(jax.checkpoint(one_block), (query_blocks, seg_blocks, pos_blocks))
    return attended.reshape(row_count, KV_HEADS * per_group * HD)

def layer(inputs, gain_one, w_query, w_key, w_value, w_out, gain_two, w_gate, w_up, w_down, segment_ids, positions):
    hidden_one = low(rms_scaled(inputs, gain_one))
    queries = low(low_back(rotate(low_back(product(hidden_one, w_query)), positions)))
    key_field = low(low_back(rotate(low_back(product(hidden_one, w_key)), positions)))
    value_field = low(low_back(product(hidden_one, w_value)))
    attended = low(low_back(attend(queries, key_field, value_field, segment_ids, positions)))
    middle = inputs + low_back(product(attended, w_out))
    hidden_two = low(rms_scaled(middle, gain_two))
    gate_pre = low_back(product(hidden_two, w_gate))
    up_pre = low_back(product(hidden_two, w_up))
    activated = low(jax.nn.silu(gate_pre) * up_pre)
    return middle + low_back(product(activated, w_down))

def reference(tokens, gain_one, w_query, w_key, w_value, w_out, gain_two, w_gate, w_up, w_down, cotangent, segment_ids, positions):
    floats = [arr.astype(jnp.float32) for arr in (tokens, gain_one, w_query, w_key, w_value, w_out, gain_two, w_gate, w_up, w_down)]

    def forward(*operands):
        return layer(*operands, segment_ids, positions)
    result, pullback = jax.vjp(forward, *floats)
    grads = pullback(cotangent.astype(jnp.float32))
    return (result.astype(jnp.bfloat16), grads[0], grads[1], grads[2], grads[3], grads[4], grads[5], grads[6], grads[7], grads[8], grads[9])
```

```python
import functools

import jax
import jax.numpy as jnp
import numpy as np
from jax import lax
from jax.experimental import pallas as pl
from jax.experimental.pallas import tpu as pltpu
from jax.sharding import PartitionSpec as P

MESH = pl.DeviceIdType.MESH
F32 = jnp.float32
BF16 = jnp.bfloat16
HD = 64
CONTS = 8
SLAB = 128
LOW = -1e30
EPS = 1e-05
MIB = 1 << 20
VMEM = pl.BlockSpec(memory_space=pltpu.VMEM)
SMEM = pl.BlockSpec(memory_space=pltpu.SMEM)


def feature_order():
    place = np.arange(768)
    p, z, r = place // 48, place // 12 % 4, place % 12
    t = (z % 2) * 32 + p * 2 + z // 2
    return t * 12 + r


ORDER = feature_order()
TO_PERM = np.zeros((768, 768), np.float32)
TO_PERM[ORDER, np.arange(768)] = 1.0


class Place:
    def __init__(self):
        self.core = lax.axis_index("grp")
        blk = lax.axis_index("blk")
        self.x = lax.rem(blk, 4)
        self.y = lax.rem(lax.div(blk, 4), 4)
        self.z = lax.axis_index("head") * 2 + lax.div(blk, 16)

    def device(self, x=None, y=None, z=None):
        x = self.x if x is None else x
        y = self.y if y is None else y
        z = self.z if z is None else z
        return (self.core, lax.rem(z, 2) * 16 + y * 4 + x, lax.div(z, 2))

    def ring(self, axis):
        return Ring(self, axis)


class Ring:
    def __init__(self, place, axis):
        self.place, self.axis = place, axis
        self.own = getattr(place, axis)
        self.next = lax.rem(self.own + 1, 4)
        self.prev = lax.rem(self.own + 3, 4)
        self.far = lax.rem(self.own + 2, 4)

    def device(self, index):
        return self.place.device(**{self.axis: index})


def enter(place, axes):
    barrier = pltpu.get_barrier_semaphore()
    partners = []
    for axis in axes:
        ring = place.ring(axis)
        partners += [ring.device(ring.next), ring.device(ring.prev)]
        if axis == "z":
            partners.append(ring.device(ring.far))
    for partner in partners:
        pl.semaphore_signal(barrier, inc=1, device_id=partner, device_id_type=MESH)
    pl.semaphore_wait(barrier, len(partners))


class Links:
    def __init__(self, send, recv):
        self.send, self.recv, self.used, self.sent = send, recv, 0, []

    def copy(self, source, target, device):
        k = self.used
        self.used += 1
        copy = pltpu.make_async_remote_copy(
            src_ref=source,
            dst_ref=target,
            send_sem=self.send.at[k],
            recv_sem=self.recv.at[k],
            device_id=device,
            device_id_type=MESH,
        )
        copy.start()
        self.sent.append(copy)
        return copy

    def finish(self):
        for copy in self.sent:
            copy.wait_send()


def together(steps):
    steps = list(steps)
    while steps:
        left = []
        for step in steps:
            try:
                next(step)
                left.append(step)
            except StopIteration:
                pass
        steps = left


def ring_gather(links, ring, slot):
    right = links.copy(slot(ring.own, None), slot(ring.own, None), ring.device(ring.next))
    left = links.copy(slot(ring.own, None), slot(ring.own, None), ring.device(ring.prev))
    yield
    right.wait_recv()
    on_right = links.copy(slot(ring.prev, 0), slot(ring.prev, 0), ring.device(ring.next))
    left.wait_recv()
    on_left = links.copy(slot(ring.next, 1), slot(ring.next, 1), ring.device(ring.prev))
    yield
    on_right.wait_recv()
    on_left.wait_recv()


def add_into(target, terms, kind):
    lead, rows, columns = target.shape
    step = 16
    for size in (128, 64, 48, 32):
        if rows % size == 0 and size * columns <= 48 * 1024:
            step = size
            break
    count = rows // step

    def body(k, carry):
        i, r = lax.div(k, count), pl.multiple_of(lax.rem(k, count) * step, step)
        total = terms[0][i, pl.ds(r, step), :].astype(F32)
        for term in terms[1:]:
            total = total + term[i, pl.ds(r, step), :].astype(F32)
        target[i, pl.ds(r, step), :] = total.astype(kind)
        return carry

    lax.fori_loop(0, lead * count, body, 0)


def ring_scatter(links, ring, part, room, target, kind):
    low, high, sum_low, sum_high, from_prev, from_next = room
    nxt, prv = ring.device(ring.next), ring.device(ring.prev)
    far_low = links.copy(part(ring.far, 0), low, nxt)
    far_high = links.copy(part(ring.far, 1), high, prv)
    next_high = links.copy(part(ring.next, 1), from_prev(1), nxt)
    prev_low = links.copy(part(ring.prev, 0), from_next(0), prv)
    yield
    far_low.wait_recv()
    add_into(sum_low, [part(ring.next, 0), low], BF16)
    next_low = links.copy(sum_low, from_prev(0), nxt)
    far_high.wait_recv()
    add_into(sum_high, [part(ring.prev, 1), high], BF16)
    prev_high = links.copy(sum_high, from_next(1), prv)
    yield
    for copy in (next_high, prev_low, next_low, prev_high):
        copy.wait_recv()
    add_into(target, [part(ring.own, None), from_prev(None), from_next(None)], kind)


def lead_part(part):
    return pl.ds(0, 4) if part is None else pl.ds(2 * part, 2)


def row_part(rows, part):
    first = (rows // 2 + 15) // 16 * 16
    if part is None:
        return 0, rows
    return (0, first) if part == 0 else (first, rows - first)


def regions(rows, columns, by_rows):
    if by_rows:
        return [(0, rows // 2, 0, columns), (rows // 2, rows // 2, 0, columns)]
    return [(0, rows, 0, columns // 2), (0, rows, columns // 2, columns // 2)]


def plane_gather(links, place, buf, by_rows):
    rows, columns = buf.shape[2:]

    def half(region, x_first):
        r0, rn, c0, cn = region

        def one(k, part):
            off, size = row_part(rn, part)
            y, x = (place.y, k) if x_first else (k, place.x)
            return buf.at[y, x, pl.ds(r0 + off, size), pl.ds(c0, cn)]

        def line(k, part):
            y, x = (k, lead_part(part)) if x_first else (lead_part(part), k)
            return buf.at[y, x, pl.ds(r0, rn), pl.ds(c0, cn)]

        yield from ring_gather(links, place.ring("x" if x_first else "y"), one)
        yield from ring_gather(links, place.ring("y" if x_first else "x"), line)

    a, b = regions(rows, columns, by_rows)
    return half(a, True), half(b, False)


def plane_scatter_room(rows, columns, by_rows):
    rooms = []
    for _, rn, _, cn in regions(rows, columns, by_rows):
        rooms += [pltpu.VMEM((2, rn, cn), BF16)] * 4 + [pltpu.VMEM((4, rn, cn), BF16)] * 3
        low, high = row_part(rn, 0)[1], row_part(rn, 1)[1]
        rooms += [pltpu.VMEM((1, low, cn), BF16), pltpu.VMEM((1, high, cn), BF16)] * 2
        rooms += [pltpu.VMEM((1, rn, cn), BF16)] * 2
    return rooms


def plane_scatter(links, place, buf, rooms, target, by_rows):
    rows, columns = buf.shape[2:]

    def half(region, room, x_first):
        r0, rn, c0, cn = region
        low, high, sum_low, sum_high, prev, nxt, lined = room[:7]
        low1, high1, sum_low1, sum_high1, prev1, nxt1 = room[7:]

        def line(k, part):
            y, x = (lead_part(part), k) if x_first else (k, lead_part(part))
            return buf.at[y, x, pl.ds(r0, rn), pl.ds(c0, cn)]

        def one(k, part):
            off, size = row_part(rn, part)
            return lined.at[pl.ds(k, 1), pl.ds(off, size), :]

        def lined_part(ref):
            return lambda part: ref.at[lead_part(part)]

        def one_part(ref):
            def view(part):
                off, size = row_part(rn, part)
                return ref.at[:, pl.ds(off, size), :]

            return view

        room_a = (low, high, sum_low, sum_high, lined_part(prev), lined_part(nxt))
        room_b = (low1, high1, sum_low1, sum_high1, one_part(prev1), one_part(nxt1))
        yield from ring_scatter(links, place.ring("x" if x_first else "y"), line, room_a, lined, BF16)
        out = target.at[:, pl.ds(r0, rn), pl.ds(c0, cn)]
        yield from ring_scatter(links, place.ring("y" if x_first else "x"), one, room_b, out, F32)

    a, b = regions(rows, columns, by_rows)
    return half(a, rooms[:13], False), half(b, rooms[13:], True)


def line_scatter_room(rows, columns):
    low, high = row_part(rows, 0)[1], row_part(rows, 1)[1]
    return [pltpu.VMEM((1, low, columns), BF16), pltpu.VMEM((1, high, columns), BF16)] * 2 + [
        pltpu.VMEM((1, rows, columns), BF16)
    ] * 2


def line_scatter(links, place, buf, room, target):
    rows = buf.shape[1]

    def part(k, half):
        off, size = row_part(rows, half)
        return buf.at[pl.ds(k, 1), pl.ds(off, size), :]

    def view(ref):
        def cut(half):
            off, size = row_part(rows, half)
            return ref.at[:, pl.ds(off, size), :]

        return cut

    low, high, sum_low, sum_high, prev, nxt = room
    yield from ring_scatter(
        links, place.ring("z"), part, (low, high, sum_low, sum_high, view(prev), view(nxt)), target, F32
    )


def line_gather(links, place, buf):
    rows = buf.shape[1]

    def slot(k, half):
        off, size = row_part(rows, half)
        return buf.at[k, pl.ds(off, size)]

    yield from ring_gather(links, place.ring("z"), slot)


def line_swap(links, place, source, target):
    ring = place.ring("z")
    copies = []
    for other in (ring.next, ring.prev, ring.far):
        copies.append(links.copy(source.at[other], target.at[ring.own], ring.device(other)))
    target[ring.own] = source[ring.own]
    yield
    for copy in copies:
        copy.wait_recv()


COPIES = {"line_gather": 4, "line_swap": 3, "plane_gather": 16, "line_scatter": 6, "plane_scatter": 24}


def exchange(collective_id, ops):
    axes = []
    for name, _, _ in ops:
        for axis in ("x", "y") if name.startswith("plane") else ("z",):
            if axis not in axes:
                axes.append(axis)
    shapes, rooms = [], []
    for name, array, by_rows in ops:
        shape = array.shape
        if name == "line_gather":
            shapes.append(jax.ShapeDtypeStruct((4,) + shape, array.dtype))
            rooms.append([])
        elif name == "line_swap":
            shapes.append(jax.ShapeDtypeStruct(shape, array.dtype))
            rooms.append([])
        elif name == "plane_gather":
            shapes.append(jax.ShapeDtypeStruct((4, 4) + shape, array.dtype))
            rooms.append([])
        elif name == "line_scatter":
            shapes.append(jax.ShapeDtypeStruct((1,) + shape[1:], F32))
            rooms.append(line_scatter_room(*shape[1:]))
        else:
            shapes.append(jax.ShapeDtypeStruct((1,) + shape[2:], F32))
            rooms.append(plane_scatter_room(shape[2], shape[3], by_rows))
    count = sum(COPIES[name] for name, _, _ in ops)
    flat = [room for group in rooms for room in group]

    def kernel(*refs):
        n = len(ops)
        ins, outs, scratch = refs[:n], refs[n : 2 * n], list(refs[2 * n :])
        send, recv = scratch[-2:]
        place = Place()
        enter(place, axes)
        links = Links(send, recv)
        steps, at = [], 0
        for (name, _, by_rows), source, target, room in zip(ops, ins, outs, rooms):
            own = scratch[at : at + len(room)]
            at += len(room)
            if name == "line_gather":
                target[place.z] = source[...]
                steps.append(line_gather(links, place, target))
            elif name == "line_swap":
                steps.append(line_swap(links, place, source, target))
            elif name == "plane_gather":
                target[place.y, place.x] = source[...]
                steps += plane_gather(links, place, target, by_rows)
            elif name == "line_scatter":
                steps.append(line_scatter(links, place, source, own, target))
            else:
                steps += plane_scatter(links, place, source, own, target, by_rows)
        together(steps)
        links.finish()

    return pl.pallas_call(
        kernel,
        out_shape=tuple(shapes),
        in_specs=[VMEM] * len(ops),
        out_specs=tuple([VMEM] * len(ops)),
        scratch_shapes=flat + [pltpu.SemaphoreType.DMA((count,))] * 2,
        compiler_params=pltpu.CompilerParams(
            collective_id=collective_id, has_side_effects=True, vmem_limit_bytes=60 * MIB
        ),
        name="exchange_" + str(collective_id),
    )(*[array for _, array, _ in ops])


def gather_weights(collective_id, to_line, down, hidden, cotangent, desc):
    columns = to_line.shape[2]
    width = columns + down.shape[1]
    count = 3 + 16 + 4 + 4 + 4 + 16

    def kernel(line_ref, down_ref, hid_ref, cot_ref, desc_ref, w_ref, hids_ref, cots_ref, descs_ref, rows, lined, send, recv):
        place = Place()
        enter(place, ("x", "y", "z"))
        links = Links(send, recv)

        def weights():
            yield from line_swap(links, place, line_ref, rows)
            i = lax.broadcasted_iota(jnp.int32, (48, 64), 0)
            k = lax.broadcasted_iota(jnp.int32, (48, 64), 1)
            pick = (k == lax.div(i, 12) * 16 + lax.rem(i, 12)).astype(BF16)
            for c in range(0, columns, 768):
                block = rows[:, :, pl.ds(c, 768)].reshape(64, 768)
                packed = jnp.dot(pick, block, preferred_element_type=F32).astype(BF16)
                w_ref[place.y, place.x, :, pl.ds(c, 768)] = packed
            w_ref[place.y, place.x, :, pl.ds(columns, 768)] = down_ref[...]
            yield
            halves = plane_gather(links, place, w_ref, False)
            while True:
                live = 0
                for half in halves:
                    live += next(half, 1) is None
                if not live:
                    return
                yield

        def describe():
            lined[place.z] = desc_ref[...]
            yield from line_gather_small(links, place, lined)
            descs_ref[place.y, place.x] = lined[0] + lined[1] + lined[2] + lined[3]
            yield from plane_gather_small(links, place, descs_ref)

        hids_ref[place.z] = hid_ref[...]
        cots_ref[place.z] = cot_ref[...]
        together(
            [
                line_gather(links, place, hids_ref),
                weights(),
                describe(),
                line_gather(links, place, cots_ref),
            ]
        )
        links.finish()

    return pl.pallas_call(
        kernel,
        out_shape=(
            jax.ShapeDtypeStruct((4, 4, 48, width), BF16),
            jax.ShapeDtypeStruct((4,) + hidden.shape, BF16),
            jax.ShapeDtypeStruct((4,) + cotangent.shape, BF16),
            jax.ShapeDtypeStruct((4, 4) + desc.shape, jnp.int32),
        ),
        in_specs=[VMEM] * 5,
        out_specs=(VMEM,) * 4,
        scratch_shapes=[
            pltpu.VMEM((4, 16, columns), BF16),
            pltpu.VMEM((4,) + desc.shape, jnp.int32),
            pltpu.SemaphoreType.DMA((count,)),
            pltpu.SemaphoreType.DMA((count,)),
        ],
        compiler_params=pltpu.CompilerParams(
            collective_id=collective_id, has_side_effects=True, vmem_limit_bytes=60 * MIB
        ),
        name="gather_weights",
    )(to_line, down, hidden, cotangent, desc)


def small_gather(links, ring, slot):
    right = links.copy(slot(ring.own), slot(ring.own), ring.device(ring.next))
    left = links.copy(slot(ring.own), slot(ring.own), ring.device(ring.prev))
    yield
    right.wait_recv()
    left.wait_recv()
    on = links.copy(slot(ring.prev), slot(ring.prev), ring.device(ring.next))
    yield
    on.wait_recv()


def line_gather_small(links, place, buf):
    yield from small_gather(links, place.ring("z"), lambda k: buf.at[k])


def plane_gather_small(links, place, buf):
    yield from small_gather(links, place.ring("x"), lambda k: buf.at[place.y, k])
    yield from small_gather(links, place.ring("y"), lambda k: buf.at[k])


def attend_kernel(meta, q_ref, kv_ref, out_ref, lse_ref):
    row = lax.broadcasted_iota(jnp.int32, (SLAB, 1), 0)
    lane = lax.broadcasted_iota(jnp.int32, (SLAB, SLAB), 1)

    def slab(s, carry):
        pos_q = meta[s, 20] + row
        queries = [q_ref[s, :, pl.ds(j * 128, 128)] for j in range(3)]

        def fold(state, places, first):
            width = len(places) * SLAB
            pos_k = first + lax.broadcasted_iota(jnp.int32, (1, width), 1)
            allowed = pos_k <= pos_q
            out = []
            for j in range(3):
                top, total, acc = state[j]
                keys = jnp.concatenate([kv_ref[at, :, pl.ds(j * 128, 128)] for at in places], 0)
                scores = lax.dot_general(queries[j], keys, (((1,), (1,)), ((), ())), preferred_element_type=F32)
                scores = jnp.where(allowed, scores, LOW)
                new_top = jnp.maximum(top, jnp.max(scores, axis=1, keepdims=True))
                weights = jnp.exp(scores - new_top)
                decay = jnp.exp(top - new_top)
                total = total * decay + jnp.sum(weights, axis=1, keepdims=True)
                acc = acc * decay + jnp.dot(weights.astype(BF16), keys, preferred_element_type=F32)
                out.append((new_top, total, acc))
            return tuple(out)

        start = tuple(
            (jnp.full((SLAB, 1), LOW, F32), jnp.zeros((SLAB, 1), F32), jnp.zeros((SLAB, SLAB), F32)) for _ in range(3)
        )

        def prompt(c, state):
            return fold(state, [meta[s, c * 4 + a] for a in range(4)], c * 512)

        def own(c, state):
            return fold(state, [meta[s, 16], meta[s, 17]], 2048)

        state = lax.fori_loop(0, meta[s, 18], prompt, start)
        state = lax.fori_loop(0, meta[s, 19], own, state)
        heads = [acc / total for _, total, acc in state]
        out_ref[s, :, 0:128] = jnp.where(lane < 64, pltpu.roll(heads[0], 64, 1), heads[1]).astype(BF16)
        out_ref[s, :, 128:256] = jnp.where(lane < 64, pltpu.roll(heads[2], 64, 1), 0.0).astype(BF16)
        logs = [top + jnp.log(total) for top, total, _ in state]
        lse_ref[s] = jnp.where(lane == 0, logs[0], jnp.where(lane == 1, logs[1], logs[2]))
        return carry

    lax.fori_loop(0, 4, slab, 0)


def attend(meta, q, kv):
    return pl.pallas_call(
        attend_kernel,
        out_shape=(jax.ShapeDtypeStruct((4, SLAB, 256), BF16), jax.ShapeDtypeStruct((4, SLAB, SLAB), F32)),
        in_specs=[SMEM, VMEM, VMEM],
        out_specs=(VMEM, VMEM),
        compiler_params=pltpu.CompilerParams(vmem_limit_bytes=60 * MIB),
        name="attend",
    )(meta, q, kv)


def attend_back_kernel(meta, q_ref, kv_ref, grad_ref, stat_ref, dq_ref, dkv_ref, acc_ref):
    lane = lax.broadcasted_iota(jnp.int32, (SLAB, SLAB), 1)
    which = lax.broadcasted_iota(jnp.int32, (8, SLAB), 0)

    def clear(k, carry):
        acc_ref[k] = jnp.zeros((SLAB, 384), F32)
        return carry

    lax.fori_loop(0, 64, clear, 0)

    def slab(s, carry):
        pos_q = meta[s, 20] + lax.broadcasted_iota(jnp.int32, (1, SLAB), 1)
        table = stat_ref[s]
        stats = [jnp.sum(jnp.where(which == k, table, 0.0), axis=0, keepdims=True) for k in range(6)]
        first = grad_ref[s, :, 0:128].astype(F32)
        last = grad_ref[s, :, 128:256].astype(F32)
        right = [pltpu.roll(first, 64, 1), first, pltpu.roll(last, 64, 1)]
        pairs = []
        for j in range(3):
            grads = jnp.where(lane < 64, 0.0, right[j]).astype(BF16)
            pairs.append(jnp.concatenate([q_ref[s, :, pl.ds(j * 128, 128)], grads], 0))
        for j in range(3):
            dq_ref[s, :, pl.ds(j * 128, 128)] = jnp.zeros((SLAB, SLAB), F32)

        def fold(places, first_key):
            width = len(places) * SLAB
            pos_k = first_key + lax.broadcasted_iota(jnp.int32, (width, 1), 0)
            allowed = pos_k <= pos_q
            for j in range(3):
                keys = jnp.concatenate([kv_ref[at, :, pl.ds(j * 128, 128)] for at in places], 0)
                both = lax.dot_general(keys, pairs[j], (((1,), (1,)), ((), ())), preferred_element_type=F32)
                weights = jnp.where(allowed, jnp.exp(both[:, :128] - stats[j]), 0.0)
                slopes = (weights * (both[:, 128:] - stats[3 + j])).astype(BF16)
                terms = jnp.dot(
                    jnp.concatenate([slopes, weights.astype(BF16)], 1), pairs[j], preferred_element_type=F32
                )
                for n, at in enumerate(places):
                    acc_ref[at, :, pl.ds(j * 128, 128)] += terms[n * 128 : (n + 1) * 128]
                dq_ref[s, :, pl.ds(j * 128, 128)] += lax.dot_general(
                    slopes, keys, (((0,), (0,)), ((), ())), preferred_element_type=F32
                )

        def prompt(c, state):
            fold([meta[s, c * 4 + a] for a in range(4)], c * 512)
            return state

        def own(c, state):
            fold([meta[s, 16], meta[s, 17]], 2048)
            return state

        lax.fori_loop(0, meta[s, 18], prompt, 0)
        lax.fori_loop(0, meta[s, 19], own, 0)
        return carry

    lax.fori_loop(0, 4, slab, 0)

    def store(k, carry):
        dkv_ref[k] = acc_ref[k].astype(BF16)
        return carry

    lax.fori_loop(0, 64, store, 0)


def attend_back(meta, q, kv, grads, stats):
    return pl.pallas_call(
        attend_back_kernel,
        out_shape=(jax.ShapeDtypeStruct((4, SLAB, 384), F32), jax.ShapeDtypeStruct((64, SLAB, 384), BF16)),
        in_specs=[SMEM, VMEM, VMEM, VMEM, VMEM],
        out_specs=(VMEM, VMEM),
        scratch_shapes=[pltpu.VMEM((64, SLAB, 384), F32)],
        compiler_params=pltpu.CompilerParams(vmem_limit_bytes=60 * MIB),
        name="attend_back",
    )(meta, q, kv, grads, stats)


def dot(left, right):
    return jnp.dot(left, right, preferred_element_type=F32)


def dot_right_t(left, right):
    return lax.dot_general(left, right, (((1,), (1,)), ((), ())), preferred_element_type=F32)


def dot_left_t(left, right):
    return lax.dot_general(left, right, (((0,), (0,)), ((), ())), preferred_element_type=F32)


def split_columns(w):
    rows = w.shape[0]
    return w.reshape(rows, 2, 16, 2, 48).transpose(3, 1, 0, 2, 4).reshape(4, rows, 768)


def join_columns(w):
    rows = w.shape[1]
    return w.reshape(2, 2, rows, 16, 48).transpose(2, 1, 3, 0, 4).reshape(rows, 3072)


def describe_queries(descs, own):
    seg, base = descs[:, :4, 0].reshape(64), descs[:, :4, 1].reshape(64)
    seg_q = lax.dynamic_slice(seg, (own * 4,), (4,))
    base_q = lax.dynamic_slice(base, (own * 4,), (4,))
    slabs = jnp.arange(64, dtype=jnp.int32)
    n = jnp.arange(18, dtype=jnp.int32)
    want = jnp.where(n[None] < 16, (seg_q // (CONTS + 1) * (CONTS + 1))[:, None], seg_q[:, None])
    hit = (seg[None, None] == want[:, :, None]) & (base[None, None] == (n * SLAB)[None, :, None])
    places = jnp.sum(jnp.where(hit, slabs[None, None], 0), axis=-1).astype(jnp.int32)
    follows = seg_q % (CONTS + 1) != 0
    blocks = jnp.where(follows, 4, base_q // 512 + 1)
    return jnp.concatenate(
        [places, blocks[:, None], follows[:, None].astype(jnp.int32), base_q[:, None], jnp.zeros((4, 3), jnp.int32)], 1
    )


def turns(base):
    positions = (base[:, None] + jnp.arange(SLAB, dtype=jnp.int32)[None]).reshape(-1)
    frequency = 10000.0 ** (-jnp.arange(32, dtype=F32) * 2.0 / HD)
    angles = positions.astype(F32)[:, None] * frequency[None]
    cosine, sine = jnp.cos(angles), jnp.sin(angles)
    rest = jnp.ones((positions.shape[0], 64), F32)
    return (
        jnp.concatenate([cosine, cosine, rest], 1)[:, None],
        jnp.concatenate([-sine, sine, 0.0 * rest], 1)[:, None],
    )


def rotate(field, cosine, sine):
    rows = field.shape[0]
    pieces = field.reshape(rows, 6, 128)
    swapped = jnp.concatenate([pieces[..., 32:64], pieces[..., :32], pieces[..., 64:]], -1)
    return pieces * cosine + swapped * sine


def per_device(
    tokens, gain_one, w_query, w_key, w_value, w_out, gain_two, w_gate, w_up, w_down, cotangent, segment_ids, positions
):
    blk, head = lax.axis_index("blk"), lax.axis_index("head")
    z, own = head * 2 + blk // 16, blk % 16
    to_perm = jnp.asarray(TO_PERM, BF16)
    first_gain, second_gain = gain_one.astype(F32)[:, None], gain_two.astype(F32)[:, None]

    def by_head(w):
        return w.reshape(12, 4, 3, HD)

    raw_qkv = jnp.stack([by_head(w_query), jnp.zeros((12, 4, 3, HD), BF16), by_head(w_key), by_head(w_value)], 3)
    raw_qkv = raw_qkv.transpose(1, 0, 2, 3, 4).reshape(4, 12, 768)
    raw_ff = jnp.concatenate([split_columns(w_gate), split_columns(w_up)], 2)
    to_line = jnp.concatenate(
        [
            (raw_qkv * first_gain).astype(BF16),
            (raw_ff * second_gain).astype(BF16),
            jnp.broadcast_to(w_out[None], (4, 12, 768)),
        ],
        2,
    )
    to_line = jnp.pad(to_line, ((0, 0), (0, 4), (0, 0)))
    seg_own = lax.dynamic_slice(segment_ids, (head * SLAB,), (1,))[0]
    base_own = lax.dynamic_slice(positions, (head * SLAB,), (1,))[0]
    row = lax.broadcasted_iota(jnp.int32, (8, SLAB), 0)
    lane = lax.broadcasted_iota(jnp.int32, (8, SLAB), 1)
    desc = jnp.where(row == z, jnp.where(lane == 0, seg_own, jnp.where(lane == 1, base_own, 0)), 0)

    inputs = tokens.astype(F32)
    scale_one = lax.rsqrt(jnp.mean(inputs * inputs, axis=-1, keepdims=True) + EPS)
    normed_one = inputs * scale_one
    normed_one_perm = dot(normed_one.astype(BF16), to_perm).astype(BF16)

    weights, line_one, line_cot, descs = gather_weights(0, to_line, w_down, normed_one_perm, cotangent, desc)
    weights = weights.reshape(768, 3840)
    line_one = line_one.reshape(512, 768)
    line_cot = line_cot.reshape(512, 768)
    w_qkv, w_ff, w_o, w_d = weights[:, :768], weights[:, 768:2304], weights[:, 2304:3072], weights[:, 3072:]
    descs = descs.reshape(16, 8, SLAB)
    meta = describe_queries(descs, own)
    cosine, sine = turns(meta[:, 20])

    qkv = rotate(dot(line_one, w_qkv), cosine, sine).reshape(512, 3, 2, 128)
    q = (qkv[:, :, 0] * 0.125).astype(BF16).reshape(4, SLAB, 384)
    kv_own = qkv[:, :, 1].astype(BF16).reshape(512, 384)
    (kv,) = exchange(1, [("plane_gather", kv_own, True)])
    kv = kv.reshape(64, SLAB, 384)
    heads_out, lse = attend(meta, q, kv)

    (attended,) = exchange(2, [("line_swap", heads_out, None)])
    attended = attended[:, :, :192].transpose(1, 0, 2).reshape(SLAB, 768)
    attended_perm = dot(attended, to_perm).astype(BF16)
    middle = inputs + dot(attended_perm, w_o)
    scale_two = lax.rsqrt(jnp.mean(middle * middle, axis=-1, keepdims=True) + EPS)
    normed_two = middle * scale_two
    normed_two_perm = dot(normed_two.astype(BF16), to_perm).astype(BF16)
    (line_two,) = exchange(3, [("line_gather", normed_two_perm, None)])
    line_two = line_two.reshape(512, 768)

    pre = dot(line_two, w_ff)
    gate_pre, up_pre = pre[:, :768], pre[:, 768:]
    sigmoid_gate = jax.nn.sigmoid(gate_pre)
    silu_gate = gate_pre * sigmoid_gate
    activated = (silu_gate * up_pre).astype(BF16)
    out_part = dot(activated, w_d).astype(BF16).reshape(4, SLAB, 768)
    grad_act = dot_right_t(line_cot, w_d)
    grad_gate = grad_act * up_pre * (sigmoid_gate * (1.0 + gate_pre * (1.0 - sigmoid_gate)))
    grad_pre = jnp.concatenate([grad_gate, grad_act * silu_gate], 1).astype(BF16)
    back_part = dot_right_t(grad_pre, w_ff).astype(BF16).reshape(4, SLAB, 768)
    ff_grads = jnp.concatenate([dot_left_t(line_two, grad_pre), dot_left_t(activated, line_cot)], 1).astype(BF16)
    back_sum, out_sum, ff_sum = exchange(
        4,
        [
            ("line_scatter", back_part, None),
            ("line_scatter", out_part, None),
            ("plane_scatter", ff_grads.reshape(4, 4, 48, 2304), False),
        ],
    )
    output = (middle + out_sum[0]).astype(BF16)

    grad_normed = dot_right_t(back_sum[0].astype(BF16), to_perm)
    grad_middle = cotangent.astype(F32) + scale_two * (
        grad_normed - normed_two * jnp.mean(grad_normed * normed_two, axis=-1, keepdims=True)
    )
    grad_low = grad_middle.astype(BF16)
    grad_attended = dot_right_t(dot_right_t(grad_low, w_o).astype(BF16), to_perm).astype(BF16)
    out_grad = dot_left_t(attended_perm, grad_low).astype(BF16).reshape(4, 4, 48, 768)
    to_heads = jnp.pad(grad_attended.reshape(SLAB, 4, 192).transpose(1, 0, 2), ((0, 0), (0, 0), (0, 64)))
    grad_heads, out_plane = exchange(5, [("line_swap", to_heads, None), ("plane_scatter", out_grad, False)])

    delta = (grad_heads.astype(F32) * heads_out.astype(F32))[:, :, :192].reshape(4, SLAB, 3, HD).sum(-1)
    stats = jnp.concatenate([lse[:, :, :3], delta, jnp.zeros((4, SLAB, 2), F32)], 2).transpose(0, 2, 1)
    dq, dkv = attend_back(meta, q, kv, grad_heads, stats)
    (dkv_own,) = exchange(6, [("plane_scatter", dkv.reshape(4, 4, 512, 384), True)])

    pieces = jnp.concatenate([dq.reshape(512, 3, 1, 128) * 0.125, dkv_own.reshape(512, 3, 1, 128)], 2)
    pieces = rotate(pieces.reshape(512, 768), cosine, -sine).reshape(512, 3, 2, 2, HD)
    blank = jnp.asarray(np.array([[1.0, 0.0], [1.0, 1.0]], np.float32))[None, None, :, :, None]
    grad_qkv = jnp.where(blank > 0, pieces, 0.0).astype(BF16).reshape(512, 768)
    one_part = dot_right_t(grad_qkv, w_qkv).astype(BF16).reshape(4, SLAB, 768)
    qkv_grads = dot_left_t(line_one, grad_qkv).astype(BF16).reshape(4, 4, 48, 768)
    one_sum, qkv_plane = exchange(7, [("line_scatter", one_part, None), ("plane_scatter", qkv_grads, False)])

    grad_normed = dot_right_t(one_sum[0].astype(BF16), to_perm)
    input_grad = grad_middle + scale_one * (
        grad_normed - normed_one * jnp.mean(grad_normed * normed_one, axis=-1, keepdims=True)
    )

    to_rows = jnp.concatenate([qkv_plane[0], ff_sum[0, :, :1536], out_plane[0]], 1).reshape(4, 12, 3072)
    to_rows = jnp.pad(to_rows, ((0, 0), (0, 4), (0, 0)))
    (from_line,) = exchange(8, [("line_swap", to_rows, None)])
    from_line = from_line[:, :12]
    got_qkv, got_ff, got_out = from_line[:, :, :768], from_line[:, :, 768:2304], from_line[:, :, 2304:]
    by_kind = got_qkv.reshape(4, 12, 3, 4, HD).transpose(3, 1, 0, 2, 4).reshape(4, 12, 768)
    gain_one_grad = jnp.sum(got_qkv * raw_qkv.astype(F32), axis=(0, 2))
    gain_two_grad = jnp.sum(got_ff * raw_ff.astype(F32), axis=(0, 2))
    return (
        output,
        input_grad,
        gain_one_grad,
        by_kind[0] * first_gain,
        by_kind[2] * first_gain,
        by_kind[3] * first_gain,
        jnp.sum(got_out, axis=0),
        gain_two_grad,
        join_columns(got_ff[:, :, :768]) * second_gain,
        join_columns(got_ff[:, :, 768:]) * second_gain,
        ff_sum[0, :, 1536:],
    )


def solution(mesh):
    rows = P(("grp", "blk", "head"), None)
    flat = P(("grp", "blk", "head"))
    weight = P(("blk", "head"), None)
    gain = P(("blk", "head"))
    ids = P(("grp", "blk"))
    in_specs = (rows, gain, weight, weight, weight, weight, gain, weight, weight, weight, rows, ids, ids)
    out_specs = (rows, rows, flat, rows, rows, rows, rows, flat, rows, rows, rows)
    return jax.shard_map(per_device, mesh=mesh, in_specs=in_specs, out_specs=out_specs, check_vma=False)
```

```python
import functools

import jax
import jax.numpy as jnp
import numpy as np
from jax import lax
from jax.experimental import pallas as pl
from jax.experimental.pallas import tpu as pltpu
from jax.sharding import PartitionSpec as P

MESH = pl.DeviceIdType.MESH
F32 = jnp.float32
BF16 = jnp.bfloat16
HD = 64
CONTS = 8
SLAB = 128
LOW = -1e30
EPS = 1e-05
LANES = (((1,), (1,)), ((), ()))
HIGHEST = lax.Precision.HIGHEST
MIB = 1 << 20
VMEM = pl.BlockSpec(memory_space=pltpu.VMEM)
SMEM = pl.BlockSpec(memory_space=pltpu.SMEM)


def feature_order():
    place = np.arange(768)
    p, z, r = place // 48, place // 12 % 4, place % 12
    t = (z % 2) * 32 + p * 2 + z // 2
    return t * 12 + r


ORDER = feature_order()
TO_PERM = np.zeros((768, 768), np.float32)
TO_PERM[ORDER, np.arange(768)] = 1.0


LANE_FREQUENCY = 10000.0 ** (-(np.arange(128) % 32) * 2.0 / HD) * (np.arange(128) < HD)
FREQUENCY = LANE_FREQUENCY.astype(np.float32)
OFFSET_ANGLES = np.arange(SLAB)[:, None] * LANE_FREQUENCY[None]
OFFSET_TURNS = np.stack([np.cos(OFFSET_ANGLES), np.sin(OFFSET_ANGLES)]).astype(np.float32)


class Place:
    def __init__(self):
        self.core = lax.axis_index("grp")
        blk = lax.axis_index("blk")
        self.x = lax.rem(blk, 4)
        self.y = lax.rem(lax.div(blk, 4), 4)
        self.z = lax.axis_index("head") * 2 + lax.div(blk, 16)

    def device(self, x=None, y=None, z=None):
        x = self.x if x is None else x
        y = self.y if y is None else y
        z = self.z if z is None else z
        return (self.core, lax.rem(z, 2) * 16 + y * 4 + x, lax.div(z, 2))

    def ring(self, axis):
        return Ring(self, axis)


class Ring:
    def __init__(self, place, axis):
        self.place, self.axis = place, axis
        self.own = getattr(place, axis)
        self.next = lax.rem(self.own + 1, 4)
        self.prev = lax.rem(self.own + 3, 4)
        self.far = lax.rem(self.own + 2, 4)

    def device(self, index):
        return self.place.device(**{self.axis: index})


def enter(place, axes):
    barrier = pltpu.get_barrier_semaphore()
    partners = []
    for axis in axes:
        ring = place.ring(axis)
        partners += [ring.device(ring.next), ring.device(ring.prev)]
        if axis == "z":
            partners.append(ring.device(ring.far))
    for partner in partners:
        pl.semaphore_signal(barrier, inc=1, device_id=partner, device_id_type=MESH)
    pl.semaphore_wait(barrier, len(partners))


class Links:
    def __init__(self, send, recv):
        self.send, self.recv, self.used, self.sent = send, recv, 0, []

    def copy(self, source, target, device):
        k = self.used
        self.used += 1
        copy = pltpu.make_async_remote_copy(
            src_ref=source,
            dst_ref=target,
            send_sem=self.send.at[k],
            recv_sem=self.recv.at[k],
            device_id=device,
            device_id_type=MESH,
        )
        copy.start()
        self.sent.append(copy)
        return copy

    def finish(self):
        for copy in self.sent:
            copy.wait_send()


def together(steps):
    steps = list(steps)
    while steps:
        left = []
        for step in steps:
            try:
                next(step)
                left.append(step)
            except StopIteration:
                pass
        steps = left


def ring_gather(links, ring, slot):
    right = links.copy(slot(ring.own, None), slot(ring.own, None), ring.device(ring.next))
    left = links.copy(slot(ring.own, None), slot(ring.own, None), ring.device(ring.prev))
    yield
    right.wait_recv()
    on_right = links.copy(slot(ring.prev, 0), slot(ring.prev, 0), ring.device(ring.next))
    left.wait_recv()
    on_left = links.copy(slot(ring.next, 1), slot(ring.next, 1), ring.device(ring.prev))
    yield
    on_right.wait_recv()
    on_left.wait_recv()


def add_into(target, terms, kind):
    lead, rows, columns = target.shape
    step = 16
    for size in (128, 64, 48, 32):
        if rows % size == 0 and size * columns <= 48 * 1024:
            step = size
            break
    count = rows // step

    def body(k, carry):
        i, r = lax.div(k, count), pl.multiple_of(lax.rem(k, count) * step, step)
        total = terms[0][i, pl.ds(r, step), :].astype(F32)
        for term in terms[1:]:
            total = total + term[i, pl.ds(r, step), :].astype(F32)
        target[i, pl.ds(r, step), :] = total.astype(kind)
        return carry

    lax.fori_loop(0, lead * count, body, 0)


def ring_scatter(links, ring, part, room, target, kind):
    low, high, sum_low, sum_high, from_prev, from_next = room
    nxt, prv = ring.device(ring.next), ring.device(ring.prev)
    far_low = links.copy(part(ring.far, 0), low, nxt)
    far_high = links.copy(part(ring.far, 1), high, prv)
    next_high = links.copy(part(ring.next, 1), from_prev(1), nxt)
    prev_low = links.copy(part(ring.prev, 0), from_next(0), prv)
    yield
    far_low.wait_recv()
    add_into(sum_low, [part(ring.next, 0), low], BF16)
    next_low = links.copy(sum_low, from_prev(0), nxt)
    far_high.wait_recv()
    add_into(sum_high, [part(ring.prev, 1), high], BF16)
    prev_high = links.copy(sum_high, from_next(1), prv)
    yield
    for copy in (next_high, prev_low, next_low, prev_high):
        copy.wait_recv()
    add_into(target, [part(ring.own, None), from_prev(None), from_next(None)], kind)


def lead_part(part):
    return pl.ds(0, 4) if part is None else pl.ds(2 * part, 2)


def row_part(rows, part):
    first = (rows // 2 + 15) // 16 * 16
    if part is None:
        return 0, rows
    return (0, first) if part == 0 else (first, rows - first)


def regions(rows, columns, by_rows):
    if by_rows:
        return [(0, rows // 2, 0, columns), (rows // 2, rows // 2, 0, columns)]
    return [(0, rows, 0, columns // 2), (0, rows, columns // 2, columns // 2)]


def plane_gather(links, place, buf, by_rows):
    rows, columns = buf.shape[2:]

    def half(region, x_first):
        r0, rn, c0, cn = region

        def one(k, part):
            off, size = row_part(rn, part)
            y, x = (place.y, k) if x_first else (k, place.x)
            return buf.at[y, x, pl.ds(r0 + off, size), pl.ds(c0, cn)]

        def line(k, part):
            y, x = (k, lead_part(part)) if x_first else (lead_part(part), k)
            return buf.at[y, x, pl.ds(r0, rn), pl.ds(c0, cn)]

        yield from ring_gather(links, place.ring("x" if x_first else "y"), one)
        yield from ring_gather(links, place.ring("y" if x_first else "x"), line)

    a, b = regions(rows, columns, by_rows)
    return half(a, True), half(b, False)


def plane_scatter_room(rows, columns, by_rows):
    rooms = []
    for _, rn, _, cn in regions(rows, columns, by_rows):
        rooms += [pltpu.VMEM((2, rn, cn), BF16)] * 4 + [pltpu.VMEM((4, rn, cn), BF16)] * 3
        low, high = row_part(rn, 0)[1], row_part(rn, 1)[1]
        rooms += [pltpu.VMEM((1, low, cn), BF16), pltpu.VMEM((1, high, cn), BF16)] * 2
        rooms += [pltpu.VMEM((1, rn, cn), BF16)] * 2
    return rooms


def plane_scatter(links, place, buf, rooms, target, by_rows):
    rows, columns = buf.shape[2:]

    def half(region, room, x_first):
        r0, rn, c0, cn = region
        low, high, sum_low, sum_high, prev, nxt, lined = room[:7]
        low1, high1, sum_low1, sum_high1, prev1, nxt1 = room[7:]

        def line(k, part):
            y, x = (lead_part(part), k) if x_first else (k, lead_part(part))
            return buf.at[y, x, pl.ds(r0, rn), pl.ds(c0, cn)]

        def one(k, part):
            off, size = row_part(rn, part)
            return lined.at[pl.ds(k, 1), pl.ds(off, size), :]

        def lined_part(ref):
            return lambda part: ref.at[lead_part(part)]

        def one_part(ref):
            def view(part):
                off, size = row_part(rn, part)
                return ref.at[:, pl.ds(off, size), :]

            return view

        room_a = (low, high, sum_low, sum_high, lined_part(prev), lined_part(nxt))
        room_b = (low1, high1, sum_low1, sum_high1, one_part(prev1), one_part(nxt1))
        yield from ring_scatter(links, place.ring("x" if x_first else "y"), line, room_a, lined, BF16)
        out = target.at[:, pl.ds(r0, rn), pl.ds(c0, cn)]
        yield from ring_scatter(links, place.ring("y" if x_first else "x"), one, room_b, out, F32)

    a, b = regions(rows, columns, by_rows)
    return half(a, rooms[:13], False), half(b, rooms[13:], True)


def line_scatter_room(rows, columns):
    low, high = row_part(rows, 0)[1], row_part(rows, 1)[1]
    return [pltpu.VMEM((1, low, columns), BF16), pltpu.VMEM((1, high, columns), BF16)] * 2 + [
        pltpu.VMEM((1, rows, columns), BF16)
    ] * 2


def line_scatter(links, place, buf, room, target):
    rows = buf.shape[1]

    def part(k, half):
        off, size = row_part(rows, half)
        return buf.at[pl.ds(k, 1), pl.ds(off, size), :]

    def view(ref):
        def cut(half):
            off, size = row_part(rows, half)
            return ref.at[:, pl.ds(off, size), :]

        return cut

    low, high, sum_low, sum_high, prev, nxt = room
    yield from ring_scatter(
        links, place.ring("z"), part, (low, high, sum_low, sum_high, view(prev), view(nxt)), target, F32
    )


def line_gather(links, place, buf):
    rows = buf.shape[1]

    def slot(k, half):
        off, size = row_part(rows, half)
        return buf.at[k, pl.ds(off, size)]

    yield from ring_gather(links, place.ring("z"), slot)


def line_swap(links, place, source, target):
    ring = place.ring("z")
    copies = []
    for other in (ring.next, ring.prev, ring.far):
        copies.append(links.copy(source.at[other], target.at[ring.own], ring.device(other)))
    target[ring.own] = source[ring.own]
    yield
    for copy in copies:
        copy.wait_recv()


def small_gather(links, ring, slot):
    right = links.copy(slot(ring.own), slot(ring.own), ring.device(ring.next))
    left = links.copy(slot(ring.own), slot(ring.own), ring.device(ring.prev))
    yield
    right.wait_recv()
    left.wait_recv()
    on = links.copy(slot(ring.prev), slot(ring.prev), ring.device(ring.next))
    yield
    on.wait_recv()


def advance(*steps):
    for step in steps:
        next(step, None)


def finish(*steps):
    together(steps)


def dot(left, right):
    return jnp.dot(left, right, preferred_element_type=F32)


def dot_right_t(left, right):
    return lax.dot_general(left, right, (((1,), (1,)), ((), ())), preferred_element_type=F32)


def pack_rows():
    i = lax.broadcasted_iota(jnp.int32, (48, 64), 0)
    k = lax.broadcasted_iota(jnp.int32, (48, 64), 1)
    return (k == lax.div(i, 12) * 16 + lax.rem(i, 12)).astype(BF16)


def spread_rows():
    k = lax.broadcasted_iota(jnp.int32, (64, 48), 0)
    i = lax.broadcasted_iota(jnp.int32, (64, 48), 1)
    return (k == lax.div(i, 12) * 16 + lax.rem(i, 12)).astype(BF16)


def merged(ref):
    rows, columns = ref.shape[0] * ref.shape[1] * ref.shape[2], ref.shape[3]
    return ref[...].reshape(rows, columns)


def mean_square(values):
    return jnp.mean(values * values, axis=-1, keepdims=True)


def norm_back(grad, normed, scale):
    return scale * (grad - normed * jnp.mean(grad * normed, axis=-1, keepdims=True))


def slab_turns(line_ref, turn_ref, s):
    rows = line_ref[s]
    cos_base, sin_base = rows[0:1], rows[1:2]
    cos_off, sin_off = turn_ref[0], turn_ref[1]
    lane = lax.broadcasted_iota(jnp.int32, (SLAB, SLAB), 1)
    sign = jnp.where(lane < 32, -1.0, jnp.where(lane < 64, 1.0, 0.0))
    return cos_base * cos_off - sin_base * sin_off, (sin_base * cos_off + cos_base * sin_off) * sign


def turned(field, cosine, sine):
    lane = lax.broadcasted_iota(jnp.int32, (SLAB, SLAB), 1)
    return field * cosine + jnp.where(lane < 32, pltpu.roll(field, 96, 1), pltpu.roll(field, 32, 1)) * sine


def front_kernel(
    tok_ref, w_ref, gain_ref, perm_ref, turn_ref, desc_ref,
    kv_ref, q_ref, wqkv_ref, wo_ref, one_ref, meta_ref, line_ref,
    for_line, for_line_o, rows, rows_o, descs, send, recv,
):
    place = Place()
    enter(place, ("x", "y", "z"))
    links = Links(send, recv)
    own = place.y * 4 + place.x

    line_ref[place.z] = desc_ref[...]
    lined = small_gather(links, place.ring("z"), lambda k: line_ref.at[k])

    w = w_ref[...].astype(F32)
    gain = gain_ref[:, 0:1]
    none = jnp.zeros((16, HD), F32)
    for z in range(4):
        pieces = []
        for j in range(3):
            c = 192 * z + 64 * j
            pieces += [w[:, c : c + 64] * gain, none, w[:, 768 + c : 832 + c] * gain, w[:, 1536 + c : 1600 + c] * gain]
        for_line[z] = jnp.concatenate(pieces, 1).astype(BF16)
        rows_o[z] = jnp.zeros((16, 768), BF16)
    for_line_o[...] = w_ref[:, pl.ds(2304, 768)]
    swap = line_swap(links, place, for_line, rows)
    advance(swap, lined)

    x = dot(tok_ref[...], perm_ref[...])
    one_ref[place.z] = (x * lax.rsqrt(mean_square(x) + EPS)).astype(BF16)
    ones = line_gather(links, place, one_ref)
    advance(ones)
    rows_o[place.z] = for_line_o[...]
    o_line = small_gather(links, place.ring("z"), lambda k: rows_o.at[k])
    finish(swap)
    wqkv_ref[place.y, place.x] = dot(pack_rows(), rows[...].reshape(64, 768)).astype(BF16)
    qkv_a, qkv_b = plane_gather(links, place, wqkv_ref, False)
    advance(qkv_a, qkv_b, lined, ones, o_line)
    advance(qkv_a, qkv_b, lined)
    finish(lined)
    total = line_ref[0] + line_ref[1] + line_ref[2] + line_ref[3]
    descs[place.y, place.x] = total
    desc_x = small_gather(links, place.ring("x"), lambda k: descs.at[place.y, k])
    desc_y = small_gather(links, place.ring("y"), lambda k: descs.at[k])
    advance(desc_x)
    advance(qkv_a, qkv_b, o_line, ones)
    finish(o_line)
    wo_ref[place.y, place.x] = dot(pack_rows(), rows_o[...].reshape(64, 768)).astype(BF16)
    finish(qkv_a, qkv_b, ones)
    o_a, o_b = plane_gather(links, place, wo_ref, False)

    halves = plane_gather(links, place, kv_ref, True)
    for half in range(2):
        lines = one_ref[2 * half : 2 * half + 2].reshape(256, 768)
        field = dot(lines, merged(wqkv_ref))
        for k in range(2):
            s = 2 * half + k
            cosine, sine = slab_turns(line_ref, turn_ref, s)
            for j in range(3):
                query = turned(field[k * SLAB : (k + 1) * SLAB, 256 * j : 256 * j + 128], cosine, sine)
                q_ref[s, :, pl.ds(128 * j, 128)] = (query * 0.125).astype(BF16)
                pair = turned(field[k * SLAB : (k + 1) * SLAB, 256 * j + 128 : 256 * j + 256], cosine, sine)
                kv_ref[place.y, place.x, pl.ds(s * SLAB, SLAB), pl.ds(128 * j, 128)] = pair.astype(BF16)
        advance(halves[half])
    advance(o_a, o_b)
    finish(desc_x)
    advance(desc_y)
    advance(*halves)
    advance(o_a, o_b)
    advance(desc_y)
    advance(*halves)
    finish(desc_y)

    table = jnp.zeros((8, SLAB), F32)
    for y in range(4):
        for x in range(4):
            table = table + descs[y, x]
    seg, base = table[2:3], table[3:4]
    lane = lax.broadcasted_iota(jnp.int32, (1, SLAB), 1)
    lane_at = lane.astype(F32)
    n = lax.broadcasted_iota(jnp.int32, (24, 1), 0)
    for s in range(4):
        mine = lane == own * 4 + s
        seg_q = jnp.sum(jnp.where(mine, seg, 0.0), axis=1, keepdims=True)
        base_q = jnp.sum(jnp.where(mine, base, 0.0), axis=1, keepdims=True)
        prompt = jnp.where(seg_q >= CONTS + 1.0, CONTS + 1.0, 0.0)
        want = jnp.where(n < 16, prompt, seg_q)
        hit = (seg == want) & (base == n.astype(F32) * SLAB) & (lane < 64)
        places = jnp.sum(jnp.where(hit, lane_at, 0.0), axis=1, keepdims=True)
        follows = jnp.where(seg_q == prompt, 0.0, 1.0)
        blocks = jnp.where(seg_q == prompt, jnp.floor(base_q * (1.0 / 512.0)) + 1.0, 4.0)
        listed = jnp.where(n == 18, blocks, jnp.where(n == 19, follows, jnp.where(n == 20, base_q, places)))
        meta_ref[pl.ds(s * 24, 24), :] = jnp.broadcast_to(listed, (24, SLAB)).astype(jnp.int32)

    together([*halves, o_a, o_b])
    links.finish()


def front(collective_id, tokens, w, gain, perm, turn, desc):
    return pl.pallas_call(
        front_kernel,
        out_shape=(
            jax.ShapeDtypeStruct((4, 4, 512, 384), BF16),
            jax.ShapeDtypeStruct((4, SLAB, 384), BF16),
            jax.ShapeDtypeStruct((4, 4, 48, 768), BF16),
            jax.ShapeDtypeStruct((4, 4, 48, 768), BF16),
            jax.ShapeDtypeStruct((4, SLAB, 768), BF16),
            jax.ShapeDtypeStruct((96, SLAB), jnp.int32),
            jax.ShapeDtypeStruct((4, 8, SLAB), F32),
        ),
        in_specs=[VMEM] * 6,
        out_specs=(VMEM,) * 7,
        scratch_shapes=[
            pltpu.VMEM((4, 16, 768), BF16),
            pltpu.VMEM((16, 768), BF16),
            pltpu.VMEM((4, 16, 768), BF16),
            pltpu.VMEM((4, 16, 768), BF16),
            pltpu.VMEM((4, 4, 8, SLAB), F32),
            pltpu.SemaphoreType.DMA((72,)),
            pltpu.SemaphoreType.DMA((72,)),
        ],
        compiler_params=pltpu.CompilerParams(
            collective_id=collective_id, has_side_effects=True, vmem_limit_bytes=60 * MIB
        ),
        name="front",
    )(tokens, w, gain, perm, turn, desc)


def middle_kernel(
    att_ref, tok_ref, cot_ref, wo_ref, w_ref, gain_ref, down_ref, perm_ref, perm_att_ref,
    out_ref, gm_ref, grads_ref, ff_ref, og_ref,
    atts, cots, for_line, rows, wff, two, mid_s, att_s, act, pre, two_t, act_t, part_out, part_back, sum_out, sum_back,
    ff_part, og_part, to_heads, *rest,
):
    send, recv = rest[-2:]
    rooms = list(rest[:-2])
    back_room, rooms = rooms[:6], rooms[6:]
    out_room, rooms = rooms[:6], rooms[6:]
    ff_room, og_room = rooms[:26], rooms[26:]
    place = Place()
    enter(place, ("x", "y", "z"))
    links = Links(send, recv)

    att_swap = line_swap(links, place, att_ref, atts)
    advance(att_swap)
    cots[place.z] = cot_ref[...]
    cot_gather = line_gather(links, place, cots)
    advance(cot_gather)

    gain = gain_ref[:, 0:1]
    for z in range(4):
        for k in range(2):
            pieces = []
            for p in range(16):
                c = 3072 * k + ((z % 2) * 32 + p * 2 + z // 2) * 48
                pieces.append(w_ref[:, c : c + 48].astype(F32) * gain)
            for_line[z, :, pl.ds(768 * k, 768)] = jnp.concatenate(pieces, 1).astype(BF16)
    w_swap = line_swap(links, place, for_line, rows)
    advance(w_swap)
    finish(att_swap)

    att = dot(atts[0], perm_att_ref[pl.ds(0, 256), :])
    for z in range(1, 4):
        att = att + dot(atts[z], perm_att_ref[pl.ds(256 * z, 256), :])
    att_s[...] = att.astype(BF16)
    mid_s[...] = tok_ref[...].astype(F32) + dot(att_s[...], merged(wo_ref))
    middle = mid_s[...]
    scale_two = lax.rsqrt(mean_square(middle) + EPS)
    two[place.z] = dot((middle * scale_two).astype(BF16), perm_ref[...]).astype(BF16)
    two_gather = line_gather(links, place, two)
    advance(cot_gather, two_gather)
    finish(w_swap)
    for c in range(0, 1536, 768):
        wff[place.y, place.x, :, pl.ds(c, 768)] = dot(
            pack_rows(), rows[:, :, pl.ds(c, 768)].reshape(64, 768)
        ).astype(BF16)
    wff[place.y, place.x, :, pl.ds(1536, 768)] = down_ref[...]
    w_a, w_b = plane_gather(links, place, wff, False)
    advance(w_a, w_b, cot_gather, two_gather)
    together([w_a, w_b, cot_gather, two_gather])

    def block(r, carry):
        at = pl.ds(pl.multiple_of(r * 256, 256), 256)
        two_b = two[pl.ds(r * 2, 2)].reshape(256, 768)
        cot_b = cots[pl.ds(r * 2, 2)].reshape(256, 768)
        gate_w = wff[:, :, :, pl.ds(0, 768)].reshape(768, 768)
        up_w = wff[:, :, :, pl.ds(768, 768)].reshape(768, 768)
        down_w = wff[:, :, :, pl.ds(1536, 768)].reshape(768, 768)
        gate = dot(two_b, gate_w)
        up = dot(two_b, up_w)
        sig = 1.0 / (1.0 + jnp.exp(-gate))
        silu = gate * sig
        act_b = (silu * up).astype(BF16)
        act[at, :] = act_b
        grad_act = dot_right_t(cot_b, down_w)
        grad_gate = (grad_act * up * (sig * (1.0 + gate * (1.0 - sig)))).astype(BF16)
        grad_up = (grad_act * silu).astype(BF16)
        pre[at, pl.ds(0, 768)] = grad_gate
        pre[at, pl.ds(768, 768)] = grad_up
        back = dot_right_t(grad_gate, gate_w) + dot_right_t(grad_up, up_w)
        part_back[pl.ds(r * 2, 2)] = back.astype(BF16).reshape(2, SLAB, 768)
        part_out[pl.ds(r * 2, 2)] = dot(act_b, down_w).astype(BF16).reshape(2, SLAB, 768)
        return carry

    lax.fori_loop(0, 2, block, 0)
    back_sum = line_scatter(links, place, part_back, back_room, sum_back)
    out_sum = line_scatter(links, place, part_out, out_room, sum_out)
    advance(back_sum)
    two_t[...] = two[...].reshape(512, 768).T

    def first_grads(c, carry):
        at = pl.ds(pl.multiple_of(c * 256, 256), 256)
        ff_part[:, :, :, at] = dot(two_t[...], pre[:, at]).astype(BF16).reshape(4, 4, 48, 256)
        return carry

    def last_grads(c, carry):
        at = pl.ds(pl.multiple_of(c * 256, 256), 256)
        to = pl.ds(pl.multiple_of(1536 + c * 256, 256), 256)
        cot_all = cots[:, :, at].reshape(512, 256)
        ff_part[:, :, :, to] = dot(act_t[...], cot_all).astype(BF16).reshape(4, 4, 48, 256)
        return carry

    lax.fori_loop(0, 3, first_grads, 0)
    advance(back_sum)
    lax.fori_loop(3, 6, first_grads, 0)
    act_t[...] = act[...].T
    lax.fori_loop(0, 3, last_grads, 0)
    ff_a, ff_b = plane_scatter(links, place, ff_part, ff_room, ff_ref, False)
    advance(ff_a, ff_b)
    finish(back_sum)
    advance(out_sum)

    grad = dot_right_t(sum_back[0].astype(BF16), perm_ref[...])
    middle = mid_s[...]
    scale_two = lax.rsqrt(mean_square(middle) + EPS)
    gm_ref[...] = cot_ref[...].astype(F32) + norm_back(grad, middle * scale_two, scale_two)
    low = gm_ref[...].astype(BF16)
    grad_att = dot_right_t(low, merged(wo_ref)).astype(BF16)
    for z in range(4):
        to_heads[z] = dot_right_t(grad_att, perm_att_ref[pl.ds(256 * z, 256), :]).astype(BF16)
    heads_swap = line_swap(links, place, to_heads, grads_ref)
    advance(heads_swap)
    advance(ff_a, ff_b, out_sum)
    og_part[...] = dot(att_s[...].T, low).astype(BF16).reshape(4, 4, 48, 768)
    og_a, og_b = plane_scatter(links, place, og_part, og_room, og_ref, False)
    advance(og_a, og_b)
    together([ff_a, ff_b, out_sum, heads_swap, og_a, og_b])
    out_ref[...] = (mid_s[...] + sum_out[0]).astype(BF16)
    links.finish()


def middle(collective_id, att, tokens, cotangent, w_o, w, gain, down, perm, perm_att):
    line = pltpu.VMEM((4, SLAB, 768), BF16)
    return pl.pallas_call(
        middle_kernel,
        out_shape=(
            jax.ShapeDtypeStruct((SLAB, 768), BF16),
            jax.ShapeDtypeStruct((SLAB, 768), F32),
            jax.ShapeDtypeStruct((4, SLAB, 256), BF16),
            jax.ShapeDtypeStruct((1, 48, 2304), F32),
            jax.ShapeDtypeStruct((1, 48, 768), F32),
        ),
        in_specs=[VMEM] * 9,
        out_specs=(VMEM,) * 5,
        scratch_shapes=[
            pltpu.VMEM((4, SLAB, 256), BF16),
            line,
            pltpu.VMEM((4, 16, 1536), BF16),
            pltpu.VMEM((4, 16, 1536), BF16),
            pltpu.VMEM((4, 4, 48, 2304), BF16),
            line,
            pltpu.VMEM((SLAB, 768), F32),
            pltpu.VMEM((SLAB, 768), BF16),
            pltpu.VMEM((512, 768), BF16),
            pltpu.VMEM((512, 1536), BF16),
            pltpu.VMEM((768, 512), BF16),
            pltpu.VMEM((768, 512), BF16),
            line,
            line,
            pltpu.VMEM((1, SLAB, 768), F32),
            pltpu.VMEM((1, SLAB, 768), F32),
            pltpu.VMEM((4, 4, 48, 2304), BF16),
            pltpu.VMEM((4, 4, 48, 768), BF16),
            pltpu.VMEM((4, SLAB, 256), BF16),
        ]
        + line_scatter_room(SLAB, 768)
        + line_scatter_room(SLAB, 768)
        + plane_scatter_room(48, 2304, False)
        + plane_scatter_room(48, 768, False)
        + [pltpu.SemaphoreType.DMA((96,))] * 2,
        compiler_params=pltpu.CompilerParams(
            collective_id=collective_id, has_side_effects=True, vmem_limit_bytes=60 * MIB
        ),
        name="middle",
    )(att, tokens, cotangent, w_o, w, gain, down, perm, perm_att)


def back_kernel(
    dq_ref, dkv_ref, wqkv_ref, one_ref, line_ref, turn_ref, gm_ref, tok_ref, perm_ref, ff_ref, og_ref,
    in_ref, got_ff_ref, got_ref,
    own_kv, d_s, one_t, part, sum_s, qkv_part, qkv_sum, ff_rows, qkv_rows, *rest,
):
    send, recv = rest[-2:]
    rooms = list(rest[:-2])
    kv_room, rooms = rooms[:26], rooms[26:]
    qkv_room, line_room = rooms[:26], rooms[26:]
    place = Place()
    enter(place, ("x", "y", "z"))
    links = Links(send, recv)

    kv_a, kv_b = plane_scatter(links, place, dkv_ref, kv_room, own_kv, True)
    advance(kv_a, kv_b)
    spread = spread_rows()
    for c in range(0, 1536, 768):
        ff_rows[:, :, pl.ds(c, 768)] = (
            dot(spread, ff_ref[0, :, pl.ds(c, 768)].astype(BF16)).astype(BF16).reshape(4, 16, 768)
        )
    ff_rows[:, :, pl.ds(1536, 768)] = dot(spread, og_ref[0].astype(BF16)).astype(BF16).reshape(4, 16, 768)
    ff_swap = line_swap(links, place, ff_rows, got_ff_ref)
    advance(ff_swap)
    lane = lax.broadcasted_iota(jnp.int32, (SLAB, SLAB), 1)
    advance(kv_a, kv_b)
    for s in range(4):
        cosine, sine = slab_turns(line_ref, turn_ref, s)
        for j in range(3):
            grad = jnp.where(lane < 64, dq_ref[s, :, pl.ds(128 * j, 128)] * 0.125, 0.0)
            d_s[pl.ds(s * SLAB, SLAB), pl.ds(256 * j, 128)] = turned(grad, cosine, -sine).astype(BF16)
    one_t[...] = one_ref[...].reshape(512, 768).T
    finish(kv_a, kv_b)
    for s in range(4):
        cosine, sine = slab_turns(line_ref, turn_ref, s)
        for j in range(3):
            grad = own_kv[0, pl.ds(s * SLAB, SLAB), pl.ds(128 * j, 128)]
            d_s[pl.ds(s * SLAB, SLAB), pl.ds(256 * j + 128, 128)] = turned(grad, cosine, -sine).astype(BF16)

    def block(r, carry):
        at = pl.ds(pl.multiple_of(r * 256, 256), 256)
        part[pl.ds(r * 2, 2)] = dot_right_t(d_s[at, :], merged(wqkv_ref)).astype(BF16).reshape(2, SLAB, 768)
        return carry

    lax.fori_loop(0, 2, block, 0)
    in_sum = line_scatter(links, place, part, line_room, sum_s)
    advance(in_sum)

    def grads(c, carry):
        at = pl.ds(pl.multiple_of(c * 256, 256), 256)
        qkv_part[:, :, :, at] = dot(one_t[...], d_s[:, at]).astype(BF16).reshape(4, 4, 48, 256)
        return carry

    lax.fori_loop(0, 3, grads, 0)
    qkv_a, qkv_b = plane_scatter(links, place, qkv_part, qkv_room, qkv_sum, False)
    advance(qkv_a, qkv_b, in_sum)
    advance(qkv_a, qkv_b)
    finish(in_sum)
    advance(qkv_a, qkv_b)
    grad = dot_right_t(sum_s[0].astype(BF16), perm_ref[...])
    x = tok_ref[...].astype(F32)
    scale = lax.rsqrt(mean_square(x) + EPS)
    in_ref[...] = gm_ref[...] + norm_back(grad, x * scale, scale)
    together([qkv_a, qkv_b])
    qkv_rows[...] = dot(spread, qkv_sum[0].astype(BF16)).astype(BF16).reshape(4, 16, 768)
    finish(ff_swap, line_swap(links, place, qkv_rows, got_ref))
    links.finish()


def back(collective_id, dq, dkv, w_qkv, one, line, turn, grad_middle, tokens, perm, ff_sum, og_sum):
    return pl.pallas_call(
        back_kernel,
        out_shape=(
            jax.ShapeDtypeStruct((SLAB, 768), F32),
            jax.ShapeDtypeStruct((4, 16, 2304), BF16),
            jax.ShapeDtypeStruct((4, 16, 768), BF16),
        ),
        in_specs=[VMEM] * 11,
        out_specs=(VMEM,) * 3,
        scratch_shapes=[
            pltpu.VMEM((1, 512, 384), F32),
            pltpu.VMEM((512, 768), BF16),
            pltpu.VMEM((768, 512), BF16),
            pltpu.VMEM((4, SLAB, 768), BF16),
            pltpu.VMEM((1, SLAB, 768), F32),
            pltpu.VMEM((4, 4, 48, 768), BF16),
            pltpu.VMEM((1, 48, 768), F32),
            pltpu.VMEM((4, 16, 2304), BF16),
            pltpu.VMEM((4, 16, 768), BF16),
        ]
        + plane_scatter_room(512, 384, True)
        + plane_scatter_room(48, 768, False)
        + line_scatter_room(SLAB, 768)
        + [pltpu.SemaphoreType.DMA((64,))] * 2,
        compiler_params=pltpu.CompilerParams(
            collective_id=collective_id, has_side_effects=True, vmem_limit_bytes=60 * MIB
        ),
        name="back",
    )(dq, dkv, w_qkv, one, line, turn, grad_middle, tokens, perm, ff_sum, og_sum)


def attend_kernel(meta, q_ref, kv_ref, out_ref, lse_ref):
    row = lax.broadcasted_iota(jnp.int32, (SLAB, 1), 0)
    lane = lax.broadcasted_iota(jnp.int32, (SLAB, SLAB), 1)

    def slab(s, carry):
        pos_q = meta[s * 24 + 20, 0] + row
        queries = [q_ref[s, :, pl.ds(j * 128, 128)] for j in range(3)]

        def fold(state, places, first):
            width = len(places) * SLAB
            pos_k = first + lax.broadcasted_iota(jnp.int32, (1, width), 1)
            allowed = pos_k <= pos_q
            out = []
            for j in range(3):
                top, total, acc = state[j]
                keys = jnp.concatenate([kv_ref[at, :, pl.ds(j * 128, 128)] for at in places], 0)
                scores = lax.dot_general(queries[j], keys, (((1,), (1,)), ((), ())), preferred_element_type=F32)
                scores = jnp.where(allowed, scores, LOW)
                new_top = jnp.maximum(top, jnp.max(scores, axis=1, keepdims=True))
                weights = jnp.exp(scores - new_top)
                decay = jnp.exp(top - new_top)
                total = total * decay + jnp.sum(weights, axis=1, keepdims=True)
                acc = acc * decay + jnp.dot(weights.astype(BF16), keys, preferred_element_type=F32)
                out.append((new_top, total, acc))
            return tuple(out)

        start = tuple(
            (jnp.full((SLAB, 1), LOW, F32), jnp.zeros((SLAB, 1), F32), jnp.zeros((SLAB, SLAB), F32)) for _ in range(3)
        )

        def prompt(c, state):
            return fold(state, [meta[s * 24 + c * 4 + a, 0] for a in range(4)], c * 512)

        def own(c, state):
            return fold(state, [meta[s * 24 + 16, 0], meta[s * 24 + 17, 0]], 2048)

        state = lax.fori_loop(0, meta[s * 24 + 18, 0], prompt, start)
        state = lax.fori_loop(0, meta[s * 24 + 19, 0], own, state)
        heads = [acc / total for _, total, acc in state]
        out_ref[s, :, 0:128] = jnp.where(lane < 64, pltpu.roll(heads[0], 64, 1), heads[1]).astype(BF16)
        out_ref[s, :, 128:256] = jnp.where(lane < 64, pltpu.roll(heads[2], 64, 1), 0.0).astype(BF16)
        logs = [top + jnp.log(total) for top, total, _ in state]
        lse_ref[s] = jnp.where(lane == 0, logs[0], jnp.where(lane == 1, logs[1], logs[2]))
        return carry

    lax.fori_loop(0, 4, slab, 0)


def attend(meta, q, kv):
    return pl.pallas_call(
        attend_kernel,
        out_shape=(jax.ShapeDtypeStruct((4, SLAB, 256), BF16), jax.ShapeDtypeStruct((4, SLAB, SLAB), F32)),
        in_specs=[SMEM, VMEM, VMEM],
        out_specs=(VMEM, VMEM),
        compiler_params=pltpu.CompilerParams(vmem_limit_bytes=60 * MIB),
        name="attend",
    )(meta, q, kv)


def attend_back_kernel(meta, q_ref, kv_ref, grad_ref, out_ref, lse_ref, dq_ref, dkv_ref, acc_ref):
    lane = lax.broadcasted_iota(jnp.int32, (SLAB, SLAB), 1)
    which = lax.broadcasted_iota(jnp.int32, (8, SLAB), 0)
    unit = (lax.broadcasted_iota(jnp.int32, (8, SLAB), 1) == which).astype(F32)
    at_lane = lax.broadcasted_iota(jnp.int32, (8, 256), 1)
    pick = (lax.div(at_lane, HD) == lax.broadcasted_iota(jnp.int32, (8, 256), 0)).astype(F32)

    def clear(k, carry):
        acc_ref[k] = jnp.zeros((SLAB, 384), F32)
        return carry

    lax.fori_loop(0, 64, clear, 0)

    def slab(s, carry):
        pos_q = meta[s * 24 + 20, 0] + lax.broadcasted_iota(jnp.int32, (1, SLAB), 1)
        first = grad_ref[s, :, 0:128].astype(F32)
        last = grad_ref[s, :, 128:256].astype(F32)
        inner = grad_ref[s].astype(F32) * out_ref[s].astype(F32)
        deltas = lax.dot_general(pick, inner, LANES, precision=HIGHEST, preferred_element_type=F32)
        logs = lax.dot_general(unit, lse_ref[s], LANES, precision=HIGHEST, preferred_element_type=F32)
        logs = [jnp.sum(jnp.where(which == k, logs, 0.0), axis=0, keepdims=True) for k in range(3)]
        deltas = [jnp.sum(jnp.where(which == k, deltas, 0.0), axis=0, keepdims=True) for k in range(3)]
        right = [pltpu.roll(first, 64, 1), first, pltpu.roll(last, 64, 1)]
        pairs = []
        for j in range(3):
            grads = jnp.where(lane < 64, 0.0, right[j]).astype(BF16)
            pairs.append(jnp.concatenate([q_ref[s, :, pl.ds(j * 128, 128)], grads], 0))
        for j in range(3):
            dq_ref[s, :, pl.ds(j * 128, 128)] = jnp.zeros((SLAB, SLAB), F32)

        def fold(places, first_key):
            width = len(places) * SLAB
            pos_k = first_key + lax.broadcasted_iota(jnp.int32, (width, 1), 0)
            allowed = pos_k <= pos_q
            for j in range(3):
                keys = jnp.concatenate([kv_ref[at, :, pl.ds(j * 128, 128)] for at in places], 0)
                both = lax.dot_general(keys, pairs[j], (((1,), (1,)), ((), ())), preferred_element_type=F32)
                weights = jnp.where(allowed, jnp.exp(both[:, :128] - logs[j]), 0.0)
                slopes = (weights * (both[:, 128:] - deltas[j])).astype(BF16)
                terms = jnp.dot(
                    jnp.concatenate([slopes, weights.astype(BF16)], 1), pairs[j], preferred_element_type=F32
                )
                for n, at in enumerate(places):
                    acc_ref[at, :, pl.ds(j * 128, 128)] += terms[n * 128 : (n + 1) * 128]
                dq_ref[s, :, pl.ds(j * 128, 128)] += lax.dot_general(
                    slopes, keys, (((0,), (0,)), ((), ())), preferred_element_type=F32
                )

        def prompt(c, state):
            fold([meta[s * 24 + c * 4 + a, 0] for a in range(4)], c * 512)
            return state

        def own(c, state):
            fold([meta[s * 24 + 16, 0], meta[s * 24 + 17, 0]], 2048)
            return state

        lax.fori_loop(0, meta[s * 24 + 18, 0], prompt, 0)
        lax.fori_loop(0, meta[s * 24 + 19, 0], own, 0)
        return carry

    lax.fori_loop(0, 4, slab, 0)

    def store(k, carry):
        dkv_ref[k] = acc_ref[k].astype(BF16)
        return carry

    lax.fori_loop(0, 64, store, 0)


def attend_back(meta, q, kv, grads, out, lse):
    return pl.pallas_call(
        attend_back_kernel,
        out_shape=(jax.ShapeDtypeStruct((4, SLAB, 384), F32), jax.ShapeDtypeStruct((64, SLAB, 384), BF16)),
        in_specs=[SMEM, VMEM, VMEM, VMEM, VMEM, VMEM],
        out_specs=(VMEM, VMEM),
        scratch_shapes=[pltpu.VMEM((64, SLAB, 384), F32)],
        compiler_params=pltpu.CompilerParams(vmem_limit_bytes=60 * MIB),
        name="attend_back",
    )(meta, q, kv, grads, out, lse)


def split_columns(w):
    rows = w.shape[0]
    return w.reshape(rows, 2, 16, 2, 48).transpose(3, 1, 0, 2, 4).reshape(4, rows, 768)


def join_columns(w):
    rows = w.shape[1]
    return w.reshape(2, 2, rows, 16, 48).transpose(2, 1, 3, 0, 4).reshape(rows, 3072)


def per_device(
    tokens, gain_one, w_query, w_key, w_value, w_out, gain_two, w_gate, w_up, w_down, cotangent, segment_ids, positions
):
    blk, head = lax.axis_index("blk"), lax.axis_index("head")
    z, own = head * 2 + blk // 16, blk % 16
    perm = jnp.asarray(TO_PERM, BF16)
    perm_att = jnp.asarray(np.pad(TO_PERM.reshape(4, 192, 768), ((0, 0), (0, 64), (0, 0))).reshape(1024, 768), BF16)
    turn = jnp.asarray(OFFSET_TURNS, F32)
    first_gain, second_gain = gain_one.astype(F32)[:, None], gain_two.astype(F32)[:, None]

    seg = segment_ids.reshape(2, SLAB)[head, 0].astype(F32)
    base = positions.reshape(2, SLAB)[head, 0].astype(F32)
    angles = base * jnp.asarray(FREQUENCY, F32)[None]
    row = lax.broadcasted_iota(jnp.int32, (8, SLAB), 0)
    lane = lax.broadcasted_iota(jnp.int32, (8, SLAB), 1)
    here = lane == own * 4 + z
    desc = jnp.where(
        row == 0,
        jnp.cos(angles),
        jnp.where(
            row == 1,
            jnp.sin(angles),
            jnp.where(here & (row == 2), seg, jnp.where(here & (row == 3), base, 0.0)),
        ),
    )
    w_attention = jnp.pad(jnp.concatenate([w_query, w_key, w_value, w_out], 1), ((0, 4), (0, 0)))
    w_ff = jnp.pad(jnp.concatenate([w_gate, w_up], 1), ((0, 4), (0, 0)))
    gain_a = jnp.broadcast_to(jnp.pad(first_gain, ((0, 4), (0, 0))), (16, SLAB))
    gain_b = jnp.broadcast_to(jnp.pad(second_gain, ((0, 4), (0, 0))), (16, SLAB))

    kv, q, w_qkv, w_o, line_one, meta, line = front(0, tokens, w_attention, gain_a, perm, turn, desc)
    kv = kv.reshape(64, SLAB, 384)
    heads_out, lse = attend(meta, q, kv)
    output, grad_middle, grad_heads, ff_sum, og_sum = middle(
        1, heads_out, tokens, cotangent, w_o, w_ff, gain_b, w_down, perm, perm_att
    )
    dq, dkv = attend_back(meta, q, kv, grad_heads, heads_out, lse)
    input_grad, got_ff, got_qkv = back(
        2, dq, dkv.reshape(4, 4, 512, 384), w_qkv, line_one, line, turn, grad_middle, tokens, perm, ff_sum, og_sum
    )

    got_out = got_ff[:, :12, 1536:].astype(F32)
    got_ff = got_ff[:, :12, :1536].astype(F32)
    got_qkv = got_qkv[:, :12].astype(F32)
    by_kind = got_qkv.reshape(4, 12, 3, 4, HD).transpose(3, 1, 0, 2, 4).reshape(4, 12, 768)
    gate_grad, up_grad = join_columns(got_ff[:, :, :768]), join_columns(got_ff[:, :, 768:])
    gain_one_grad = jnp.sum(by_kind[0] * w_query + by_kind[2] * w_key + by_kind[3] * w_value, axis=1)
    gain_two_grad = jnp.sum(gate_grad * w_gate + up_grad * w_up, axis=1)
    return (
        output,
        input_grad,
        gain_one_grad,
        by_kind[0] * first_gain,
        by_kind[2] * first_gain,
        by_kind[3] * first_gain,
        jnp.sum(got_out, axis=0),
        gain_two_grad,
        gate_grad * second_gain,
        up_grad * second_gain,
        ff_sum[0, :, 1536:],
    )


def solution(mesh):
    rows = P(("grp", "blk", "head"), None)
    flat = P(("grp", "blk", "head"))
    weight = P(("blk", "head"), None)
    gain = P(("blk", "head"))
    ids = P(("grp", "blk"))
    in_specs = (rows, gain, weight, weight, weight, weight, gain, weight, weight, weight, rows, ids, ids)
    out_specs = (rows, rows, flat, rows, rows, rows, rows, flat, rows, rows, rows)
    return jax.shard_map(per_device, mesh=mesh, in_specs=in_specs, out_specs=out_specs, check_vma=False)
```

```python
import math

import jax
import jax.numpy as jnp
import numpy as np
from jax import lax
from jax.experimental import pallas as pl
from jax.experimental.pallas import tpu as pltpu
from jax.sharding import PartitionSpec as P

MESH = pl.DeviceIdType.MESH
F32 = jnp.float32
BF16 = jnp.bfloat16
HD = 64
CONTS = 8
SLAB = 128
LOW = -1e30
EPS = 1e-05
LANES = (((1,), (1,)), ((), ()))
HIGHEST = lax.Precision.HIGHEST
MIB = 1 << 20
VMEM = pl.BlockSpec(memory_space=pltpu.VMEM)
SMEM = pl.BlockSpec(memory_space=pltpu.SMEM)


def feature_order():
    place = np.arange(768)
    p, z, r = place // 48, place // 12 % 4, place % 12
    t = (z % 2) * 32 + p * 2 + z // 2
    return t * 12 + r


ORDER = feature_order()
TO_PERM = np.zeros((768, 768), np.float32)
TO_PERM[ORDER, np.arange(768)] = 1.0


ATT_PERM = np.pad(TO_PERM.reshape(4, 192, 768), ((0, 0), (0, 64), (0, 0))).reshape(1024, 768)
OUT_PERM = np.pad(ATT_PERM.reshape(1024, 16, 4, 12).transpose(0, 2, 1, 3), ((0, 0), (0, 0), (0, 0), (0, 4))).reshape(1024, 1024)
LANE_FREQUENCY = 10000.0 ** (-(np.arange(128) % 32) * 2.0 / HD) * (np.arange(128) < HD)
FREQUENCY = LANE_FREQUENCY.astype(np.float32)
OFFSET_ANGLES = np.arange(SLAB)[:, None] * LANE_FREQUENCY[None]
OFFSET_TURNS = np.stack([np.cos(OFFSET_ANGLES), np.sin(OFFSET_ANGLES)]).astype(np.float32)


class Place:
    def __init__(self):
        self.core = lax.axis_index("grp")
        blk = lax.axis_index("blk")
        self.blk, self.head = blk, lax.axis_index("head")
        self.x = lax.rem(blk, 4)
        self.y = lax.rem(lax.div(blk, 4), 4)
        self.z = self.head * 2 + lax.div(blk, 16)

    def other_core(self):
        return (1 - self.core, self.blk, self.head)

    def device(self, x=None, y=None, z=None):
        x = self.x if x is None else x
        y = self.y if y is None else y
        z = self.z if z is None else z
        return (self.core, lax.rem(z, 2) * 16 + y * 4 + x, lax.div(z, 2))

    def ring(self, axis):
        return Ring(self, axis)


class Ring:
    def __init__(self, place, axis):
        self.place, self.axis = place, axis
        self.own = getattr(place, axis)
        self.next = lax.rem(self.own + 1, 4)
        self.prev = lax.rem(self.own + 3, 4)
        self.far = lax.rem(self.own + 2, 4)

    def device(self, index):
        return self.place.device(**{self.axis: index})


def enter(place, axes, far=False):
    barrier = pltpu.get_barrier_semaphore()
    partners = []
    for axis in axes:
        if axis == "core":
            partners.append(place.other_core())
            continue
        ring = place.ring(axis)
        partners += [ring.device(ring.next), ring.device(ring.prev)]
        if axis == "z" or far:
            partners.append(ring.device(ring.far))
    for partner in partners:
        pl.semaphore_signal(barrier, inc=1, device_id=partner, device_id_type=MESH)
    pl.semaphore_wait(barrier, len(partners))


class Links:
    def __init__(self, send, recv):
        self.send, self.recv, self.used, self.sent = send, recv, 0, []

    def copy(self, source, target, device):
        k = self.used
        self.used += 1
        copy = pltpu.make_async_remote_copy(
            src_ref=source,
            dst_ref=target,
            send_sem=self.send.at[k],
            recv_sem=self.recv.at[k],
            device_id=device,
            device_id_type=MESH,
        )
        copy.start()
        self.sent.append(copy)
        return copy

    def finish(self, count=None):
        count = len(self.sent) if count is None else count
        for copy in self.sent[:count]:
            copy.wait_send()
        del self.sent[:count]


def together(steps):
    steps = list(steps)
    while steps:
        left = []
        for step in steps:
            try:
                next(step)
                left.append(step)
            except StopIteration:
                pass
        steps = left


def ring_gather(links, ring, slot):
    right = links.copy(slot(ring.own, None), slot(ring.own, None), ring.device(ring.next))
    left = links.copy(slot(ring.own, None), slot(ring.own, None), ring.device(ring.prev))
    yield
    right.wait_recv()
    on_right = links.copy(slot(ring.prev, 0), slot(ring.prev, 0), ring.device(ring.next))
    left.wait_recv()
    on_left = links.copy(slot(ring.next, 1), slot(ring.next, 1), ring.device(ring.prev))
    yield
    on_right.wait_recv()
    on_left.wait_recv()


def add_into(target, terms, kind):
    *lead, rows, columns = target.shape
    step = 16
    for size in (128, 64, 48, 32):
        if rows % size == 0 and size * columns <= 48 * 1024:
            step = size
            break
    count = rows // step

    def body(k, carry):
        at, rest = [], lax.div(k, count)
        for size in reversed(lead):
            at.insert(0, lax.rem(rest, size))
            rest = lax.div(rest, size)
        at = (*at, pl.ds(pl.multiple_of(lax.rem(k, count) * step, step), step), slice(None))
        total = terms[0][at].astype(F32)
        for term in terms[1:]:
            total = total + term[at].astype(F32)
        target[at] = total.astype(kind)
        return carry

    lax.fori_loop(0, math.prod(lead) * count, body, 0)


def ring_scatter(links, ring, part, room, target, kind):
    low, high, sum_low, sum_high, from_prev, from_next = room
    nxt, prv = ring.device(ring.next), ring.device(ring.prev)
    far_low = links.copy(part(ring.far, 0), low, nxt)
    far_high = links.copy(part(ring.far, 1), high, prv)
    next_high = links.copy(part(ring.next, 1), from_prev(1), nxt)
    prev_low = links.copy(part(ring.prev, 0), from_next(0), prv)
    yield
    far_low.wait_recv()
    add_into(sum_low, [part(ring.next, 0), low], BF16)
    next_low = links.copy(sum_low, from_prev(0), nxt)
    far_high.wait_recv()
    add_into(sum_high, [part(ring.prev, 1), high], BF16)
    prev_high = links.copy(sum_high, from_next(1), prv)
    yield
    for copy in (next_high, prev_low, next_low, prev_high):
        copy.wait_recv()
    add_into(target, [part(ring.own, None), from_prev(None), from_next(None)], kind)


def lead_part(part):
    return pl.ds(0, 4) if part is None else pl.ds(2 * part, 2)


def row_part(rows, part):
    first = (rows // 2 + 15) // 16 * 16
    if part is None:
        return 0, rows
    return (0, first) if part == 0 else (first, rows - first)


def regions(rows, columns, by_rows):
    if by_rows:
        return [(0, rows // 2, 0, columns), (rows // 2, rows // 2, 0, columns)]
    return [(0, rows, 0, columns // 2), (0, rows, columns // 2, columns // 2)]


def plane_gather(links, place, buf, by_rows):
    rows, columns = buf.shape[2:]

    def half(region, x_first):
        r0, rn, c0, cn = region

        def one(k, part):
            off, size = row_part(rn, part)
            y, x = (place.y, k) if x_first else (k, place.x)
            return buf.at[y, x, pl.ds(r0 + off, size), pl.ds(c0, cn)]

        def line(k, part):
            y, x = (k, lead_part(part)) if x_first else (lead_part(part), k)
            return buf.at[y, x, pl.ds(r0, rn), pl.ds(c0, cn)]

        yield from ring_gather(links, place.ring("x" if x_first else "y"), one)
        yield from ring_gather(links, place.ring("y" if x_first else "x"), line)

    a, b = regions(rows, columns, by_rows)
    return half(a, True), half(b, False)


def plane_scatter_room(rows, columns, by_rows):
    rooms = []
    for _, rn, _, cn in regions(rows, columns, by_rows):
        rooms += [pltpu.VMEM((2, rn, cn), BF16)] * 4 + [pltpu.VMEM((4, rn, cn), BF16)] * 3
        low, high = row_part(rn, 0)[1], row_part(rn, 1)[1]
        rooms += [pltpu.VMEM((1, low, cn), BF16), pltpu.VMEM((1, high, cn), BF16)] * 2
        rooms += [pltpu.VMEM((1, rn, cn), BF16)] * 2
    return rooms


def plane_scatter(links, place, buf, rooms, target, by_rows):
    rows, columns = buf.shape[2:]

    def half(region, room, x_first):
        r0, rn, c0, cn = region
        low, high, sum_low, sum_high, prev, nxt, lined = room[:7]
        low1, high1, sum_low1, sum_high1, prev1, nxt1 = room[7:]

        def line(k, part):
            y, x = (lead_part(part), k) if x_first else (k, lead_part(part))
            return buf.at[y, x, pl.ds(r0, rn), pl.ds(c0, cn)]

        def one(k, part):
            off, size = row_part(rn, part)
            return lined.at[pl.ds(k, 1), pl.ds(off, size), :]

        def lined_part(ref):
            return lambda part: ref.at[lead_part(part)]

        def one_part(ref):
            def view(part):
                off, size = row_part(rn, part)
                return ref.at[:, pl.ds(off, size), :]

            return view

        room_a = (low, high, sum_low, sum_high, lined_part(prev), lined_part(nxt))
        room_b = (low1, high1, sum_low1, sum_high1, one_part(prev1), one_part(nxt1))
        yield from ring_scatter(links, place.ring("x" if x_first else "y"), line, room_a, lined, BF16)
        out = target.at[:, pl.ds(r0, rn), pl.ds(c0, cn)]
        yield from ring_scatter(links, place.ring("y" if x_first else "x"), one, room_b, out, F32)

    a, b = regions(rows, columns, by_rows)
    return half(a, rooms[:13], False), half(b, rooms[13:], True)


SMALL_ROOM = [pltpu.VMEM((3, 4, 16, 384), BF16), pltpu.VMEM((4, 16, 384), BF16), pltpu.VMEM((3, 1, 16, 384), BF16)] * 2


def direct_scatter(links, ring, part, room, target, kind):
    copies = []
    for k, to in enumerate((ring.next, ring.prev, ring.far)):
        copies.append(links.copy(part(to), room.at[k], ring.device(to)))
    yield
    for copy in copies:
        copy.wait_recv()
    add_into(target, [part(ring.own), room.at[0], room.at[1], room.at[2]], kind)


def small_scatter(links, place, buf, rooms, target):
    def half(c0, room, x_first):
        columns = pl.ds(c0, 384)
        firsts, lined, lasts = room

        def line(k):
            return buf.at[:, k, :, columns] if x_first else buf.at[k, :, :, columns]

        yield from direct_scatter(links, place.ring("x" if x_first else "y"), line, firsts, lined, BF16)
        out = target.at[:, :, columns]
        yield from direct_scatter(
            links, place.ring("y" if x_first else "x"), lambda k: lined.at[pl.ds(k, 1)], lasts, out, F32
        )

    return half(0, rooms[:3], False), half(384, rooms[3:], True)


def line_scatter_room(rows, columns):
    low, high = row_part(rows, 0)[1], row_part(rows, 1)[1]
    return [pltpu.VMEM((1, low, columns), BF16), pltpu.VMEM((1, high, columns), BF16)] * 2 + [
        pltpu.VMEM((1, rows, columns), BF16)
    ] * 2


def line_scatter(links, place, buf, room, target):
    rows = buf.shape[1]

    def part(k, half):
        off, size = row_part(rows, half)
        return buf.at[pl.ds(k, 1), pl.ds(off, size), :]

    def view(ref):
        def cut(half):
            off, size = row_part(rows, half)
            return ref.at[:, pl.ds(off, size), :]

        return cut

    low, high, sum_low, sum_high, prev, nxt = room
    yield from ring_scatter(
        links, place.ring("z"), part, (low, high, sum_low, sum_high, view(prev), view(nxt)), target, F32
    )


def line_gather(links, place, buf):
    rows = buf.shape[1]

    def slot(k, half):
        off, size = row_part(rows, half)
        return buf.at[k, pl.ds(off, size)]

    yield from ring_gather(links, place.ring("z"), slot)


def line_swap(links, place, source, target):
    ring = place.ring("z")
    copies = []
    for other in (ring.next, ring.prev, ring.far):
        copies.append(links.copy(source.at[other], target.at[ring.own], ring.device(other)))
    target[ring.own] = source[ring.own]
    yield
    for copy in copies:
        copy.wait_recv()


def small_gather(links, ring, slot):
    right = links.copy(slot(ring.own), slot(ring.own), ring.device(ring.next))
    left = links.copy(slot(ring.own), slot(ring.own), ring.device(ring.prev))
    yield
    right.wait_recv()
    left.wait_recv()
    on = links.copy(slot(ring.prev), slot(ring.prev), ring.device(ring.next))
    yield
    on.wait_recv()


def shared_gather(links, place, buf):
    half = buf.shape[3] // 2
    flip = place.core == 1
    columns = pl.ds(pl.multiple_of(place.core * half, 128), half)
    first, second = jnp.where(flip, place.y, place.x), jnp.where(flip, place.x, place.y)
    first_next, first_prev, first_far = [lax.rem(first + k, 4) for k in (1, 3, 2)]
    second_next, second_prev, second_far = [lax.rem(second + k, 4) for k in (1, 3, 2)]

    def block(s, f, part=None):
        y, x = jnp.where(flip, f, s), jnp.where(flip, s, f)
        rows = pl.ds(0, 48) if part is None else (pl.ds(0, 32) if part == 0 else pl.ds(32, 16))
        return buf.at[y, x, rows, columns]

    def device(s, f):
        return place.device(x=jnp.where(flip, s, f), y=jnp.where(flip, f, s))

    def send(s, f, to, part=None):
        return links.copy(block(s, f, part), block(s, f, part), to)

    handed = []

    def hand(s, f):
        handed.append(links.copy(block(s, f), block(s, f), place.other_core()))

    on_right, on_left = device(second, first_next), device(second, first_prev)
    up, down = device(second_next, first), device(second_prev, first)
    order = (first, first_prev, first_next, first_far)
    ups, downs = [], []

    def line(k):
        ups.append(send(second, order[k], up))
        downs.append(send(second, order[k], down))

    right = send(second, first, on_right)
    left = send(second, first, on_left)
    line(0)
    yield
    right.wait_recv()
    far_low = send(second, first_prev, on_right, 0)
    line(1)
    left.wait_recv()
    far_high = send(second, first_next, on_left, 1)
    line(2)
    hand(second, first_prev)
    hand(second, first_next)
    yield
    far_low.wait_recv()
    far_high.wait_recv()
    line(3)
    hand(second, first_far)
    yield
    far = []
    for k in range(4):
        ups[k].wait_recv()
        if k < 2:
            far.append(send(second_prev, order[k], up))
        hand(second_prev, order[k])
        downs[k].wait_recv()
        if k >= 2:
            far.append(send(second_next, order[k], down))
        hand(second_next, order[k])
    yield
    for k in range(4):
        far[k].wait_recv()
        hand(second_far, order[k])
    yield
    for copy in handed:
        copy.wait_recv()


def advance(*steps):
    for step in steps:
        next(step, None)


def finish(*steps):
    together(steps)


def dot(left, right):
    return jnp.dot(left, right, preferred_element_type=F32)


def dot_right_t(left, right):
    return lax.dot_general(left, right, LANES, preferred_element_type=F32)


def pack_rows():
    i = lax.broadcasted_iota(jnp.int32, (48, 64), 0)
    k = lax.broadcasted_iota(jnp.int32, (48, 64), 1)
    return (k == lax.div(i, 12) * 16 + lax.rem(i, 12)).astype(BF16)


def spread_rows():
    k = lax.broadcasted_iota(jnp.int32, (64, 48), 0)
    i = lax.broadcasted_iota(jnp.int32, (64, 48), 1)
    return (k == lax.div(i, 12) * 16 + lax.rem(i, 12)).astype(BF16)


def merged(ref):
    rows, columns = ref.shape[0] * ref.shape[1] * ref.shape[2], ref.shape[3]
    return ref[...].reshape(rows, columns)


def mean_square(values):
    return jnp.mean(values * values, axis=-1, keepdims=True)


def norm_back(grad, normed, scale):
    return scale * (grad - normed * jnp.mean(grad * normed, axis=-1, keepdims=True))


def slab_turns(line_ref, turn_ref, s):
    rows = line_ref[s]
    cos_base, sin_base = rows[0:1], rows[1:2]
    cos_off, sin_off = turn_ref[0], turn_ref[1]
    lane = lax.broadcasted_iota(jnp.int32, (SLAB, SLAB), 1)
    sign = jnp.where(lane < 32, -1.0, jnp.where(lane < 64, 1.0, 0.0))
    return cos_base * cos_off - sin_base * sin_off, (sin_base * cos_off + cos_base * sin_off) * sign


def turned(field, cosine, sine):
    lane = lax.broadcasted_iota(jnp.int32, (SLAB, SLAB), 1)
    return field * cosine + jnp.where(lane < 32, pltpu.roll(field, 96, 1), pltpu.roll(field, 32, 1)) * sine


def half_rows(values, k):
    return values[k * SLAB : (k + 1) * SLAB]


def direct_gather(links, place, buf):
    half = buf.shape[3] // 2
    ring_x, ring_y = place.ring("x"), place.ring("y")
    a, b = pl.ds(0, half), pl.ds(half, half)

    def spread(ring, view):
        return [links.copy(view, view, ring.device(k)) for k in (ring.next, ring.prev, ring.far)]

    first = spread(ring_x, buf.at[place.y, place.x, :, a])
    second = spread(ring_y, buf.at[place.y, place.x, :, b])
    yield
    for copy in first:
        copy.wait_recv()
    first = spread(ring_y, buf.at[place.y, :, :, a])
    for copy in second:
        copy.wait_recv()
    second = spread(ring_x, buf.at[:, place.x, :, b])
    yield
    for copy in first + second:
        copy.wait_recv()


def slab_place(at):
    return lax.div(at, 16), lax.rem(lax.div(at, 4), 4), lax.rem(at, 4)


def slab_gather(links, place, buf):
    def half(z0, x_first):
        def one(k, part):
            y, x = (place.y, k) if x_first else (k, place.x)
            return buf.at[y, x, pl.ds(z0, 2) if part is None else pl.ds(z0 + part, 1)]

        def line(k, part):
            y, x = (k, lead_part(part)) if x_first else (lead_part(part), k)
            return buf.at[y, x, pl.ds(z0, 2)]

        yield from ring_gather(links, place.ring("x" if x_first else "y"), one)
        yield from ring_gather(links, place.ring("y" if x_first else "x"), line)

    return half(0, True), half(2, False)


def slab_scatter_room():
    few, many = pltpu.VMEM((2, 2, SLAB, SLAB), BF16), pltpu.VMEM((4, 2, SLAB, SLAB), BF16)
    one, two = pltpu.VMEM((1, SLAB, SLAB), BF16), pltpu.VMEM((2, SLAB, SLAB), BF16)
    return ([few] * 4 + [many] * 3 + [one] * 4 + [two] * 2) * 2


def slab_scatter(links, place, buf, rooms, target):
    def half(z0, room, x_first):
        low, high, sum_low, sum_high, prev, nxt, lined = room[:7]
        low1, high1, sum_low1, sum_high1, prev1, nxt1 = room[7:]

        def line(k, part):
            y, x = (lead_part(part), k) if x_first else (k, lead_part(part))
            return buf.at[y, x, pl.ds(z0, 2)]

        def one(k, part):
            return lined.at[k] if part is None else lined.at[k, pl.ds(part, 1)]

        def lined_part(ref):
            return lambda part: ref.at[lead_part(part)]

        def one_part(ref):
            return lambda part: ref.at[pl.ds(0, 2) if part is None else pl.ds(part, 1)]

        room_a = (low, high, sum_low, sum_high, lined_part(prev), lined_part(nxt))
        room_b = (low1, high1, sum_low1, sum_high1, one_part(prev1), one_part(nxt1))
        yield from ring_scatter(links, place.ring("x" if x_first else "y"), line, room_a, lined, BF16)
        out = target.at[pl.ds(z0, 2)]
        yield from ring_scatter(links, place.ring("y" if x_first else "x"), one, room_b, out, F32)

    return half(0, rooms[:13], False), half(2, rooms[13:], True)


def keys_of(kv_ref, table, s, first, count):
    places = [slab_place(jnp.clip(table[s * 24 + first + k, 0], 0, 63)) for k in range(count)]
    return jnp.concatenate([kv_ref[y, x, z] for y, x, z in places], 0)


def query_positions(table, s, shape, axis):
    return table[s * 24 + 20, 0] + lax.broadcasted_iota(jnp.int32, shape, axis)


def attend_head(j, table, q_ref, kv_ref, top_ref, sum_ref, acc_ref, between):
    def fold(s, first, count, first_key):
        keys = keys_of(kv_ref, table, s, first, count)
        width = count * SLAB
        pos_q = query_positions(table, s, (SLAB, 1), 0)
        pos_k = first_key + lax.broadcasted_iota(jnp.int32, (1, width), 1)
        scores = dot_right_t(q_ref[s, :, pl.ds(j * 128, 128)], keys)
        scores = jnp.where(pos_k <= pos_q, scores, LOW)
        top = top_ref[s]
        new_top = jnp.maximum(top, jnp.max(scores, axis=1, keepdims=True))
        weights = jnp.exp(scores - new_top[:, 0:1])
        decay = jnp.exp(top - new_top)
        sum_ref[s] = sum_ref[s] * decay + jnp.sum(weights, axis=1, keepdims=True)
        acc_ref[s] = acc_ref[s] * decay + dot(weights.astype(BF16), keys)
        top_ref[s] = new_top

    for s in range(4):
        top_ref[s] = jnp.full((SLAB, SLAB), LOW, F32)
        sum_ref[s] = jnp.zeros((SLAB, SLAB), F32)
        acc_ref[s] = jnp.zeros((SLAB, SLAB), F32)

    def prompt(c, carry):
        for s in range(4):
            fold(s, c * 4, 4, c * 512)
        return carry

    lax.fori_loop(0, 2, prompt, 0)
    between(0)
    lax.fori_loop(2, 4, prompt, 0)
    between(1)
    for s in range(4):
        fold(s, 16, 2, 2048)


def attend_back_head(j, table, q_ref, kv_ref, grad_ref, logs, deltas, dq_ref, terms_ref, pair_ref, between):
    lane = lax.broadcasted_iota(jnp.int32, (SLAB, SLAB), 1)
    for s in range(4):
        grads = grad_ref[s, :, pl.ds(128 * (j // 2), 128)].astype(F32)
        if j != 1:
            grads = pltpu.roll(grads, 64, 1)
        pair_ref[s, pl.ds(0, SLAB)] = q_ref[s, :, pl.ds(j * 128, 128)]
        pair_ref[s, pl.ds(SLAB, SLAB)] = jnp.where(lane < 64, 0.0, grads).astype(BF16)
        dq_ref[s] = jnp.zeros((SLAB, SLAB), F32)

    def fold(s, first, count, first_key):
        keys = keys_of(kv_ref, table, s, first, count)
        width = count * SLAB
        pos_q = query_positions(table, s, (1, SLAB), 1)
        pos_k = first_key + lax.broadcasted_iota(jnp.int32, (width, 1), 0)
        pair = pair_ref[s]
        both = dot_right_t(keys, pair)
        weights = jnp.where(pos_k <= pos_q, jnp.exp(both[:, :SLAB] - logs[s]), 0.0)
        slopes = (weights * (both[:, SLAB:] - deltas[s])).astype(BF16)
        terms = dot(jnp.concatenate([slopes, weights.astype(BF16)], 1), pair)
        terms_ref[s, pl.ds(first, count)] = terms.astype(BF16).reshape(count, SLAB, SLAB)
        dq_ref[s] += lax.dot_general(slopes, keys, (((0,), (0,)), ((), ())), preferred_element_type=F32)

    def prompt(c, carry):
        for s in range(4):
            fold(s, c * 4, 4, c * 512)
        return carry

    lax.fori_loop(0, 2, prompt, 0)
    between(0)
    lax.fori_loop(2, 4, prompt, 0)
    between(1)
    for s in range(4):
        fold(s, 16, 2, 2048)


def sum_terms(table, terms_ref, part_ref):
    def slab(t, carry):
        places = [jnp.clip(table[96 + s, t], 0, 18) for s in range(4)]
        total = terms_ref[0, places[0]].astype(F32)
        for s in range(1, 4):
            total = total + terms_ref[s, places[s]].astype(F32)
        y, x, z = slab_place(t)
        part_ref[y, x, z] = total.astype(BF16)
        return carry

    lax.fori_loop(0, 64, slab, 0)


def lookups(total, own, meta_ref):
    seg, base = total[2:3], total[3:4]
    lane = lax.broadcasted_iota(jnp.int32, (1, SLAB), 1)
    lane_at = lane.astype(F32)
    n = lax.broadcasted_iota(jnp.int32, (24, 1), 0)
    back_rows = jnp.zeros((8, SLAB), F32)
    back_row = lax.broadcasted_iota(jnp.int32, (8, 1), 0)
    for s in range(4):
        mine = lane == own * 4 + s
        seg_q = jnp.sum(jnp.where(mine, seg, 0.0), axis=1, keepdims=True)
        base_q = jnp.sum(jnp.where(mine, base, 0.0), axis=1, keepdims=True)
        prompt = jnp.where(seg_q >= CONTS + 1.0, CONTS + 1.0, 0.0)
        want = jnp.where(n < 16, prompt, seg_q)
        hit = (seg == want) & (base == n.astype(F32) * SLAB) & (lane < 64)
        places = jnp.max(jnp.where(hit, lane_at, 0.0), axis=1, keepdims=True)
        listed = jnp.where(n == 20, base_q, places)
        meta_ref[pl.ds(s * 24, 24), :] = jnp.broadcast_to(listed, (24, SLAB)).astype(jnp.int32)
        visible = (seg == prompt) | (seg == seg_q)
        places = jnp.where(visible, jnp.minimum(base * (1.0 / SLAB), 17.0), 18.0)
        back_rows = jnp.where(back_row == s, places, back_rows)
    meta_ref[pl.ds(96, 8), :] = back_rows.astype(jnp.int32)


def layer_kernel(
    tok_ref, cot_ref, w_ref, ff_ref, down_ref, gain_ref, perm_ref, turn_ref, desc_ref, perm_att_hbm, out_perm_hbm,
    out_ref, in_ref, down_sum_ref, got_ff_ref, got_ref, got_out_ref,
    perm_att, out_perm, const_sem, line_ref, descs, meta_ref, table, table_sem,
    for_line, for_line_ff, rows, rows_o, rows_ff, one, cots, wqkv, wo, wff, q_ref, kv0, kv1, kv2,
    tops, sums, accs, att_ref, lse_ref, atts, att_s, mid_s, gm_s, two, act, pre, turn_t, part, part_out, sum_z, sum_out,
    to_heads, grads_ref, terms, pairs, kv_own, d_s, qkv_sum, ff_sum,
    og_part, og_sum, og_next, *rest,
):
    send, recv = rest[-2:]
    rooms = list(rest[:-2])

    def take(count):
        out = rooms[:count]
        del rooms[:count]
        return out

    back_room, ff_room, out_room = take(6), take(26), take(6)
    kv_rooms = [take(26) for _ in range(3)]
    qkv_room, in_room, og_line_room, og_room = take(26), take(6), take(6), take(6)
    kvs = (kv0, kv1, kv2)

    const_copies = [
        pltpu.make_async_copy(perm_att_hbm, perm_att, const_sem.at[0]),
        pltpu.make_async_copy(out_perm_hbm, out_perm, const_sem.at[1]),
    ]
    for copy in const_copies:
        copy.start()
    place = Place()
    enter(place, ("x", "y", "z", "core"), True)
    links = Links(send, recv)
    own = place.y * 4 + place.x

    line_ref[place.z] = desc_ref[...]
    lined = small_gather(links, place.ring("z"), lambda k: line_ref.at[k])
    w = w_ref[...].astype(F32)
    gain = gain_ref[:, 0:1]
    none = jnp.zeros((16, HD), F32)
    for z in range(4):
        pieces = []
        for j in range(3):
            c = 192 * z + 64 * j
            pieces += [w[:, c : c + 64] * gain, none, w[:, 768 + c : 832 + c] * gain, w[:, 1536 + c : 1600 + c] * gain]
        for_line[z] = jnp.concatenate(pieces, 1).astype(BF16)
    swap = line_swap(links, place, for_line, rows)
    advance(swap, lined)
    x = dot(tok_ref[...], perm_ref[...])
    one[place.z] = (x * lax.rsqrt(mean_square(x) + EPS)).astype(BF16)
    ones = line_gather(links, place, one)
    advance(ones)
    finish(swap)
    wqkv[place.y, place.x] = dot(pack_rows(), rows[...].reshape(64, 768)).astype(BF16)
    qkv = direct_gather(links, place, wqkv)
    advance(qkv)
    gain = gain_ref[:, 1:2]
    for z in range(4):
        for k in range(2):
            pieces = []
            for p in range(16):
                c = 3072 * k + ((z % 2) * 32 + p * 2 + z // 2) * 48
                pieces.append(ff_ref[:, c : c + 48].astype(F32) * gain)
            for_line_ff[z, :, pl.ds(768 * k, 768)] = jnp.concatenate(pieces, 1).astype(BF16)
    advance(lined, ones)
    advance(qkv)
    finish(lined)
    descs[place.y, place.x] = line_ref[0] + line_ref[1] + line_ref[2] + line_ref[3]
    desc_x = small_gather(links, place.ring("x"), lambda k: descs.at[place.y, k])
    desc_y = small_gather(links, place.ring("y"), lambda k: descs.at[k])
    advance(desc_x)
    finish(ones)
    rows_o[place.z] = w_ref[:, pl.ds(2304, 768)]
    o_line = small_gather(links, place.ring("z"), lambda k: rows_o.at[k])
    ff_swap = line_swap(links, place, for_line_ff, rows_ff)
    cots[place.z] = cot_ref[...]
    cot_gather = line_gather(links, place, cots)
    advance(o_line, ff_swap, cot_gather)
    finish(qkv)

    lines = one[...].reshape(512, 768)
    gathers = []
    for j in range(3):
        field = dot(lines, wqkv[:, :, :, pl.ds(256 * j, 256)].reshape(768, 256))
        for s in range(4):
            cosine, sine = slab_turns(line_ref, turn_ref, s)
            query = turned(half_rows(field[:, 0:128], s), cosine, sine)
            q_ref[s, :, pl.ds(128 * j, 128)] = (query * 0.125).astype(BF16)
            pair = turned(half_rows(field[:, 128:256], s), cosine, sine)
            kvs[j][place.y, place.x, s] = pair.astype(BF16)
        gathers.append(slab_gather(links, place, kvs[j]))
        advance(*gathers[j])
    advance(desc_x)
    for j in range(3):
        advance(*gathers[j])
    finish(desc_x)
    advance(desc_y)
    advance(*gathers[0])
    advance(desc_y, o_line)
    advance(*gathers[0])
    advance(*gathers[1])
    finish(desc_y)
    total = jnp.zeros((8, SLAB), F32)
    for y in range(4):
        for k in range(4):
            total = total + descs[y, k]
    lookups(total, own, meta_ref)
    copy = pltpu.make_async_copy(meta_ref, table, table_sem)
    copy.start()
    copy.wait()
    finish(ff_swap, o_line)
    wo[place.y, place.x] = dot(pack_rows(), rows_o[...].reshape(64, 768)).astype(BF16)
    for c in range(0, 1536, 768):
        wff[place.y, place.x, :, pl.ds(c, 768)] = dot(
            pack_rows(), rows_ff[:, :, pl.ds(c, 768)].reshape(64, 768)
        ).astype(BF16)
    wff[place.y, place.x, :, pl.ds(1536, 768)] = down_ref[...]
    advance(cot_gather)
    for copy in const_copies:
        copy.wait()

    lane = lax.broadcasted_iota(jnp.int32, (SLAB, SLAB), 1)
    o_gather = direct_gather(links, place, wo)
    w_gather = shared_gather(links, place, wff)
    for j in range(3):
        finish(*gathers[j])

        def between(k, j=j):
            if j == 0 and k == 1:
                advance(*gathers[1])
                advance(*gathers[2])
            if j == 1 and k == 0:
                advance(cot_gather)
            if j == 1 and k == 1:
                advance(*gathers[2])
            if j == 2:
                advance(o_gather)
                advance(w_gather)

        if j == 2:
            advance(o_gather)
            advance(w_gather)
        attend_head(j, table, q_ref, kvs[j], tops, sums, accs, between)
        for s in range(4):
            head = accs[s] / sums[s]
            if j == 0:
                att_ref[s, :, 0:128] = jnp.where(lane < 64, pltpu.roll(head, 64, 1), 0.0).astype(BF16)
            elif j == 1:
                att_ref[s, :, 0:128] = jnp.where(lane < 64, att_ref[s, :, 0:128].astype(F32), head).astype(BF16)
            else:
                att_ref[s, :, 128:256] = jnp.where(lane < 64, pltpu.roll(head, 64, 1), 0.0).astype(BF16)
            logs = tops[s] + jnp.log(sums[s])
            lse_ref[s] = logs if j == 0 else jnp.where(lane == j, logs, lse_ref[s])
    att_swap = line_swap(links, place, att_ref, atts)
    advance(att_swap)
    finish(cot_gather, o_gather)
    advance(w_gather)
    finish(att_swap)

    att = dot(atts[0], perm_att[pl.ds(0, 256), :])
    for z in range(1, 4):
        att = att + dot(atts[z], perm_att[pl.ds(256 * z, 256), :])
    att_s[...] = att.astype(BF16)
    mid_s[...] = tok_ref[...].astype(F32) + dot(att_s[...], merged(wo))
    middle = mid_s[...]
    scale_two = lax.rsqrt(mean_square(middle) + EPS)
    two[place.z] = dot((middle * scale_two).astype(BF16), perm_ref[...]).astype(BF16)
    two_gather = line_gather(links, place, two)
    advance(two_gather)
    advance(w_gather)
    att = dot(atts[0], out_perm[pl.ds(0, 256), :])
    for z in range(1, 4):
        att = att + dot(atts[z], out_perm[pl.ds(256 * z, 256), :])
    att_by_z = att.astype(BF16).T
    advance(two_gather)
    together([w_gather, two_gather])

    def block(r, carry):
        at = pl.ds(pl.multiple_of(r * 256, 256), 256)
        two_b = two[pl.ds(r * 2, 2)].reshape(256, 768)
        cot_b = cots[pl.ds(r * 2, 2)].reshape(256, 768)
        gate_w = wff[:, :, :, pl.ds(0, 768)].reshape(768, 768)
        up_w = wff[:, :, :, pl.ds(768, 768)].reshape(768, 768)
        down_w = wff[:, :, :, pl.ds(1536, 768)].reshape(768, 768)
        gate = dot(two_b, gate_w)
        up = dot(two_b, up_w)
        sig = 1.0 / (1.0 + jnp.exp(-gate))
        silu = gate * sig
        act_b = (silu * up).astype(BF16)
        act[at, :] = act_b
        grad_act = dot_right_t(cot_b, down_w)
        grad_gate = (grad_act * up * (sig * (1.0 + gate * (1.0 - sig)))).astype(BF16)
        grad_up = (grad_act * silu).astype(BF16)
        pre[at, pl.ds(0, 768)] = grad_gate
        pre[at, pl.ds(768, 768)] = grad_up
        back = dot_right_t(grad_gate, gate_w) + dot_right_t(grad_up, up_w)
        part[pl.ds(r * 2, 2)] = back.astype(BF16).reshape(2, SLAB, 768)
        part_out[pl.ds(r * 2, 2)] = dot(act_b, down_w).astype(BF16).reshape(2, SLAB, 768)
        return carry

    lax.fori_loop(0, 2, block, 0)
    links.finish()
    back_sum = line_scatter(links, place, part, back_room, sum_z)
    advance(back_sum)
    turn_t[...] = two[...].reshape(512, 768).T

    def first_grads(c, carry):
        at = pl.ds(pl.multiple_of(c * 256, 256), 256)
        wff[:, :, :, at] = dot(turn_t[...], pre[:, at]).astype(BF16).reshape(4, 4, 48, 256)
        return carry

    def last_grads(c, carry):
        at = pl.ds(pl.multiple_of(c * 256, 256), 256)
        to = pl.ds(pl.multiple_of(1536 + c * 256, 256), 256)
        cot_all = cots[:, :, at].reshape(512, 256)
        wff[:, :, :, to] = dot(turn_t[...], cot_all).astype(BF16).reshape(4, 4, 48, 256)
        return carry

    lax.fori_loop(0, 6, first_grads, 0)
    advance(back_sum)
    turn_t[...] = act[...].T
    lax.fori_loop(0, 3, last_grads, 0)
    ff = plane_scatter(links, place, wff, ff_room, ff_sum, False)
    advance(*ff)
    finish(back_sum)
    links.finish(6)

    grad = dot_right_t(sum_z[0].astype(BF16), perm_ref[...])
    middle = mid_s[...]
    scale_two = lax.rsqrt(mean_square(middle) + EPS)
    gm_s[...] = cot_ref[...].astype(F32) + norm_back(grad, middle * scale_two, scale_two)
    low = gm_s[...].astype(BF16)
    grad_att = dot_right_t(low, merged(wo)).astype(BF16)
    for z in range(4):
        to_heads[z] = dot_right_t(grad_att, perm_att[pl.ds(256 * z, 256), :]).astype(BF16)
    heads_swap = line_swap(links, place, to_heads, grads_ref)
    advance(heads_swap)
    out_sum = line_scatter(links, place, part_out, out_room, sum_out)
    advance(out_sum)
    turn_t[...] = one[...].reshape(512, 768).T
    og_part[...] = dot(att_by_z, low).astype(BF16).reshape(4, 256, 768)
    for s in range(4):
        terms[s, 18] = jnp.zeros((SLAB, SLAB), BF16)
    finish(heads_swap)
    advance(*ff)

    which = lax.broadcasted_iota(jnp.int32, (8, SLAB), 0)
    unit = (lax.broadcasted_iota(jnp.int32, (8, SLAB), 1) == which).astype(F32)
    at_lane = lax.broadcasted_iota(jnp.int32, (8, 256), 1)
    pick = (lax.div(at_lane, HD) == lax.broadcasted_iota(jnp.int32, (8, 256), 0)).astype(F32)
    logs, deltas = [], []
    for s in range(4):
        inner = grads_ref[s].astype(F32) * att_ref[s].astype(F32)
        delta = lax.dot_general(pick, inner, LANES, precision=HIGHEST, preferred_element_type=F32)
        log = lax.dot_general(unit, lse_ref[s], LANES, precision=HIGHEST, preferred_element_type=F32)
        logs.append([jnp.sum(jnp.where(which == k, log, 0.0), axis=0, keepdims=True) for k in range(3)])
        deltas.append([jnp.sum(jnp.where(which == k, delta, 0.0), axis=0, keepdims=True) for k in range(3)])

    scatters = []

    def keys_back(j):
        for s in range(4):
            cosine, sine = slab_turns(line_ref, turn_ref, s)
            grad = kv_own[j, s]
            d_s[pl.ds(s * SLAB, SLAB), pl.ds(256 * j + 128, 128)] = turned(grad, cosine, -sine).astype(BF16)
        at = pl.ds(256 * j, 256)
        wo[:, :, :, at] = dot(turn_t[...], d_s[:, at]).astype(BF16).reshape(4, 4, 48, 256)

    og_line = line_scatter(links, place, og_part, og_line_room, og_sum)
    spread = spread_rows()
    for j in range(3):

        def between(k, j=j):
            if j == 0:
                advance(*ff)
                if k == 0:
                    advance(out_sum)
            if j == 1:
                advance(*scatters[0])
            if j == 2 and k == 0:
                advance(*scatters[0])
                advance(*scatters[1])
            if j == 2 and k == 1:
                finish(*scatters[0])
                advance(*scatters[1])

        attend_back_head(
            j, table, q_ref, kvs[j], grads_ref, [v[j] for v in logs], [v[j] for v in deltas], accs, terms, pairs, between
        )
        sum_terms(table, terms, kvs[j])
        scatters.append(slab_scatter(links, place, kvs[j], kv_rooms[j], kv_own.at[j]))
        advance(*scatters[j])
        for s in range(4):
            cosine, sine = slab_turns(line_ref, turn_ref, s)
            grad = jnp.where(lane < 64, accs[s] * 0.125, 0.0)
            d_s[pl.ds(s * SLAB, SLAB), pl.ds(256 * j, 128)] = turned(grad, cosine, -sine).astype(BF16)
        if j == 0:
            finish(out_sum)
            advance(og_line)
            out_ref[...] = (mid_s[...] + sum_out[0]).astype(BF16)
            finish(*ff)
            down_sum_ref[...] = ff_sum[0, :, pl.ds(1536, 768)]
            for c in range(0, 1536, 768):
                for_line_ff[:, :, pl.ds(c, 768)] = (
                    dot(spread, ff_sum[0, :, pl.ds(c, 768)].astype(BF16)).astype(BF16).reshape(4, 16, 768)
                )
            grads_swap = line_swap(links, place, for_line_ff, got_ff_ref)
            advance(grads_swap)
        if j == 1:
            advance(og_line)

    advance(*scatters[2])
    advance(*scatters[1])
    keys_back(0)
    finish(og_line, grads_swap)
    og_next[...] = og_sum[0].astype(BF16).reshape(4, 4, 16, 768)
    finish(*scatters[1])
    advance(*scatters[2])
    keys_back(1)
    og = small_scatter(links, place, og_next, og_room, got_out_ref)
    advance(*scatters[2])
    advance(*og)
    finish(*scatters[2])
    for s in range(4):
        cosine, sine = slab_turns(line_ref, turn_ref, s)
        grad = kv_own[2, s]
        d_s[pl.ds(s * SLAB, SLAB), pl.ds(640, 128)] = turned(grad, cosine, -sine).astype(BF16)

    def last_block(r, carry):
        at = pl.ds(pl.multiple_of(r * 256, 256), 256)
        part[pl.ds(r * 2, 2)] = dot_right_t(d_s[at, :], merged(wqkv)).astype(BF16).reshape(2, SLAB, 768)
        return carry

    lax.fori_loop(0, 2, last_block, 0)
    in_sum = line_scatter(links, place, part, in_room, sum_z)
    advance(in_sum)
    at = pl.ds(512, 256)
    wo[:, :, :, at] = dot(turn_t[...], d_s[:, at]).astype(BF16).reshape(4, 4, 48, 256)
    qkv = plane_scatter(links, place, wo, qkv_room, qkv_sum, False)
    advance(*qkv)
    advance(*og)
    advance(*qkv)
    advance(in_sum)
    advance(*qkv)
    advance(*og)
    finish(in_sum)
    grad = dot_right_t(sum_z[0].astype(BF16), perm_ref[...])
    x = tok_ref[...].astype(F32)
    scale = lax.rsqrt(mean_square(x) + EPS)
    in_ref[...] = gm_s[...] + norm_back(grad, x * scale, scale)
    finish(*qkv)
    for_line[...] = dot(spread, qkv_sum[0].astype(BF16)).astype(BF16).reshape(4, 16, 768)
    last = line_swap(links, place, for_line, got_ref)
    advance(last)
    finish(*og)
    finish(last)
    links.finish()


LINE = pltpu.VMEM((4, SLAB, 768), BF16)
KV = pltpu.VMEM((4, 4, 4, SLAB, SLAB), BF16)
OUTS = [
    ((SLAB, 768), BF16),
    ((SLAB, 768), F32),
    ((48, 768), F32),
    ((4, 16, 1536), BF16),
    ((4, 16, 768), BF16),
    ((1, 16, 768), F32),
]
ROOM = (
    [
        pltpu.VMEM((1024, 768), BF16),
        pltpu.VMEM((1024, 1024), BF16),
        pltpu.SemaphoreType.DMA((2,)),
        pltpu.VMEM((4, 8, SLAB), F32),
        pltpu.VMEM((4, 4, 8, SLAB), F32),
        pltpu.VMEM((104, SLAB), jnp.int32),
        pltpu.SMEM((104, SLAB), jnp.int32),
        pltpu.SemaphoreType.DMA,
        pltpu.VMEM((4, 16, 768), BF16),
        pltpu.VMEM((4, 16, 1536), BF16),
        pltpu.VMEM((4, 16, 768), BF16),
        pltpu.VMEM((4, 16, 768), BF16),
        pltpu.VMEM((4, 16, 1536), BF16),
        LINE,
        LINE,
        pltpu.VMEM((4, 4, 48, 768), BF16),
        pltpu.VMEM((4, 4, 48, 768), BF16),
        pltpu.VMEM((4, 4, 48, 2304), BF16),
        pltpu.VMEM((4, SLAB, 384), BF16),
        KV,
        KV,
        KV,
        pltpu.VMEM((4, SLAB, SLAB), F32),
        pltpu.VMEM((4, SLAB, SLAB), F32),
        pltpu.VMEM((4, SLAB, SLAB), F32),
        pltpu.VMEM((4, SLAB, 256), BF16),
        pltpu.VMEM((4, SLAB, SLAB), F32),
        pltpu.VMEM((4, SLAB, 256), BF16),
        pltpu.VMEM((SLAB, 768), BF16),
        pltpu.VMEM((SLAB, 768), F32),
        pltpu.VMEM((SLAB, 768), F32),
        LINE,
        pltpu.VMEM((512, 768), BF16),
        pltpu.VMEM((512, 1536), BF16),
        pltpu.VMEM((768, 512), BF16),
        LINE,
        LINE,
        pltpu.VMEM((1, SLAB, 768), F32),
        pltpu.VMEM((1, SLAB, 768), F32),
        pltpu.VMEM((4, SLAB, 256), BF16),
        pltpu.VMEM((4, SLAB, 256), BF16),
        pltpu.VMEM((4, 19, SLAB, SLAB), BF16),
        pltpu.VMEM((4, 256, SLAB), BF16),
        pltpu.VMEM((3, 4, SLAB, SLAB), F32),
        pltpu.VMEM((512, 768), BF16),
        pltpu.VMEM((1, 48, 768), F32),
        pltpu.VMEM((1, 48, 2304), F32),
        pltpu.VMEM((4, 256, 768), BF16),
        pltpu.VMEM((1, 256, 768), F32),
        pltpu.VMEM((4, 4, 16, 768), BF16),
    ]
    + line_scatter_room(SLAB, 768)
    + plane_scatter_room(48, 2304, False)
    + line_scatter_room(SLAB, 768)
    + slab_scatter_room() * 3
    + plane_scatter_room(48, 768, False)
    + line_scatter_room(SLAB, 768)
    + line_scatter_room(256, 768)
    + SMALL_ROOM
)


def join_columns(w):
    rows = w.shape[1]
    return w.reshape(2, 2, rows, 16, 48).transpose(2, 1, 3, 0, 4).reshape(rows, 3072)


def per_device(
    tokens, gain_one, w_query, w_key, w_value, w_out, gain_two, w_gate, w_up, w_down, cotangent, segment_ids, positions
):
    blk, head = lax.axis_index("blk"), lax.axis_index("head")
    z, own = head * 2 + blk // 16, blk % 16
    perm = jnp.asarray(TO_PERM, BF16)
    perm_att = jnp.asarray(ATT_PERM, BF16)
    out_perm = jnp.asarray(OUT_PERM, BF16)
    turn = jnp.asarray(OFFSET_TURNS, F32)
    first_gain, second_gain = gain_one.astype(F32)[:, None], gain_two.astype(F32)[:, None]

    seg = segment_ids.reshape(2, SLAB)[head, 0].astype(F32)
    base = positions.reshape(2, SLAB)[head, 0].astype(F32)
    angles = base * jnp.asarray(FREQUENCY, F32)[None]
    row = lax.broadcasted_iota(jnp.int32, (8, SLAB), 0)
    lane = lax.broadcasted_iota(jnp.int32, (8, SLAB), 1)
    here = lane == own * 4 + z
    desc = jnp.where(
        row == 0,
        jnp.cos(angles),
        jnp.where(
            row == 1,
            jnp.sin(angles),
            jnp.where(here & (row == 2), seg, jnp.where(here & (row == 3), base, 0.0)),
        ),
    )
    w_attention = jnp.pad(jnp.concatenate([w_query, w_key, w_value, w_out], 1), ((0, 4), (0, 0)))
    w_ff = jnp.pad(jnp.concatenate([w_gate, w_up], 1), ((0, 4), (0, 0)))
    gains = jnp.pad(jnp.concatenate([first_gain, second_gain], 1), ((0, 4), (0, SLAB - 2)))

    output, input_grad, down_grad, got_ff, got_qkv, got_out = pl.pallas_call(
        layer_kernel,
        out_shape=tuple(jax.ShapeDtypeStruct(shape, kind) for shape, kind in OUTS),
        in_specs=[VMEM] * 9 + [pl.BlockSpec(memory_space=pl.ANY)] * 2,
        out_specs=tuple([VMEM] * len(OUTS)),
        scratch_shapes=ROOM + [pltpu.SemaphoreType.DMA((320,))] * 2,
        compiler_params=pltpu.CompilerParams(collective_id=0, has_side_effects=True, vmem_limit_bytes=62 * MIB),
        name="layer",
    )(tokens, cotangent, w_attention, w_ff, w_down, gains, perm, turn, desc, perm_att, out_perm)

    got_ff = got_ff[:, :12].astype(F32)
    got_qkv = got_qkv[:, :12].astype(F32)
    by_kind = got_qkv.reshape(4, 12, 3, 4, HD).transpose(3, 1, 0, 2, 4).reshape(4, 12, 768)
    gate_grad, up_grad = join_columns(got_ff[:, :, :768]), join_columns(got_ff[:, :, 768:])
    gain_one_grad = jnp.sum(by_kind[0] * w_query + by_kind[2] * w_key + by_kind[3] * w_value, axis=1)
    gain_two_grad = jnp.sum(gate_grad * w_gate + up_grad * w_up, axis=1)
    return (
        output,
        input_grad,
        gain_one_grad,
        by_kind[0] * first_gain,
        by_kind[2] * first_gain,
        by_kind[3] * first_gain,
        got_out[0, :12],
        gain_two_grad,
        gate_grad * second_gain,
        up_grad * second_gain,
        down_grad,
    )


def solution(mesh):
    rows = P(("grp", "blk", "head"), None)
    flat = P(("grp", "blk", "head"))
    weight = P(("blk", "head"), None)
    gain = P(("blk", "head"))
    ids = P(("grp", "blk"))
    in_specs = (rows, gain, weight, weight, weight, weight, gain, weight, weight, weight, rows, ids, ids)
    out_specs = (rows, rows, flat, rows, rows, rows, rows, flat, rows, rows, rows)
    return jax.shard_map(per_device, mesh=mesh, in_specs=in_specs, out_specs=out_specs, check_vma=False)
```

```python
import math

import jax
import jax.numpy as jnp
import numpy as np
from jax import lax
from jax.experimental import pallas as pl
from jax.experimental.pallas import tpu as pltpu
from jax.sharding import PartitionSpec as P

MESH = pl.DeviceIdType.MESH
F32 = jnp.float32
BF16 = jnp.bfloat16
HD = 64
CONTS = 8
SLAB = 128
LOW = -1e30
EPS = 1e-05
LANES = (((1,), (1,)), ((), ()))
HIGHEST = lax.Precision.HIGHEST
MIB = 1 << 20
VMEM = pl.BlockSpec(memory_space=pltpu.VMEM)
SMEM = pl.BlockSpec(memory_space=pltpu.SMEM)


def feature_order():
    place = np.arange(768)
    p, z, r = place // 48, place // 12 % 4, place % 12
    t = (z % 2) * 32 + p * 2 + z // 2
    return t * 12 + r


ORDER = feature_order()
TO_PERM = np.zeros((768, 768), np.float32)
TO_PERM[ORDER, np.arange(768)] = 1.0


ATT_PERM = np.pad(TO_PERM.reshape(4, 192, 768), ((0, 0), (0, 64), (0, 0))).reshape(1024, 768)
OUT_PERM = np.pad(ATT_PERM.reshape(1024, 16, 4, 12).transpose(0, 2, 1, 3), ((0, 0), (0, 0), (0, 0), (0, 4))).reshape(1024, 1024)
LANE_FREQUENCY = 10000.0 ** (-(np.arange(128) % 32) * 2.0 / HD) * (np.arange(128) < HD)
OFFSET_ANGLES = np.arange(SLAB)[:, None] * LANE_FREQUENCY[None]
BASE_ANGLES = SLAB * np.arange(24)[:, None] * LANE_FREQUENCY[None]
BASE_TURNS = np.stack([np.cos(BASE_ANGLES), np.sin(BASE_ANGLES)]).astype(np.float32)
OFFSET_TURNS = np.stack([np.cos(OFFSET_ANGLES), np.sin(OFFSET_ANGLES)]).astype(np.float32)


class Place:
    def __init__(self):
        self.core = lax.axis_index("grp")
        blk = lax.axis_index("blk")
        self.blk, self.head = blk, lax.axis_index("head")
        self.x = lax.rem(blk, 4)
        self.y = lax.rem(lax.div(blk, 4), 4)
        self.z = self.head * 2 + lax.div(blk, 16)

    def other_core(self):
        return (1 - self.core, self.blk, self.head)

    def device(self, x=None, y=None, z=None):
        x = self.x if x is None else x
        y = self.y if y is None else y
        z = self.z if z is None else z
        return (self.core, lax.rem(z, 2) * 16 + y * 4 + x, lax.div(z, 2))

    def ring(self, axis):
        return Ring(self, axis)


class Ring:
    def __init__(self, place, axis):
        self.place, self.axis = place, axis
        self.own = getattr(place, axis)
        self.next = lax.rem(self.own + 1, 4)
        self.prev = lax.rem(self.own + 3, 4)
        self.far = lax.rem(self.own + 2, 4)

    def device(self, index):
        return self.place.device(**{self.axis: index})


def announce(place):
    partners = [place.other_core()]
    for axis in ("x", "y", "z"):
        ring = place.ring(axis)
        partners += [ring.device(ring.next), ring.device(ring.prev), ring.device(ring.far)]
    barrier = pltpu.get_barrier_semaphore()
    for partner in partners:
        pl.semaphore_signal(barrier, inc=1, device_id=partner, device_id_type=MESH)
    return len(partners)


def enter(partners):
    pl.semaphore_wait(pltpu.get_barrier_semaphore(), partners)


class Links:
    def __init__(self, send, recv):
        self.send, self.recv, self.used, self.sent = send, recv, 0, []

    def copy(self, source, target, device):
        k = self.used
        self.used += 1
        copy = pltpu.make_async_remote_copy(
            src_ref=source,
            dst_ref=target,
            send_sem=self.send.at[k],
            recv_sem=self.recv.at[k],
            device_id=device,
            device_id_type=MESH,
        )
        copy.start()
        self.sent.append(copy)
        return copy

    def finish(self, count=None):
        count = len(self.sent) if count is None else count
        for copy in self.sent[:count]:
            copy.wait_send()
        del self.sent[:count]


def together(steps):
    steps = list(steps)
    while steps:
        left = []
        for step in steps:
            try:
                next(step)
                left.append(step)
            except StopIteration:
                pass
        steps = left


def ring_gather(links, ring, slot):
    right = links.copy(slot(ring.own, None), slot(ring.own, None), ring.device(ring.next))
    left = links.copy(slot(ring.own, None), slot(ring.own, None), ring.device(ring.prev))
    yield
    right.wait_recv()
    on_right = links.copy(slot(ring.prev, 0), slot(ring.prev, 0), ring.device(ring.next))
    left.wait_recv()
    on_left = links.copy(slot(ring.next, 1), slot(ring.next, 1), ring.device(ring.prev))
    yield
    on_right.wait_recv()
    on_left.wait_recv()


def add_into(target, terms, kind):
    *lead, rows, columns = target.shape
    step = 16
    for size in (128, 64, 48, 32):
        if rows % size == 0 and size * columns <= 48 * 1024:
            step = size
            break
    count = rows // step

    def body(k, carry):
        at, rest = [], lax.div(k, count)
        for size in reversed(lead):
            at.insert(0, lax.rem(rest, size))
            rest = lax.div(rest, size)
        at = (*at, pl.ds(pl.multiple_of(lax.rem(k, count) * step, step), step), slice(None))
        total = terms[0][at].astype(kind)
        for term in terms[1:]:
            total = total + term[at].astype(kind)
        target[at] = total
        return carry

    trips = math.prod(lead) * count
    lax.fori_loop(0, trips, body, 0, unroll=2 if trips % 2 == 0 else 1)


def ring_scatter(links, ring, part, room, target, kind):
    low, high, sum_low, sum_high, from_prev, from_next = room
    nxt, prv = ring.device(ring.next), ring.device(ring.prev)
    far_low = links.copy(part(ring.far, 0), low, nxt)
    far_high = links.copy(part(ring.far, 1), high, prv)
    next_high = links.copy(part(ring.next, 1), from_prev(1), nxt)
    prev_low = links.copy(part(ring.prev, 0), from_next(0), prv)
    yield
    far_low.wait_recv()
    add_into(sum_low, [part(ring.next, 0), low], BF16)
    next_low = links.copy(sum_low, from_prev(0), nxt)
    far_high.wait_recv()
    add_into(sum_high, [part(ring.prev, 1), high], BF16)
    prev_high = links.copy(sum_high, from_next(1), prv)
    yield
    for copy in (next_high, prev_low, next_low, prev_high):
        copy.wait_recv()
    add_into(target, [part(ring.own, None), from_prev(None), from_next(None)], kind)


def lead_part(part):
    return pl.ds(0, 4) if part is None else pl.ds(2 * part, 2)


def row_part(rows, part):
    first = (rows // 2 + 15) // 16 * 16
    if part is None:
        return 0, rows
    return (0, first) if part == 0 else (first, rows - first)


def regions(rows, columns, by_rows):
    if by_rows:
        return [(0, rows // 2, 0, columns), (rows // 2, rows // 2, 0, columns)]
    return [(0, rows, 0, columns // 2), (0, rows, columns // 2, columns // 2)]


def plane_gather(links, place, buf, by_rows):
    rows, columns = buf.shape[2:]

    def half(region, x_first):
        r0, rn, c0, cn = region

        def one(k, part):
            off, size = row_part(rn, part)
            y, x = (place.y, k) if x_first else (k, place.x)
            return buf.at[y, x, pl.ds(r0 + off, size), pl.ds(c0, cn)]

        def line(k, part):
            y, x = (k, lead_part(part)) if x_first else (lead_part(part), k)
            return buf.at[y, x, pl.ds(r0, rn), pl.ds(c0, cn)]

        yield from ring_gather(links, place.ring("x" if x_first else "y"), one)
        yield from ring_gather(links, place.ring("y" if x_first else "x"), line)

    a, b = regions(rows, columns, by_rows)
    return half(a, True), half(b, False)


def plane_scatter_room(rows, columns, by_rows):
    rooms = []
    for _, rn, _, cn in regions(rows, columns, by_rows):
        rooms += [pltpu.VMEM((2, rn, cn), BF16)] * 4 + [pltpu.VMEM((4, rn, cn), BF16)] * 3
        low, high = row_part(rn, 0)[1], row_part(rn, 1)[1]
        rooms += [pltpu.VMEM((1, low, cn), BF16), pltpu.VMEM((1, high, cn), BF16)] * 2
        rooms += [pltpu.VMEM((1, rn, cn), BF16)] * 2
    return rooms


def plane_scatter(links, place, buf, rooms, target, by_rows):
    rows, columns = buf.shape[2:]

    def half(region, room, x_first):
        r0, rn, c0, cn = region
        low, high, sum_low, sum_high, prev, nxt, lined = room[:7]
        low1, high1, sum_low1, sum_high1, prev1, nxt1 = room[7:]

        def line(k, part):
            y, x = (lead_part(part), k) if x_first else (k, lead_part(part))
            return buf.at[y, x, pl.ds(r0, rn), pl.ds(c0, cn)]

        def one(k, part):
            off, size = row_part(rn, part)
            return lined.at[pl.ds(k, 1), pl.ds(off, size), :]

        def lined_part(ref):
            return lambda part: ref.at[lead_part(part)]

        def one_part(ref):
            def view(part):
                off, size = row_part(rn, part)
                return ref.at[:, pl.ds(off, size), :]

            return view

        room_a = (low, high, sum_low, sum_high, lined_part(prev), lined_part(nxt))
        room_b = (low1, high1, sum_low1, sum_high1, one_part(prev1), one_part(nxt1))
        yield from ring_scatter(links, place.ring("x" if x_first else "y"), line, room_a, lined, BF16)
        out = target.at[:, pl.ds(r0, rn), pl.ds(c0, cn)]
        yield from ring_scatter(links, place.ring("y" if x_first else "x"), one, room_b, out, F32)

    a, b = regions(rows, columns, by_rows)
    return half(a, rooms[:13], False), half(b, rooms[13:], True)


def small_scatter_room(rows, columns):
    half = columns // 2
    return [
        pltpu.VMEM((3, 4, rows, half), BF16),
        pltpu.VMEM((4, rows, half), BF16),
        pltpu.VMEM((3, 1, rows, half), BF16),
    ] * 2


def direct_scatter(links, ring, part, room, target, kind):
    copies = []
    for k, to in enumerate((ring.next, ring.prev, ring.far)):
        copies.append(links.copy(part(to), room.at[k], ring.device(to)))
    yield
    for copy in copies:
        copy.wait_recv()
    add_into(target, [part(ring.own), room.at[0], room.at[1], room.at[2]], kind)


def small_scatter(links, place, buf, c0, width, rooms, target):
    size = width // 2

    def half(first, room, x_first):
        columns = pl.ds(first, size)
        firsts, lined, lasts = room

        def line(k):
            return buf.at[:, k, :, columns] if x_first else buf.at[k, :, :, columns]

        yield from direct_scatter(links, place.ring("x" if x_first else "y"), line, firsts, lined, BF16)
        out = target.at[:, :, columns]
        yield from direct_scatter(
            links, place.ring("y" if x_first else "x"), lambda k: lined.at[pl.ds(k, 1)], lasts, out, F32
        )

    return half(c0, rooms[:3], False), half(c0 + size, rooms[3:], True)


def line_scatter_room(rows, columns):
    low, high = row_part(rows, 0)[1], row_part(rows, 1)[1]
    return [pltpu.VMEM((1, low, columns), BF16), pltpu.VMEM((1, high, columns), BF16)] * 2 + [
        pltpu.VMEM((1, rows, columns), BF16)
    ] * 2


def line_scatter(links, place, buf, room, target):
    rows = buf.shape[1]

    def part(k, half):
        off, size = row_part(rows, half)
        return buf.at[pl.ds(k, 1), pl.ds(off, size), :]

    def view(ref):
        def cut(half):
            off, size = row_part(rows, half)
            return ref.at[:, pl.ds(off, size), :]

        return cut

    low, high, sum_low, sum_high, prev, nxt = room
    yield from ring_scatter(
        links, place.ring("z"), part, (low, high, sum_low, sum_high, view(prev), view(nxt)), target, F32
    )


def line_gather(links, place, buf):
    rows = buf.shape[1]

    def slot(k, half):
        off, size = row_part(rows, half)
        return buf.at[k, pl.ds(off, size)]

    yield from ring_gather(links, place.ring("z"), slot)


def line_swap(links, place, source, target):
    ring = place.ring("z")
    copies = []
    for other in (ring.next, ring.prev, ring.far):
        copies.append(links.copy(source.at[other], target.at[ring.own], ring.device(other)))
    target[ring.own] = source[ring.own]
    yield
    for copy in copies:
        copy.wait_recv()


def small_gather(links, ring, slot):
    right = links.copy(slot(ring.own), slot(ring.own), ring.device(ring.next))
    left = links.copy(slot(ring.own), slot(ring.own), ring.device(ring.prev))
    yield
    right.wait_recv()
    left.wait_recv()
    on = links.copy(slot(ring.prev), slot(ring.prev), ring.device(ring.next))
    yield
    on.wait_recv()


def shared_gather(links, place, buf):
    half = buf.shape[3] // 2
    flip = place.core == 1
    columns = pl.ds(pl.multiple_of(place.core * half, 128), half)
    first, second = jnp.where(flip, place.y, place.x), jnp.where(flip, place.x, place.y)
    first_next, first_prev, first_far = [lax.rem(first + k, 4) for k in (1, 3, 2)]
    second_next, second_prev, second_far = [lax.rem(second + k, 4) for k in (1, 3, 2)]

    def block(s, f, part=None):
        y, x = jnp.where(flip, f, s), jnp.where(flip, s, f)
        rows = pl.ds(0, 48) if part is None else (pl.ds(0, 32) if part == 0 else pl.ds(32, 16))
        return buf.at[y, x, rows, columns]

    def device(s, f):
        return place.device(x=jnp.where(flip, s, f), y=jnp.where(flip, f, s))

    def send(s, f, to, part=None):
        return links.copy(block(s, f, part), block(s, f, part), to)

    handed = []

    def hand(s, f):
        handed.append(links.copy(block(s, f), block(s, f), place.other_core()))

    on_right, on_left = device(second, first_next), device(second, first_prev)
    up, down = device(second_next, first), device(second_prev, first)
    order = (first, first_prev, first_next, first_far)
    ups, downs = [], []

    def line(k):
        ups.append(send(second, order[k], up))
        downs.append(send(second, order[k], down))

    right = send(second, first, on_right)
    left = send(second, first, on_left)
    line(0)
    yield
    right.wait_recv()
    far_low = send(second, first_prev, on_right, 0)
    line(1)
    left.wait_recv()
    far_high = send(second, first_next, on_left, 1)
    line(2)
    hand(second, first_prev)
    hand(second, first_next)
    yield
    far_low.wait_recv()
    far_high.wait_recv()
    line(3)
    hand(second, first_far)
    yield
    far = []
    for k in range(4):
        ups[k].wait_recv()
        if k < 2:
            far.append(send(second_prev, order[k], up))
        hand(second_prev, order[k])
        downs[k].wait_recv()
        if k >= 2:
            far.append(send(second_next, order[k], down))
        hand(second_next, order[k])
    yield
    for k in range(4):
        far[k].wait_recv()
        hand(second_far, order[k])
    yield
    for copy in handed:
        copy.wait_recv()


def advance(*steps):
    for step in steps:
        next(step, None)


def finish(*steps):
    together(steps)


def dot(left, right):
    return jnp.dot(left, right, preferred_element_type=F32)


def dot_right_t(left, right):
    return lax.dot_general(left, right, LANES, preferred_element_type=F32)


def pack_rows():
    i = lax.broadcasted_iota(jnp.int32, (48, 64), 0)
    k = lax.broadcasted_iota(jnp.int32, (48, 64), 1)
    return (k == lax.div(i, 12) * 16 + lax.rem(i, 12)).astype(BF16)


def spread_rows():
    k = lax.broadcasted_iota(jnp.int32, (64, 48), 0)
    i = lax.broadcasted_iota(jnp.int32, (64, 48), 1)
    return (k == lax.div(i, 12) * 16 + lax.rem(i, 12)).astype(BF16)


def merged(ref):
    rows, columns = ref.shape[0] * ref.shape[1] * ref.shape[2], ref.shape[3]
    return ref[...].reshape(rows, columns)


def mean_square(values):
    return jnp.mean(values * values, axis=-1, keepdims=True)


def norm_back(grad, normed, scale):
    return scale * (grad - normed * jnp.mean(grad * normed, axis=-1, keepdims=True))


def slab_turns(line_ref, turn_ref, s):
    rows = line_ref[s]
    cos_base, sin_base = rows[0:1], rows[1:2]
    cos_off, sin_off = turn_ref[0], turn_ref[1]
    lane = lax.broadcasted_iota(jnp.int32, (SLAB, SLAB), 1)
    sign = jnp.where(lane < 32, -1.0, jnp.where(lane < 64, 1.0, 0.0))
    return cos_base * cos_off - sin_base * sin_off, (sin_base * cos_off + cos_base * sin_off) * sign


def turned(field, cosine, sine):
    lane = lax.broadcasted_iota(jnp.int32, (SLAB, SLAB), 1)
    return field * cosine + jnp.where(lane < 32, pltpu.roll(field, 96, 1), pltpu.roll(field, 32, 1)) * sine


def half_rows(values, k):
    return values[k * SLAB : (k + 1) * SLAB]


def direct_gather(links, place, buf, first, second):
    ring_x, ring_y = place.ring("x"), place.ring("y")
    a, b = pl.ds(*first), pl.ds(*second)

    def spread(ring, view):
        return [links.copy(view, view, ring.device(k)) for k in (ring.next, ring.prev, ring.far)]

    over_x = spread(ring_x, buf.at[place.y, place.x, :, a])
    over_y = spread(ring_y, buf.at[place.y, place.x, :, b])
    yield
    for copy in over_x:
        copy.wait_recv()
    over_x = spread(ring_y, buf.at[place.y, :, :, a])
    for copy in over_y:
        copy.wait_recv()
    over_y = spread(ring_x, buf.at[:, place.x, :, b])
    yield
    for copy in over_x + over_y:
        copy.wait_recv()


def slab_place(at):
    return lax.div(at, 16), lax.rem(lax.div(at, 4), 4), lax.rem(at, 4)


def flow_gather(links, over, along, block):
    s, f = along.own, over.own
    on_right, on_left = over.device(over.next), over.device(over.prev)
    up, down = along.device(along.next), along.device(along.prev)
    order = (f, over.prev, over.next, over.far)
    ups, downs, far = [], [], []

    def send(s, f, to, part=None):
        return links.copy(block(s, f, part), block(s, f, part), to)

    def line(k):
        ups.append(send(s, order[k], up))
        downs.append(send(s, order[k], down))

    right, left = send(s, f, on_right), send(s, f, on_left)
    line(0)
    yield
    right.wait_recv()
    far_low = send(s, over.prev, on_right, 0)
    left.wait_recv()
    far_high = send(s, over.next, on_left, 1)
    line(1)
    line(2)
    yield
    far_low.wait_recv()
    far_high.wait_recv()
    line(3)
    yield
    for k in range(4):
        ups[k].wait_recv()
        if k < 2:
            far.append(send(along.prev, order[k], up))
        downs[k].wait_recv()
        if k >= 2:
            far.append(send(along.next, order[k], down))
    yield
    for copy in far:
        copy.wait_recv()


def slab_gather(links, place, buf):
    ring_x, ring_y = place.ring("x"), place.ring("y")

    def slabs(z0, part):
        return pl.ds(z0, 2) if part is None else pl.ds(z0 + part, 1)

    return (
        flow_gather(links, ring_x, ring_y, lambda s, f, part: buf.at[s, f, slabs(0, part)]),
        flow_gather(links, ring_y, ring_x, lambda s, f, part: buf.at[f, s, slabs(2, part)]),
    )


def slab_scatter_room():
    few, many = pltpu.VMEM((2, 2, SLAB, SLAB), BF16), pltpu.VMEM((4, 2, SLAB, SLAB), BF16)
    one, two = pltpu.VMEM((1, SLAB, SLAB), BF16), pltpu.VMEM((2, SLAB, SLAB), BF16)
    return ([few] * 4 + [many] * 3 + [one] * 4 + [two] * 2) * 2


def slab_scatter(links, place, buf, rooms, target):
    def half(z0, room, x_first):
        low, high, sum_low, sum_high, prev, nxt, lined = room[:7]
        low1, high1, sum_low1, sum_high1, prev1, nxt1 = room[7:]

        def line(k, part):
            y, x = (lead_part(part), k) if x_first else (k, lead_part(part))
            return buf.at[y, x, pl.ds(z0, 2)]

        def one(k, part):
            return lined.at[k] if part is None else lined.at[k, pl.ds(part, 1)]

        def lined_part(ref):
            return lambda part: ref.at[lead_part(part)]

        def one_part(ref):
            return lambda part: ref.at[pl.ds(0, 2) if part is None else pl.ds(part, 1)]

        room_a = (low, high, sum_low, sum_high, lined_part(prev), lined_part(nxt))
        room_b = (low1, high1, sum_low1, sum_high1, one_part(prev1), one_part(nxt1))
        yield from ring_scatter(links, place.ring("x" if x_first else "y"), line, room_a, lined, BF16)
        out = target.at[pl.ds(z0, 2)]
        yield from ring_scatter(links, place.ring("y" if x_first else "x"), one, room_b, out, F32)

    return half(0, rooms[:13], False), half(2, rooms[13:], True)


def keys_of(kv_ref, table, s, first, count):
    places = [slab_place(jnp.clip(table[s * 24 + first + k, 0], 0, 63)) for k in range(count)]
    return jnp.concatenate([kv_ref[y, x, z] for y, x, z in places], 0)


def query_positions(table, s, shape, axis):
    return table[s * 24 + 20, 0] + lax.broadcasted_iota(jnp.int32, shape, axis)


def attend_head(j, table, q_ref, kv_ref, top_ref, sum_ref, acc_ref, between):
    def fold(s, first, count, first_key):
        keys = keys_of(kv_ref, table, s, first, count)
        width = count * SLAB
        pos_q = query_positions(table, s, (SLAB, 1), 0)
        pos_k = first_key + lax.broadcasted_iota(jnp.int32, (1, width), 1)
        scores = dot_right_t(q_ref[s, :, pl.ds(j * 128, 128)], keys)
        scores = jnp.where(pos_k <= pos_q, scores, LOW)
        top = top_ref[s]
        new_top = jnp.maximum(top, jnp.max(scores, axis=1, keepdims=True))
        weights = jnp.exp(scores - new_top[:, 0:1])
        decay = jnp.exp(top - new_top)
        sum_ref[s] = sum_ref[s] * decay + jnp.sum(weights, axis=1, keepdims=True)
        acc_ref[s] = acc_ref[s] * decay + dot(weights.astype(BF16), keys)
        top_ref[s] = new_top

    for s in range(4):
        top_ref[s] = jnp.full((SLAB, SLAB), LOW, F32)
        sum_ref[s] = jnp.zeros((SLAB, SLAB), F32)
        acc_ref[s] = jnp.zeros((SLAB, SLAB), F32)

    def prompt(c, carry):
        for s in range(4):
            fold(s, c * 4, 4, c * 512)
        return carry

    lax.fori_loop(0, 2, prompt, 0)
    between(0)
    lax.fori_loop(2, 4, prompt, 0)
    between(1)
    for s in range(4):
        fold(s, 16, 2, 2048)


def attend_back_head(j, table, q_ref, kv_ref, grad_ref, logs, deltas, dq_ref, terms_ref, pair_ref, between):
    lane = lax.broadcasted_iota(jnp.int32, (SLAB, SLAB), 1)
    for s in range(4):
        grads = grad_ref[s, :, pl.ds(128 * (j // 2), 128)].astype(F32)
        if j != 1:
            grads = pltpu.roll(grads, 64, 1)
        pair_ref[s, pl.ds(0, SLAB)] = q_ref[s, :, pl.ds(j * 128, 128)]
        pair_ref[s, pl.ds(SLAB, SLAB)] = jnp.where(lane < 64, 0.0, grads).astype(BF16)
        dq_ref[s] = jnp.zeros((SLAB, SLAB), F32)

    def fold(s, first, count, first_key):
        keys = keys_of(kv_ref, table, s, first, count)
        width = count * SLAB
        pos_q = query_positions(table, s, (1, SLAB), 1)
        pos_k = first_key + lax.broadcasted_iota(jnp.int32, (width, 1), 0)
        pair = pair_ref[s]
        both = dot_right_t(keys, pair)
        weights = jnp.where(pos_k <= pos_q, jnp.exp(both[:, :SLAB] - logs[s]), 0.0)
        slopes = (weights * (both[:, SLAB:] - deltas[s])).astype(BF16)
        terms = dot(jnp.concatenate([slopes, weights.astype(BF16)], 1), pair)
        terms_ref[s, pl.ds(first, count)] = terms.astype(BF16).reshape(count, SLAB, SLAB)
        dq_ref[s] += lax.dot_general(slopes, keys, (((0,), (0,)), ((), ())), preferred_element_type=F32)

    def prompt(c, carry):
        for s in range(4):
            fold(s, c * 4, 4, c * 512)
        return carry

    lax.fori_loop(0, 2, prompt, 0)
    between(0)
    lax.fori_loop(2, 4, prompt, 0)
    between(1)
    for s in range(4):
        fold(s, 16, 2, 2048)


def sum_terms(table, terms_ref, part_ref):
    def slab(t, carry):
        places = [jnp.clip(table[96 + s, t], 0, 18) for s in range(4)]
        total = terms_ref[0, places[0]].astype(F32)
        for s in range(1, 4):
            total = total + terms_ref[s, places[s]].astype(F32)
        y, x, z = slab_place(t)
        part_ref[y, x, z] = total.astype(BF16)
        return carry

    lax.fori_loop(0, 64, slab, 0, unroll=4)


def lookups(total, own, meta_ref):
    seg, base = total[2:3], total[3:4]
    lane = lax.broadcasted_iota(jnp.int32, (1, SLAB), 1)
    lane_at = lane.astype(F32)
    n = lax.broadcasted_iota(jnp.int32, (24, 1), 0)
    back_rows = jnp.zeros((8, SLAB), F32)
    back_row = lax.broadcasted_iota(jnp.int32, (8, 1), 0)
    for s in range(4):
        mine = lane == own * 4 + s
        seg_q = jnp.sum(jnp.where(mine, seg, 0.0), axis=1, keepdims=True)
        base_q = jnp.sum(jnp.where(mine, base, 0.0), axis=1, keepdims=True)
        prompt = jnp.where(seg_q >= CONTS + 1.0, CONTS + 1.0, 0.0)
        want = jnp.where(n < 16, prompt, seg_q)
        hit = (seg == want) & (base == n.astype(F32) * SLAB) & (lane < 64)
        places = jnp.max(jnp.where(hit, lane_at, 0.0), axis=1, keepdims=True)
        listed = jnp.where(n == 20, base_q, places)
        meta_ref[pl.ds(s * 24, 24), :] = jnp.broadcast_to(listed, (24, SLAB)).astype(jnp.int32)
        visible = (seg == prompt) | (seg == seg_q)
        places = jnp.where(visible, jnp.minimum(base * (1.0 / SLAB), 17.0), 18.0)
        back_rows = jnp.where(back_row == s, places, back_rows)
    meta_ref[pl.ds(96, 8), :] = back_rows.astype(jnp.int32)


def column_of(gain_ref):
    i = lax.broadcasted_iota(jnp.int32, (12, 12), 0)
    k = lax.broadcasted_iota(jnp.int32, (12, 12), 1)
    return jnp.sum(jnp.where(i == k, gain_ref[...].astype(F32), 0.0), axis=1, keepdims=True)


def plane_columns(z):
    return [((z % 2) * 32 + p * 2 + z // 2) * 48 for p in range(16)]


def own_slab(place, at, seg_ref, pos_ref, base_ref):
    lane = lax.broadcasted_iota(jnp.int32, (1, SLAB), 1)
    high = place.head == 1
    seg = jnp.where(high, seg_ref[1:2], seg_ref[0:1]).astype(F32)
    base = (jnp.where(high, pos_ref[1:2], pos_ref[0:1]) - lane).astype(F32)
    m = lax.broadcasted_iota(jnp.int32, (24, SLAB), 0).astype(F32)
    cosine, sine = [
        jnp.sum(jnp.where(m == base * (1.0 / SLAB), base_ref[k], 0.0), axis=0, keepdims=True) for k in range(2)
    ]
    row = lax.broadcasted_iota(jnp.int32, (8, SLAB), 0)
    here = (lane == at) & (row >= 2)
    facts = jnp.where(here, jnp.where(row == 2, seg, jnp.where(row == 3, base, 0.0)), 0.0)
    return jnp.where(row == 0, cosine, jnp.where(row == 1, sine, facts))


def finish_kernel(
    ff_ref, qkv_ref, og_ref, wq_ref, wk_ref, wv_ref, gate_ref, up_ref, gain1_ref, gain2_ref, out_in, grad_in, down_in,
    out_ref, grad_ref, dgain1_ref, dq_ref, dk_ref, dv_ref, do_ref, dgain2_ref, dgate_ref, dup_ref, down_ref,
):
    out_ref[...] = out_in[...]
    grad_ref[...] = grad_in[...]
    down_ref[...] = down_in[...]
    i = lax.broadcasted_iota(jnp.int32, (12, 12), 0)
    k = lax.broadcasted_iota(jnp.int32, (12, 12), 1)

    def row_of(column):
        return jnp.sum(jnp.where(i == k, column, 0.0), axis=0, keepdims=True)

    gain = column_of(gain1_ref)
    grads = [qkv_ref[z].astype(F32)[:12] for z in range(4)]
    total = jnp.zeros((12, 1), F32)
    for c, w_ref, to_ref in ((128, wq_ref, dq_ref), (0, wk_ref, dk_ref), (64, wv_ref, dv_ref)):
        grad = jnp.concatenate([grads[z][:, 256 * j + c : 256 * j + c + HD] for z in range(4) for j in range(3)], 1)
        total = total + jnp.sum(grad * w_ref[...].astype(F32), axis=1, keepdims=True)
        to_ref[...] = grad * gain
    dgain1_ref[...] = row_of(total)
    do_ref[...] = og_ref[0, pl.ds(0, 12)]

    gain = column_of(gain2_ref)
    total = jnp.zeros((12, 1), F32)
    for k_at, w_ref, to_ref in ((0, gate_ref, dgate_ref), (768, up_ref, dup_ref)):
        pieces = {}
        for z in range(4):
            grad = ff_ref[z, :, pl.ds(k_at, 768)].astype(F32)[:12]
            for p, c in enumerate(plane_columns(z)):
                pieces[c] = grad[:, 48 * p : 48 * p + 48]
        grad = jnp.concatenate([pieces[c] for c in sorted(pieces)], 1)
        total = total + jnp.sum(grad * w_ref[...].astype(F32), axis=1, keepdims=True)
        to_ref[...] = grad * gain
    dgain2_ref[...] = row_of(total)


def layer_kernel(
    tok_ref, cot_ref, wq_ref, wk_ref, wv_ref, wo_ref, gate_ref, up_ref, down_ref, gain1_ref, gain2_ref, seg_ref, pos_ref,
    perm_ref, turn_ref, base_ref, perm_att_hbm, out_perm_hbm,
    out_ref, in_ref, down_sum_ref, got_ff_ref, got_ref, got_out_ref,
    perm_att, out_perm, const_sem, line_ref, descs, meta_ref, table, table_sem,
    for_line, for_line_ff, rows, rows_o, rows_ff, one, cots, wqkv, wo, wff, q_ref, kv0, kv1, kv2,
    tops, sums, accs, att_ref, lse_ref, atts, att_s, mid_s, gm_s, two, act, pre, turn_t, part, part_out, sum_z, sum_out,
    to_heads, grads_ref, terms, pairs, kv_own, d_s, qkv_sum, ff_sum,
    og_part, og_sum, og_next, *rest,
):
    send, recv = rest[-2:]
    rooms = list(rest[:-2])

    def take(count):
        out = rooms[:count]
        del rooms[:count]
        return out

    back_room, ff_room, out_room = take(6), take(26), take(6)
    kv_rooms = [take(26) for _ in range(3)]
    qkv_rooms = [take(6) for _ in range(3)]
    in_room, og_line_room, og_room = take(6), take(6), take(6)
    kvs = (kv0, kv1, kv2)

    const_copies = [
        pltpu.make_async_copy(perm_att_hbm, perm_att, const_sem.at[0]),
        pltpu.make_async_copy(out_perm_hbm, out_perm, const_sem.at[1]),
    ]
    for copy in const_copies:
        copy.start()
    place = Place()
    partners = announce(place)
    links = Links(send, recv)
    own = place.y * 4 + place.x

    line_ref[place.z] = own_slab(place, own * 4 + place.z, seg_ref, pos_ref, base_ref)
    lined = small_gather(links, place.ring("z"), lambda k: line_ref.at[k])
    gain = column_of(gain1_ref)
    w_q, w_k, w_v = [ref[...].astype(F32) * gain for ref in (wq_ref, wk_ref, wv_ref)]
    none, blank = jnp.zeros((12, HD), F32), jnp.zeros((4, 768), F32)
    for z in range(4):
        pieces, last = [], []
        for j in range(3):
            at = slice(192 * z + 64 * j, 192 * z + 64 * j + 64)
            pieces += [w_k[:, at], w_v[:, at]]
            last += [w_q[:, at], none]
        pieces += last
        for_line[z] = jnp.concatenate([jnp.concatenate(pieces, 1), blank], 0).astype(BF16)
    x = dot(tok_ref[...], perm_ref[...])
    one[place.z] = (x * lax.rsqrt(mean_square(x) + EPS)).astype(BF16)
    enter(partners)
    swap = line_swap(links, place, for_line, rows)
    advance(swap, lined)
    ones = line_gather(links, place, one)
    advance(ones)
    finish(swap)
    wqkv[place.y, place.x] = dot(pack_rows(), rows[...].reshape(64, 768)).astype(BF16)
    kv_gather = direct_gather(links, place, wqkv, (0, 256), (256, 128))
    q_gather = direct_gather(links, place, wqkv, (512, 256), (384, 128))
    advance(kv_gather)
    gain = column_of(gain2_ref)
    for k, ref in enumerate((gate_ref, up_ref)):
        w = ref[...].astype(F32) * gain
        for z in range(4):
            pieces = [w[:, c : c + 48] for c in plane_columns(z)]
            for_line_ff[z, :, pl.ds(768 * k, 768)] = jnp.concatenate([jnp.concatenate(pieces, 1), blank], 0).astype(BF16)
    advance(lined, kv_gather, ones)
    advance(q_gather)
    finish(lined)
    descs[place.y, place.x] = line_ref[0] + line_ref[1] + line_ref[2] + line_ref[3]
    desc_x = small_gather(links, place.ring("x"), lambda k: descs.at[place.y, k])
    desc_y = small_gather(links, place.ring("y"), lambda k: descs.at[k])
    advance(desc_x)
    finish(ones, kv_gather)
    rows_o[place.z] = jnp.concatenate([wo_ref[...].astype(F32), blank], 0).astype(BF16)
    o_line = small_gather(links, place.ring("z"), lambda k: rows_o.at[k])
    ff_swap = line_swap(links, place, for_line_ff, rows_ff)
    cots[place.z] = cot_ref[...]
    cot_gather = line_gather(links, place, cots)

    lines = one[...].reshape(512, 768)
    gathers = [slab_gather(links, place, kv) for kv in kvs]
    for j in range(3):
        field = dot(lines, wqkv[:, :, :, pl.ds(128 * j, 128)].reshape(768, 128))
        for s in range(4):
            cosine, sine = slab_turns(line_ref, turn_ref, s)
            kvs[j][place.y, place.x, s] = turned(half_rows(field, s), cosine, sine).astype(BF16)
        if j < 2:
            advance(*gathers[j])
    advance(o_line, ff_swap, cot_gather)
    advance(q_gather, desc_x)
    advance(*gathers[0])
    advance(*gathers[0])
    finish(desc_x)
    advance(desc_y)
    advance(*gathers[1])
    advance(*gathers[2])
    advance(desc_y, o_line)
    finish(q_gather)
    field = dot(lines, wqkv[:, :, :, pl.ds(384, 384)].reshape(768, 384))
    for s in range(4):
        cosine, sine = slab_turns(line_ref, turn_ref, s)
        for j in range(3):
            query = turned(half_rows(field[:, 128 * j : 128 * j + 128], s), cosine, sine)
            q_ref[s, :, pl.ds(128 * j, 128)] = (query * 0.125).astype(BF16)
    advance(*gathers[0])
    advance(*gathers[1])
    finish(desc_y)
    total = jnp.zeros((8, SLAB), F32)
    for y in range(4):
        for k in range(4):
            total = total + descs[y, k]
    lookups(total, own, meta_ref)
    copy = pltpu.make_async_copy(meta_ref, table, table_sem)
    copy.start()
    copy.wait()
    finish(ff_swap, o_line)
    wo[place.y, place.x] = dot(pack_rows(), rows_o[...].reshape(64, 768)).astype(BF16)
    for c in range(0, 1536, 768):
        wff[place.y, place.x, :, pl.ds(c, 768)] = dot(
            pack_rows(), rows_ff[:, :, pl.ds(c, 768)].reshape(64, 768)
        ).astype(BF16)
    wff[place.y, place.x, :, pl.ds(1536, 768)] = down_ref[...]
    advance(cot_gather)
    for copy in const_copies:
        copy.wait()

    lane = lax.broadcasted_iota(jnp.int32, (SLAB, SLAB), 1)
    o_gather = direct_gather(links, place, wo, (0, 384), (384, 384))
    w_gather = shared_gather(links, place, wff)
    for j in range(3):
        finish(*gathers[j])

        def between(k, j=j):
            if j == 0 and k == 0:
                advance(*gathers[1])
                advance(*gathers[2])
            if j == 0 and k == 1:
                advance(*gathers[2])
            if j == 1 and k == 0:
                advance(cot_gather)
                links.finish(40)
            if j == 1 and k == 1:
                advance(*gathers[2])
            if j == 2 and k == 0:
                links.finish(40)
            if j == 2 and k == 1:
                advance(o_gather)
                advance(w_gather)

        if j == 2:
            advance(o_gather)
            advance(w_gather)
        attend_head(j, table, q_ref, kvs[j], tops, sums, accs, between)
        for s in range(4):
            head = accs[s] / sums[s]
            if j == 0:
                att_ref[s, :, 0:128] = jnp.where(lane < 64, pltpu.roll(head, 64, 1), 0.0).astype(BF16)
            elif j == 1:
                att_ref[s, :, 0:128] = jnp.where(lane < 64, att_ref[s, :, 0:128].astype(F32), head).astype(BF16)
            else:
                att_ref[s, :, 128:256] = jnp.where(lane < 64, pltpu.roll(head, 64, 1), 0.0).astype(BF16)
            logs = tops[s] + jnp.log(sums[s])
            lse_ref[s] = logs if j == 0 else jnp.where(lane == j, logs, lse_ref[s])
    att_swap = line_swap(links, place, att_ref, atts)
    advance(att_swap)
    advance(w_gather)
    finish(cot_gather)
    links.finish(40)
    finish(att_swap, o_gather)

    att = dot(atts[0], perm_att[pl.ds(0, 256), :])
    for z in range(1, 4):
        att = att + dot(atts[z], perm_att[pl.ds(256 * z, 256), :])
    att_s[...] = att.astype(BF16)
    mid_s[...] = tok_ref[...].astype(F32) + dot(att_s[...], merged(wo))
    middle = mid_s[...]
    scale_two = lax.rsqrt(mean_square(middle) + EPS)
    two[place.z] = dot((middle * scale_two).astype(BF16), perm_ref[...]).astype(BF16)
    two_gather = line_gather(links, place, two)
    advance(two_gather)
    advance(w_gather)
    att = dot(atts[0], out_perm[pl.ds(0, 256), :])
    for z in range(1, 4):
        att = att + dot(atts[z], out_perm[pl.ds(256 * z, 256), :])
    att_by_z = att.astype(BF16).T
    advance(two_gather)
    together([w_gather, two_gather])

    def block(r, carry):
        at = pl.ds(pl.multiple_of(r * 256, 256), 256)
        two_b = two[pl.ds(r * 2, 2)].reshape(256, 768)
        cot_b = cots[pl.ds(r * 2, 2)].reshape(256, 768)
        gate_w = wff[:, :, :, pl.ds(0, 768)].reshape(768, 768)
        up_w = wff[:, :, :, pl.ds(768, 768)].reshape(768, 768)
        down_w = wff[:, :, :, pl.ds(1536, 768)].reshape(768, 768)
        gate = dot(two_b, gate_w)
        up = dot(two_b, up_w)
        sig = 1.0 / (1.0 + jnp.exp(-gate))
        silu = gate * sig
        act_b = (silu * up).astype(BF16)
        act[at, :] = act_b
        grad_act = dot_right_t(cot_b, down_w)
        grad_gate = (grad_act * up * (sig * (1.0 + gate * (1.0 - sig)))).astype(BF16)
        grad_up = (grad_act * silu).astype(BF16)
        pre[at, pl.ds(0, 768)] = grad_gate
        pre[at, pl.ds(768, 768)] = grad_up
        back = dot_right_t(grad_gate, gate_w) + dot_right_t(grad_up, up_w)
        part[pl.ds(r * 2, 2)] = back.astype(BF16).reshape(2, SLAB, 768)
        return carry

    def out_block(r, carry):
        at = pl.ds(pl.multiple_of(r * 256, 256), 256)
        down_w = wff[:, :, :, pl.ds(1536, 768)].reshape(768, 768)
        part_out[pl.ds(r * 2, 2)] = dot(act[at, :], down_w).astype(BF16).reshape(2, SLAB, 768)
        return carry

    lax.fori_loop(0, 2, block, 0)
    links.finish()
    back_sum = line_scatter(links, place, part, back_room, sum_z)
    advance(back_sum)
    lax.fori_loop(0, 2, out_block, 0)
    turn_t[...] = two[...].reshape(512, 768).T

    def first_grads(c, carry):
        at = pl.ds(pl.multiple_of(c * 256, 256), 256)
        wff[:, :, :, at] = dot(turn_t[...], pre[:, at]).astype(BF16).reshape(4, 4, 48, 256)
        return carry

    def last_grads(c, carry):
        at = pl.ds(pl.multiple_of(c * 256, 256), 256)
        to = pl.ds(pl.multiple_of(1536 + c * 256, 256), 256)
        cot_all = cots[:, :, at].reshape(512, 256)
        wff[:, :, :, to] = dot(turn_t[...], cot_all).astype(BF16).reshape(4, 4, 48, 256)
        return carry

    lax.fori_loop(0, 6, first_grads, 0)
    advance(back_sum)
    turn_t[...] = act[...].T
    lax.fori_loop(0, 3, last_grads, 0)
    ff = plane_scatter(links, place, wff, ff_room, ff_sum, False)
    advance(*ff)
    finish(back_sum)
    links.finish(6)

    grad = dot_right_t(sum_z[0].astype(BF16), perm_ref[...])
    middle = mid_s[...]
    scale_two = lax.rsqrt(mean_square(middle) + EPS)
    gm_s[...] = cot_ref[...].astype(F32) + norm_back(grad, middle * scale_two, scale_two)
    low = gm_s[...].astype(BF16)
    grad_att = dot_right_t(low, merged(wo)).astype(BF16)
    for z in range(4):
        to_heads[z] = dot_right_t(grad_att, perm_att[pl.ds(256 * z, 256), :]).astype(BF16)
    heads_swap = line_swap(links, place, to_heads, grads_ref)
    advance(heads_swap)
    out_sum = line_scatter(links, place, part_out, out_room, sum_out)
    advance(out_sum)
    turn_t[...] = one[...].reshape(512, 768).T
    og_part[...] = dot(att_by_z, low).astype(BF16).reshape(4, 256, 768)
    for s in range(4):
        terms[s, 18] = jnp.zeros((SLAB, SLAB), BF16)
    finish(heads_swap)
    advance(*ff)

    which = lax.broadcasted_iota(jnp.int32, (8, SLAB), 0)
    unit = (lax.broadcasted_iota(jnp.int32, (8, SLAB), 1) == which).astype(F32)
    at_lane = lax.broadcasted_iota(jnp.int32, (8, 256), 1)
    pick = (lax.div(at_lane, HD) == lax.broadcasted_iota(jnp.int32, (8, 256), 0)).astype(F32)
    logs, deltas = [], []
    for s in range(4):
        inner = grads_ref[s].astype(F32) * att_ref[s].astype(F32)
        delta = lax.dot_general(pick, inner, LANES, precision=HIGHEST, preferred_element_type=F32)
        log = lax.dot_general(unit, lse_ref[s], LANES, precision=HIGHEST, preferred_element_type=F32)
        logs.append([jnp.sum(jnp.where(which == k, log, 0.0), axis=0, keepdims=True) for k in range(3)])
        deltas.append([jnp.sum(jnp.where(which == k, delta, 0.0), axis=0, keepdims=True) for k in range(3)])

    scatters = []

    def keys_turn(j):
        for s in range(4):
            cosine, sine = slab_turns(line_ref, turn_ref, s)
            d_s[pl.ds(s * SLAB, SLAB), pl.ds(128 * j, 128)] = turned(kv_own[j, s], cosine, -sine).astype(BF16)

    def keys_grads(j):
        pair = jnp.concatenate([d_s[:, pl.ds(128 * j, 128)], d_s[:, pl.ds(384 + 128 * j, 128)]], 1)
        wo[:, :, :, pl.ds(256 * j, 256)] = dot(turn_t[...], pair).astype(BF16).reshape(4, 4, 48, 256)
        scatter = small_scatter(links, place, wo, 256 * j, 256, qkv_rooms[j], qkv_sum)
        advance(*scatter)
        return scatter

    og_line = line_scatter(links, place, og_part, og_line_room, og_sum)
    spread = spread_rows()
    for j in range(3):

        def between(k, j=j):
            if j == 0:
                advance(*ff)
                if k == 0:
                    advance(out_sum)
            if j == 1:
                advance(*scatters[0])
            if j == 2 and k == 0:
                advance(*scatters[0])
                advance(*scatters[1])
            if j == 2 and k == 1:
                finish(*scatters[0])
                advance(*scatters[1])

        attend_back_head(
            j, table, q_ref, kvs[j], grads_ref, [v[j] for v in logs], [v[j] for v in deltas], accs, terms, pairs, between
        )
        sum_terms(table, terms, kvs[j])
        scatters.append(slab_scatter(links, place, kvs[j], kv_rooms[j], kv_own.at[j]))
        advance(*scatters[j])
        for s in range(4):
            cosine, sine = slab_turns(line_ref, turn_ref, s)
            grad = jnp.where(lane < 64, accs[s] * 0.125, 0.0)
            d_s[pl.ds(s * SLAB, SLAB), pl.ds(384 + 128 * j, 128)] = turned(grad, cosine, -sine).astype(BF16)
        if j == 0:
            finish(out_sum)
            advance(og_line)
            out_ref[...] = (mid_s[...] + sum_out[0]).astype(BF16)
            finish(*ff)
            down_sum_ref[...] = ff_sum[0, :, pl.ds(1536, 768)]
            for c in range(0, 1536, 768):
                for_line_ff[:, :, pl.ds(c, 768)] = (
                    dot(spread, ff_sum[0, :, pl.ds(c, 768)].astype(BF16)).astype(BF16).reshape(4, 16, 768)
                )
            grads_swap = line_swap(links, place, for_line_ff, got_ff_ref)
            advance(grads_swap)
        if j == 1:
            advance(og_line)

    advance(*scatters[2])
    advance(*scatters[1])
    keys_turn(0)
    qkv = list(keys_grads(0))
    finish(og_line, grads_swap)
    og_next[...] = og_sum[0].astype(BF16).reshape(4, 4, 16, 768)
    links.finish(60)
    finish(*scatters[1])
    advance(*scatters[2])
    keys_turn(1)
    qkv += keys_grads(1)
    og = small_scatter(links, place, og_next, 0, 768, og_room, got_out_ref)
    advance(*og)
    advance(*scatters[2])
    links.finish(60)
    advance(*qkv)
    finish(*scatters[2])
    keys_turn(2)

    def last_block(r, carry):
        at = pl.ds(pl.multiple_of(r * 256, 256), 256)
        part[pl.ds(r * 2, 2)] = dot_right_t(d_s[at, :], merged(wqkv)).astype(BF16).reshape(2, SLAB, 768)
        return carry

    lax.fori_loop(0, 2, last_block, 0)
    in_sum = line_scatter(links, place, part, in_room, sum_z)
    advance(in_sum)
    last_qkv = keys_grads(2)
    finish(*qkv)
    advance(*og)
    advance(in_sum)
    advance(*last_qkv)
    finish(*og)
    links.finish(len(links.sent) - 12)
    finish(*last_qkv)
    for_line[...] = dot(spread, qkv_sum[0].astype(BF16)).astype(BF16).reshape(4, 16, 768)
    last = line_swap(links, place, for_line, got_ref)
    advance(last)
    finish(in_sum)
    grad = dot_right_t(sum_z[0].astype(BF16), perm_ref[...])
    x = tok_ref[...].astype(F32)
    scale = lax.rsqrt(mean_square(x) + EPS)
    in_ref[...] = gm_s[...] + norm_back(grad, x * scale, scale)
    links.finish()
    finish(last)


LINE = pltpu.VMEM((4, SLAB, 768), BF16)
KV = pltpu.VMEM((4, 4, 4, SLAB, SLAB), BF16)
OUTS = [
    ((SLAB, 768), BF16),
    ((SLAB, 768), F32),
    ((48, 768), F32),
    ((4, 16, 1536), BF16),
    ((4, 16, 768), BF16),
    ((1, 16, 768), F32),
]
ROOM = (
    [
        pltpu.VMEM((1024, 768), BF16),
        pltpu.VMEM((1024, 1024), BF16),
        pltpu.SemaphoreType.DMA((2,)),
        pltpu.VMEM((4, 8, SLAB), F32),
        pltpu.VMEM((4, 4, 8, SLAB), F32),
        pltpu.VMEM((104, SLAB), jnp.int32),
        pltpu.SMEM((104, SLAB), jnp.int32),
        pltpu.SemaphoreType.DMA,
        pltpu.VMEM((4, 16, 768), BF16),
        pltpu.VMEM((4, 16, 1536), BF16),
        pltpu.VMEM((4, 16, 768), BF16),
        pltpu.VMEM((4, 16, 768), BF16),
        pltpu.VMEM((4, 16, 1536), BF16),
        LINE,
        LINE,
        pltpu.VMEM((4, 4, 48, 768), BF16),
        pltpu.VMEM((4, 4, 48, 768), BF16),
        pltpu.VMEM((4, 4, 48, 2304), BF16),
        pltpu.VMEM((4, SLAB, 384), BF16),
        KV,
        KV,
        KV,
        pltpu.VMEM((4, SLAB, SLAB), F32),
        pltpu.VMEM((4, SLAB, SLAB), F32),
        pltpu.VMEM((4, SLAB, SLAB), F32),
        pltpu.VMEM((4, SLAB, 256), BF16),
        pltpu.VMEM((4, SLAB, SLAB), F32),
        pltpu.VMEM((4, SLAB, 256), BF16),
        pltpu.VMEM((SLAB, 768), BF16),
        pltpu.VMEM((SLAB, 768), F32),
        pltpu.VMEM((SLAB, 768), F32),
        LINE,
        pltpu.VMEM((512, 768), BF16),
        pltpu.VMEM((512, 1536), BF16),
        pltpu.VMEM((768, 512), BF16),
        LINE,
        LINE,
        pltpu.VMEM((1, SLAB, 768), F32),
        pltpu.VMEM((1, SLAB, 768), F32),
        pltpu.VMEM((4, SLAB, 256), BF16),
        pltpu.VMEM((4, SLAB, 256), BF16),
        pltpu.VMEM((4, 19, SLAB, SLAB), BF16),
        pltpu.VMEM((4, 256, SLAB), BF16),
        pltpu.VMEM((3, 4, SLAB, SLAB), F32),
        pltpu.VMEM((512, 768), BF16),
        pltpu.VMEM((1, 48, 768), F32),
        pltpu.VMEM((1, 48, 2304), F32),
        pltpu.VMEM((4, 256, 768), BF16),
        pltpu.VMEM((1, 256, 768), F32),
        pltpu.VMEM((4, 4, 16, 768), BF16),
    ]
    + line_scatter_room(SLAB, 768)
    + plane_scatter_room(48, 2304, False)
    + line_scatter_room(SLAB, 768)
    + slab_scatter_room() * 3
    + small_scatter_room(48, 256) * 3
    + line_scatter_room(SLAB, 768)
    + line_scatter_room(256, 768)
    + small_scatter_room(16, 768)
)


def per_device(
    tokens, gain_one, w_query, w_key, w_value, w_out, gain_two, w_gate, w_up, w_down, cotangent, segment_ids, positions
):
    gains = (gain_one.reshape(1, 12), gain_two.reshape(1, 12))
    output, input_grad, down_grad, got_ff, got_qkv, got_out = pl.pallas_call(
        layer_kernel,
        out_shape=tuple(jax.ShapeDtypeStruct(shape, kind) for shape, kind in OUTS),
        in_specs=[VMEM] * 16 + [pl.BlockSpec(memory_space=pl.ANY)] * 2,
        out_specs=tuple([VMEM] * len(OUTS)),
        scratch_shapes=ROOM + [pltpu.SemaphoreType.DMA((400,))] * 2,
        compiler_params=pltpu.CompilerParams(collective_id=0, has_side_effects=True, vmem_limit_bytes=62 * MIB),
        name="layer",
    )(
        tokens, cotangent, w_query, w_key, w_value, w_out, w_gate, w_up, w_down, *gains,
        segment_ids.reshape(2, SLAB), positions.reshape(2, SLAB),
        jnp.asarray(TO_PERM, BF16), jnp.asarray(OFFSET_TURNS, F32), jnp.asarray(BASE_TURNS, F32),
        jnp.asarray(ATT_PERM, BF16), jnp.asarray(OUT_PERM, BF16),
    )
    small, square, wide = [jax.ShapeDtypeStruct((rows, columns), F32) for rows, columns in ((1, 12), (12, 768), (12, 3072))]
    output, input_grad, gain_one_grad, dq, dk, dv, do, gain_two_grad, dgate, dup, down_grad = pl.pallas_call(
        finish_kernel,
        out_shape=(*[jax.ShapeDtypeStruct(*OUTS[k]) for k in range(2)], small, square, square, square, square, small, wide, wide,
                   jax.ShapeDtypeStruct(*OUTS[2])),
        in_specs=[VMEM] * 13,
        out_specs=(VMEM,) * 11,
        name="finish",
    )(got_ff, got_qkv, got_out, w_query, w_key, w_value, w_gate, w_up, *gains, output, input_grad, down_grad)
    return (
        output, input_grad, gain_one_grad.reshape(12), dq, dk, dv, do, gain_two_grad.reshape(12), dgate, dup, down_grad
    )


def solution(mesh):
    rows = P(("grp", "blk", "head"), None)
    flat = P(("grp", "blk", "head"))
    weight = P(("blk", "head"), None)
    gain = P(("blk", "head"))
    ids = P(("grp", "blk"))
    in_specs = (rows, gain, weight, weight, weight, weight, gain, weight, weight, weight, rows, ids, ids)
    out_specs = (rows, rows, flat, rows, rows, rows, rows, flat, rows, rows, rows)
    return jax.shard_map(per_device, mesh=mesh, in_specs=in_specs, out_specs=out_specs, check_vma=False)
```

```python
import math

import jax
import jax.numpy as jnp
import numpy as np
from jax import lax
from jax.experimental import pallas as pl
from jax.experimental.pallas import tpu as pltpu
from jax.sharding import PartitionSpec as P

MESH = pl.DeviceIdType.MESH
F32 = jnp.float32
BF16 = jnp.bfloat16
HD = 64
CONTS = 8
SLAB = 128
LOW = -1e30
EPS = 1e-05
LANES = (((1,), (1,)), ((), ()))
HIGHEST = lax.Precision.HIGHEST
MIB = 1 << 20
VMEM = pl.BlockSpec(memory_space=pltpu.VMEM)
SMEM = pl.BlockSpec(memory_space=pltpu.SMEM)


def feature_order():
    place = np.arange(768)
    p, z, r = place // 48, place // 12 % 4, place % 12
    t = (z % 2) * 32 + p * 2 + z // 2
    return t * 12 + r


ORDER = feature_order()
TO_PERM = np.zeros((768, 768), np.float32)
TO_PERM[ORDER, np.arange(768)] = 1.0


ATT_PERM = np.pad(TO_PERM.reshape(4, 192, 768), ((0, 0), (0, 64), (0, 0))).reshape(1024, 768)
OUT_PERM = np.pad(ATT_PERM.reshape(1024, 16, 4, 12).transpose(0, 2, 1, 3), ((0, 0), (0, 0), (0, 0), (0, 4))).reshape(1024, 1024)
LANE_FREQUENCY = 10000.0 ** (-(np.arange(128) % 32) * 2.0 / HD) * (np.arange(128) < HD)
OFFSET_ANGLES = np.arange(SLAB)[:, None] * LANE_FREQUENCY[None]
BASE_ANGLES = SLAB * np.arange(24)[:, None] * LANE_FREQUENCY[None]
BASE_TURNS = np.stack([np.cos(BASE_ANGLES), np.sin(BASE_ANGLES)]).astype(np.float32)
OFFSET_TURNS = np.stack([np.cos(OFFSET_ANGLES), np.sin(OFFSET_ANGLES)]).astype(np.float32)


class Place:
    def __init__(self):
        self.core = lax.axis_index("grp")
        blk = lax.axis_index("blk")
        self.blk, self.head = blk, lax.axis_index("head")
        self.x = lax.rem(blk, 4)
        self.y = lax.rem(lax.div(blk, 4), 4)
        self.z = self.head * 2 + lax.div(blk, 16)

    def other_core(self):
        return (1 - self.core, self.blk, self.head)

    def device(self, x=None, y=None, z=None):
        x = self.x if x is None else x
        y = self.y if y is None else y
        z = self.z if z is None else z
        return (self.core, lax.rem(z, 2) * 16 + y * 4 + x, lax.div(z, 2))

    def ring(self, axis):
        return Ring(self, axis)


class Ring:
    def __init__(self, place, axis):
        self.place, self.axis = place, axis
        self.own = getattr(place, axis)
        self.next = lax.rem(self.own + 1, 4)
        self.prev = lax.rem(self.own + 3, 4)
        self.far = lax.rem(self.own + 2, 4)

    def device(self, index):
        return self.place.device(**{self.axis: index})


def announce(place):
    partners = [place.other_core()]
    for axis in ("x", "y", "z"):
        ring = place.ring(axis)
        partners += [ring.device(ring.next), ring.device(ring.prev), ring.device(ring.far)]
    barrier = pltpu.get_barrier_semaphore()
    for partner in partners:
        pl.semaphore_signal(barrier, inc=1, device_id=partner, device_id_type=MESH)
    return len(partners)


def enter(partners):
    pl.semaphore_wait(pltpu.get_barrier_semaphore(), partners)


class Links:
    def __init__(self, send, recv):
        self.send, self.recv, self.sends, self.recvs, self.sent = send, recv, 0, 0, []

    def send_slot(self):
        self.sends += 1
        return self.send.at[self.sends - 1]

    def recv_slot(self):
        self.recvs += 1
        return self.recv.at[self.recvs - 1]

    def start(self, source, target, device, send, recv):
        copy = pltpu.make_async_remote_copy(
            src_ref=source, dst_ref=target, send_sem=send, recv_sem=recv, device_id=device, device_id_type=MESH
        )
        copy.start()
        return copy

    def copy(self, source, target, device):
        copy = self.start(source, target, device, self.send_slot(), self.recv_slot())
        self.sent.append(copy.wait_send)
        return copy

    def group(self, copies, view, recv=None):
        send = self.send_slot()
        slots = [self.recv_slot()] * len(copies) if recv is None else recv
        for (source, target, device), slot in zip(copies, slots):
            self.start(source, target, device, send, slot)
        self.sent.append(lambda: self.arrived(view, send))
        return lambda: self.arrived(view, slots[0])

    def arrived(self, view, semaphore):
        pltpu.make_async_copy(view, view, semaphore).wait()

    def finish(self, count=None):
        count = len(self.sent) if count is None else count
        for wait in self.sent[:count]:
            wait()
        del self.sent[:count]


def together(steps):
    steps = list(steps)
    while steps:
        left = []
        for step in steps:
            try:
                next(step)
                left.append(step)
            except StopIteration:
                pass
        steps = left


def ring_gather(links, ring, slot):
    right = links.copy(slot(ring.own, None), slot(ring.own, None), ring.device(ring.next))
    left = links.copy(slot(ring.own, None), slot(ring.own, None), ring.device(ring.prev))
    yield
    right.wait_recv()
    on_right = links.copy(slot(ring.prev, 0), slot(ring.prev, 0), ring.device(ring.next))
    left.wait_recv()
    on_left = links.copy(slot(ring.next, 1), slot(ring.next, 1), ring.device(ring.prev))
    yield
    on_right.wait_recv()
    on_left.wait_recv()


def add_into(target, terms, kind):
    *lead, rows, columns = target.shape
    step = 16
    for size in (128, 64, 48, 32):
        if rows % size == 0 and size * columns <= 48 * 1024:
            step = size
            break
    count = rows // step

    def body(k, carry):
        at, rest = [], lax.div(k, count)
        for size in reversed(lead):
            at.insert(0, lax.rem(rest, size))
            rest = lax.div(rest, size)
        at = (*at, pl.ds(pl.multiple_of(lax.rem(k, count) * step, step), step), slice(None))
        total = terms[0][at].astype(kind)
        for term in terms[1:]:
            total = total + term[at].astype(kind)
        target[at] = total
        return carry

    trips = math.prod(lead) * count
    lax.fori_loop(0, trips, body, 0, unroll=2 if trips % 2 == 0 else 1)


def ring_scatter(links, ring, part, room, target, kind):
    low, high, sum_low, sum_high, from_prev, from_next = room
    nxt, prv = ring.device(ring.next), ring.device(ring.prev)
    far_low = links.copy(part(ring.far, 0), low, nxt)
    far_high = links.copy(part(ring.far, 1), high, prv)
    next_high = links.copy(part(ring.next, 1), from_prev(1), nxt)
    prev_low = links.copy(part(ring.prev, 0), from_next(0), prv)
    yield
    far_low.wait_recv()
    add_into(sum_low, [part(ring.next, 0), low], BF16)
    next_low = links.copy(sum_low, from_prev(0), nxt)
    far_high.wait_recv()
    add_into(sum_high, [part(ring.prev, 1), high], BF16)
    prev_high = links.copy(sum_high, from_next(1), prv)
    yield
    for copy in (next_high, prev_low, next_low, prev_high):
        copy.wait_recv()
    add_into(target, [part(ring.own, None), from_prev(None), from_next(None)], kind)


def lead_part(part):
    return pl.ds(0, 4) if part is None else pl.ds(2 * part, 2)


def row_part(rows, part):
    first = (rows // 2 + 15) // 16 * 16
    if part is None:
        return 0, rows
    return (0, first) if part == 0 else (first, rows - first)


def regions(rows, columns, by_rows):
    if by_rows:
        return [(0, rows // 2, 0, columns), (rows // 2, rows // 2, 0, columns)]
    return [(0, rows, 0, columns // 2), (0, rows, columns // 2, columns // 2)]


def plane_gather(links, place, buf, by_rows):
    rows, columns = buf.shape[2:]

    def half(region, x_first):
        r0, rn, c0, cn = region

        def one(k, part):
            off, size = row_part(rn, part)
            y, x = (place.y, k) if x_first else (k, place.x)
            return buf.at[y, x, pl.ds(r0 + off, size), pl.ds(c0, cn)]

        def line(k, part):
            y, x = (k, lead_part(part)) if x_first else (lead_part(part), k)
            return buf.at[y, x, pl.ds(r0, rn), pl.ds(c0, cn)]

        yield from ring_gather(links, place.ring("x" if x_first else "y"), one)
        yield from ring_gather(links, place.ring("y" if x_first else "x"), line)

    a, b = regions(rows, columns, by_rows)
    return half(a, True), half(b, False)


def plane_scatter_room(rows, columns, by_rows):
    rooms = []
    for _, rn, _, cn in regions(rows, columns, by_rows):
        rooms += [pltpu.VMEM((2, rn, cn), BF16)] * 4 + [pltpu.VMEM((4, rn, cn), BF16)] * 3
        low, high = row_part(rn, 0)[1], row_part(rn, 1)[1]
        rooms += [pltpu.VMEM((1, low, cn), BF16), pltpu.VMEM((1, high, cn), BF16)] * 2
        rooms += [pltpu.VMEM((1, rn, cn), BF16)] * 2
    return rooms


def plane_scatter(links, place, buf, rooms, target, by_rows):
    rows, columns = buf.shape[2:]

    def half(region, room, x_first):
        r0, rn, c0, cn = region
        low, high, sum_low, sum_high, prev, nxt, lined = room[:7]
        low1, high1, sum_low1, sum_high1, prev1, nxt1 = room[7:]

        def line(k, part):
            y, x = (lead_part(part), k) if x_first else (k, lead_part(part))
            return buf.at[y, x, pl.ds(r0, rn), pl.ds(c0, cn)]

        def one(k, part):
            off, size = row_part(rn, part)
            return lined.at[pl.ds(k, 1), pl.ds(off, size), :]

        def lined_part(ref):
            return lambda part: ref.at[lead_part(part)]

        def one_part(ref):
            def view(part):
                off, size = row_part(rn, part)
                return ref.at[:, pl.ds(off, size), :]

            return view

        room_a = (low, high, sum_low, sum_high, lined_part(prev), lined_part(nxt))
        room_b = (low1, high1, sum_low1, sum_high1, one_part(prev1), one_part(nxt1))
        yield from ring_scatter(links, place.ring("x" if x_first else "y"), line, room_a, lined, BF16)
        out = target.at[:, pl.ds(r0, rn), pl.ds(c0, cn)]
        yield from ring_scatter(links, place.ring("y" if x_first else "x"), one, room_b, out, F32)

    a, b = regions(rows, columns, by_rows)
    return half(a, rooms[:13], False), half(b, rooms[13:], True)


def small_scatter_room(rows, *sizes):
    rooms = []
    for size in sizes:
        rooms += [
            pltpu.VMEM((3, 4, rows, size), BF16),
            pltpu.VMEM((4, rows, size), BF16),
            pltpu.VMEM((3, 1, rows, size), BF16),
        ]
    return rooms


def direct_scatter(links, ring, part, room, target, kind):
    copies = [(part(to), room.at[k], ring.device(to)) for k, to in enumerate((ring.next, ring.prev, ring.far))]
    arrived = links.group(copies, room)
    yield
    arrived()
    add_into(target, [part(ring.own), room.at[0], room.at[1], room.at[2]], kind)


def small_scatter(links, place, buf, first, second, rooms, target):
    def half(region, room, x_first):
        columns = pl.ds(*region)
        firsts, lined, lasts = room

        def line(k):
            return buf.at[:, k, :, columns] if x_first else buf.at[k, :, :, columns]

        yield from direct_scatter(links, place.ring("x" if x_first else "y"), line, firsts, lined, BF16)
        out = target.at[:, :, columns]
        yield from direct_scatter(
            links, place.ring("y" if x_first else "x"), lambda k: lined.at[pl.ds(k, 1)], lasts, out, F32
        )

    return half(first, rooms[:3], False), half(second, rooms[3:], True)


def line_scatter_room(rows, columns):
    low, high = row_part(rows, 0)[1], row_part(rows, 1)[1]
    return [pltpu.VMEM((1, low, columns), BF16), pltpu.VMEM((1, high, columns), BF16)] * 2 + [
        pltpu.VMEM((1, rows, columns), BF16)
    ] * 2


def line_scatter(links, place, buf, room, target):
    rows = buf.shape[1]

    def part(k, half):
        off, size = row_part(rows, half)
        return buf.at[pl.ds(k, 1), pl.ds(off, size), :]

    def view(ref):
        def cut(half):
            off, size = row_part(rows, half)
            return ref.at[:, pl.ds(off, size), :]

        return cut

    low, high, sum_low, sum_high, prev, nxt = room
    yield from ring_scatter(
        links, place.ring("z"), part, (low, high, sum_low, sum_high, view(prev), view(nxt)), target, F32
    )


def line_gather(links, place, buf):
    rows = buf.shape[1]

    def slot(k, half):
        off, size = row_part(rows, half)
        return buf.at[k, pl.ds(off, size)]

    yield from ring_gather(links, place.ring("z"), slot)


def line_swap(links, place, source, target):
    ring = place.ring("z")
    copies = []
    for other in (ring.next, ring.prev, ring.far):
        copies.append(links.copy(source.at[other], target.at[ring.own], ring.device(other)))
    target[ring.own] = source[ring.own]
    yield
    for copy in copies:
        copy.wait_recv()


def small_gather(links, ring, slot, three):
    own = slot(ring.own)
    arrived = links.group([(own, own, ring.device(k)) for k in (ring.next, ring.prev, ring.far)], three)
    yield
    arrived()


def shared_gather(links, place, buf, start, size):
    half = size // 2
    flip = place.core == 1
    columns = pl.ds(pl.multiple_of(start + place.core * half, 128), half)
    first, second = jnp.where(flip, place.y, place.x), jnp.where(flip, place.x, place.y)
    first_next, first_prev, first_far = [lax.rem(first + k, 4) for k in (1, 3, 2)]
    second_next, second_prev, second_far = [lax.rem(second + k, 4) for k in (1, 3, 2)]

    def block(s, f, part=None):
        y, x = jnp.where(flip, f, s), jnp.where(flip, s, f)
        rows = pl.ds(0, 48) if part is None else (pl.ds(0, 32) if part == 0 else pl.ds(32, 16))
        return buf.at[y, x, rows, columns]

    def device(s, f):
        return place.device(x=jnp.where(flip, s, f), y=jnp.where(flip, f, s))

    def send(s, f, to, part=None):
        return links.copy(block(s, f, part), block(s, f, part), to)

    handed = []

    def hands(view):
        pair = links.send_slot(), links.recv_slot()
        links.sent.append(lambda: links.arrived(view, pair[0]))
        handed.append(lambda: links.arrived(view, pair[1]))
        return lambda s, f: links.start(block(s, f), block(s, f), place.other_core(), *pair)

    on_right, on_left = device(second, first_next), device(second, first_prev)
    up, down = device(second_next, first), device(second_prev, first)
    order = (first, first_prev, first_next, first_far)
    ups, downs = [], []

    def line(k):
        ups.append(send(second, order[k], up))
        downs.append(send(second, order[k], down))

    right = send(second, first, on_right)
    left = send(second, first, on_left)
    line(0)
    yield
    right.wait_recv()
    far_low = send(second, first_prev, on_right, 0)
    line(1)
    left.wait_recv()
    far_high = send(second, first_next, on_left, 1)
    line(2)
    hand = hands(buf.at[0, pl.ds(0, 2), :, columns])
    hand(second, first_prev)
    hand(second, first_next)
    yield
    far_low.wait_recv()
    far_high.wait_recv()
    line(3)
    hands(buf.at[0, 0, :, columns])(second, first_far)
    yield
    far = []
    hand = hands(buf.at[pl.ds(0, 2), :, :, columns])
    for k in range(4):
        ups[k].wait_recv()
        if k < 2:
            far.append(send(second_prev, order[k], up))
        hand(second_prev, order[k])
        downs[k].wait_recv()
        if k >= 2:
            far.append(send(second_next, order[k], down))
        hand(second_next, order[k])
    yield
    hand = hands(buf.at[0, :, :, columns])
    for k in range(4):
        far[k].wait_recv()
        hand(second_far, order[k])
    yield
    for wait in handed:
        wait()


def advance(*steps):
    for step in steps:
        next(step, None)


def finish(*steps):
    together(steps)


def dot(left, right):
    return jnp.dot(left, right, preferred_element_type=F32)


def dot_right_t(left, right):
    return lax.dot_general(left, right, LANES, preferred_element_type=F32)


def pack_rows():
    i = lax.broadcasted_iota(jnp.int32, (48, 64), 0)
    k = lax.broadcasted_iota(jnp.int32, (48, 64), 1)
    return (k == lax.div(i, 12) * 16 + lax.rem(i, 12)).astype(BF16)


def spread_rows():
    k = lax.broadcasted_iota(jnp.int32, (64, 48), 0)
    i = lax.broadcasted_iota(jnp.int32, (64, 48), 1)
    return (k == lax.div(i, 12) * 16 + lax.rem(i, 12)).astype(BF16)


def merged(ref):
    rows, columns = ref.shape[0] * ref.shape[1] * ref.shape[2], ref.shape[3]
    return ref[...].reshape(rows, columns)


def mean_square(values):
    return jnp.mean(values * values, axis=-1, keepdims=True)


def norm_back(grad, normed, scale):
    return scale * (grad - normed * jnp.mean(grad * normed, axis=-1, keepdims=True))


def slab_turns(line_ref, turn_ref, s):
    rows = line_ref[s]
    cos_base, sin_base = rows[0:1], rows[1:2]
    cos_off, sin_off = turn_ref[0], turn_ref[1]
    lane = lax.broadcasted_iota(jnp.int32, (SLAB, SLAB), 1)
    sign = jnp.where(lane < 32, -1.0, jnp.where(lane < 64, 1.0, 0.0))
    return cos_base * cos_off - sin_base * sin_off, (sin_base * cos_off + cos_base * sin_off) * sign


def turned(field, cosine, sine):
    lane = lax.broadcasted_iota(jnp.int32, (SLAB, SLAB), 1)
    return field * cosine + jnp.where(lane < 32, pltpu.roll(field, 96, 1), pltpu.roll(field, 32, 1)) * sine


def half_rows(values, k):
    return values[k * SLAB : (k + 1) * SLAB]


def direct_gather(links, place, buf, first, second):
    ring_x, ring_y = place.ring("x"), place.ring("y")
    a, b = pl.ds(*first), pl.ds(*second)

    def spread(ring, view, size):
        return links.group([(view, view, ring.device(k)) for k in (ring.next, ring.prev, ring.far)], size)

    over_x = spread(ring_x, buf.at[place.y, place.x, :, a], buf.at[0, pl.ds(0, 3), :, a])
    over_y = spread(ring_y, buf.at[place.y, place.x, :, b], buf.at[0, pl.ds(0, 3), :, b])
    yield
    over_x()
    over_x = spread(ring_y, buf.at[place.y, :, :, a], buf.at[pl.ds(0, 3), :, :, a])
    over_y()
    over_y = spread(ring_x, buf.at[:, place.x, :, b], buf.at[pl.ds(0, 3), :, :, b])
    yield
    over_x()
    over_y()


def turned_view(buf, flip):
    def view(along, over):
        first, second = (over, along) if flip else (along, over)
        return buf.at[first, second, pl.ds(2 if flip else 0, 2)]

    return view


def slab_gather_half(links, along, over, view):
    three, four = pl.ds(1, 3), pl.ds(0, 4)
    own = view(0, 0)
    over_arrived = links.group(
        [
            (own, view(0, 3), over.device(over.next)),
            (own, view(0, 1), over.device(over.prev)),
            (own, view(0, 2), over.device(over.far)),
        ],
        view(0, three),
    )
    up, down = along.device(along.next), along.device(along.prev)
    lines = [links.recv_slot(), links.recv_slot()]
    links.group([(own, view(3, 0), up), (own, view(1, 0), down)], view(0, pl.ds(0, 2)), lines)
    yield
    over_arrived()
    rest = view(0, three)
    links.group([(rest, view(3, three), up), (rest, view(1, three), down)], view(pl.ds(0, 2), three), lines)
    yield
    low, high = pl.ds(0, 2), pl.ds(2, 2)
    links.arrived(view(3, four), lines[0])
    far = [links.recv_slot()] * 2
    send = links.send_slot()
    links.start(view(3, low), view(2, low), up, send, far[0])
    links.arrived(view(1, four), lines[1])
    links.start(view(1, high), view(2, high), down, send, far[1])
    links.sent.append(lambda: links.arrived(view(0, four), send))
    yield
    links.arrived(view(2, four), far[0])


def slab_gather(links, place, buf):
    ring_x, ring_y = place.ring("x"), place.ring("y")
    return (
        slab_gather_half(links, ring_y, ring_x, turned_view(buf, False)),
        slab_gather_half(links, ring_x, ring_y, turned_view(buf, True)),
    )


def slab_scatter_room():
    many, line = pltpu.VMEM((2, 2, SLAB, SLAB), BF16), pltpu.VMEM((4, 2, SLAB, SLAB), BF16)
    return ([many] * 2 + [line] * 3 + [pltpu.VMEM((3, 2, SLAB, SLAB), BF16)]) * 2


def slab_scatter_half(links, along, over, view, room, target):
    low, high, prev, nxt, lined, lasts = room
    lo, hi, four = pl.ds(0, 2), pl.ds(2, 2), pl.ds(0, 4)
    up, down = along.device(along.next), along.device(along.prev)
    slots = [links.recv_slot() for _ in range(4)]
    links.group(
        [
            (view(2, lo), low, up),
            (view(2, hi), high, down),
            (view(1, hi), prev.at[hi], up),
            (view(3, lo), nxt.at[lo], down),
        ],
        view(lo, four),
        slots,
    )
    yield
    links.arrived(low, slots[0])
    add_into(view(1, lo), [view(1, lo), low], BF16)
    send = links.send_slot()
    links.start(view(1, lo), prev.at[lo], up, send, slots[2])
    links.arrived(high, slots[1])
    add_into(view(3, hi), [view(3, hi), high], BF16)
    links.start(view(3, hi), nxt.at[hi], down, send, slots[3])
    links.sent.append(lambda: links.arrived(view(0, four), send))
    yield
    links.arrived(prev, slots[2])
    links.arrived(nxt, slots[3])
    add_into(lined, [view(0, four), prev, nxt], BF16)
    arrived = links.group(
        [
            (lined.at[1], lasts.at[0], over.device(over.next)),
            (lined.at[3], lasts.at[1], over.device(over.prev)),
            (lined.at[2], lasts.at[2], over.device(over.far)),
        ],
        lasts,
    )
    yield
    arrived()
    add_into(target, [lined.at[0], lasts.at[0], lasts.at[1], lasts.at[2]], F32)


def slab_scatter(links, place, buf, rooms, target):
    ring_x, ring_y = place.ring("x"), place.ring("y")
    return (
        slab_scatter_half(links, ring_y, ring_x, turned_view(buf, False), rooms[:6], target.at[pl.ds(0, 2)]),
        slab_scatter_half(links, ring_x, ring_y, turned_view(buf, True), rooms[6:], target.at[pl.ds(2, 2)]),
    )


def slab_place(at):
    return lax.div(at, 16), lax.rem(lax.div(at, 4), 4), lax.rem(at, 4)


def keys_of(kv_ref, table, s, first, count):
    places = [slab_place(jnp.clip(table[s * 24 + first + k, 0], 0, 63)) for k in range(count)]
    return jnp.concatenate([kv_ref[y, x, z] for y, x, z in places], 0)


def query_positions(table, s, shape, axis):
    return table[s * 24 + 20, 0] + lax.broadcasted_iota(jnp.int32, shape, axis)


def attend_head(j, table, q_ref, kv_ref, top_ref, sum_ref, acc_ref, between):
    def fold(s, first, count, first_key):
        keys = keys_of(kv_ref, table, s, first, count)
        width = count * SLAB
        pos_q = query_positions(table, s, (1, SLAB), 1)
        pos_k = first_key + lax.broadcasted_iota(jnp.int32, (width, 1), 0)
        scores = dot_right_t(keys, q_ref[s, :, pl.ds(j * 128, 128)])
        scores = jnp.where(pos_k <= pos_q, scores, LOW)
        top, total = top_ref[s][0:1], sum_ref[s][0:1]
        new_top = jnp.maximum(top, jnp.max(scores, axis=0, keepdims=True))
        weights = jnp.exp(scores - new_top)
        decay = jnp.exp(top - new_top)
        total = total * decay + jnp.sum(weights, axis=0, keepdims=True)
        sums = lax.dot_general(keys, weights.astype(BF16), (((0,), (0,)), ((), ())), preferred_element_type=F32)
        acc_ref[s] = acc_ref[s] * decay + sums
        top_ref[s] = jnp.broadcast_to(new_top, (8, SLAB))
        sum_ref[s] = jnp.broadcast_to(total, (8, SLAB))

    for s in range(4):
        top_ref[s] = jnp.full((8, SLAB), LOW, F32)
        sum_ref[s] = jnp.zeros((8, SLAB), F32)
        acc_ref[s] = jnp.zeros((SLAB, SLAB), F32)

    def prompt(c, carry):
        for s in range(4):
            fold(s, c * 4, 4, c * 512)
        return carry

    lax.fori_loop(0, 2, prompt, 0)
    between(0)
    lax.fori_loop(2, 4, prompt, 0)
    between(1)
    for s in range(4):
        fold(s, 16, 2, 2048)


def attend_back_head(j, table, q_ref, kv_ref, grad_ref, logs, deltas, dq_ref, terms_ref, pair_ref, between):
    lane = lax.broadcasted_iota(jnp.int32, (SLAB, SLAB), 1)
    for s in range(4):
        grads = grad_ref[s, :, pl.ds(128 * (j // 2), 128)].astype(F32)
        if j != 1:
            grads = pltpu.roll(grads, 64, 1)
        pair_ref[s, pl.ds(0, SLAB)] = q_ref[s, :, pl.ds(j * 128, 128)]
        pair_ref[s, pl.ds(SLAB, SLAB)] = jnp.where(lane < 64, 0.0, grads).astype(BF16)
        dq_ref[s] = jnp.zeros((SLAB, SLAB), F32)

    def fold(s, first, count, first_key):
        keys = keys_of(kv_ref, table, s, first, count)
        width = count * SLAB
        pos_q = query_positions(table, s, (1, SLAB), 1)
        pos_k = first_key + lax.broadcasted_iota(jnp.int32, (width, 1), 0)
        pair = pair_ref[s]
        both = dot_right_t(keys, pair)
        weights = jnp.where(pos_k <= pos_q, jnp.exp(both[:, :SLAB] - logs[s]), 0.0)
        slopes = (weights * (both[:, SLAB:] - deltas[s])).astype(BF16)
        terms = dot(jnp.concatenate([slopes, weights.astype(BF16)], 1), pair)
        terms_ref[s, pl.ds(first, count)] = terms.astype(BF16).reshape(count, SLAB, SLAB)
        dq_ref[s] += lax.dot_general(slopes, keys, (((0,), (0,)), ((), ())), preferred_element_type=F32)

    def prompt(c, carry):
        for s in range(4):
            fold(s, c * 4, 4, c * 512)
        return carry

    lax.fori_loop(0, 2, prompt, 0)
    between(0)
    lax.fori_loop(2, 4, prompt, 0)
    between(1)
    for s in range(4):
        fold(s, 16, 2, 2048)
    between(2)


def sum_terms(place, table, terms_ref, part_ref):
    def block(t, carry):
        dy, dx = lax.div(t, 4), lax.rem(t, 4)
        at = lax.rem(dy + place.y, 4) * 16 + lax.rem(dx + place.x, 4) * 4
        for dz in range(4):
            places = [jnp.clip(table[96 + s, at + dz], 0, 18) for s in range(4)]
            total = terms_ref[0, places[0]].astype(F32)
            for s in range(1, 4):
                total = total + terms_ref[s, places[s]].astype(F32)
            part_ref[dy, dx, dz] = total.astype(BF16)
        return carry

    lax.fori_loop(0, 16, block, 0)


def lookups(total, place, meta_ref):
    seg, base = total[2:3], total[3:4]
    lane = lax.broadcasted_iota(jnp.int32, (1, SLAB), 1)
    from_here = lax.rem(lax.div(lane, 16) + 4 - place.y, 4) * 16 + lax.rem(lax.rem(lax.div(lane, 4), 4) + 4 - place.x, 4) * 4
    lane_at = (from_here + lax.rem(lane, 4)).astype(F32)
    own = place.y * 4 + place.x
    n = lax.broadcasted_iota(jnp.int32, (24, 1), 0)
    back_rows = jnp.zeros((8, SLAB), F32)
    back_row = lax.broadcasted_iota(jnp.int32, (8, 1), 0)
    for s in range(4):
        mine = lane == own * 4 + s
        seg_q = jnp.sum(jnp.where(mine, seg, 0.0), axis=1, keepdims=True)
        base_q = jnp.sum(jnp.where(mine, base, 0.0), axis=1, keepdims=True)
        prompt = jnp.where(seg_q >= CONTS + 1.0, CONTS + 1.0, 0.0)
        want = jnp.where(n < 16, prompt, seg_q)
        hit = (seg == want) & (base == n.astype(F32) * SLAB) & (lane < 64)
        places = jnp.max(jnp.where(hit, lane_at, 0.0), axis=1, keepdims=True)
        listed = jnp.where(n == 20, base_q, places)
        meta_ref[pl.ds(s * 24, 24), :] = jnp.broadcast_to(listed, (24, SLAB)).astype(jnp.int32)
        visible = (seg == prompt) | (seg == seg_q)
        places = jnp.where(visible, jnp.minimum(base * (1.0 / SLAB), 17.0), 18.0)
        back_rows = jnp.where(back_row == s, places, back_rows)
    meta_ref[pl.ds(96, 8), :] = back_rows.astype(jnp.int32)


def column_of(gain_ref):
    i = lax.broadcasted_iota(jnp.int32, (12, 12), 0)
    k = lax.broadcasted_iota(jnp.int32, (12, 12), 1)
    return jnp.sum(jnp.where(i == k, gain_ref[...].astype(F32), 0.0), axis=1, keepdims=True)


def plane_columns(z):
    return [((z % 2) * 32 + p * 2 + z // 2) * 48 for p in range(16)]


def own_slab(place, at, seg_ref, pos_ref, base_ref):
    lane = lax.broadcasted_iota(jnp.int32, (1, SLAB), 1)
    high = place.head == 1
    seg = jnp.where(high, seg_ref[1:2], seg_ref[0:1]).astype(F32)
    base = (jnp.where(high, pos_ref[1:2], pos_ref[0:1]) - lane).astype(F32)
    m = lax.broadcasted_iota(jnp.int32, (24, SLAB), 0).astype(F32)
    cosine, sine = [
        jnp.sum(jnp.where(m == base * (1.0 / SLAB), base_ref[k], 0.0), axis=0, keepdims=True) for k in range(2)
    ]
    row = lax.broadcasted_iota(jnp.int32, (8, SLAB), 0)
    here = (lane == at) & (row >= 2)
    facts = jnp.where(here, jnp.where(row == 2, seg, jnp.where(row == 3, base, 0.0)), 0.0)
    return jnp.where(row == 0, cosine, jnp.where(row == 1, sine, facts))


def finish_kernel(
    ff_ref, qkv_ref, og_ref, wq_ref, wk_ref, wv_ref, gate_ref, up_ref, gain1_ref, gain2_ref, out_in, grad_in, down_in,
    out_ref, grad_ref, dgain1_ref, dq_ref, dk_ref, dv_ref, do_ref, dgain2_ref, dgate_ref, dup_ref, down_ref,
):
    out_ref[...] = out_in[...]
    grad_ref[...] = grad_in[...]
    down_ref[...] = down_in[...]
    i = lax.broadcasted_iota(jnp.int32, (12, 12), 0)
    k = lax.broadcasted_iota(jnp.int32, (12, 12), 1)

    def row_of(column):
        return jnp.sum(jnp.where(i == k, column, 0.0), axis=0, keepdims=True)

    gain = column_of(gain1_ref)
    grads = [qkv_ref[z].astype(F32)[:12] for z in range(4)]
    total = jnp.zeros((12, 1), F32)
    for c, w_ref, to_ref in ((384, wq_ref, dq_ref), (0, wk_ref, dk_ref), (64, wv_ref, dv_ref)):
        step = 64 if c == 384 else 128
        grad = jnp.concatenate([grads[z][:, step * j + c : step * j + c + HD] for z in range(4) for j in range(3)], 1)
        total = total + jnp.sum(grad * w_ref[...].astype(F32), axis=1, keepdims=True)
        to_ref[...] = grad * gain
    dgain1_ref[...] = row_of(total)
    do_ref[...] = og_ref[0, pl.ds(0, 12)]

    gain = column_of(gain2_ref)
    total = jnp.zeros((12, 1), F32)
    for k_at, w_ref, to_ref in ((0, gate_ref, dgate_ref), (768, up_ref, dup_ref)):
        pieces = {}
        for z in range(4):
            grad = ff_ref[z, :, pl.ds(k_at, 768)].astype(F32)[:12]
            for p, c in enumerate(plane_columns(z)):
                pieces[c] = grad[:, 48 * p : 48 * p + 48]
        grad = jnp.concatenate([pieces[c] for c in sorted(pieces)], 1)
        total = total + jnp.sum(grad * w_ref[...].astype(F32), axis=1, keepdims=True)
        to_ref[...] = grad * gain
    dgain2_ref[...] = row_of(total)


def layer_kernel(
    tok_ref, cot_ref, wq_ref, wk_ref, wv_ref, wo_ref, gate_ref, up_ref, down_ref, gain1_ref, gain2_ref, seg_ref, pos_ref,
    perm_ref, turn_ref, base_ref, perm_att_hbm, out_perm_hbm,
    out_ref, in_ref, down_sum_ref, got_ff_ref, got_ref, got_out_ref,
    perm_att, out_perm, const_sem, line_ref, descs, meta_ref, table, table_sem,
    for_line, for_line_ff, rows, rows_o, rows_ff, one, cots, wqkv, wo, wff, q_ref, kv0, kv1, kv2,
    tops, sums, accs, heads, att_ref, lse_ref, atts, att_s, mid_s, gm_s, two, act, pre, turn_t, part, part_out, sum_z, sum_out,
    to_heads, grads_ref, terms, pairs, kv_own, d_s, qkv_sum, ff_sum,
    og_part, og_sum, og_next, *rest,
):
    send, recv = rest[-2:]
    rooms = list(rest[:-2])

    def take(count):
        out = rooms[:count]
        del rooms[:count]
        return out

    back_room, ff_room, out_room = take(6), take(26), take(6)
    kv_rooms = [take(12) for _ in range(3)]
    qkv_rooms = [take(6) for _ in range(2)]
    in_room, og_line_room, og_room = take(6), take(6), take(6)
    kvs = (kv0, kv1, kv2)

    const_copies = [
        pltpu.make_async_copy(perm_att_hbm, perm_att, const_sem.at[0]),
        pltpu.make_async_copy(out_perm_hbm, out_perm, const_sem.at[1]),
    ]
    for copy in const_copies:
        copy.start()
    place = Place()
    partners = announce(place)
    links = Links(send, recv)
    own = place.y * 4 + place.x

    line_ref[place.z] = own_slab(place, own * 4 + place.z, seg_ref, pos_ref, base_ref)
    lined = small_gather(links, place.ring("z"), lambda k: line_ref.at[k], line_ref.at[pl.ds(0, 3)])
    gain = column_of(gain1_ref)
    w_q, w_k, w_v = [ref[...].astype(F32) * gain for ref in (wq_ref, wk_ref, wv_ref)]
    none, blank = jnp.zeros((12, HD), F32), jnp.zeros((4, 768), F32)
    for z in range(4):
        pieces, last = [], []
        for j in range(3):
            at = slice(192 * z + 64 * j, 192 * z + 64 * j + 64)
            pieces += [w_k[:, at], w_v[:, at]]
            last.append(w_q[:, at])
        pieces += [*last, none]
        for_line[z] = jnp.concatenate([jnp.concatenate(pieces, 1), blank[:, :640]], 0).astype(BF16)
    x = dot(tok_ref[...], perm_ref[...])
    one[place.z] = (x * lax.rsqrt(mean_square(x) + EPS)).astype(BF16)
    enter(partners)
    swap = line_swap(links, place, for_line, rows)
    advance(swap, lined)
    rows_o[place.z] = jnp.concatenate([wo_ref[...].astype(F32), blank], 0).astype(BF16)
    o_line = small_gather(links, place.ring("z"), lambda k: rows_o.at[k], rows_o.at[pl.ds(0, 3)])
    advance(o_line)
    ones = line_gather(links, place, one)
    finish(swap)
    advance(ones)
    wqkv[place.y, place.x] = dot(pack_rows(), rows[...].reshape(64, 640)).astype(BF16)
    kv_gather = direct_gather(links, place, wqkv, (0, 256), (256, 128))
    q_gather = shared_gather(links, place, wqkv, 384, 256)
    advance(kv_gather)
    finish(lined, o_line)
    wo[place.y, place.x] = dot(pack_rows(), rows_o[...].reshape(64, 768)).astype(BF16)
    o_gather = shared_gather(links, place, wo, 0, 768)
    descs[place.y, place.x] = line_ref[0] + line_ref[1] + line_ref[2] + line_ref[3]
    desc_x = small_gather(links, place.ring("x"), lambda k: descs.at[place.y, k], descs.at[0, pl.ds(0, 3)])
    desc_y = small_gather(links, place.ring("y"), lambda k: descs.at[k], descs.at[pl.ds(0, 3)])
    advance(desc_x)
    gain = column_of(gain2_ref)
    for k, ref in enumerate((gate_ref, up_ref)):
        w = ref[...].astype(F32) * gain
        for z in range(4):
            pieces = [w[:, c : c + 48] for c in plane_columns(z)]
            for_line_ff[z, :, pl.ds(768 * k, 768)] = jnp.concatenate([jnp.concatenate(pieces, 1), blank], 0).astype(BF16)
    advance(kv_gather)
    finish(desc_x)
    advance(desc_y)
    advance(q_gather)
    advance(o_gather)
    advance(ones)
    ff_swap = line_swap(links, place, for_line_ff, rows_ff)
    cots[place.z] = cot_ref[...]
    cot_gather = line_gather(links, place, cots)
    finish(desc_y)
    total = jnp.zeros((8, SLAB), F32)
    for y in range(4):
        for k in range(4):
            total = total + descs[y, k]
    lookups(total, place, meta_ref)
    table_copy = pltpu.make_async_copy(meta_ref, table, table_sem)
    table_copy.start()
    finish(ones, kv_gather)
    advance(q_gather)
    advance(o_gather)

    lines = one[...].reshape(512, 768)
    gathers = [slab_gather(links, place, kv) for kv in kvs]
    for j in range(3):
        field = dot(lines, wqkv[:, :, :, pl.ds(128 * j, 128)].reshape(768, 128))
        for s in range(4):
            cosine, sine = slab_turns(line_ref, turn_ref, s)
            kvs[j][0, 0, s] = turned(half_rows(field, s), cosine, sine).astype(BF16)
        if j < 2:
            advance(*gathers[j])
    advance(ff_swap, cot_gather)
    advance(o_gather)
    advance(q_gather)
    advance(*gathers[0])
    advance(*gathers[2])
    advance(q_gather)
    finish(q_gather)
    field = dot(lines, wqkv[:, :, :, pl.ds(384, 256)].reshape(768, 256))
    lane = lax.broadcasted_iota(jnp.int32, (SLAB, SLAB), 1)
    for s in range(4):
        cosine, sine = slab_turns(line_ref, turn_ref, s)
        first, last = half_rows(field[:, 0:128], s), half_rows(field[:, 128:256], s)
        for j, query in enumerate((first, pltpu.roll(first, 64, 1), last)):
            query = turned(jnp.where(lane < 64, query * 0.125, 0.0), cosine, sine)
            q_ref[s, :, pl.ds(128 * j, 128)] = query.astype(BF16)
    advance(*gathers[1])
    advance(o_gather)
    finish(ff_swap)
    for c in range(0, 1536, 768):
        wff[place.y, place.x, :, pl.ds(c, 768)] = dot(
            pack_rows(), rows_ff[:, :, pl.ds(c, 768)].reshape(64, 768)
        ).astype(BF16)
    wff[place.y, place.x, :, pl.ds(1536, 768)] = down_ref[...]
    table_copy.wait()
    for copy in const_copies:
        copy.wait()
    advance(*gathers[0])
    advance(*gathers[2])
    advance(cot_gather)

    lane = lax.broadcasted_iota(jnp.int32, (SLAB, SLAB), 1)
    for s in range(4):
        heads[s, pl.ds(192, 64), :] = jnp.zeros((64, SLAB), F32)
    w_gather = shared_gather(links, place, wff, 0, 2304)
    for j in range(3):
        finish(*gathers[j])

        def between(k, j=j):
            if j == 0 and k == 0:
                links.finish(8)
            if j == 0 and k == 1:
                advance(*gathers[1])
            if j == 1 and k == 0:
                finish(cot_gather)
                links.finish(8)
            if j == 1 and k == 1:
                advance(o_gather)

        if j == 2:
            advance(w_gather)
        attend_head(j, table, q_ref, kvs[j], tops, sums, accs, between)
        for s in range(4):
            heads[s, pl.ds(64 * j, 64), :] = accs[s, pl.ds(64, 64), :] / sums[s][0:1]
            lse_ref[j, s] = tops[s] + jnp.log(sums[s])
        if j == 0:
            advance(*gathers[2])
    for s in range(4):
        att_ref[s, :, 0:128] = heads[s, pl.ds(0, 128), :].T.astype(BF16)
        att_ref[s, :, 128:256] = heads[s, pl.ds(128, 128), :].T.astype(BF16)
    att_swap = line_swap(links, place, att_ref, atts)
    advance(att_swap)
    advance(w_gather)
    links.finish(20)
    finish(att_swap, o_gather)
    advance(w_gather)

    att = dot(atts[0], perm_att[pl.ds(0, 256), :])
    for z in range(1, 4):
        att = att + dot(atts[z], perm_att[pl.ds(256 * z, 256), :])
    att_s[...] = att.astype(BF16)
    mid_s[...] = tok_ref[...].astype(F32) + dot(att_s[...], merged(wo))
    middle = mid_s[...]
    scale_two = lax.rsqrt(mean_square(middle) + EPS)
    two[place.z] = dot((middle * scale_two).astype(BF16), perm_ref[...]).astype(BF16)
    two_gather = line_gather(links, place, two)
    advance(two_gather)
    advance(w_gather)
    att = dot(atts[0], out_perm[pl.ds(0, 256), :])
    for z in range(1, 4):
        att = att + dot(atts[z], out_perm[pl.ds(256 * z, 256), :])
    att_by_z = att.astype(BF16).T
    advance(two_gather)
    together([w_gather, two_gather])

    def block():
        two_b = two[...].reshape(512, 768)
        cot_b = cots[...].reshape(512, 768)
        gate_w = wff[:, :, :, pl.ds(0, 768)].reshape(768, 768)
        up_w = wff[:, :, :, pl.ds(768, 768)].reshape(768, 768)
        down_w = wff[:, :, :, pl.ds(1536, 768)].reshape(768, 768)
        gate = dot(two_b, gate_w)
        up = dot(two_b, up_w)
        sig = 1.0 / (1.0 + jnp.exp(-gate))
        silu = gate * sig
        act_b = (silu * up).astype(BF16)
        act[...] = act_b
        grad_act = dot_right_t(cot_b, down_w)
        grad_gate = (grad_act * up * (sig * (1.0 + gate * (1.0 - sig)))).astype(BF16)
        grad_up = (grad_act * silu).astype(BF16)
        pre[:, pl.ds(0, 768)] = grad_gate
        pre[:, pl.ds(768, 768)] = grad_up
        back = dot_right_t(grad_gate, gate_w) + dot_right_t(grad_up, up_w)
        part[...] = back.astype(BF16).reshape(4, SLAB, 768)

    def out_block(r, carry):
        at = pl.ds(pl.multiple_of(r * 256, 256), 256)
        down_w = wff[:, :, :, pl.ds(1536, 768)].reshape(768, 768)
        part_out[pl.ds(r * 2, 2)] = dot(act[at, :], down_w).astype(BF16).reshape(2, SLAB, 768)
        return carry

    block()
    links.finish()
    back_sum = line_scatter(links, place, part, back_room, sum_z)
    advance(back_sum)
    lax.fori_loop(0, 2, out_block, 0)
    turn_t[...] = two[...].reshape(512, 768).T

    def first_grads(c, carry):
        at = pl.ds(pl.multiple_of(c * 256, 256), 256)
        wff[:, :, :, at] = dot(turn_t[...], pre[:, at]).astype(BF16).reshape(4, 4, 48, 256)
        return carry

    def last_grads(c, carry):
        at = pl.ds(pl.multiple_of(c * 256, 256), 256)
        to = pl.ds(pl.multiple_of(1536 + c * 256, 256), 256)
        cot_all = cots[:, :, at].reshape(512, 256)
        wff[:, :, :, to] = dot(turn_t[...], cot_all).astype(BF16).reshape(4, 4, 48, 256)
        return carry

    lax.fori_loop(0, 6, first_grads, 0)
    advance(back_sum)
    turn_t[...] = act[...].T
    lax.fori_loop(0, 3, last_grads, 0)
    ff = plane_scatter(links, place, wff, ff_room, ff_sum, False)
    advance(*ff)
    finish(back_sum)
    links.finish(6)

    grad = dot_right_t(sum_z[0].astype(BF16), perm_ref[...])
    middle = mid_s[...]
    scale_two = lax.rsqrt(mean_square(middle) + EPS)
    gm_s[...] = cot_ref[...].astype(F32) + norm_back(grad, middle * scale_two, scale_two)
    low = gm_s[...].astype(BF16)
    grad_att = dot_right_t(low, merged(wo)).astype(BF16)
    for z in range(4):
        to_heads[z] = dot_right_t(grad_att, perm_att[pl.ds(256 * z, 256), :]).astype(BF16)
    heads_swap = line_swap(links, place, to_heads, grads_ref)
    advance(heads_swap)
    out_sum = line_scatter(links, place, part_out, out_room, sum_out)
    advance(out_sum)
    turn_t[...] = one[...].reshape(512, 768).T
    og_part[...] = dot(att_by_z, low).astype(BF16).reshape(4, 256, 768)
    for s in range(4):
        terms[s, 18] = jnp.zeros((SLAB, SLAB), BF16)
    finish(heads_swap)

    which = lax.broadcasted_iota(jnp.int32, (8, SLAB), 0)
    at_lane = lax.broadcasted_iota(jnp.int32, (8, 256), 1)
    pick = (lax.div(at_lane, HD) == lax.broadcasted_iota(jnp.int32, (8, 256), 0)).astype(F32)
    logs, deltas = [], []
    for s in range(4):
        inner = grads_ref[s].astype(F32) * att_ref[s].astype(F32)
        delta = lax.dot_general(pick, inner, LANES, precision=HIGHEST, preferred_element_type=F32)
        logs.append([lse_ref[j, s][0:1] for j in range(3)])
        deltas.append([jnp.sum(jnp.where(which == k, delta, 0.0), axis=0, keepdims=True) for k in range(3)])

    scatters = []

    def keys_turn(j):
        for s in range(4):
            cosine, sine = slab_turns(line_ref, turn_ref, s)
            d_s[pl.ds(s * SLAB, SLAB), pl.ds(128 * j, 128)] = turned(kv_own[j, s], cosine, -sine).astype(BF16)

    def qkv_grads(columns, first, second, room):
        for c in columns:
            wo[:, :, :, pl.ds(c, 128)] = dot(turn_t[...], d_s[:, pl.ds(c, 128)]).astype(BF16).reshape(4, 4, 48, 128)
        scatter = small_scatter(links, place, wo, first, second, room, qkv_sum)
        advance(*scatter)
        return scatter

    og_line = line_scatter(links, place, og_part, og_line_room, og_sum)
    spread = spread_rows()
    for j in range(3):

        def between(k, j=j):
            if j == 0 and k == 0:
                advance(*ff)
                advance(out_sum)
            if j == 1 and k == 0:
                advance(*ff)
                links.finish(8)
            if j == 1 and k == 2:
                advance(*scatters[0])
            if j == 2 and k == 0:
                advance(*ff)
                links.finish(4)
            if j == 2 and k == 1:
                advance(*scatters[0])
            if j == 2 and k == 2:
                advance(*scatters[1])

        attend_back_head(
            j, table, q_ref, kvs[j], grads_ref, [v[j] for v in logs], [v[j] for v in deltas], accs, terms, pairs, between
        )
        sum_terms(place, table, terms, kvs[j])
        scatters.append(slab_scatter(links, place, kvs[j], kv_rooms[j], kv_own.at[j]))
        advance(*scatters[j])
        for s in range(4):
            cosine, sine = slab_turns(line_ref, turn_ref, s)
            grad = turned(jnp.where(lane < 64, accs[s] * 0.125, 0.0), cosine, -sine)
            to = (pl.ds(s * SLAB, SLAB), pl.ds(384 + 128 * (j // 2), 128))
            if j == 1:
                grad = jnp.where(lane < 64, d_s[to].astype(F32), pltpu.roll(grad, 64, 1))
            d_s[to] = grad.astype(BF16)
        if j == 0:
            finish(out_sum)
            advance(og_line)
            out_ref[...] = (mid_s[...] + sum_out[0]).astype(BF16)
        if j == 1:
            advance(og_line)

    finish(*scatters[0])
    finish(*ff)
    down_sum_ref[...] = ff_sum[0, :, pl.ds(1536, 768)]
    for c in range(0, 1536, 768):
        for_line_ff[:, :, pl.ds(c, 768)] = (
            dot(spread, ff_sum[0, :, pl.ds(c, 768)].astype(BF16)).astype(BF16).reshape(4, 16, 768)
        )
    finish(og_line)
    grads_swap = line_swap(links, place, for_line_ff, got_ff_ref)
    advance(grads_swap)
    keys_turn(0)
    og_next[...] = og_sum[0].astype(BF16).reshape(4, 4, 16, 768)
    links.finish(12)
    advance(*scatters[1])
    advance(*scatters[2])
    finish(*scatters[1])
    keys_turn(1)
    advance(*scatters[2])
    qkv = qkv_grads((0, 128, 384), (0, 256), (384, 128), qkv_rooms[0])
    og = small_scatter(links, place, og_next, (0, 384), (384, 384), og_room, got_out_ref)
    advance(*og)
    links.finish(12)
    finish(*scatters[2])
    keys_turn(2)

    def last_block(r, carry):
        at = pl.ds(pl.multiple_of(r * 256, 256), 256)
        part[pl.ds(r * 2, 2)] = dot_right_t(d_s[at, :], merged(wqkv)).astype(BF16).reshape(2, SLAB, 768)
        return carry

    lax.fori_loop(0, 2, last_block, 0)
    in_sum = line_scatter(links, place, part, in_room, sum_z)
    advance(in_sum)
    last_qkv = qkv_grads((256, 512), (256, 128), (512, 128), qkv_rooms[1])
    advance(*qkv)
    finish(grads_swap)
    advance(in_sum)
    advance(*last_qkv)
    advance(*og)
    finish(*qkv)
    links.finish(len(links.sent) - 4)
    finish(*last_qkv)
    for_line[...] = dot(spread, qkv_sum[0].astype(BF16)).astype(BF16).reshape(4, 16, 640)
    last = line_swap(links, place, for_line, got_ref)
    advance(last)
    finish(*og)
    finish(in_sum)
    grad = dot_right_t(sum_z[0].astype(BF16), perm_ref[...])
    x = tok_ref[...].astype(F32)
    scale = lax.rsqrt(mean_square(x) + EPS)
    in_ref[...] = gm_s[...] + norm_back(grad, x * scale, scale)
    links.finish()
    finish(last)


SENDS, RECVS = 200, 212
LINE = pltpu.VMEM((4, SLAB, 768), BF16)
KV = pltpu.VMEM((4, 4, 4, SLAB, SLAB), BF16)
OUTS = [
    ((SLAB, 768), BF16),
    ((SLAB, 768), F32),
    ((48, 768), F32),
    ((4, 16, 1536), BF16),
    ((4, 16, 640), BF16),
    ((1, 16, 768), F32),
]
ROOM = (
    [
        pltpu.VMEM((1024, 768), BF16),
        pltpu.VMEM((1024, 1024), BF16),
        pltpu.SemaphoreType.DMA((2,)),
        pltpu.VMEM((4, 8, SLAB), F32),
        pltpu.VMEM((4, 4, 8, SLAB), F32),
        pltpu.VMEM((104, SLAB), jnp.int32),
        pltpu.SMEM((104, SLAB), jnp.int32),
        pltpu.SemaphoreType.DMA,
        pltpu.VMEM((4, 16, 640), BF16),
        pltpu.VMEM((4, 16, 1536), BF16),
        pltpu.VMEM((4, 16, 640), BF16),
        pltpu.VMEM((4, 16, 768), BF16),
        pltpu.VMEM((4, 16, 1536), BF16),
        LINE,
        LINE,
        pltpu.VMEM((4, 4, 48, 640), BF16),
        pltpu.VMEM((4, 4, 48, 768), BF16),
        pltpu.VMEM((4, 4, 48, 2304), BF16),
        pltpu.VMEM((4, SLAB, 384), BF16),
        KV,
        KV,
        KV,
        pltpu.VMEM((4, 8, SLAB), F32),
        pltpu.VMEM((4, 8, SLAB), F32),
        pltpu.VMEM((4, SLAB, SLAB), F32),
        pltpu.VMEM((4, 256, SLAB), F32),
        pltpu.VMEM((4, SLAB, 256), BF16),
        pltpu.VMEM((3, 4, 8, SLAB), F32),
        pltpu.VMEM((4, SLAB, 256), BF16),
        pltpu.VMEM((SLAB, 768), BF16),
        pltpu.VMEM((SLAB, 768), F32),
        pltpu.VMEM((SLAB, 768), F32),
        LINE,
        pltpu.VMEM((512, 768), BF16),
        pltpu.VMEM((512, 1536), BF16),
        pltpu.VMEM((768, 512), BF16),
        LINE,
        LINE,
        pltpu.VMEM((1, SLAB, 768), F32),
        pltpu.VMEM((1, SLAB, 768), F32),
        pltpu.VMEM((4, SLAB, 256), BF16),
        pltpu.VMEM((4, SLAB, 256), BF16),
        pltpu.VMEM((4, 19, SLAB, SLAB), BF16),
        pltpu.VMEM((4, 256, SLAB), BF16),
        pltpu.VMEM((3, 4, SLAB, SLAB), F32),
        pltpu.VMEM((512, 640), BF16),
        pltpu.VMEM((1, 48, 640), F32),
        pltpu.VMEM((1, 48, 2304), F32),
        pltpu.VMEM((4, 256, 768), BF16),
        pltpu.VMEM((1, 256, 768), F32),
        pltpu.VMEM((4, 4, 16, 768), BF16),
    ]
    + line_scatter_room(SLAB, 768)
    + plane_scatter_room(48, 2304, False)
    + line_scatter_room(SLAB, 768)
    + slab_scatter_room() * 3
    + small_scatter_room(48, 256, 128)
    + small_scatter_room(48, 128, 128)
    + line_scatter_room(SLAB, 768)
    + line_scatter_room(256, 768)
    + small_scatter_room(16, 384, 384)
)


def per_device(
    tokens, gain_one, w_query, w_key, w_value, w_out, gain_two, w_gate, w_up, w_down, cotangent, segment_ids, positions
):
    gains = (gain_one.reshape(1, 12), gain_two.reshape(1, 12))
    output, input_grad, down_grad, got_ff, got_qkv, got_out = pl.pallas_call(
        layer_kernel,
        out_shape=tuple(jax.ShapeDtypeStruct(shape, kind) for shape, kind in OUTS),
        in_specs=[VMEM] * 16 + [pl.BlockSpec(memory_space=pl.ANY)] * 2,
        out_specs=tuple([VMEM] * len(OUTS)),
        scratch_shapes=ROOM
        + [pltpu.SemaphoreType.DMA((SENDS,)), pltpu.SemaphoreType.DMA((RECVS,))],
        compiler_params=pltpu.CompilerParams(collective_id=0, has_side_effects=True, vmem_limit_bytes=62 * MIB),
        name="layer",
    )(
        tokens, cotangent, w_query, w_key, w_value, w_out, w_gate, w_up, w_down, *gains,
        segment_ids.reshape(2, SLAB), positions.reshape(2, SLAB),
        jnp.asarray(TO_PERM, BF16), jnp.asarray(OFFSET_TURNS, F32), jnp.asarray(BASE_TURNS, F32),
        jnp.asarray(ATT_PERM, BF16), jnp.asarray(OUT_PERM, BF16),
    )
    small, square, wide = [jax.ShapeDtypeStruct((rows, columns), F32) for rows, columns in ((1, 12), (12, 768), (12, 3072))]
    output, input_grad, gain_one_grad, dq, dk, dv, do, gain_two_grad, dgate, dup, down_grad = pl.pallas_call(
        finish_kernel,
        out_shape=(*[jax.ShapeDtypeStruct(*OUTS[k]) for k in range(2)], small, square, square, square, square, small, wide, wide,
                   jax.ShapeDtypeStruct(*OUTS[2])),
        in_specs=[VMEM] * 13,
        out_specs=(VMEM,) * 11,
        name="finish",
    )(got_ff, got_qkv, got_out, w_query, w_key, w_value, w_gate, w_up, *gains, output, input_grad, down_grad)
    return (
        output, input_grad, gain_one_grad.reshape(12), dq, dk, dv, do, gain_two_grad.reshape(12), dgate, dup, down_grad
    )


def solution(mesh):
    rows = P(("grp", "blk", "head"), None)
    flat = P(("grp", "blk", "head"))
    weight = P(("blk", "head"), None)
    gain = P(("blk", "head"))
    ids = P(("grp", "blk"))
    in_specs = (rows, gain, weight, weight, weight, weight, gain, weight, weight, weight, rows, ids, ids)
    out_specs = (rows, rows, flat, rows, rows, rows, rows, flat, rows, rows, rows)
    return jax.shard_map(per_device, mesh=mesh, in_specs=in_specs, out_specs=out_specs, check_vma=False)
```

```python
import math

import jax
import jax.numpy as jnp
import numpy as np
from jax import lax
from jax.experimental import pallas as pl
from jax.experimental.pallas import tpu as pltpu
from jax.sharding import PartitionSpec as P

MESH = pl.DeviceIdType.MESH
F32 = jnp.float32
BF16 = jnp.bfloat16
HD = 64
CONTS = 8
SLAB = 128
LOW = -1e30
EPS = 1e-05
LANES = (((1,), (1,)), ((), ()))
HIGHEST = lax.Precision.HIGHEST
MIB = 1 << 20
VMEM = pl.BlockSpec(memory_space=pltpu.VMEM)
SMEM = pl.BlockSpec(memory_space=pltpu.SMEM)


def feature_order():
    place = np.arange(768)
    p, z, r = place // 48, place // 12 % 4, place % 12
    t = (z % 2) * 32 + p * 2 + z // 2
    return t * 12 + r


ORDER = feature_order()
TO_PERM = np.zeros((768, 768), np.float32)
TO_PERM[ORDER, np.arange(768)] = 1.0


ATT_PERM = np.pad(TO_PERM.reshape(4, 192, 768), ((0, 0), (0, 64), (0, 0))).reshape(1024, 768)
OUT_PERM = np.pad(ATT_PERM.reshape(1024, 16, 4, 12).transpose(0, 2, 1, 3), ((0, 0), (0, 0), (0, 0), (0, 4))).reshape(1024, 1024)
LANE_FREQUENCY = 10000.0 ** (-(np.arange(128) % 32) * 2.0 / HD) * (np.arange(128) < HD)
OFFSET_ANGLES = np.arange(SLAB)[:, None] * LANE_FREQUENCY[None]
BASE_ANGLES = SLAB * np.arange(24)[:, None] * LANE_FREQUENCY[None]
BASE_TURNS = np.stack([np.cos(BASE_ANGLES), np.sin(BASE_ANGLES)]).astype(np.float32)
OFFSET_TURNS = np.stack([np.cos(OFFSET_ANGLES), np.sin(OFFSET_ANGLES)]).astype(np.float32)


class Place:
    def __init__(self):
        self.core = lax.axis_index("grp")
        blk = lax.axis_index("blk")
        self.blk, self.head = blk, lax.axis_index("head")
        self.x = lax.rem(blk, 4)
        self.y = lax.rem(lax.div(blk, 4), 4)
        self.z = self.head * 2 + lax.div(blk, 16)

    def other_core(self):
        return (1 - self.core, self.blk, self.head)

    def device(self, x=None, y=None, z=None):
        x = self.x if x is None else x
        y = self.y if y is None else y
        z = self.z if z is None else z
        return (self.core, lax.rem(z, 2) * 16 + y * 4 + x, lax.div(z, 2))

    def ring(self, axis):
        return Ring(self, axis)


class Ring:
    def __init__(self, place, axis):
        self.place, self.axis = place, axis
        self.own = getattr(place, axis)
        self.next = lax.rem(self.own + 1, 4)
        self.prev = lax.rem(self.own + 3, 4)
        self.far = lax.rem(self.own + 2, 4)

    def device(self, index):
        return self.place.device(**{self.axis: index})


def announce(place):
    partners = [place.other_core()]
    for axis in ("x", "y", "z"):
        ring = place.ring(axis)
        partners += [ring.device(ring.next), ring.device(ring.prev), ring.device(ring.far)]
    barrier = pltpu.get_barrier_semaphore()
    for partner in partners:
        pl.semaphore_signal(barrier, inc=1, device_id=partner, device_id_type=MESH)
    return len(partners)


def enter(partners):
    pl.semaphore_wait(pltpu.get_barrier_semaphore(), partners)


class Links:
    def __init__(self, send, recv):
        self.send, self.recv, self.sends, self.recvs, self.sent = send, recv, 0, 0, []

    def send_slot(self):
        self.sends += 1
        return self.send.at[self.sends - 1]

    def recv_slot(self):
        self.recvs += 1
        return self.recv.at[self.recvs - 1]

    def start(self, source, target, device, send, recv):
        copy = pltpu.make_async_remote_copy(
            src_ref=source, dst_ref=target, send_sem=send, recv_sem=recv, device_id=device, device_id_type=MESH
        )
        copy.start()
        return copy

    def copy(self, source, target, device):
        copy = self.start(source, target, device, self.send_slot(), self.recv_slot())
        self.sent.append(copy.wait_send)
        return copy

    def group(self, copies, view, recv=None):
        send = self.send_slot()
        slots = [self.recv_slot()] * len(copies) if recv is None else recv
        for (source, target, device), slot in zip(copies, slots):
            self.start(source, target, device, send, slot)
        self.sent.append(lambda: self.arrived(view, send))
        return lambda: self.arrived(view, slots[0])

    def arrived(self, view, semaphore):
        pltpu.make_async_copy(view, view, semaphore).wait()

    def finish(self, count=None):
        count = len(self.sent) if count is None else count
        for wait in self.sent[:count]:
            wait()
        del self.sent[:count]


def together(steps):
    steps = list(steps)
    while steps:
        left = []
        for step in steps:
            try:
                next(step)
                left.append(step)
            except StopIteration:
                pass
        steps = left


def ring_gather(links, ring, slot):
    right = links.copy(slot(ring.own, None), slot(ring.own, None), ring.device(ring.next))
    left = links.copy(slot(ring.own, None), slot(ring.own, None), ring.device(ring.prev))
    yield
    right.wait_recv()
    on_right = links.copy(slot(ring.prev, 0), slot(ring.prev, 0), ring.device(ring.next))
    left.wait_recv()
    on_left = links.copy(slot(ring.next, 1), slot(ring.next, 1), ring.device(ring.prev))
    yield
    on_right.wait_recv()
    on_left.wait_recv()


def add_into(target, terms, kind):
    *lead, rows, columns = target.shape
    step = 16
    for size in (128, 64, 48, 32):
        if rows % size == 0 and size * columns <= 48 * 1024:
            step = size
            break
    count = rows // step

    def body(k, carry):
        at, rest = [], lax.div(k, count)
        for size in reversed(lead):
            at.insert(0, lax.rem(rest, size))
            rest = lax.div(rest, size)
        at = (*at, pl.ds(pl.multiple_of(lax.rem(k, count) * step, step), step), slice(None))
        total = terms[0][at].astype(kind)
        for term in terms[1:]:
            total = total + term[at].astype(kind)
        target[at] = total
        return carry

    trips = math.prod(lead) * count
    lax.fori_loop(0, trips, body, 0, unroll=2 if trips % 2 == 0 else 1)


def ring_scatter(links, ring, part, room, target, kind):
    low, high, sum_low, sum_high, from_prev, from_next = room
    nxt, prv = ring.device(ring.next), ring.device(ring.prev)
    far_low = links.copy(part(ring.far, 0), low, nxt)
    far_high = links.copy(part(ring.far, 1), high, prv)
    next_high = links.copy(part(ring.next, 1), from_prev(1), nxt)
    prev_low = links.copy(part(ring.prev, 0), from_next(0), prv)
    yield
    far_low.wait_recv()
    add_into(sum_low, [part(ring.next, 0), low], BF16)
    next_low = links.copy(sum_low, from_prev(0), nxt)
    far_high.wait_recv()
    add_into(sum_high, [part(ring.prev, 1), high], BF16)
    prev_high = links.copy(sum_high, from_next(1), prv)
    yield
    for copy in (next_high, prev_low, next_low, prev_high):
        copy.wait_recv()
    add_into(target, [part(ring.own, None), from_prev(None), from_next(None)], kind)


def lead_part(part):
    return pl.ds(0, 4) if part is None else pl.ds(2 * part, 2)


def row_part(rows, part):
    first = (rows // 2 + 15) // 16 * 16
    if part is None:
        return 0, rows
    return (0, first) if part == 0 else (first, rows - first)


def regions(rows, columns, by_rows):
    if by_rows:
        return [(0, rows // 2, 0, columns), (rows // 2, rows // 2, 0, columns)]
    return [(0, rows, 0, columns // 2), (0, rows, columns // 2, columns // 2)]


def plane_gather(links, place, buf, by_rows):
    rows, columns = buf.shape[2:]

    def half(region, x_first):
        r0, rn, c0, cn = region

        def one(k, part):
            off, size = row_part(rn, part)
            y, x = (place.y, k) if x_first else (k, place.x)
            return buf.at[y, x, pl.ds(r0 + off, size), pl.ds(c0, cn)]

        def line(k, part):
            y, x = (k, lead_part(part)) if x_first else (lead_part(part), k)
            return buf.at[y, x, pl.ds(r0, rn), pl.ds(c0, cn)]

        yield from ring_gather(links, place.ring("x" if x_first else "y"), one)
        yield from ring_gather(links, place.ring("y" if x_first else "x"), line)

    a, b = regions(rows, columns, by_rows)
    return half(a, True), half(b, False)


def plane_scatter_room(rows, columns, by_rows):
    rooms = []
    for _, rn, _, cn in regions(rows, columns, by_rows):
        rooms += [pltpu.VMEM((2, rn, cn), BF16)] * 4 + [pltpu.VMEM((4, rn, cn), BF16)] * 3
        low, high = row_part(rn, 0)[1], row_part(rn, 1)[1]
        rooms += [pltpu.VMEM((1, low, cn), BF16), pltpu.VMEM((1, high, cn), BF16)] * 2
        rooms += [pltpu.VMEM((1, rn, cn), BF16)] * 2
    return rooms


def plane_scatter(links, place, buf, rooms, target, by_rows):
    rows, columns = buf.shape[2:]

    def half(region, room, x_first):
        r0, rn, c0, cn = region
        low, high, sum_low, sum_high, prev, nxt, lined = room[:7]
        low1, high1, sum_low1, sum_high1, prev1, nxt1 = room[7:]

        def line(k, part):
            y, x = (lead_part(part), k) if x_first else (k, lead_part(part))
            return buf.at[y, x, pl.ds(r0, rn), pl.ds(c0, cn)]

        def one(k, part):
            off, size = row_part(rn, part)
            return lined.at[pl.ds(k, 1), pl.ds(off, size), :]

        def lined_part(ref):
            return lambda part: ref.at[lead_part(part)]

        def one_part(ref):
            def view(part):
                off, size = row_part(rn, part)
                return ref.at[:, pl.ds(off, size), :]

            return view

        room_a = (low, high, sum_low, sum_high, lined_part(prev), lined_part(nxt))
        room_b = (low1, high1, sum_low1, sum_high1, one_part(prev1), one_part(nxt1))
        yield from ring_scatter(links, place.ring("x" if x_first else "y"), line, room_a, lined, BF16)
        out = target.at[:, pl.ds(r0, rn), pl.ds(c0, cn)]
        yield from ring_scatter(links, place.ring("y" if x_first else "x"), one, room_b, out, F32)

    a, b = regions(rows, columns, by_rows)
    return half(a, rooms[:13], False), half(b, rooms[13:], True)


def small_scatter_room(rows, *sizes):
    rooms = []
    for size in sizes:
        rooms += [
            pltpu.VMEM((3, 4, rows, size), BF16),
            pltpu.VMEM((4, rows, size), BF16),
            pltpu.VMEM((3, 1, rows, size), BF16),
        ]
    return rooms


def direct_scatter(links, ring, part, room, target, kind):
    copies = [(part(to), room.at[k], ring.device(to)) for k, to in enumerate((ring.next, ring.prev, ring.far))]
    arrived = links.group(copies, room)
    yield
    arrived()
    add_into(target, [part(ring.own), room.at[0], room.at[1], room.at[2]], kind)


def small_scatter(links, place, buf, first, second, rooms, target):
    def half(region, room, x_first):
        columns = pl.ds(*region)
        firsts, lined, lasts = room

        def line(k):
            return buf.at[:, k, :, columns] if x_first else buf.at[k, :, :, columns]

        yield from direct_scatter(links, place.ring("x" if x_first else "y"), line, firsts, lined, BF16)
        out = target.at[:, :, columns]
        yield from direct_scatter(
            links, place.ring("y" if x_first else "x"), lambda k: lined.at[pl.ds(k, 1)], lasts, out, F32
        )

    return half(first, rooms[:3], False), half(second, rooms[3:], True)


def line_scatter_room(rows, columns):
    low, high = row_part(rows, 0)[1], row_part(rows, 1)[1]
    return [pltpu.VMEM((1, low, columns), BF16), pltpu.VMEM((1, high, columns), BF16)] * 2 + [
        pltpu.VMEM((1, rows, columns), BF16)
    ] * 2


def line_scatter(links, place, buf, room, target):
    rows = buf.shape[1]

    def part(k, half):
        off, size = row_part(rows, half)
        return buf.at[pl.ds(k, 1), pl.ds(off, size), :]

    def view(ref):
        def cut(half):
            off, size = row_part(rows, half)
            return ref.at[:, pl.ds(off, size), :]

        return cut

    low, high, sum_low, sum_high, prev, nxt = room
    yield from ring_scatter(
        links, place.ring("z"), part, (low, high, sum_low, sum_high, view(prev), view(nxt)), target, F32
    )


def line_gather(links, place, buf):
    rows = buf.shape[1]

    def slot(k, half):
        off, size = row_part(rows, half)
        return buf.at[k, pl.ds(off, size)]

    yield from ring_gather(links, place.ring("z"), slot)


def line_swap(links, place, source, target):
    ring = place.ring("z")
    copies = [(source.at[other], target.at[ring.own], ring.device(other)) for other in (ring.next, ring.prev, ring.far)]
    arrived = links.group(copies, target.at[pl.ds(0, 3)])
    target[ring.own] = source[ring.own]
    yield
    arrived()


def small_gather(links, ring, slot, three):
    own = slot(ring.own)
    arrived = links.group([(own, own, ring.device(k)) for k in (ring.next, ring.prev, ring.far)], three)
    yield
    arrived()


def shared_gather(links, place, buf, start, size):
    half = size // 2
    flip = place.core == 1
    columns = pl.ds(pl.multiple_of(start + place.core * half, 128), half)
    first, second = jnp.where(flip, place.y, place.x), jnp.where(flip, place.x, place.y)
    first_next, first_prev, first_far = [lax.rem(first + k, 4) for k in (1, 3, 2)]
    second_next, second_prev, second_far = [lax.rem(second + k, 4) for k in (1, 3, 2)]

    def block(s, f, part=None):
        y, x = jnp.where(flip, f, s), jnp.where(flip, s, f)
        rows = pl.ds(0, 48) if part is None else (pl.ds(0, 32) if part == 0 else pl.ds(32, 16))
        return buf.at[y, x, rows, columns]

    def device(s, f):
        return place.device(x=jnp.where(flip, s, f), y=jnp.where(flip, f, s))

    def send(s, f, to, part=None):
        return links.copy(block(s, f, part), block(s, f, part), to)

    handed = []

    def hands(view):
        pair = links.send_slot(), links.recv_slot()
        links.sent.append(lambda: links.arrived(view, pair[0]))
        handed.append(lambda: links.arrived(view, pair[1]))
        return lambda s, f: links.start(block(s, f), block(s, f), place.other_core(), *pair)

    on_right, on_left = device(second, first_next), device(second, first_prev)
    up, down = device(second_next, first), device(second_prev, first)
    order = (first, first_prev, first_next, first_far)
    ups, downs = [], []

    def line(k):
        ups.append(send(second, order[k], up))
        downs.append(send(second, order[k], down))

    right = send(second, first, on_right)
    left = send(second, first, on_left)
    line(0)
    yield
    right.wait_recv()
    far_low = send(second, first_prev, on_right, 0)
    line(1)
    left.wait_recv()
    far_high = send(second, first_next, on_left, 1)
    line(2)
    hand = hands(buf.at[0, pl.ds(0, 2), :, columns])
    hand(second, first_prev)
    hand(second, first_next)
    yield
    far_low.wait_recv()
    far_high.wait_recv()
    line(3)
    hands(buf.at[0, 0, :, columns])(second, first_far)
    yield
    far = []
    hand = hands(buf.at[pl.ds(0, 2), :, :, columns])
    for k in range(4):
        ups[k].wait_recv()
        if k < 2:
            far.append(send(second_prev, order[k], up))
        hand(second_prev, order[k])
        downs[k].wait_recv()
        if k >= 2:
            far.append(send(second_next, order[k], down))
        hand(second_next, order[k])
    yield
    hand = hands(buf.at[0, :, :, columns])
    for k in range(4):
        far[k].wait_recv()
        hand(second_far, order[k])
    yield
    for wait in handed:
        wait()


def advance(*steps):
    for step in steps:
        next(step, None)


def finish(*steps):
    together(steps)


def dot(left, right):
    return jnp.dot(left, right, preferred_element_type=F32)


def dot_right_t(left, right):
    return lax.dot_general(left, right, LANES, preferred_element_type=F32)


def pack_rows():
    i = lax.broadcasted_iota(jnp.int32, (48, 64), 0)
    k = lax.broadcasted_iota(jnp.int32, (48, 64), 1)
    return (k == lax.div(i, 12) * 16 + lax.rem(i, 12)).astype(BF16)


def spread_rows():
    k = lax.broadcasted_iota(jnp.int32, (64, 48), 0)
    i = lax.broadcasted_iota(jnp.int32, (64, 48), 1)
    return (k == lax.div(i, 12) * 16 + lax.rem(i, 12)).astype(BF16)


def merged(ref):
    rows, columns = ref.shape[0] * ref.shape[1] * ref.shape[2], ref.shape[3]
    return ref[...].reshape(rows, columns)


def mean_square(values):
    return jnp.mean(values * values, axis=-1, keepdims=True)


def norm_back(grad, normed, scale):
    return scale * (grad - normed * jnp.mean(grad * normed, axis=-1, keepdims=True))


def slab_turns(line_ref, turn_ref, s):
    rows = line_ref[s]
    cos_base, sin_base = rows[0:1], rows[1:2]
    cos_off, sin_off = turn_ref[0], turn_ref[1]
    lane = lax.broadcasted_iota(jnp.int32, (SLAB, SLAB), 1)
    sign = jnp.where(lane < 32, -1.0, jnp.where(lane < 64, 1.0, 0.0))
    return cos_base * cos_off - sin_base * sin_off, (sin_base * cos_off + cos_base * sin_off) * sign


def turned(field, cosine, sine):
    lane = lax.broadcasted_iota(jnp.int32, (SLAB, SLAB), 1)
    return field * cosine + jnp.where(lane < 32, pltpu.roll(field, 96, 1), pltpu.roll(field, 32, 1)) * sine


def half_rows(values, k):
    return values[k * SLAB : (k + 1) * SLAB]


def direct_gather(links, place, buf, first, second):
    ring_x, ring_y = place.ring("x"), place.ring("y")
    a, b = pl.ds(*first), pl.ds(*second)

    def spread(ring, view, size):
        return links.group([(view, view, ring.device(k)) for k in (ring.next, ring.prev, ring.far)], size)

    over_x = spread(ring_x, buf.at[place.y, place.x, :, a], buf.at[0, pl.ds(0, 3), :, a])
    over_y = spread(ring_y, buf.at[place.y, place.x, :, b], buf.at[0, pl.ds(0, 3), :, b])
    yield
    over_x()
    over_x = spread(ring_y, buf.at[place.y, :, :, a], buf.at[pl.ds(0, 3), :, :, a])
    over_y()
    over_y = spread(ring_x, buf.at[:, place.x, :, b], buf.at[pl.ds(0, 3), :, :, b])
    yield
    over_x()
    over_y()


def turned_view(buf, flip):
    def view(along, over):
        first, second = (over, along) if flip else (along, over)
        return buf.at[first, second, pl.ds(2 if flip else 0, 2)]

    return view


def slab_gather_half(links, along, over, view):
    three, four = pl.ds(1, 3), pl.ds(0, 4)
    own = view(0, 0)
    over_arrived = links.group(
        [
            (own, view(0, 3), over.device(over.next)),
            (own, view(0, 1), over.device(over.prev)),
            (own, view(0, 2), over.device(over.far)),
        ],
        view(0, three),
    )
    up, down = along.device(along.next), along.device(along.prev)
    lines = [links.recv_slot(), links.recv_slot()]
    links.group([(own, view(3, 0), up), (own, view(1, 0), down)], view(0, pl.ds(0, 2)), lines)
    yield
    over_arrived()
    rest = view(0, three)
    links.group([(rest, view(3, three), up), (rest, view(1, three), down)], view(pl.ds(0, 2), three), lines)
    yield
    low, high = pl.ds(0, 2), pl.ds(2, 2)
    links.arrived(view(3, four), lines[0])
    far = [links.recv_slot()] * 2
    send = links.send_slot()
    links.start(view(3, low), view(2, low), up, send, far[0])
    links.arrived(view(1, four), lines[1])
    links.start(view(1, high), view(2, high), down, send, far[1])
    links.sent.append(lambda: links.arrived(view(0, four), send))
    yield
    links.arrived(view(2, four), far[0])


def slab_gather(links, place, buf):
    ring_x, ring_y = place.ring("x"), place.ring("y")
    return (
        slab_gather_half(links, ring_y, ring_x, turned_view(buf, False)),
        slab_gather_half(links, ring_x, ring_y, turned_view(buf, True)),
    )


def slab_scatter_room():
    many, line = pltpu.VMEM((2, 2, SLAB, SLAB), BF16), pltpu.VMEM((4, 2, SLAB, SLAB), BF16)
    return ([many] * 2 + [line] * 3 + [pltpu.VMEM((3, 2, SLAB, SLAB), BF16)]) * 2


def slab_scatter_half(links, along, over, view, room, target):
    low, high, prev, nxt, lined, lasts = room
    lo, hi, four = pl.ds(0, 2), pl.ds(2, 2), pl.ds(0, 4)
    up, down = along.device(along.next), along.device(along.prev)
    slots = [links.recv_slot() for _ in range(4)]
    links.group(
        [
            (view(2, lo), low, up),
            (view(2, hi), high, down),
            (view(1, hi), prev.at[hi], up),
            (view(3, lo), nxt.at[lo], down),
        ],
        view(lo, four),
        slots,
    )
    yield
    links.arrived(low, slots[0])
    add_into(view(1, lo), [view(1, lo), low], BF16)
    send = links.send_slot()
    links.start(view(1, lo), prev.at[lo], up, send, slots[2])
    links.arrived(high, slots[1])
    add_into(view(3, hi), [view(3, hi), high], BF16)
    links.start(view(3, hi), nxt.at[hi], down, send, slots[3])
    links.sent.append(lambda: links.arrived(view(0, four), send))
    yield
    links.arrived(prev, slots[2])
    links.arrived(nxt, slots[3])
    add_into(lined, [view(0, four), prev, nxt], BF16)
    arrived = links.group(
        [
            (lined.at[1], lasts.at[0], over.device(over.next)),
            (lined.at[3], lasts.at[1], over.device(over.prev)),
            (lined.at[2], lasts.at[2], over.device(over.far)),
        ],
        lasts,
    )
    yield
    arrived()
    add_into(target, [lined.at[0], lasts.at[0], lasts.at[1], lasts.at[2]], F32)


def slab_scatter(links, place, buf, rooms, target):
    ring_x, ring_y = place.ring("x"), place.ring("y")
    return (
        slab_scatter_half(links, ring_y, ring_x, turned_view(buf, False), rooms[:6], target.at[pl.ds(0, 2)]),
        slab_scatter_half(links, ring_x, ring_y, turned_view(buf, True), rooms[6:], target.at[pl.ds(2, 2)]),
    )


def slab_place(at):
    return lax.div(at, 16), lax.rem(lax.div(at, 4), 4), lax.rem(at, 4)


def keys_of(kv_ref, table, s, first, count):
    places = [slab_place(jnp.clip(table[s * 24 + first + k, 0], 0, 63)) for k in range(count)]
    return jnp.concatenate([kv_ref[y, x, z] for y, x, z in places], 0)


def query_positions(table, s, shape, axis):
    return table[s * 24 + 20, 0] + lax.broadcasted_iota(jnp.int32, shape, axis)


def attend_head(j, table, q_ref, kv_ref, top_ref, sum_ref, acc_ref, between):
    def fold(s, first, count, first_key):
        keys = keys_of(kv_ref, table, s, first, count)
        width = count * SLAB
        pos_q = query_positions(table, s, (1, SLAB), 1)
        pos_k = first_key + lax.broadcasted_iota(jnp.int32, (width, 1), 0)
        scores = dot_right_t(keys, q_ref[s, :, pl.ds(j * 128, 128)])
        scores = jnp.where(pos_k <= pos_q, scores, LOW)
        top, total = top_ref[s][0:1], sum_ref[s][0:1]
        new_top = jnp.maximum(top, jnp.max(scores, axis=0, keepdims=True))
        weights = jnp.exp(scores - new_top)
        decay = jnp.exp(top - new_top)
        total = total * decay + jnp.sum(weights, axis=0, keepdims=True)
        sums = lax.dot_general(keys, weights.astype(BF16), (((0,), (0,)), ((), ())), preferred_element_type=F32)
        acc_ref[s] = acc_ref[s] * decay + sums
        top_ref[s] = jnp.broadcast_to(new_top, (8, SLAB))
        sum_ref[s] = jnp.broadcast_to(total, (8, SLAB))

    for s in range(4):
        top_ref[s] = jnp.full((8, SLAB), LOW, F32)
        sum_ref[s] = jnp.zeros((8, SLAB), F32)
        acc_ref[s] = jnp.zeros((SLAB, SLAB), F32)

    def prompt(c, carry):
        for s in range(4):
            fold(s, c * 4, 4, c * 512)
        return carry

    lax.fori_loop(0, 2, prompt, 0)
    between(0)
    lax.fori_loop(2, 4, prompt, 0)
    between(1)
    for s in range(4):
        fold(s, 16, 2, 2048)


def attend_back_head(j, table, q_ref, kv_ref, grad_ref, logs, deltas, dq_ref, terms_ref, pair_ref, between):
    lane = lax.broadcasted_iota(jnp.int32, (SLAB, SLAB), 1)
    for s in range(4):
        grads = grad_ref[s, :, pl.ds(128 * (j // 2), 128)].astype(F32)
        if j != 1:
            grads = pltpu.roll(grads, 64, 1)
        pair_ref[s, pl.ds(0, SLAB)] = q_ref[s, :, pl.ds(j * 128, 128)]
        pair_ref[s, pl.ds(SLAB, SLAB)] = jnp.where(lane < 64, 0.0, grads).astype(BF16)
        dq_ref[s] = jnp.zeros((SLAB, SLAB), F32)

    def fold(s, first, count, first_key):
        keys = keys_of(kv_ref, table, s, first, count)
        width = count * SLAB
        pos_q = query_positions(table, s, (1, SLAB), 1)
        pos_k = first_key + lax.broadcasted_iota(jnp.int32, (width, 1), 0)
        pair = pair_ref[s]
        both = dot_right_t(keys, pair)
        weights = jnp.where(pos_k <= pos_q, jnp.exp(both[:, :SLAB] - logs[s]), 0.0)
        slopes = (weights * (both[:, SLAB:] - deltas[s])).astype(BF16)
        terms = dot(jnp.concatenate([slopes, weights.astype(BF16)], 1), pair)
        terms_ref[s, pl.ds(first, count)] = terms.astype(BF16).reshape(count, SLAB, SLAB)
        dq_ref[s] += lax.dot_general(slopes, keys, (((0,), (0,)), ((), ())), preferred_element_type=F32)

    def prompt(c, carry):
        for s in range(4):
            fold(s, c * 4, 4, c * 512)
        return carry

    lax.fori_loop(0, 2, prompt, 0)
    between(0)
    lax.fori_loop(2, 4, prompt, 0)
    between(1)
    for s in range(4):
        fold(s, 16, 2, 2048)
    between(2)


def sum_terms(place, table, terms_ref, part_ref):
    def block(t, carry):
        dy, dx = lax.div(t, 4), lax.rem(t, 4)
        at = lax.rem(dy + place.y, 4) * 16 + lax.rem(dx + place.x, 4) * 4
        for dz in range(4):
            places = [jnp.clip(table[96 + s, at + dz], 0, 18) for s in range(4)]
            total = terms_ref[0, places[0]].astype(F32)
            for s in range(1, 4):
                total = total + terms_ref[s, places[s]].astype(F32)
            part_ref[dy, dx, dz] = total.astype(BF16)
        return carry

    lax.fori_loop(0, 16, block, 0)


def lookups(total, place, meta_ref):
    seg, base = total[2:3], total[3:4]
    lane = lax.broadcasted_iota(jnp.int32, (1, SLAB), 1)
    from_here = lax.rem(lax.div(lane, 16) + 4 - place.y, 4) * 16 + lax.rem(lax.rem(lax.div(lane, 4), 4) + 4 - place.x, 4) * 4
    lane_at = (from_here + lax.rem(lane, 4)).astype(F32)
    own = place.y * 4 + place.x
    n = lax.broadcasted_iota(jnp.int32, (24, 1), 0)
    back_rows = jnp.zeros((8, SLAB), F32)
    back_row = lax.broadcasted_iota(jnp.int32, (8, 1), 0)
    for s in range(4):
        mine = lane == own * 4 + s
        seg_q = jnp.sum(jnp.where(mine, seg, 0.0), axis=1, keepdims=True)
        base_q = jnp.sum(jnp.where(mine, base, 0.0), axis=1, keepdims=True)
        prompt = jnp.where(seg_q >= CONTS + 1.0, CONTS + 1.0, 0.0)
        want = jnp.where(n < 16, prompt, seg_q)
        hit = (seg == want) & (base == n.astype(F32) * SLAB) & (lane < 64)
        places = jnp.max(jnp.where(hit, lane_at, 0.0), axis=1, keepdims=True)
        listed = jnp.where(n == 20, base_q, places)
        meta_ref[pl.ds(s * 24, 24), :] = jnp.broadcast_to(listed, (24, SLAB)).astype(jnp.int32)
        visible = (seg == prompt) | (seg == seg_q)
        places = jnp.where(visible, jnp.minimum(base * (1.0 / SLAB), 17.0), 18.0)
        back_rows = jnp.where(back_row == s, places, back_rows)
    meta_ref[pl.ds(96, 8), :] = back_rows.astype(jnp.int32)


def column_of(gain_ref):
    i = lax.broadcasted_iota(jnp.int32, (12, 12), 0)
    k = lax.broadcasted_iota(jnp.int32, (12, 12), 1)
    return jnp.sum(jnp.where(i == k, gain_ref[...].astype(F32), 0.0), axis=1, keepdims=True)


def plane_columns(z):
    return [((z % 2) * 32 + p * 2 + z // 2) * 48 for p in range(16)]


def own_slab(place, at, seg_ref, pos_ref, base_ref):
    lane = lax.broadcasted_iota(jnp.int32, (1, SLAB), 1)
    high = place.head == 1
    seg = jnp.where(high, seg_ref[1:2], seg_ref[0:1]).astype(F32)
    base = (jnp.where(high, pos_ref[1:2], pos_ref[0:1]) - lane).astype(F32)
    m = lax.broadcasted_iota(jnp.int32, (24, SLAB), 0).astype(F32)
    cosine, sine = [
        jnp.sum(jnp.where(m == base * (1.0 / SLAB), base_ref[k], 0.0), axis=0, keepdims=True) for k in range(2)
    ]
    row = lax.broadcasted_iota(jnp.int32, (8, SLAB), 0)
    here = (lane == at) & (row >= 2)
    facts = jnp.where(here, jnp.where(row == 2, seg, jnp.where(row == 3, base, 0.0)), 0.0)
    return jnp.where(row == 0, cosine, jnp.where(row == 1, sine, facts))


def finish_kernel(
    ff_ref, qkv_ref, og_ref, wq_ref, wk_ref, wv_ref, gate_ref, up_ref, gain1_ref, gain2_ref, out_in, grad_in, down_in,
    out_ref, grad_ref, dgain1_ref, dq_ref, dk_ref, dv_ref, do_ref, dgain2_ref, dgate_ref, dup_ref, down_ref,
):
    out_ref[...] = out_in[...]
    grad_ref[...] = grad_in[...]
    down_ref[...] = down_in[...]
    i = lax.broadcasted_iota(jnp.int32, (12, 12), 0)
    k = lax.broadcasted_iota(jnp.int32, (12, 12), 1)

    def row_of(column):
        return jnp.sum(jnp.where(i == k, column, 0.0), axis=0, keepdims=True)

    gain = column_of(gain1_ref)
    grads = [qkv_ref[z].astype(F32)[:12] for z in range(4)]
    total = jnp.zeros((12, 1), F32)
    for c, w_ref, to_ref in ((384, wq_ref, dq_ref), (0, wk_ref, dk_ref), (64, wv_ref, dv_ref)):
        step = 64 if c == 384 else 128
        grad = jnp.concatenate([grads[z][:, step * j + c : step * j + c + HD] for z in range(4) for j in range(3)], 1)
        total = total + jnp.sum(grad * w_ref[...].astype(F32), axis=1, keepdims=True)
        to_ref[...] = grad * gain
    dgain1_ref[...] = row_of(total)
    do_ref[...] = og_ref[0, pl.ds(0, 12)]

    gain = column_of(gain2_ref)
    total = jnp.zeros((12, 1), F32)
    for k_at, w_ref, to_ref in ((0, gate_ref, dgate_ref), (768, up_ref, dup_ref)):
        pieces = {}
        for z in range(4):
            grad = ff_ref[z, :, pl.ds(k_at, 768)].astype(F32)[:12]
            for p, c in enumerate(plane_columns(z)):
                pieces[c] = grad[:, 48 * p : 48 * p + 48]
        grad = jnp.concatenate([pieces[c] for c in sorted(pieces)], 1)
        total = total + jnp.sum(grad * w_ref[...].astype(F32), axis=1, keepdims=True)
        to_ref[...] = grad * gain
    dgain2_ref[...] = row_of(total)


def layer_kernel(
    tok_ref, cot_hbm, wq_ref, wk_ref, wv_ref, wo_ref, gate_ref, up_ref, down_hbm, gain1_ref, gain2_ref, seg_ref, pos_ref,
    perm_hbm, turn_hbm, base_ref, perm_att_hbm, out_perm_hbm,
    out_ref, in_ref, down_sum_ref, got_ff_ref, got_ref, got_out_ref,
    perm_ref, turn_ref, cot_ref, down_ref, perm_att, out_perm, const_sem, line_ref, descs, meta_ref, table, table_sem,
    for_line, for_line_ff, rows, rows_o, rows_ff, one, cots, wqkv, wo, wff, q_ref, kv0, kv1, kv2,
    tops, sums, accs, heads, att_ref, lse_ref, atts, att_s, mid_s, gm_s, two, act, pre, turn_t, part, part_out, sum_z, sum_out,
    to_heads, grads_ref, terms, pairs, kv_own, d_s, qkv_sum, ff_sum,
    og_part, og_sum, og_next, *rest,
):
    send, recv = rest[-2:]
    rooms = list(rest[:-2])

    def take(count):
        out = rooms[:count]
        del rooms[:count]
        return out

    back_room, ff_room, out_room = take(6), take(26), take(6)
    kv_rooms = [take(12) for _ in range(3)]
    qkv_rooms = [take(6) for _ in range(2)]
    in_room, og_line_room, og_room = take(6), take(6), take(6)
    kvs = (kv0, kv1, kv2)

    pairs_in = (
        (perm_hbm, perm_ref), (turn_hbm, turn_ref), (cot_hbm, cot_ref),
        (down_hbm, down_ref), (perm_att_hbm, perm_att), (out_perm_hbm, out_perm),
    )
    loads = [pltpu.make_async_copy(source, target, const_sem.at[n]) for n, (source, target) in enumerate(pairs_in)]
    for load in loads:
        load.start()
    place = Place()
    partners = announce(place)
    links = Links(send, recv)
    own = place.y * 4 + place.x

    line_ref[place.z] = own_slab(place, own * 4 + place.z, seg_ref, pos_ref, base_ref)
    lined = small_gather(links, place.ring("z"), lambda k: line_ref.at[k], line_ref.at[pl.ds(0, 3)])
    gain = column_of(gain1_ref)
    w_q, w_k, w_v = [ref[...].astype(F32) * gain for ref in (wq_ref, wk_ref, wv_ref)]
    none, blank = jnp.zeros((12, HD), F32), jnp.zeros((4, 768), F32)
    for z in range(4):
        pieces, last = [], []
        for j in range(3):
            at = slice(192 * z + 64 * j, 192 * z + 64 * j + 64)
            pieces += [w_k[:, at], w_v[:, at]]
            last.append(w_q[:, at])
        pieces += [*last, none]
        for_line[z] = jnp.concatenate([jnp.concatenate(pieces, 1), blank[:, :640]], 0).astype(BF16)
    loads[0].wait()
    x = dot(tok_ref[...], perm_ref[...])
    one[place.z] = (x * lax.rsqrt(mean_square(x) + EPS)).astype(BF16)
    enter(partners)
    swap = line_swap(links, place, for_line, rows)
    advance(swap, lined)
    rows_o[place.z] = jnp.concatenate([wo_ref[...].astype(F32), blank], 0).astype(BF16)
    o_line = small_gather(links, place.ring("z"), lambda k: rows_o.at[k], rows_o.at[pl.ds(0, 3)])
    advance(o_line)
    ones = line_gather(links, place, one)
    finish(swap)
    advance(ones)
    wqkv[place.y, place.x] = dot(pack_rows(), rows[...].reshape(64, 640)).astype(BF16)
    kv_gather = direct_gather(links, place, wqkv, (0, 256), (256, 128))
    q_gather = shared_gather(links, place, wqkv, 384, 256)
    advance(kv_gather)
    finish(lined, o_line)
    wo[place.y, place.x] = dot(pack_rows(), rows_o[...].reshape(64, 768)).astype(BF16)
    o_gather = shared_gather(links, place, wo, 0, 768)
    descs[place.y, place.x] = line_ref[0] + line_ref[1] + line_ref[2] + line_ref[3]
    desc_x = small_gather(links, place.ring("x"), lambda k: descs.at[place.y, k], descs.at[0, pl.ds(0, 3)])
    desc_y = small_gather(links, place.ring("y"), lambda k: descs.at[k], descs.at[pl.ds(0, 3)])
    advance(desc_x)
    for load in loads[1:]:
        load.wait()
    gain = column_of(gain2_ref)
    for k, ref in enumerate((gate_ref, up_ref)):
        w = ref[...].astype(F32) * gain
        for z in range(4):
            pieces = [w[:, c : c + 48] for c in plane_columns(z)]
            for_line_ff[z, :, pl.ds(768 * k, 768)] = jnp.concatenate([jnp.concatenate(pieces, 1), blank], 0).astype(BF16)
    advance(kv_gather)
    finish(desc_x)
    advance(desc_y)
    advance(q_gather)
    advance(o_gather)
    advance(ones)
    ff_swap = line_swap(links, place, for_line_ff, rows_ff)
    cots[place.z] = cot_ref[...]
    cot_gather = line_gather(links, place, cots)
    finish(desc_y)
    total = jnp.zeros((8, SLAB), F32)
    for y in range(4):
        for k in range(4):
            total = total + descs[y, k]
    lookups(total, place, meta_ref)
    table_copy = pltpu.make_async_copy(meta_ref, table, table_sem)
    table_copy.start()
    finish(ones, kv_gather)
    advance(q_gather)
    advance(o_gather)

    lines = one[...].reshape(512, 768)
    gathers = [slab_gather(links, place, kv) for kv in kvs]
    for j in range(3):
        field = dot(lines, wqkv[:, :, :, pl.ds(128 * j, 128)].reshape(768, 128))
        for s in range(4):
            cosine, sine = slab_turns(line_ref, turn_ref, s)
            kvs[j][0, 0, s] = turned(half_rows(field, s), cosine, sine).astype(BF16)
        if j < 2:
            advance(*gathers[j])
    advance(ff_swap, cot_gather)
    advance(q_gather)
    advance(*gathers[0])
    advance(*gathers[2])
    advance(*gathers[1])
    advance(q_gather)
    advance(o_gather)
    advance(*gathers[0])
    finish(q_gather)
    field = dot(lines, wqkv[:, :, :, pl.ds(384, 256)].reshape(768, 256))
    lane = lax.broadcasted_iota(jnp.int32, (SLAB, SLAB), 1)
    for s in range(4):
        cosine, sine = slab_turns(line_ref, turn_ref, s)
        first, last = half_rows(field[:, 0:128], s), half_rows(field[:, 128:256], s)
        for j, query in enumerate((first, pltpu.roll(first, 64, 1), last)):
            query = turned(jnp.where(lane < 64, query * 0.125, 0.0), cosine, sine)
            q_ref[s, :, pl.ds(128 * j, 128)] = query.astype(BF16)
    advance(*gathers[2])
    finish(ff_swap)
    for c in range(0, 1536, 768):
        wff[place.y, place.x, :, pl.ds(c, 768)] = dot(
            pack_rows(), rows_ff[:, :, pl.ds(c, 768)].reshape(64, 768)
        ).astype(BF16)
    wff[place.y, place.x, :, pl.ds(1536, 768)] = down_ref[...]
    table_copy.wait()
    advance(o_gather)
    advance(cot_gather)

    lane = lax.broadcasted_iota(jnp.int32, (SLAB, SLAB), 1)
    for s in range(4):
        heads[s, pl.ds(192, 64), :] = jnp.zeros((64, SLAB), F32)
    w_gather = shared_gather(links, place, wff, 0, 2304)
    for j in range(3):
        finish(*gathers[j])

        def between(k, j=j):
            if j == 0 and k == 0:
                links.finish(8)
            if j == 0 and k == 1:
                advance(*gathers[1])
            if j == 1 and k == 0:
                finish(cot_gather)
                links.finish(8)
            if j == 1 and k == 1:
                advance(o_gather)

        if j == 2:
            advance(w_gather)
        attend_head(j, table, q_ref, kvs[j], tops, sums, accs, between)
        for s in range(4):
            heads[s, pl.ds(64 * j, 64), :] = accs[s, pl.ds(64, 64), :] / sums[s][0:1]
            lse_ref[j, s] = tops[s] + jnp.log(sums[s])
        if j == 0:
            advance(*gathers[2])
    for s in range(4):
        att_ref[s, :, 0:128] = heads[s, pl.ds(0, 128), :].T.astype(BF16)
        att_ref[s, :, 128:256] = heads[s, pl.ds(128, 128), :].T.astype(BF16)
    att_swap = line_swap(links, place, att_ref, atts)
    advance(att_swap)
    advance(w_gather)
    links.finish(20)
    finish(att_swap, o_gather)
    advance(w_gather)

    att = dot(atts[0], perm_att[pl.ds(0, 256), :])
    for z in range(1, 4):
        att = att + dot(atts[z], perm_att[pl.ds(256 * z, 256), :])
    att_s[...] = att.astype(BF16)
    mid_s[...] = tok_ref[...].astype(F32) + dot(att_s[...], merged(wo))
    middle = mid_s[...]
    scale_two = lax.rsqrt(mean_square(middle) + EPS)
    two[place.z] = dot((middle * scale_two).astype(BF16), perm_ref[...]).astype(BF16)
    two_gather = line_gather(links, place, two)
    advance(two_gather)
    advance(w_gather)
    att = dot(atts[0], out_perm[pl.ds(0, 256), :])
    for z in range(1, 4):
        att = att + dot(atts[z], out_perm[pl.ds(256 * z, 256), :])
    att_by_z = att.astype(BF16).T
    advance(two_gather)
    together([w_gather, two_gather])

    def block():
        two_b = two[...].reshape(512, 768)
        cot_b = cots[...].reshape(512, 768)
        gate_w = wff[:, :, :, pl.ds(0, 768)].reshape(768, 768)
        up_w = wff[:, :, :, pl.ds(768, 768)].reshape(768, 768)
        down_w = wff[:, :, :, pl.ds(1536, 768)].reshape(768, 768)
        gate = dot(two_b, gate_w)
        up = dot(two_b, up_w)
        sig = 1.0 / (1.0 + jnp.exp(-gate))
        silu = gate * sig
        act_b = (silu * up).astype(BF16)
        act[...] = act_b
        grad_act = dot_right_t(cot_b, down_w)
        grad_gate = (grad_act * up * (sig * (1.0 + gate * (1.0 - sig)))).astype(BF16)
        grad_up = (grad_act * silu).astype(BF16)
        pre[:, pl.ds(0, 768)] = grad_gate
        pre[:, pl.ds(768, 768)] = grad_up
        back = dot_right_t(grad_gate, gate_w) + dot_right_t(grad_up, up_w)
        part[...] = back.astype(BF16).reshape(4, SLAB, 768)

    def out_block(r, carry):
        at = pl.ds(pl.multiple_of(r * 256, 256), 256)
        down_w = wff[:, :, :, pl.ds(1536, 768)].reshape(768, 768)
        part_out[pl.ds(r * 2, 2)] = dot(act[at, :], down_w).astype(BF16).reshape(2, SLAB, 768)
        return carry

    block()
    links.finish()
    back_sum = line_scatter(links, place, part, back_room, sum_z)
    advance(back_sum)
    lax.fori_loop(0, 2, out_block, 0)
    turn_t[...] = two[...].reshape(512, 768).T

    def first_grads(c, carry):
        at = pl.ds(pl.multiple_of(c * 256, 256), 256)
        wff[:, :, :, at] = dot(turn_t[...], pre[:, at]).astype(BF16).reshape(4, 4, 48, 256)
        return carry

    def last_grads(c, carry):
        at = pl.ds(pl.multiple_of(c * 256, 256), 256)
        to = pl.ds(pl.multiple_of(1536 + c * 256, 256), 256)
        cot_all = cots[:, :, at].reshape(512, 256)
        wff[:, :, :, to] = dot(turn_t[...], cot_all).astype(BF16).reshape(4, 4, 48, 256)
        return carry

    lax.fori_loop(0, 6, first_grads, 0)
    advance(back_sum)
    turn_t[...] = act[...].T
    lax.fori_loop(0, 3, last_grads, 0)
    ff = plane_scatter(links, place, wff, ff_room, ff_sum, False)
    advance(*ff)
    finish(back_sum)
    links.finish(6)

    grad = dot_right_t(sum_z[0].astype(BF16), perm_ref[...])
    middle = mid_s[...]
    scale_two = lax.rsqrt(mean_square(middle) + EPS)
    gm_s[...] = cot_ref[...].astype(F32) + norm_back(grad, middle * scale_two, scale_two)
    low = gm_s[...].astype(BF16)
    grad_att = dot_right_t(low, merged(wo)).astype(BF16)
    for z in range(4):
        to_heads[z] = dot_right_t(grad_att, perm_att[pl.ds(256 * z, 256), :]).astype(BF16)
    heads_swap = line_swap(links, place, to_heads, grads_ref)
    advance(heads_swap)
    out_sum = line_scatter(links, place, part_out, out_room, sum_out)
    advance(out_sum)
    turn_t[...] = one[...].reshape(512, 768).T
    og_part[...] = dot(att_by_z, low).astype(BF16).reshape(4, 256, 768)
    for s in range(4):
        terms[s, 18] = jnp.zeros((SLAB, SLAB), BF16)
    finish(heads_swap)

    which = lax.broadcasted_iota(jnp.int32, (8, SLAB), 0)
    at_lane = lax.broadcasted_iota(jnp.int32, (8, 256), 1)
    pick = (lax.div(at_lane, HD) == lax.broadcasted_iota(jnp.int32, (8, 256), 0)).astype(F32)
    logs, deltas = [], []
    for s in range(4):
        inner = grads_ref[s].astype(F32) * att_ref[s].astype(F32)
        delta = lax.dot_general(pick, inner, LANES, precision=HIGHEST, preferred_element_type=F32)
        logs.append([lse_ref[j, s][0:1] for j in range(3)])
        deltas.append([jnp.sum(jnp.where(which == k, delta, 0.0), axis=0, keepdims=True) for k in range(3)])

    scatters = []

    def keys_turn(j):
        for s in range(4):
            cosine, sine = slab_turns(line_ref, turn_ref, s)
            d_s[pl.ds(s * SLAB, SLAB), pl.ds(128 * j, 128)] = turned(kv_own[j, s], cosine, -sine).astype(BF16)

    def qkv_grads(columns, first, second, room):
        for c in columns:
            wo[:, :, :, pl.ds(c, 128)] = dot(turn_t[...], d_s[:, pl.ds(c, 128)]).astype(BF16).reshape(4, 4, 48, 128)
        scatter = small_scatter(links, place, wo, first, second, room, qkv_sum)
        advance(*scatter)
        return scatter

    og_line = line_scatter(links, place, og_part, og_line_room, og_sum)
    spread = spread_rows()
    for j in range(3):

        def between(k, j=j):
            if j == 0 and k == 0:
                advance(*ff)
                advance(out_sum)
            if j == 1 and k == 0:
                advance(*ff)
                links.finish(8)
            if j == 1 and k == 2:
                advance(*scatters[0])
            if j == 2 and k == 0:
                advance(*ff)
                links.finish(4)
            if j == 2 and k == 1:
                advance(*scatters[0])
            if j == 2 and k == 2:
                advance(*scatters[1])

        attend_back_head(
            j, table, q_ref, kvs[j], grads_ref, [v[j] for v in logs], [v[j] for v in deltas], accs, terms, pairs, between
        )
        sum_terms(place, table, terms, kvs[j])
        scatters.append(slab_scatter(links, place, kvs[j], kv_rooms[j], kv_own.at[j]))
        advance(*scatters[j])
        for s in range(4):
            cosine, sine = slab_turns(line_ref, turn_ref, s)
            grad = turned(jnp.where(lane < 64, accs[s] * 0.125, 0.0), cosine, -sine)
            to = (pl.ds(s * SLAB, SLAB), pl.ds(384 + 128 * (j // 2), 128))
            if j == 1:
                grad = jnp.where(lane < 64, d_s[to].astype(F32), pltpu.roll(grad, 64, 1))
            d_s[to] = grad.astype(BF16)
        if j == 0:
            finish(out_sum)
            advance(og_line)
            out_ref[...] = (mid_s[...] + sum_out[0]).astype(BF16)
        if j == 1:
            advance(og_line)

    finish(*scatters[0])
    finish(*ff)
    down_sum_ref[...] = ff_sum[0, :, pl.ds(1536, 768)]
    for c in range(0, 1536, 768):
        for_line_ff[:, :, pl.ds(c, 768)] = (
            dot(spread, ff_sum[0, :, pl.ds(c, 768)].astype(BF16)).astype(BF16).reshape(4, 16, 768)
        )
    finish(og_line)
    grads_swap = line_swap(links, place, for_line_ff, got_ff_ref)
    advance(grads_swap)
    keys_turn(0)
    og_next[...] = og_sum[0].astype(BF16).reshape(4, 4, 16, 768)
    links.finish(12)
    advance(*scatters[1])
    advance(*scatters[2])
    finish(*scatters[1])
    keys_turn(1)
    advance(*scatters[2])
    qkv = qkv_grads((0, 128, 384), (0, 256), (384, 128), qkv_rooms[0])
    og = small_scatter(links, place, og_next, (0, 384), (384, 384), og_room, got_out_ref)
    advance(*og)
    links.finish(12)
    finish(*scatters[2])
    keys_turn(2)

    def last_block(r, carry):
        at = pl.ds(pl.multiple_of(r * 256, 256), 256)
        part[pl.ds(r * 2, 2)] = dot_right_t(d_s[at, :], merged(wqkv)).astype(BF16).reshape(2, SLAB, 768)
        return carry

    lax.fori_loop(0, 2, last_block, 0)
    in_sum = line_scatter(links, place, part, in_room, sum_z)
    advance(in_sum)
    last_qkv = qkv_grads((256, 512), (256, 128), (512, 128), qkv_rooms[1])
    advance(*qkv)
    finish(grads_swap)
    advance(in_sum)
    advance(*last_qkv)
    advance(*og)
    finish(*qkv)
    links.finish(len(links.sent) - 4)
    finish(*last_qkv)
    for_line[...] = dot(spread, qkv_sum[0].astype(BF16)).astype(BF16).reshape(4, 16, 640)
    last = line_swap(links, place, for_line, got_ref)
    advance(last)
    finish(*og)
    finish(in_sum)
    grad = dot_right_t(sum_z[0].astype(BF16), perm_ref[...])
    x = tok_ref[...].astype(F32)
    scale = lax.rsqrt(mean_square(x) + EPS)
    in_ref[...] = gm_s[...] + norm_back(grad, x * scale, scale)
    links.finish()
    finish(last)


SENDS, RECVS = 188, 200
LINE = pltpu.VMEM((4, SLAB, 768), BF16)
KV = pltpu.VMEM((4, 4, 4, SLAB, SLAB), BF16)
OUTS = [
    ((SLAB, 768), BF16),
    ((SLAB, 768), F32),
    ((48, 768), F32),
    ((4, 16, 1536), BF16),
    ((4, 16, 640), BF16),
    ((1, 16, 768), F32),
]
ROOM = (
    [
        pltpu.VMEM((768, 768), BF16),
        pltpu.VMEM((2, SLAB, SLAB), F32),
        pltpu.VMEM((SLAB, 768), BF16),
        pltpu.VMEM((48, 768), BF16),
        pltpu.VMEM((1024, 768), BF16),
        pltpu.VMEM((1024, 1024), BF16),
        pltpu.SemaphoreType.DMA((6,)),
        pltpu.VMEM((4, 8, SLAB), F32),
        pltpu.VMEM((4, 4, 8, SLAB), F32),
        pltpu.VMEM((104, SLAB), jnp.int32),
        pltpu.SMEM((104, SLAB), jnp.int32),
        pltpu.SemaphoreType.DMA,
        pltpu.VMEM((4, 16, 640), BF16),
        pltpu.VMEM((4, 16, 1536), BF16),
        pltpu.VMEM((4, 16, 640), BF16),
        pltpu.VMEM((4, 16, 768), BF16),
        pltpu.VMEM((4, 16, 1536), BF16),
        LINE,
        LINE,
        pltpu.VMEM((4, 4, 48, 640), BF16),
        pltpu.VMEM((4, 4, 48, 768), BF16),
        pltpu.VMEM((4, 4, 48, 2304), BF16),
        pltpu.VMEM((4, SLAB, 384), BF16),
        KV,
        KV,
        KV,
        pltpu.VMEM((4, 8, SLAB), F32),
        pltpu.VMEM((4, 8, SLAB), F32),
        pltpu.VMEM((4, SLAB, SLAB), F32),
        pltpu.VMEM((4, 256, SLAB), F32),
        pltpu.VMEM((4, SLAB, 256), BF16),
        pltpu.VMEM((3, 4, 8, SLAB), F32),
        pltpu.VMEM((4, SLAB, 256), BF16),
        pltpu.VMEM((SLAB, 768), BF16),
        pltpu.VMEM((SLAB, 768), F32),
        pltpu.VMEM((SLAB, 768), F32),
        LINE,
        pltpu.VMEM((512, 768), BF16),
        pltpu.VMEM((512, 1536), BF16),
        pltpu.VMEM((768, 512), BF16),
        LINE,
        LINE,
        pltpu.VMEM((1, SLAB, 768), F32),
        pltpu.VMEM((1, SLAB, 768), F32),
        pltpu.VMEM((4, SLAB, 256), BF16),
        pltpu.VMEM((4, SLAB, 256), BF16),
        pltpu.VMEM((4, 19, SLAB, SLAB), BF16),
        pltpu.VMEM((4, 256, SLAB), BF16),
        pltpu.VMEM((3, 4, SLAB, SLAB), F32),
        pltpu.VMEM((512, 640), BF16),
        pltpu.VMEM((1, 48, 640), F32),
        pltpu.VMEM((1, 48, 2304), F32),
        pltpu.VMEM((4, 256, 768), BF16),
        pltpu.VMEM((1, 256, 768), F32),
        pltpu.VMEM((4, 4, 16, 768), BF16),
    ]
    + line_scatter_room(SLAB, 768)
    + plane_scatter_room(48, 2304, False)
    + line_scatter_room(SLAB, 768)
    + slab_scatter_room() * 3
    + small_scatter_room(48, 256, 128)
    + small_scatter_room(48, 128, 128)
    + line_scatter_room(SLAB, 768)
    + line_scatter_room(256, 768)
    + small_scatter_room(16, 384, 384)
)


def per_device(
    tokens, gain_one, w_query, w_key, w_value, w_out, gain_two, w_gate, w_up, w_down, cotangent, segment_ids, positions
):
    gains = (gain_one.reshape(1, 12), gain_two.reshape(1, 12))
    anywhere = pl.BlockSpec(memory_space=pl.ANY)
    output, input_grad, down_grad, got_ff, got_qkv, got_out = pl.pallas_call(
        layer_kernel,
        out_shape=tuple(jax.ShapeDtypeStruct(shape, kind) for shape, kind in OUTS),
        in_specs=[anywhere if k in (1, 8, 13, 14, 16, 17) else VMEM for k in range(18)],
        out_specs=tuple([VMEM] * len(OUTS)),
        scratch_shapes=ROOM
        + [pltpu.SemaphoreType.DMA((SENDS,)), pltpu.SemaphoreType.DMA((RECVS,))],
        compiler_params=pltpu.CompilerParams(collective_id=0, has_side_effects=True, vmem_limit_bytes=62 * MIB),
        name="layer",
    )(
        tokens, cotangent, w_query, w_key, w_value, w_out, w_gate, w_up, w_down, *gains,
        segment_ids.reshape(2, SLAB), positions.reshape(2, SLAB),
        jnp.asarray(TO_PERM, BF16), jnp.asarray(OFFSET_TURNS, F32), jnp.asarray(BASE_TURNS, F32),
        jnp.asarray(ATT_PERM, BF16), jnp.asarray(OUT_PERM, BF16),
    )
    small, square, wide = [jax.ShapeDtypeStruct((rows, columns), F32) for rows, columns in ((1, 12), (12, 768), (12, 3072))]
    output, input_grad, gain_one_grad, dq, dk, dv, do, gain_two_grad, dgate, dup, down_grad = pl.pallas_call(
        finish_kernel,
        out_shape=(*[jax.ShapeDtypeStruct(*OUTS[k]) for k in range(2)], small, square, square, square, square, small, wide, wide,
                   jax.ShapeDtypeStruct(*OUTS[2])),
        in_specs=[VMEM] * 13,
        out_specs=(VMEM,) * 11,
        name="finish",
    )(got_ff, got_qkv, got_out, w_query, w_key, w_value, w_gate, w_up, *gains, output, input_grad, down_grad)
    return (
        output, input_grad, gain_one_grad.reshape(12), dq, dk, dv, do, gain_two_grad.reshape(12), dgate, dup, down_grad
    )


def solution(mesh):
    rows = P(("grp", "blk", "head"), None)
    flat = P(("grp", "blk", "head"))
    weight = P(("blk", "head"), None)
    gain = P(("blk", "head"))
    ids = P(("grp", "blk"))
    in_specs = (rows, gain, weight, weight, weight, weight, gain, weight, weight, weight, rows, ids, ids)
    out_specs = (rows, rows, flat, rows, rows, rows, rows, flat, rows, rows, rows)
    return jax.shard_map(per_device, mesh=mesh, in_specs=in_specs, out_specs=out_specs, check_vma=False)
```

```python
import math

import jax
import jax.numpy as jnp
import numpy as np
from jax import lax
from jax.experimental import pallas as pl
from jax.experimental.pallas import tpu as pltpu
from jax.sharding import PartitionSpec as P

MESH = pl.DeviceIdType.MESH
F32 = jnp.float32
BF16 = jnp.bfloat16
HD = 64
CONTS = 8
SLAB = 128
LOW = -1e30
EPS = 1e-05
LANES = (((1,), (1,)), ((), ()))
HIGHEST = lax.Precision.HIGHEST
MIB = 1 << 20
VMEM = pl.BlockSpec(memory_space=pltpu.VMEM)
SMEM = pl.BlockSpec(memory_space=pltpu.SMEM)


def feature_order():
    place = np.arange(768)
    p, z, r = place // 48, place // 12 % 4, place % 12
    t = (z % 2) * 32 + p * 2 + z // 2
    return t * 12 + r


ORDER = feature_order()
TO_PERM = np.zeros((768, 768), np.float32)
TO_PERM[ORDER, np.arange(768)] = 1.0


ATT_PERM = np.pad(TO_PERM.reshape(4, 192, 768), ((0, 0), (0, 64), (0, 0))).reshape(1024, 768)
OUT_PERM = np.pad(ATT_PERM.reshape(1024, 16, 4, 12).transpose(0, 2, 1, 3), ((0, 0), (0, 0), (0, 0), (0, 4))).reshape(1024, 1024)
LANE_FREQUENCY = 10000.0 ** (-(np.arange(128) % 32) * 2.0 / HD) * (np.arange(128) < HD)
OFFSET_ANGLES = np.arange(SLAB)[:, None] * LANE_FREQUENCY[None]
BASE_ANGLES = SLAB * np.arange(24)[:, None] * LANE_FREQUENCY[None]
BASE_TURNS = np.stack([np.cos(BASE_ANGLES), np.sin(BASE_ANGLES)]).astype(np.float32)
OFFSET_TURNS = np.stack([np.cos(OFFSET_ANGLES), np.sin(OFFSET_ANGLES)]).astype(np.float32)


class Place:
    def __init__(self):
        self.core = lax.axis_index("grp")
        blk = lax.axis_index("blk")
        self.blk, self.head = blk, lax.axis_index("head")
        self.x = lax.rem(blk, 4)
        self.y = lax.rem(lax.div(blk, 4), 4)
        self.z = self.head * 2 + lax.div(blk, 16)

    def other_core(self):
        return (1 - self.core, self.blk, self.head)

    def device(self, x=None, y=None, z=None):
        x = self.x if x is None else x
        y = self.y if y is None else y
        z = self.z if z is None else z
        return (self.core, lax.rem(z, 2) * 16 + y * 4 + x, lax.div(z, 2))

    def ring(self, axis):
        return Ring(self, axis)


class Ring:
    def __init__(self, place, axis):
        self.place, self.axis = place, axis
        self.own = getattr(place, axis)
        self.next = lax.rem(self.own + 1, 4)
        self.prev = lax.rem(self.own + 3, 4)
        self.far = lax.rem(self.own + 2, 4)

    def device(self, index):
        return self.place.device(**{self.axis: index})


def announce(place):
    partners = [place.other_core()]
    for axis in ("x", "y", "z"):
        ring = place.ring(axis)
        partners += [ring.device(ring.next), ring.device(ring.prev), ring.device(ring.far)]
    barrier = pltpu.get_barrier_semaphore()
    for partner in partners:
        pl.semaphore_signal(barrier, inc=1, device_id=partner, device_id_type=MESH)
    return len(partners)


def enter(partners):
    pl.semaphore_wait(pltpu.get_barrier_semaphore(), partners)


class Links:
    def __init__(self, send, recv):
        self.send, self.recv, self.sends, self.recvs, self.sent = send, recv, 0, 0, []

    def send_slot(self):
        self.sends += 1
        return self.send.at[self.sends - 1]

    def recv_slot(self):
        self.recvs += 1
        return self.recv.at[self.recvs - 1]

    def start(self, source, target, device, send, recv):
        copy = pltpu.make_async_remote_copy(
            src_ref=source, dst_ref=target, send_sem=send, recv_sem=recv, device_id=device, device_id_type=MESH
        )
        copy.start()
        return copy

    def copy(self, source, target, device):
        copy = self.start(source, target, device, self.send_slot(), self.recv_slot())
        self.sent.append(copy.wait_send)
        return copy

    def group(self, copies, view, recv=None):
        send = self.send_slot()
        slots = [self.recv_slot()] * len(copies) if recv is None else recv
        for (source, target, device), slot in zip(copies, slots):
            self.start(source, target, device, send, slot)
        self.sent.append(lambda: self.arrived(view, send))
        return lambda: self.arrived(view, slots[0])

    def arrived(self, view, semaphore):
        pltpu.make_async_copy(view, view, semaphore).wait()

    def finish(self, count=None):
        count = len(self.sent) if count is None else count
        for wait in self.sent[:count]:
            wait()
        del self.sent[:count]


def together(steps):
    steps = list(steps)
    while steps:
        left = []
        for step in steps:
            try:
                next(step)
                left.append(step)
            except StopIteration:
                pass
        steps = left


def ring_gather(links, ring, slot):
    right = links.copy(slot(ring.own, None), slot(ring.own, None), ring.device(ring.next))
    left = links.copy(slot(ring.own, None), slot(ring.own, None), ring.device(ring.prev))
    yield
    right.wait_recv()
    on_right = links.copy(slot(ring.prev, 0), slot(ring.prev, 0), ring.device(ring.next))
    left.wait_recv()
    on_left = links.copy(slot(ring.next, 1), slot(ring.next, 1), ring.device(ring.prev))
    yield
    on_right.wait_recv()
    on_left.wait_recv()


def add_into(target, terms, kind):
    *lead, rows, columns = target.shape
    step = 16
    for size in (128, 64, 48, 32):
        if rows % size == 0 and size * columns <= 48 * 1024:
            step = size
            break
    count = rows // step

    def body(k, carry):
        at, rest = [], lax.div(k, count)
        for size in reversed(lead):
            at.insert(0, lax.rem(rest, size))
            rest = lax.div(rest, size)
        at = (*at, pl.ds(pl.multiple_of(lax.rem(k, count) * step, step), step), slice(None))
        total = terms[0][at].astype(kind)
        for term in terms[1:]:
            total = total + term[at].astype(kind)
        target[at] = total
        return carry

    trips = math.prod(lead) * count
    lax.fori_loop(0, trips, body, 0, unroll=2 if trips % 2 == 0 else 1)


def ring_scatter(links, ring, part, room, target, kind):
    low, high, sum_low, sum_high, from_prev, from_next = room
    nxt, prv = ring.device(ring.next), ring.device(ring.prev)
    far_low = links.copy(part(ring.far, 0), low, nxt)
    far_high = links.copy(part(ring.far, 1), high, prv)
    next_high = links.copy(part(ring.next, 1), from_prev(1), nxt)
    prev_low = links.copy(part(ring.prev, 0), from_next(0), prv)
    yield
    far_low.wait_recv()
    add_into(sum_low, [part(ring.next, 0), low], BF16)
    next_low = links.copy(sum_low, from_prev(0), nxt)
    far_high.wait_recv()
    add_into(sum_high, [part(ring.prev, 1), high], BF16)
    prev_high = links.copy(sum_high, from_next(1), prv)
    yield
    for copy in (next_high, prev_low, next_low, prev_high):
        copy.wait_recv()
    add_into(target, [part(ring.own, None), from_prev(None), from_next(None)], kind)


def lead_part(part):
    return pl.ds(0, 4) if part is None else pl.ds(2 * part, 2)


def row_part(rows, part):
    first = (rows // 2 + 15) // 16 * 16
    if part is None:
        return 0, rows
    return (0, first) if part == 0 else (first, rows - first)


def regions(rows, columns, by_rows):
    if by_rows:
        return [(0, rows // 2, 0, columns), (rows // 2, rows // 2, 0, columns)]
    return [(0, rows, 0, columns // 2), (0, rows, columns // 2, columns // 2)]


def plane_gather(links, place, buf, by_rows):
    rows, columns = buf.shape[2:]

    def half(region, x_first):
        r0, rn, c0, cn = region

        def one(k, part):
            off, size = row_part(rn, part)
            y, x = (place.y, k) if x_first else (k, place.x)
            return buf.at[y, x, pl.ds(r0 + off, size), pl.ds(c0, cn)]

        def line(k, part):
            y, x = (k, lead_part(part)) if x_first else (lead_part(part), k)
            return buf.at[y, x, pl.ds(r0, rn), pl.ds(c0, cn)]

        yield from ring_gather(links, place.ring("x" if x_first else "y"), one)
        yield from ring_gather(links, place.ring("y" if x_first else "x"), line)

    a, b = regions(rows, columns, by_rows)
    return half(a, True), half(b, False)


def plane_scatter_room(rows, columns, by_rows):
    rooms = []
    for _, rn, _, cn in regions(rows, columns, by_rows):
        rooms += [pltpu.VMEM((2, rn, cn), BF16)] * 4 + [pltpu.VMEM((4, rn, cn), BF16)] * 3
        low, high = row_part(rn, 0)[1], row_part(rn, 1)[1]
        rooms += [pltpu.VMEM((1, low, cn), BF16), pltpu.VMEM((1, high, cn), BF16)] * 2
        rooms += [pltpu.VMEM((1, rn, cn), BF16)] * 2
    return rooms


def plane_scatter(links, place, buf, rooms, target, by_rows):
    rows, columns = buf.shape[2:]

    def half(region, room, x_first):
        r0, rn, c0, cn = region
        low, high, sum_low, sum_high, prev, nxt, lined = room[:7]
        low1, high1, sum_low1, sum_high1, prev1, nxt1 = room[7:]

        def line(k, part):
            y, x = (lead_part(part), k) if x_first else (k, lead_part(part))
            return buf.at[y, x, pl.ds(r0, rn), pl.ds(c0, cn)]

        def one(k, part):
            off, size = row_part(rn, part)
            return lined.at[pl.ds(k, 1), pl.ds(off, size), :]

        def lined_part(ref):
            return lambda part: ref.at[lead_part(part)]

        def one_part(ref):
            def view(part):
                off, size = row_part(rn, part)
                return ref.at[:, pl.ds(off, size), :]

            return view

        room_a = (low, high, sum_low, sum_high, lined_part(prev), lined_part(nxt))
        room_b = (low1, high1, sum_low1, sum_high1, one_part(prev1), one_part(nxt1))
        yield from ring_scatter(links, place.ring("x" if x_first else "y"), line, room_a, lined, BF16)
        out = target.at[:, pl.ds(r0, rn), pl.ds(c0, cn)]
        yield from ring_scatter(links, place.ring("y" if x_first else "x"), one, room_b, out, F32)

    a, b = regions(rows, columns, by_rows)
    return half(a, rooms[:13], False), half(b, rooms[13:], True)


def small_scatter_room(rows, *sizes):
    rooms = []
    for size in sizes:
        rooms += [
            pltpu.VMEM((3, 4, rows, size), BF16),
            pltpu.VMEM((4, rows, size), BF16),
            pltpu.VMEM((3, 1, rows, size), BF16),
        ]
    return rooms


def direct_scatter(links, ring, part, room, target, kind):
    copies = [(part(to), room.at[k], ring.device(to)) for k, to in enumerate((ring.next, ring.prev, ring.far))]
    arrived = links.group(copies, room)
    yield
    arrived()
    add_into(target, [part(ring.own), room.at[0], room.at[1], room.at[2]], kind)


def small_scatter(links, place, buf, first, second, rooms, target):
    def half(region, room, x_first):
        columns = pl.ds(*region)
        firsts, lined, lasts = room

        def line(k):
            return buf.at[:, k, :, columns] if x_first else buf.at[k, :, :, columns]

        yield from direct_scatter(links, place.ring("x" if x_first else "y"), line, firsts, lined, BF16)
        out = target.at[:, :, columns]
        yield from direct_scatter(
            links, place.ring("y" if x_first else "x"), lambda k: lined.at[pl.ds(k, 1)], lasts, out, F32
        )

    return half(first, rooms[:3], False), half(second, rooms[3:], True)


def line_scatter_room(rows, columns):
    low, high = row_part(rows, 0)[1], row_part(rows, 1)[1]
    return [pltpu.VMEM((1, low, columns), BF16), pltpu.VMEM((1, high, columns), BF16)] * 2 + [
        pltpu.VMEM((1, rows, columns), BF16)
    ] * 2


def line_scatter(links, place, buf, room, target):
    rows = buf.shape[1]

    def part(k, half):
        off, size = row_part(rows, half)
        return buf.at[pl.ds(k, 1), pl.ds(off, size), :]

    def view(ref):
        def cut(half):
            off, size = row_part(rows, half)
            return ref.at[:, pl.ds(off, size), :]

        return cut

    low, high, sum_low, sum_high, prev, nxt = room
    yield from ring_scatter(
        links, place.ring("z"), part, (low, high, sum_low, sum_high, view(prev), view(nxt)), target, F32
    )


def line_gather(links, place, buf):
    rows = buf.shape[1]

    def slot(k, half):
        off, size = row_part(rows, half)
        return buf.at[k, pl.ds(off, size)]

    yield from ring_gather(links, place.ring("z"), slot)


def line_swap(links, place, source, target):
    ring = place.ring("z")
    copies = [(source.at[other], target.at[ring.own], ring.device(other)) for other in (ring.next, ring.prev, ring.far)]
    arrived = links.group(copies, target.at[pl.ds(0, 3)])
    target[ring.own] = source[ring.own]
    yield
    arrived()


def small_gather(links, ring, slot, three):
    own = slot(ring.own)
    arrived = links.group([(own, own, ring.device(k)) for k in (ring.next, ring.prev, ring.far)], three)
    yield
    arrived()


def shared_gather(links, place, buf, start, size):
    half = size // 2
    flip = place.core == 1
    columns = pl.ds(pl.multiple_of(start + place.core * half, 128), half)
    first, second = jnp.where(flip, place.y, place.x), jnp.where(flip, place.x, place.y)
    first_next, first_prev, first_far = [lax.rem(first + k, 4) for k in (1, 3, 2)]
    second_next, second_prev, second_far = [lax.rem(second + k, 4) for k in (1, 3, 2)]

    def block(s, f, part=None):
        y, x = jnp.where(flip, f, s), jnp.where(flip, s, f)
        rows = pl.ds(0, 48) if part is None else (pl.ds(0, 32) if part == 0 else pl.ds(32, 16))
        return buf.at[y, x, rows, columns]

    def device(s, f):
        return place.device(x=jnp.where(flip, s, f), y=jnp.where(flip, f, s))

    def send(s, f, to, part=None):
        return links.copy(block(s, f, part), block(s, f, part), to)

    handed = []

    def hands(view):
        pair = links.send_slot(), links.recv_slot()
        links.sent.append(lambda: links.arrived(view, pair[0]))
        handed.append(lambda: links.arrived(view, pair[1]))
        return lambda s, f: links.start(block(s, f), block(s, f), place.other_core(), *pair)

    on_right, on_left = device(second, first_next), device(second, first_prev)
    up, down = device(second_next, first), device(second_prev, first)
    order = (first, first_prev, first_next, first_far)
    ups, downs = [], []

    def line(k):
        ups.append(send(second, order[k], up))
        downs.append(send(second, order[k], down))

    right = send(second, first, on_right)
    left = send(second, first, on_left)
    line(0)
    yield
    right.wait_recv()
    far_low = send(second, first_prev, on_right, 0)
    line(1)
    left.wait_recv()
    far_high = send(second, first_next, on_left, 1)
    line(2)
    hand = hands(buf.at[0, pl.ds(0, 2), :, columns])
    hand(second, first_prev)
    hand(second, first_next)
    yield
    far_low.wait_recv()
    far_high.wait_recv()
    line(3)
    hands(buf.at[0, 0, :, columns])(second, first_far)
    yield
    far = []
    hand = hands(buf.at[pl.ds(0, 2), :, :, columns])
    for k in range(4):
        ups[k].wait_recv()
        if k < 2:
            far.append(send(second_prev, order[k], up))
        hand(second_prev, order[k])
        downs[k].wait_recv()
        if k >= 2:
            far.append(send(second_next, order[k], down))
        hand(second_next, order[k])
    yield
    hand = hands(buf.at[0, :, :, columns])
    for k in range(4):
        far[k].wait_recv()
        hand(second_far, order[k])
    yield
    for wait in handed:
        wait()


def advance(*steps):
    for step in steps:
        next(step, None)


def finish(*steps):
    together(steps)


def dot(left, right):
    return jnp.dot(left, right, preferred_element_type=F32)


def dot_right_t(left, right):
    return lax.dot_general(left, right, LANES, preferred_element_type=F32)


def pack_rows():
    i = lax.broadcasted_iota(jnp.int32, (48, 64), 0)
    k = lax.broadcasted_iota(jnp.int32, (48, 64), 1)
    return (k == lax.div(i, 12) * 16 + lax.rem(i, 12)).astype(BF16)


def spread_rows():
    k = lax.broadcasted_iota(jnp.int32, (64, 48), 0)
    i = lax.broadcasted_iota(jnp.int32, (64, 48), 1)
    return (k == lax.div(i, 12) * 16 + lax.rem(i, 12)).astype(BF16)


def merged(ref):
    rows, columns = ref.shape[0] * ref.shape[1] * ref.shape[2], ref.shape[3]
    return ref[...].reshape(rows, columns)


def mean_square(values):
    return jnp.mean(values * values, axis=-1, keepdims=True)


def norm_back(grad, normed, scale):
    return scale * (grad - normed * jnp.mean(grad * normed, axis=-1, keepdims=True))


def slab_turns(line_ref, turn_ref, s):
    rows = line_ref[s]
    cos_base, sin_base = rows[0:1], rows[1:2]
    cos_off, sin_off = turn_ref[0], turn_ref[1]
    lane = lax.broadcasted_iota(jnp.int32, (SLAB, SLAB), 1)
    sign = jnp.where(lane < 32, -1.0, jnp.where(lane < 64, 1.0, 0.0))
    return cos_base * cos_off - sin_base * sin_off, (sin_base * cos_off + cos_base * sin_off) * sign


def turned(field, cosine, sine):
    lane = lax.broadcasted_iota(jnp.int32, (SLAB, SLAB), 1)
    return field * cosine + jnp.where(lane < 32, pltpu.roll(field, 96, 1), pltpu.roll(field, 32, 1)) * sine


def half_rows(values, k):
    return values[k * SLAB : (k + 1) * SLAB]


def direct_gather(links, place, buf, first, second):
    ring_x, ring_y = place.ring("x"), place.ring("y")
    a, b = pl.ds(*first), pl.ds(*second)

    def spread(ring, view, size):
        return links.group([(view, view, ring.device(k)) for k in (ring.next, ring.prev, ring.far)], size)

    over_x = spread(ring_x, buf.at[place.y, place.x, :, a], buf.at[0, pl.ds(0, 3), :, a])
    over_y = spread(ring_y, buf.at[place.y, place.x, :, b], buf.at[0, pl.ds(0, 3), :, b])
    yield
    over_x()
    over_x = spread(ring_y, buf.at[place.y, :, :, a], buf.at[pl.ds(0, 3), :, :, a])
    over_y()
    over_y = spread(ring_x, buf.at[:, place.x, :, b], buf.at[pl.ds(0, 3), :, :, b])
    yield
    over_x()
    over_y()


def turned_view(buf, flip):
    def view(along, over):
        first, second = (over, along) if flip else (along, over)
        return buf.at[first, second, pl.ds(2 if flip else 0, 2)]

    return view


def slab_gather_half(links, along, over, view):
    three, four = pl.ds(1, 3), pl.ds(0, 4)
    own = view(0, 0)
    over_arrived = links.group(
        [
            (own, view(0, 3), over.device(over.next)),
            (own, view(0, 1), over.device(over.prev)),
            (own, view(0, 2), over.device(over.far)),
        ],
        view(0, three),
    )
    up, down = along.device(along.next), along.device(along.prev)
    lines = [links.recv_slot(), links.recv_slot()]
    links.group([(own, view(3, 0), up), (own, view(1, 0), down)], view(0, pl.ds(0, 2)), lines)
    yield
    over_arrived()
    rest = view(0, three)
    links.group([(rest, view(3, three), up), (rest, view(1, three), down)], view(pl.ds(0, 2), three), lines)
    yield
    low, high = pl.ds(0, 2), pl.ds(2, 2)
    links.arrived(view(3, four), lines[0])
    far = [links.recv_slot()] * 2
    send = links.send_slot()
    links.start(view(3, low), view(2, low), up, send, far[0])
    links.arrived(view(1, four), lines[1])
    links.start(view(1, high), view(2, high), down, send, far[1])
    links.sent.append(lambda: links.arrived(view(0, four), send))
    yield
    links.arrived(view(2, four), far[0])


def slab_gather(links, place, buf):
    ring_x, ring_y = place.ring("x"), place.ring("y")
    return (
        slab_gather_half(links, ring_y, ring_x, turned_view(buf, False)),
        slab_gather_half(links, ring_x, ring_y, turned_view(buf, True)),
    )


def slab_scatter_room():
    many, line = pltpu.VMEM((2, 2, SLAB, SLAB), BF16), pltpu.VMEM((4, 2, SLAB, SLAB), BF16)
    return ([many] * 2 + [line] * 3 + [pltpu.VMEM((3, 2, SLAB, SLAB), BF16)]) * 2


def slab_scatter_half(links, along, over, view, room, target):
    low, high, prev, nxt, lined, lasts = room
    lo, hi, four = pl.ds(0, 2), pl.ds(2, 2), pl.ds(0, 4)
    up, down = along.device(along.next), along.device(along.prev)
    slots = [links.recv_slot() for _ in range(4)]
    links.group(
        [
            (view(2, lo), low, up),
            (view(2, hi), high, down),
            (view(1, hi), prev.at[hi], up),
            (view(3, lo), nxt.at[lo], down),
        ],
        view(lo, four),
        slots,
    )
    yield
    links.arrived(low, slots[0])
    add_into(view(1, lo), [view(1, lo), low], BF16)
    send = links.send_slot()
    links.start(view(1, lo), prev.at[lo], up, send, slots[2])
    links.arrived(high, slots[1])
    add_into(view(3, hi), [view(3, hi), high], BF16)
    links.start(view(3, hi), nxt.at[hi], down, send, slots[3])
    links.sent.append(lambda: links.arrived(view(0, four), send))
    yield
    links.arrived(prev, slots[2])
    links.arrived(nxt, slots[3])
    add_into(lined, [view(0, four), prev, nxt], BF16)
    arrived = links.group(
        [
            (lined.at[1], lasts.at[0], over.device(over.next)),
            (lined.at[3], lasts.at[1], over.device(over.prev)),
            (lined.at[2], lasts.at[2], over.device(over.far)),
        ],
        lasts,
    )
    yield
    arrived()
    add_into(target, [lined.at[0], lasts.at[0], lasts.at[1], lasts.at[2]], F32)


def slab_scatter(links, place, buf, rooms, target):
    ring_x, ring_y = place.ring("x"), place.ring("y")
    return (
        slab_scatter_half(links, ring_y, ring_x, turned_view(buf, False), rooms[:6], target.at[pl.ds(0, 2)]),
        slab_scatter_half(links, ring_x, ring_y, turned_view(buf, True), rooms[6:], target.at[pl.ds(2, 2)]),
    )


def slab_place(at):
    return lax.div(at, 16), lax.rem(lax.div(at, 4), 4), lax.rem(at, 4)


def keys_of(kv_ref, table, s, first, count):
    places = [slab_place(jnp.clip(table[s * 24 + first + k, 0], 0, 63)) for k in range(count)]
    return jnp.concatenate([kv_ref[y, x, z] for y, x, z in places], 0)


def query_positions(table, s, shape, axis):
    return table[s * 24 + 20, 0] + lax.broadcasted_iota(jnp.int32, shape, axis)


def attend_head(j, table, q_ref, kv_ref, top_ref, sum_ref, acc_ref, between):
    def fold(s, first, count, first_key):
        keys = keys_of(kv_ref, table, s, first, count)
        width = count * SLAB
        pos_q = query_positions(table, s, (1, SLAB), 1)
        pos_k = first_key + lax.broadcasted_iota(jnp.int32, (width, 1), 0)
        scores = dot_right_t(keys, q_ref[s, :, pl.ds(j * 128, 128)])
        scores = jnp.where(pos_k <= pos_q, scores, LOW)
        top, total = top_ref[s][0:1], sum_ref[s][0:1]
        new_top = jnp.maximum(top, jnp.max(scores, axis=0, keepdims=True))
        weights = jnp.exp(scores - new_top)
        decay = jnp.exp(top - new_top)
        total = total * decay + jnp.sum(weights, axis=0, keepdims=True)
        sums = lax.dot_general(keys, weights.astype(BF16), (((0,), (0,)), ((), ())), preferred_element_type=F32)
        acc_ref[s] = acc_ref[s] * decay + sums
        top_ref[s] = jnp.broadcast_to(new_top, (8, SLAB))
        sum_ref[s] = jnp.broadcast_to(total, (8, SLAB))

    for s in range(4):
        top_ref[s] = jnp.full((8, SLAB), LOW, F32)
        sum_ref[s] = jnp.zeros((8, SLAB), F32)
        acc_ref[s] = jnp.zeros((SLAB, SLAB), F32)

    def prompt(c, carry):
        for s in range(4):
            fold(s, c * 4, 4, c * 512)
        return carry

    lax.fori_loop(0, 2, prompt, 0)
    between(0)
    lax.fori_loop(2, 4, prompt, 0)
    between(1)
    for s in range(4):
        fold(s, 16, 2, 2048)


def attend_back_head(j, table, q_ref, kv_ref, grad_ref, logs, deltas, dq_ref, terms_ref, pair_ref, between):
    lane = lax.broadcasted_iota(jnp.int32, (SLAB, SLAB), 1)
    for s in range(4):
        grads = grad_ref[s, :, pl.ds(128 * (j // 2), 128)].astype(F32)
        if j != 1:
            grads = pltpu.roll(grads, 64, 1)
        pair_ref[s, pl.ds(0, SLAB)] = q_ref[s, :, pl.ds(j * 128, 128)]
        pair_ref[s, pl.ds(SLAB, SLAB)] = jnp.where(lane < 64, 0.0, grads).astype(BF16)
        dq_ref[s] = jnp.zeros((SLAB, SLAB), F32)

    def fold(s, first, count, first_key):
        keys = keys_of(kv_ref, table, s, first, count)
        width = count * SLAB
        pos_q = query_positions(table, s, (1, SLAB), 1)
        pos_k = first_key + lax.broadcasted_iota(jnp.int32, (width, 1), 0)
        pair = pair_ref[s]
        both = dot_right_t(keys, pair)
        weights = jnp.where(pos_k <= pos_q, jnp.exp(both[:, :SLAB] - logs[s]), 0.0)
        slopes = (weights * (both[:, SLAB:] - deltas[s])).astype(BF16)
        terms = dot(jnp.concatenate([slopes, weights.astype(BF16)], 1), pair)
        terms_ref[s, pl.ds(first, count)] = terms.astype(BF16).reshape(count, SLAB, SLAB)
        dq_ref[s] += lax.dot_general(slopes, keys, (((0,), (0,)), ((), ())), preferred_element_type=F32)

    def prompt(c, carry):
        for s in range(4):
            fold(s, c * 4, 4, c * 512)
        return carry

    lax.fori_loop(0, 2, prompt, 0)
    between(0)
    lax.fori_loop(2, 4, prompt, 0)
    between(1)
    for s in range(4):
        fold(s, 16, 2, 2048)
    between(2)


def sum_terms(place, table, terms_ref, part_ref):
    def block(t, carry):
        dy, dx = lax.div(t, 4), lax.rem(t, 4)
        at = lax.rem(dy + place.y, 4) * 16 + lax.rem(dx + place.x, 4) * 4
        for dz in range(4):
            places = [jnp.clip(table[96 + s, at + dz], 0, 18) for s in range(4)]
            total = terms_ref[0, places[0]].astype(F32)
            for s in range(1, 4):
                total = total + terms_ref[s, places[s]].astype(F32)
            part_ref[dy, dx, dz] = total.astype(BF16)
        return carry

    lax.fori_loop(0, 16, block, 0)


def lookups(total, place, meta_ref):
    seg, base = total[2:3], total[3:4]
    lane = lax.broadcasted_iota(jnp.int32, (1, SLAB), 1)
    from_here = lax.rem(lax.div(lane, 16) + 4 - place.y, 4) * 16 + lax.rem(lax.rem(lax.div(lane, 4), 4) + 4 - place.x, 4) * 4
    lane_at = (from_here + lax.rem(lane, 4)).astype(F32)
    own = place.y * 4 + place.x
    n = lax.broadcasted_iota(jnp.int32, (24, 1), 0)
    back_rows = jnp.zeros((8, SLAB), F32)
    back_row = lax.broadcasted_iota(jnp.int32, (8, 1), 0)
    for s in range(4):
        mine = lane == own * 4 + s
        seg_q = jnp.sum(jnp.where(mine, seg, 0.0), axis=1, keepdims=True)
        base_q = jnp.sum(jnp.where(mine, base, 0.0), axis=1, keepdims=True)
        prompt = jnp.where(seg_q >= CONTS + 1.0, CONTS + 1.0, 0.0)
        want = jnp.where(n < 16, prompt, seg_q)
        hit = (seg == want) & (base == n.astype(F32) * SLAB) & (lane < 64)
        places = jnp.max(jnp.where(hit, lane_at, 0.0), axis=1, keepdims=True)
        listed = jnp.where(n == 20, base_q, places)
        meta_ref[pl.ds(s * 24, 24), :] = jnp.broadcast_to(listed, (24, SLAB)).astype(jnp.int32)
        visible = (seg == prompt) | (seg == seg_q)
        places = jnp.where(visible, jnp.minimum(base * (1.0 / SLAB), 17.0), 18.0)
        back_rows = jnp.where(back_row == s, places, back_rows)
    meta_ref[pl.ds(96, 8), :] = back_rows.astype(jnp.int32)


def column_of(gain_ref):
    i = lax.broadcasted_iota(jnp.int32, (12, 12), 0)
    k = lax.broadcasted_iota(jnp.int32, (12, 12), 1)
    return jnp.sum(jnp.where(i == k, gain_ref[...].astype(F32), 0.0), axis=1, keepdims=True)


def plane_columns(z):
    return [((z % 2) * 32 + p * 2 + z // 2) * 48 for p in range(16)]


def own_slab(place, at, seg_ref, pos_ref, base_ref):
    lane = lax.broadcasted_iota(jnp.int32, (1, SLAB), 1)
    high = place.head == 1
    seg = jnp.where(high, seg_ref[1:2], seg_ref[0:1]).astype(F32)
    base = (jnp.where(high, pos_ref[1:2], pos_ref[0:1]) - lane).astype(F32)
    m = lax.broadcasted_iota(jnp.int32, (24, SLAB), 0).astype(F32)
    cosine, sine = [
        jnp.sum(jnp.where(m == base * (1.0 / SLAB), base_ref[k], 0.0), axis=0, keepdims=True) for k in range(2)
    ]
    row = lax.broadcasted_iota(jnp.int32, (8, SLAB), 0)
    here = (lane == at) & (row >= 2)
    facts = jnp.where(here, jnp.where(row == 2, seg, jnp.where(row == 3, base, 0.0)), 0.0)
    return jnp.where(row == 0, cosine, jnp.where(row == 1, sine, facts))


def finish_kernel(
    ff_ref, qkv_ref, og_ref, wq_ref, wk_ref, wv_ref, gate_ref, up_ref, gain1_ref, gain2_ref, out_in, grad_in, down_in,
    out_ref, grad_ref, dgain1_ref, dq_ref, dk_ref, dv_ref, do_ref, dgain2_ref, dgate_ref, dup_ref, down_ref,
):
    out_ref[...] = out_in[...]
    grad_ref[...] = grad_in[...]
    down_ref[...] = down_in[...]
    i = lax.broadcasted_iota(jnp.int32, (12, 12), 0)
    k = lax.broadcasted_iota(jnp.int32, (12, 12), 1)

    def row_of(column):
        return jnp.sum(jnp.where(i == k, column, 0.0), axis=0, keepdims=True)

    gain = column_of(gain1_ref)
    grads = [qkv_ref[z].astype(F32)[:12] for z in range(4)]
    total = jnp.zeros((12, 1), F32)
    for c, w_ref, to_ref in ((384, wq_ref, dq_ref), (0, wk_ref, dk_ref), (64, wv_ref, dv_ref)):
        step = 64 if c == 384 else 128
        grad = jnp.concatenate([grads[z][:, step * j + c : step * j + c + HD] for z in range(4) for j in range(3)], 1)
        total = total + jnp.sum(grad * w_ref[...].astype(F32), axis=1, keepdims=True)
        to_ref[...] = grad * gain
    dgain1_ref[...] = row_of(total)
    do_ref[...] = og_ref[0, pl.ds(0, 12)]

    gain = column_of(gain2_ref)
    total = jnp.zeros((12, 1), F32)
    for k_at, w_ref, to_ref in ((0, gate_ref, dgate_ref), (768, up_ref, dup_ref)):
        pieces = {}
        for z in range(4):
            grad = ff_ref[z, :, pl.ds(k_at, 768)].astype(F32)[:12]
            for p, c in enumerate(plane_columns(z)):
                pieces[c] = grad[:, 48 * p : 48 * p + 48]
        grad = jnp.concatenate([pieces[c] for c in sorted(pieces)], 1)
        total = total + jnp.sum(grad * w_ref[...].astype(F32), axis=1, keepdims=True)
        to_ref[...] = grad * gain
    dgain2_ref[...] = row_of(total)


def layer_kernel(
    tok_ref, cot_hbm, wq_ref, wk_ref, wv_ref, wo_ref, gate_ref, up_ref, down_hbm, gain1_ref, gain2_ref, seg_ref, pos_ref,
    perm_hbm, turn_hbm, base_ref, perm_att_hbm, out_perm_hbm,
    out_ref, in_ref, down_sum_ref, got_ff_ref, got_ref, got_out_ref,
    perm_ref, turn_ref, cot_ref, down_ref, perm_att, out_perm, const_sem, line_ref, descs, meta_ref, table, table_sem,
    for_line, for_line_ff, rows, rows_o, rows_ff, one, cots, wqkv, wo, wff, q_ref, kv0, kv1, kv2,
    tops, sums, accs, heads, att_ref, lse_ref, atts, wo_heads, mid_s, gm_s, two, act, pre, turn_t, part, part_out, sum_z, sum_out,
    to_heads, grads_ref, terms, pairs, kv_own, d_s, qkv_sum, ff_sum,
    og_part, og_sum, og_next, *rest,
):
    send, recv = rest[-2:]
    rooms = list(rest[:-2])

    def take(count):
        out = rooms[:count]
        del rooms[:count]
        return out

    back_room, ff_room, out_room = take(6), take(26), take(6)
    kv_rooms = [take(12) for _ in range(3)]
    qkv_rooms = [take(6) for _ in range(2)]
    in_room, og_line_room, og_room = take(6), take(6), take(6)
    kvs = (kv0, kv1, kv2)

    pairs_in = (
        (perm_hbm, perm_ref), (turn_hbm, turn_ref), (cot_hbm, cot_ref),
        (down_hbm, down_ref), (perm_att_hbm, perm_att), (out_perm_hbm, out_perm),
    )
    loads = [pltpu.make_async_copy(source, target, const_sem.at[n]) for n, (source, target) in enumerate(pairs_in)]
    for load in loads:
        load.start()
    place = Place()
    partners = announce(place)
    links = Links(send, recv)
    own = place.y * 4 + place.x

    line_ref[place.z] = own_slab(place, own * 4 + place.z, seg_ref, pos_ref, base_ref)
    lined = small_gather(links, place.ring("z"), lambda k: line_ref.at[k], line_ref.at[pl.ds(0, 3)])
    gain = column_of(gain1_ref)
    w_q, w_k, w_v = [ref[...].astype(F32) * gain for ref in (wq_ref, wk_ref, wv_ref)]
    none, blank = jnp.zeros((12, HD), F32), jnp.zeros((4, 768), F32)
    for z in range(4):
        pieces, last = [], []
        for j in range(3):
            at = slice(192 * z + 64 * j, 192 * z + 64 * j + 64)
            pieces += [w_k[:, at], w_v[:, at]]
            last.append(w_q[:, at])
        pieces += [*last, none]
        for_line[z] = jnp.concatenate([jnp.concatenate(pieces, 1), blank[:, :640]], 0).astype(BF16)
    loads[0].wait()
    x = dot(tok_ref[...], perm_ref[...])
    one[place.z] = (x * lax.rsqrt(mean_square(x) + EPS)).astype(BF16)
    enter(partners)
    swap = line_swap(links, place, for_line, rows)
    advance(swap, lined)
    rows_o[place.z] = jnp.concatenate([wo_ref[...].astype(F32), blank], 0).astype(BF16)
    o_line = small_gather(links, place.ring("z"), lambda k: rows_o.at[k], rows_o.at[pl.ds(0, 3)])
    advance(o_line)
    ones = line_gather(links, place, one)
    finish(swap)
    advance(ones)
    wqkv[place.y, place.x] = dot(pack_rows(), rows[...].reshape(64, 640)).astype(BF16)
    kv_gather = direct_gather(links, place, wqkv, (0, 256), (256, 128))
    q_gather = shared_gather(links, place, wqkv, 384, 256)
    advance(kv_gather)
    finish(lined, o_line)
    wo[place.y, place.x] = dot(pack_rows(), rows_o[...].reshape(64, 768)).astype(BF16)
    o_gather = shared_gather(links, place, wo, 0, 768)
    descs[place.y, place.x] = line_ref[0] + line_ref[1] + line_ref[2] + line_ref[3]
    desc_x = small_gather(links, place.ring("x"), lambda k: descs.at[place.y, k], descs.at[0, pl.ds(0, 3)])
    desc_y = small_gather(links, place.ring("y"), lambda k: descs.at[k], descs.at[pl.ds(0, 3)])
    advance(desc_x)
    for load in loads[1:]:
        load.wait()
    gain = column_of(gain2_ref)
    for k, ref in enumerate((gate_ref, up_ref)):
        w = ref[...].astype(F32) * gain
        for z in range(4):
            pieces = [w[:, c : c + 48] for c in plane_columns(z)]
            for_line_ff[z, :, pl.ds(768 * k, 768)] = jnp.concatenate([jnp.concatenate(pieces, 1), blank], 0).astype(BF16)
    advance(q_gather)
    advance(o_gather)
    advance(kv_gather)
    finish(desc_x)
    advance(desc_y)
    advance(ones)
    advance(q_gather)
    advance(o_gather)
    ff_swap = line_swap(links, place, for_line_ff, rows_ff)
    cots[place.z] = cot_ref[...]
    cot_gather = line_gather(links, place, cots)
    finish(desc_y)
    total = jnp.zeros((8, SLAB), F32)
    for y in range(4):
        for k in range(4):
            total = total + descs[y, k]
    lookups(total, place, meta_ref)
    table_copy = pltpu.make_async_copy(meta_ref, table, table_sem)
    table_copy.start()
    finish(ones, kv_gather)
    advance(q_gather)
    advance(o_gather)

    lines = one[...].reshape(512, 768)
    gathers = [slab_gather(links, place, kv) for kv in kvs]
    for j in range(3):
        field = dot(lines, wqkv[:, :, :, pl.ds(128 * j, 128)].reshape(768, 128))
        for s in range(4):
            cosine, sine = slab_turns(line_ref, turn_ref, s)
            kvs[j][0, 0, s] = turned(half_rows(field, s), cosine, sine).astype(BF16)
        if j < 2:
            advance(*gathers[j])
    advance(ff_swap, cot_gather)
    advance(q_gather)
    advance(*gathers[0])
    advance(*gathers[2])
    advance(q_gather)
    advance(*gathers[1])
    advance(o_gather)
    advance(*gathers[0])
    finish(q_gather)
    field = dot(lines, wqkv[:, :, :, pl.ds(384, 256)].reshape(768, 256))
    lane = lax.broadcasted_iota(jnp.int32, (SLAB, SLAB), 1)
    for s in range(4):
        cosine, sine = slab_turns(line_ref, turn_ref, s)
        first, last = half_rows(field[:, 0:128], s), half_rows(field[:, 128:256], s)
        for j, query in enumerate((first, pltpu.roll(first, 64, 1), last)):
            query = turned(jnp.where(lane < 64, query * 0.125, 0.0), cosine, sine)
            q_ref[s, :, pl.ds(128 * j, 128)] = query.astype(BF16)
    advance(*gathers[2])
    finish(ff_swap)
    for c in range(0, 1536, 768):
        wff[place.y, place.x, :, pl.ds(c, 768)] = dot(
            pack_rows(), rows_ff[:, :, pl.ds(c, 768)].reshape(64, 768)
        ).astype(BF16)
    wff[place.y, place.x, :, pl.ds(1536, 768)] = down_ref[...]
    table_copy.wait()
    advance(cot_gather)
    advance(*gathers[1])

    lane = lax.broadcasted_iota(jnp.int32, (SLAB, SLAB), 1)
    for s in range(4):
        heads[s, pl.ds(192, 64), :] = jnp.zeros((64, SLAB), F32)
    w_gather = shared_gather(links, place, wff, 0, 2304)
    for j in range(3):
        finish(*gathers[j])

        def between(k, j=j):
            if j == 0 and k == 0:
                links.finish(8)
            if j == 0 and k == 1:
                advance(*gathers[2])
                advance(o_gather)
            if j == 1 and k == 0:
                finish(cot_gather)
                links.finish(8)
            if j == 1 and k == 1:
                advance(o_gather)

        if j == 2:
            advance(w_gather)
        attend_head(j, table, q_ref, kvs[j], tops, sums, accs, between)
        for s in range(4):
            heads[s, pl.ds(64 * j, 64), :] = accs[s, pl.ds(64, 64), :] / sums[s][0:1]
            lse_ref[j, s] = tops[s] + jnp.log(sums[s])
    for s in range(4):
        att_ref[s, :, 0:128] = heads[s, pl.ds(0, 128), :].T.astype(BF16)
        att_ref[s, :, 128:256] = heads[s, pl.ds(128, 128), :].T.astype(BF16)
    att_swap = line_swap(links, place, att_ref, atts)
    advance(att_swap)
    advance(w_gather)
    links.finish(20)
    finish(o_gather)
    for z in range(4):
        wo_heads[z] = dot(perm_att[pl.ds(256 * z, 256), :], merged(wo)).astype(BF16)
    finish(att_swap)
    advance(w_gather)

    middle = tok_ref[...].astype(F32)
    for z in range(4):
        middle = middle + dot(atts[z], wo_heads[z])
    mid_s[...] = middle
    middle = mid_s[...]
    scale_two = lax.rsqrt(mean_square(middle) + EPS)
    two[place.z] = dot((middle * scale_two).astype(BF16), perm_ref[...]).astype(BF16)
    two_gather = line_gather(links, place, two)
    advance(two_gather)
    advance(w_gather)
    att = dot(atts[0], out_perm[pl.ds(0, 256), :])
    for z in range(1, 4):
        att = att + dot(atts[z], out_perm[pl.ds(256 * z, 256), :])
    att_by_z = att.astype(BF16).T
    advance(two_gather)
    together([w_gather, two_gather])

    def block():
        two_b = two[...].reshape(512, 768)
        cot_b = cots[...].reshape(512, 768)
        gate_w = wff[:, :, :, pl.ds(0, 768)].reshape(768, 768)
        up_w = wff[:, :, :, pl.ds(768, 768)].reshape(768, 768)
        down_w = wff[:, :, :, pl.ds(1536, 768)].reshape(768, 768)
        gate = dot(two_b, gate_w)
        up = dot(two_b, up_w)
        sig = 1.0 / (1.0 + jnp.exp(-gate))
        silu = gate * sig
        act_b = (silu * up).astype(BF16)
        act[...] = act_b
        grad_act = dot_right_t(cot_b, down_w)
        grad_gate = (grad_act * up * (sig * (1.0 + gate * (1.0 - sig)))).astype(BF16)
        grad_up = (grad_act * silu).astype(BF16)
        pre[:, pl.ds(0, 768)] = grad_gate
        pre[:, pl.ds(768, 768)] = grad_up
        back = dot_right_t(grad_gate, gate_w) + dot_right_t(grad_up, up_w)
        part[...] = back.astype(BF16).reshape(4, SLAB, 768)

    def out_block(r, carry):
        at = pl.ds(pl.multiple_of(r * 256, 256), 256)
        down_w = wff[:, :, :, pl.ds(1536, 768)].reshape(768, 768)
        part_out[pl.ds(r * 2, 2)] = dot(act[at, :], down_w).astype(BF16).reshape(2, SLAB, 768)
        return carry

    block()
    links.finish()
    back_sum = line_scatter(links, place, part, back_room, sum_z)
    advance(back_sum)
    lax.fori_loop(0, 2, out_block, 0)
    turn_t[...] = two[...].reshape(512, 768).T

    def first_grads(c, carry):
        at = pl.ds(pl.multiple_of(c * 256, 256), 256)
        wff[:, :, :, at] = dot(turn_t[...], pre[:, at]).astype(BF16).reshape(4, 4, 48, 256)
        return carry

    def last_grads(c, carry):
        at = pl.ds(pl.multiple_of(c * 256, 256), 256)
        to = pl.ds(pl.multiple_of(1536 + c * 256, 256), 256)
        cot_all = cots[:, :, at].reshape(512, 256)
        wff[:, :, :, to] = dot(turn_t[...], cot_all).astype(BF16).reshape(4, 4, 48, 256)
        return carry

    lax.fori_loop(0, 6, first_grads, 0)
    advance(back_sum)
    turn_t[...] = act[...].T
    lax.fori_loop(0, 3, last_grads, 0)
    ff = plane_scatter(links, place, wff, ff_room, ff_sum, False)
    advance(*ff)
    finish(back_sum)
    links.finish(6)

    grad = dot_right_t(sum_z[0].astype(BF16), perm_ref[...])
    middle = mid_s[...]
    scale_two = lax.rsqrt(mean_square(middle) + EPS)
    gm_s[...] = cot_ref[...].astype(F32) + norm_back(grad, middle * scale_two, scale_two)
    low = gm_s[...].astype(BF16)
    for z in range(4):
        to_heads[z] = dot_right_t(low, wo_heads[z]).astype(BF16)
    heads_swap = line_swap(links, place, to_heads, grads_ref)
    advance(heads_swap)
    out_sum = line_scatter(links, place, part_out, out_room, sum_out)
    advance(out_sum)
    turn_t[...] = one[...].reshape(512, 768).T
    og_part[...] = dot(att_by_z, low).astype(BF16).reshape(4, 256, 768)
    for s in range(4):
        terms[s, 18] = jnp.zeros((SLAB, SLAB), BF16)
    finish(heads_swap)

    which = lax.broadcasted_iota(jnp.int32, (8, SLAB), 0)
    at_lane = lax.broadcasted_iota(jnp.int32, (8, 256), 1)
    pick = (lax.div(at_lane, HD) == lax.broadcasted_iota(jnp.int32, (8, 256), 0)).astype(F32)
    logs, deltas = [], []
    for s in range(4):
        inner = grads_ref[s].astype(F32) * att_ref[s].astype(F32)
        delta = lax.dot_general(pick, inner, LANES, precision=HIGHEST, preferred_element_type=F32)
        logs.append([lse_ref[j, s][0:1] for j in range(3)])
        deltas.append([jnp.sum(jnp.where(which == k, delta, 0.0), axis=0, keepdims=True) for k in range(3)])

    scatters = []

    def keys_turn(j):
        for s in range(4):
            cosine, sine = slab_turns(line_ref, turn_ref, s)
            d_s[pl.ds(s * SLAB, SLAB), pl.ds(128 * j, 128)] = turned(kv_own[j, s], cosine, -sine).astype(BF16)

    def qkv_grads(columns, first, second, room):
        for c in columns:
            wo[:, :, :, pl.ds(c, 128)] = dot(turn_t[...], d_s[:, pl.ds(c, 128)]).astype(BF16).reshape(4, 4, 48, 128)
        return small_scatter(links, place, wo, first, second, room, qkv_sum)

    og_line = line_scatter(links, place, og_part, og_line_room, og_sum)
    spread = spread_rows()
    for j in range(3):

        def between(k, j=j):
            if j == 0 and k == 0:
                advance(*ff)
                advance(out_sum)
            if j == 1 and k == 0:
                advance(*ff)
                links.finish(8)
            if j == 1 and k == 2:
                advance(*scatters[0])
            if j == 2 and k == 0:
                advance(*ff)
                links.finish(4)
            if j == 2 and k == 1:
                advance(*scatters[0])
            if j == 2 and k == 2:
                advance(*scatters[1])

        attend_back_head(
            j, table, q_ref, kvs[j], grads_ref, [v[j] for v in logs], [v[j] for v in deltas], accs, terms, pairs, between
        )
        sum_terms(place, table, terms, kvs[j])
        scatters.append(slab_scatter(links, place, kvs[j], kv_rooms[j], kv_own.at[j]))
        advance(*scatters[j])
        for s in range(4):
            cosine, sine = slab_turns(line_ref, turn_ref, s)
            grad = turned(jnp.where(lane < 64, accs[s] * 0.125, 0.0), cosine, -sine)
            to = (pl.ds(s * SLAB, SLAB), pl.ds(384 + 128 * (j // 2), 128))
            if j == 1:
                grad = jnp.where(lane < 64, d_s[to].astype(F32), pltpu.roll(grad, 64, 1))
            d_s[to] = grad.astype(BF16)
        if j == 0:
            finish(out_sum)
            advance(og_line)
            out_ref[...] = (mid_s[...] + sum_out[0]).astype(BF16)
        if j == 1:
            advance(og_line)

    finish(*scatters[0])
    finish(*ff)
    down_sum_ref[...] = ff_sum[0, :, pl.ds(1536, 768)]
    for c in range(0, 1536, 768):
        for_line_ff[:, :, pl.ds(c, 768)] = (
            dot(spread, ff_sum[0, :, pl.ds(c, 768)].astype(BF16)).astype(BF16).reshape(4, 16, 768)
        )
    finish(og_line)
    grads_swap = line_swap(links, place, for_line_ff, got_ff_ref)
    advance(grads_swap)
    keys_turn(0)
    og_next[...] = og_sum[0].astype(BF16).reshape(4, 4, 16, 768)
    links.finish(12)
    advance(*scatters[1])
    advance(*scatters[2])
    finish(*scatters[1])
    keys_turn(1)
    advance(*scatters[2])
    qkv = qkv_grads((0, 128, 384), (0, 256), (384, 128), qkv_rooms[0])
    og = small_scatter(links, place, og_next, (0, 384), (384, 384), og_room, got_out_ref)
    links.finish(12)
    finish(*scatters[2])
    advance(*qkv)
    keys_turn(2)

    def last_block(r, carry):
        at = pl.ds(pl.multiple_of(r * 256, 256), 256)
        part[pl.ds(r * 2, 2)] = dot_right_t(d_s[at, :], merged(wqkv)).astype(BF16).reshape(2, SLAB, 768)
        return carry

    lax.fori_loop(0, 2, last_block, 0)
    in_sum = line_scatter(links, place, part, in_room, sum_z)
    advance(in_sum)
    last_qkv = qkv_grads((256, 512), (256, 128), (512, 128), qkv_rooms[1])
    advance(*last_qkv)
    advance(*og)
    advance(*qkv)
    finish(grads_swap)
    advance(in_sum)
    advance(*last_qkv)
    advance(*og)
    finish(*qkv)
    links.finish(len(links.sent) - 4)
    finish(*last_qkv)
    for_line[...] = dot(spread, qkv_sum[0].astype(BF16)).astype(BF16).reshape(4, 16, 640)
    last = line_swap(links, place, for_line, got_ref)
    advance(last)
    finish(*og)
    finish(in_sum)
    grad = dot_right_t(sum_z[0].astype(BF16), perm_ref[...])
    x = tok_ref[...].astype(F32)
    scale = lax.rsqrt(mean_square(x) + EPS)
    in_ref[...] = gm_s[...] + norm_back(grad, x * scale, scale)
    links.finish()
    finish(last)


SENDS, RECVS = 188, 200
LINE = pltpu.VMEM((4, SLAB, 768), BF16)
KV = pltpu.VMEM((4, 4, 4, SLAB, SLAB), BF16)
OUTS = [
    ((SLAB, 768), BF16),
    ((SLAB, 768), F32),
    ((48, 768), F32),
    ((4, 16, 1536), BF16),
    ((4, 16, 640), BF16),
    ((1, 16, 768), F32),
]
ROOM = (
    [
        pltpu.VMEM((768, 768), BF16),
        pltpu.VMEM((2, SLAB, SLAB), F32),
        pltpu.VMEM((SLAB, 768), BF16),
        pltpu.VMEM((48, 768), BF16),
        pltpu.VMEM((1024, 768), BF16),
        pltpu.VMEM((1024, 1024), BF16),
        pltpu.SemaphoreType.DMA((6,)),
        pltpu.VMEM((4, 8, SLAB), F32),
        pltpu.VMEM((4, 4, 8, SLAB), F32),
        pltpu.VMEM((104, SLAB), jnp.int32),
        pltpu.SMEM((104, SLAB), jnp.int32),
        pltpu.SemaphoreType.DMA,
        pltpu.VMEM((4, 16, 640), BF16),
        pltpu.VMEM((4, 16, 1536), BF16),
        pltpu.VMEM((4, 16, 640), BF16),
        pltpu.VMEM((4, 16, 768), BF16),
        pltpu.VMEM((4, 16, 1536), BF16),
        LINE,
        LINE,
        pltpu.VMEM((4, 4, 48, 640), BF16),
        pltpu.VMEM((4, 4, 48, 768), BF16),
        pltpu.VMEM((4, 4, 48, 2304), BF16),
        pltpu.VMEM((4, SLAB, 384), BF16),
        KV,
        KV,
        KV,
        pltpu.VMEM((4, 8, SLAB), F32),
        pltpu.VMEM((4, 8, SLAB), F32),
        pltpu.VMEM((4, SLAB, SLAB), F32),
        pltpu.VMEM((4, 256, SLAB), F32),
        pltpu.VMEM((4, SLAB, 256), BF16),
        pltpu.VMEM((3, 4, 8, SLAB), F32),
        pltpu.VMEM((4, SLAB, 256), BF16),
        pltpu.VMEM((4, 256, 768), BF16),
        pltpu.VMEM((SLAB, 768), F32),
        pltpu.VMEM((SLAB, 768), F32),
        LINE,
        pltpu.VMEM((512, 768), BF16),
        pltpu.VMEM((512, 1536), BF16),
        pltpu.VMEM((768, 512), BF16),
        LINE,
        LINE,
        pltpu.VMEM((1, SLAB, 768), F32),
        pltpu.VMEM((1, SLAB, 768), F32),
        pltpu.VMEM((4, SLAB, 256), BF16),
        pltpu.VMEM((4, SLAB, 256), BF16),
        pltpu.VMEM((4, 19, SLAB, SLAB), BF16),
        pltpu.VMEM((4, 256, SLAB), BF16),
        pltpu.VMEM((3, 4, SLAB, SLAB), F32),
        pltpu.VMEM((512, 640), BF16),
        pltpu.VMEM((1, 48, 640), F32),
        pltpu.VMEM((1, 48, 2304), F32),
        pltpu.VMEM((4, 256, 768), BF16),
        pltpu.VMEM((1, 256, 768), F32),
        pltpu.VMEM((4, 4, 16, 768), BF16),
    ]
    + line_scatter_room(SLAB, 768)
    + plane_scatter_room(48, 2304, False)
    + line_scatter_room(SLAB, 768)
    + slab_scatter_room() * 3
    + small_scatter_room(48, 256, 128)
    + small_scatter_room(48, 128, 128)
    + line_scatter_room(SLAB, 768)
    + line_scatter_room(256, 768)
    + small_scatter_room(16, 384, 384)
)


def per_device(
    tokens, gain_one, w_query, w_key, w_value, w_out, gain_two, w_gate, w_up, w_down, cotangent, segment_ids, positions
):
    gains = (gain_one.reshape(1, 12), gain_two.reshape(1, 12))
    anywhere = pl.BlockSpec(memory_space=pl.ANY)
    output, input_grad, down_grad, got_ff, got_qkv, got_out = pl.pallas_call(
        layer_kernel,
        out_shape=tuple(jax.ShapeDtypeStruct(shape, kind) for shape, kind in OUTS),
        in_specs=[anywhere if k in (1, 8, 13, 14, 16, 17) else VMEM for k in range(18)],
        out_specs=tuple([VMEM] * len(OUTS)),
        scratch_shapes=ROOM
        + [pltpu.SemaphoreType.DMA((SENDS,)), pltpu.SemaphoreType.DMA((RECVS,))],
        compiler_params=pltpu.CompilerParams(collective_id=0, has_side_effects=True, vmem_limit_bytes=62 * MIB),
        name="layer",
    )(
        tokens, cotangent, w_query, w_key, w_value, w_out, w_gate, w_up, w_down, *gains,
        segment_ids.reshape(2, SLAB), positions.reshape(2, SLAB),
        jnp.asarray(TO_PERM, BF16), jnp.asarray(OFFSET_TURNS, F32), jnp.asarray(BASE_TURNS, F32),
        jnp.asarray(ATT_PERM, BF16), jnp.asarray(OUT_PERM, BF16),
    )
    small, square, wide = [jax.ShapeDtypeStruct((rows, columns), F32) for rows, columns in ((1, 12), (12, 768), (12, 3072))]
    output, input_grad, gain_one_grad, dq, dk, dv, do, gain_two_grad, dgate, dup, down_grad = pl.pallas_call(
        finish_kernel,
        out_shape=(*[jax.ShapeDtypeStruct(*OUTS[k]) for k in range(2)], small, square, square, square, square, small, wide, wide,
                   jax.ShapeDtypeStruct(*OUTS[2])),
        in_specs=[VMEM] * 13,
        out_specs=(VMEM,) * 11,
        name="finish",
    )(got_ff, got_qkv, got_out, w_query, w_key, w_value, w_gate, w_up, *gains, output, input_grad, down_grad)
    return (
        output, input_grad, gain_one_grad.reshape(12), dq, dk, dv, do, gain_two_grad.reshape(12), dgate, dup, down_grad
    )


def solution(mesh):
    rows = P(("grp", "blk", "head"), None)
    flat = P(("grp", "blk", "head"))
    weight = P(("blk", "head"), None)
    gain = P(("blk", "head"))
    ids = P(("grp", "blk"))
    in_specs = (rows, gain, weight, weight, weight, weight, gain, weight, weight, weight, rows, ids, ids)
    out_specs = (rows, rows, flat, rows, rows, rows, rows, flat, rows, rows, rows)
    return jax.shard_map(per_device, mesh=mesh, in_specs=in_specs, out_specs=out_specs, check_vma=False)
```

```python
import math

import jax
import jax.numpy as jnp
import numpy as np
from jax import lax
from jax.experimental import pallas as pl
from jax.experimental.pallas import tpu as pltpu
from jax.sharding import PartitionSpec as P

MESH = pl.DeviceIdType.MESH
F32 = jnp.float32
BF16 = jnp.bfloat16
HD = 64
CONTS = 8
SLAB = 128
LOW = -1e30
EPS = 1e-05
LANES = (((1,), (1,)), ((), ()))
HIGHEST = lax.Precision.HIGHEST
MIB = 1 << 20
VMEM = pl.BlockSpec(memory_space=pltpu.VMEM)
SMEM = pl.BlockSpec(memory_space=pltpu.SMEM)


def feature_order():
    place = np.arange(768)
    p, z, r = place // 48, place // 12 % 4, place % 12
    t = (z % 2) * 32 + p * 2 + z // 2
    return t * 12 + r


ORDER = feature_order()
TO_PERM = np.zeros((768, 768), np.float32)
TO_PERM[ORDER, np.arange(768)] = 1.0


ATT_PERM = np.pad(TO_PERM.reshape(4, 192, 768), ((0, 0), (0, 64), (0, 0))).reshape(1024, 768)
OUT_PERM = np.pad(ATT_PERM.reshape(1024, 16, 4, 12).transpose(0, 2, 1, 3), ((0, 0), (0, 0), (0, 0), (0, 4))).reshape(1024, 1024)
LANE_FREQUENCY = 10000.0 ** (-(np.arange(128) % 32) * 2.0 / HD) * (np.arange(128) < HD)
OFFSET_ANGLES = np.arange(SLAB)[:, None] * LANE_FREQUENCY[None]
BASE_ANGLES = SLAB * np.arange(24)[:, None] * LANE_FREQUENCY[None]
BASE_TURNS = np.stack([np.cos(BASE_ANGLES), np.sin(BASE_ANGLES)]).astype(np.float32)
OFFSET_TURNS = np.stack([np.cos(OFFSET_ANGLES), np.sin(OFFSET_ANGLES)]).astype(np.float32)


class Place:
    def __init__(self):
        self.core = lax.axis_index("grp")
        blk = lax.axis_index("blk")
        self.blk, self.head = blk, lax.axis_index("head")
        self.x = lax.rem(blk, 4)
        self.y = lax.rem(lax.div(blk, 4), 4)
        self.z = self.head * 2 + lax.div(blk, 16)

    def other_core(self):
        return (1 - self.core, self.blk, self.head)

    def device(self, x=None, y=None, z=None):
        x = self.x if x is None else x
        y = self.y if y is None else y
        z = self.z if z is None else z
        return (self.core, lax.rem(z, 2) * 16 + y * 4 + x, lax.div(z, 2))

    def ring(self, axis):
        return Ring(self, axis)


class Ring:
    def __init__(self, place, axis):
        self.place, self.axis = place, axis
        self.own = getattr(place, axis)
        self.next = lax.rem(self.own + 1, 4)
        self.prev = lax.rem(self.own + 3, 4)
        self.far = lax.rem(self.own + 2, 4)

    def device(self, index):
        return self.place.device(**{self.axis: index})


def announce(place):
    partners = [place.other_core()]
    for axis in ("x", "y", "z"):
        ring = place.ring(axis)
        partners += [ring.device(ring.next), ring.device(ring.prev), ring.device(ring.far)]
    barrier = pltpu.get_barrier_semaphore()
    for partner in partners:
        pl.semaphore_signal(barrier, inc=1, device_id=partner, device_id_type=MESH)
    return len(partners)


def enter(partners):
    pl.semaphore_wait(pltpu.get_barrier_semaphore(), partners)


class Links:
    def __init__(self, send, recv):
        self.send, self.recv, self.sends, self.recvs, self.sent = send, recv, 0, 0, []

    def send_slot(self):
        self.sends += 1
        return self.send.at[self.sends - 1]

    def recv_slot(self):
        self.recvs += 1
        return self.recv.at[self.recvs - 1]

    def start(self, source, target, device, send, recv):
        copy = pltpu.make_async_remote_copy(
            src_ref=source, dst_ref=target, send_sem=send, recv_sem=recv, device_id=device, device_id_type=MESH
        )
        copy.start()
        return copy

    def copy(self, source, target, device):
        copy = self.start(source, target, device, self.send_slot(), self.recv_slot())
        self.sent.append(copy.wait_send)
        return copy

    def group(self, copies, view, recv=None):
        send = self.send_slot()
        slots = [self.recv_slot()] * len(copies) if recv is None else recv
        for (source, target, device), slot in zip(copies, slots):
            self.start(source, target, device, send, slot)
        self.sent.append(lambda: self.arrived(view, send))
        return lambda: self.arrived(view, slots[0])

    def arrived(self, view, semaphore):
        pltpu.make_async_copy(view, view, semaphore).wait()

    def finish(self, count=None):
        count = len(self.sent) if count is None else count
        for wait in self.sent[:count]:
            wait()
        del self.sent[:count]


def together(steps):
    steps = list(steps)
    while steps:
        left = []
        for step in steps:
            try:
                next(step)
                left.append(step)
            except StopIteration:
                pass
        steps = left


def ring_gather(links, ring, slot):
    right = links.copy(slot(ring.own, None), slot(ring.own, None), ring.device(ring.next))
    left = links.copy(slot(ring.own, None), slot(ring.own, None), ring.device(ring.prev))
    yield
    right.wait_recv()
    on_right = links.copy(slot(ring.prev, 0), slot(ring.prev, 0), ring.device(ring.next))
    left.wait_recv()
    on_left = links.copy(slot(ring.next, 1), slot(ring.next, 1), ring.device(ring.prev))
    yield
    on_right.wait_recv()
    on_left.wait_recv()


def add_into(target, terms, kind):
    *lead, rows, columns = target.shape
    step = 16
    for size in (128, 64, 48, 32):
        if rows % size == 0 and size * columns <= 48 * 1024:
            step = size
            break
    count = rows // step

    def body(k, carry):
        at, rest = [], lax.div(k, count)
        for size in reversed(lead):
            at.insert(0, lax.rem(rest, size))
            rest = lax.div(rest, size)
        at = (*at, pl.ds(pl.multiple_of(lax.rem(k, count) * step, step), step), slice(None))
        total = terms[0][at].astype(kind)
        for term in terms[1:]:
            total = total + term[at].astype(kind)
        target[at] = total
        return carry

    trips = math.prod(lead) * count
    lax.fori_loop(0, trips, body, 0, unroll=2 if trips % 2 == 0 else 1)


def ring_scatter(links, ring, part, room, target, kind):
    low, high, sum_low, sum_high, from_prev, from_next = room
    nxt, prv = ring.device(ring.next), ring.device(ring.prev)
    far_low = links.copy(part(ring.far, 0), low, nxt)
    far_high = links.copy(part(ring.far, 1), high, prv)
    next_high = links.copy(part(ring.next, 1), from_prev(1), nxt)
    prev_low = links.copy(part(ring.prev, 0), from_next(0), prv)
    yield
    far_low.wait_recv()
    add_into(sum_low, [part(ring.next, 0), low], BF16)
    next_low = links.copy(sum_low, from_prev(0), nxt)
    far_high.wait_recv()
    add_into(sum_high, [part(ring.prev, 1), high], BF16)
    prev_high = links.copy(sum_high, from_next(1), prv)
    yield
    for copy in (next_high, prev_low, next_low, prev_high):
        copy.wait_recv()
    add_into(target, [part(ring.own, None), from_prev(None), from_next(None)], kind)


def lead_part(part):
    return pl.ds(0, 4) if part is None else pl.ds(2 * part, 2)


def row_part(rows, part):
    first = (rows // 2 + 15) // 16 * 16
    if part is None:
        return 0, rows
    return (0, first) if part == 0 else (first, rows - first)


def regions(rows, columns, by_rows):
    if by_rows:
        return [(0, rows // 2, 0, columns), (rows // 2, rows // 2, 0, columns)]
    return [(0, rows, 0, columns // 2), (0, rows, columns // 2, columns // 2)]


def plane_gather(links, place, buf, by_rows):
    rows, columns = buf.shape[2:]

    def half(region, x_first):
        r0, rn, c0, cn = region

        def one(k, part):
            off, size = row_part(rn, part)
            y, x = (place.y, k) if x_first else (k, place.x)
            return buf.at[y, x, pl.ds(r0 + off, size), pl.ds(c0, cn)]

        def line(k, part):
            y, x = (k, lead_part(part)) if x_first else (lead_part(part), k)
            return buf.at[y, x, pl.ds(r0, rn), pl.ds(c0, cn)]

        yield from ring_gather(links, place.ring("x" if x_first else "y"), one)
        yield from ring_gather(links, place.ring("y" if x_first else "x"), line)

    a, b = regions(rows, columns, by_rows)
    return half(a, True), half(b, False)


def plane_scatter_room(rows, columns, by_rows):
    rooms = []
    for _, rn, _, cn in regions(rows, columns, by_rows):
        rooms += [pltpu.VMEM((2, rn, cn), BF16)] * 4 + [pltpu.VMEM((4, rn, cn), BF16)] * 3
        low, high = row_part(rn, 0)[1], row_part(rn, 1)[1]
        rooms += [pltpu.VMEM((1, low, cn), BF16), pltpu.VMEM((1, high, cn), BF16)] * 2
        rooms += [pltpu.VMEM((1, rn, cn), BF16)] * 2
    return rooms


def plane_scatter(links, place, buf, rooms, target, by_rows):
    rows, columns = buf.shape[2:]

    def half(region, room, x_first):
        r0, rn, c0, cn = region
        low, high, sum_low, sum_high, prev, nxt, lined = room[:7]
        low1, high1, sum_low1, sum_high1, prev1, nxt1 = room[7:]

        def line(k, part):
            y, x = (lead_part(part), k) if x_first else (k, lead_part(part))
            return buf.at[y, x, pl.ds(r0, rn), pl.ds(c0, cn)]

        def one(k, part):
            off, size = row_part(rn, part)
            return lined.at[pl.ds(k, 1), pl.ds(off, size), :]

        def lined_part(ref):
            return lambda part: ref.at[lead_part(part)]

        def one_part(ref):
            def view(part):
                off, size = row_part(rn, part)
                return ref.at[:, pl.ds(off, size), :]

            return view

        room_a = (low, high, sum_low, sum_high, lined_part(prev), lined_part(nxt))
        room_b = (low1, high1, sum_low1, sum_high1, one_part(prev1), one_part(nxt1))
        yield from ring_scatter(links, place.ring("x" if x_first else "y"), line, room_a, lined, BF16)
        out = target.at[:, pl.ds(r0, rn), pl.ds(c0, cn)]
        yield from ring_scatter(links, place.ring("y" if x_first else "x"), one, room_b, out, F32)

    a, b = regions(rows, columns, by_rows)
    return half(a, rooms[:13], False), half(b, rooms[13:], True)


def small_scatter_room(rows, *sizes):
    rooms = []
    for size in sizes:
        rooms += [
            pltpu.VMEM((3, 4, rows, size), BF16),
            pltpu.VMEM((4, rows, size), BF16),
            pltpu.VMEM((3, 1, rows, size), BF16),
        ]
    return rooms


def direct_scatter(links, ring, part, room, target, kind):
    copies = [(part(to), room.at[k], ring.device(to)) for k, to in enumerate((ring.next, ring.prev, ring.far))]
    arrived = links.group(copies, room)
    yield
    arrived()
    add_into(target, [part(ring.own), room.at[0], room.at[1], room.at[2]], kind)


def small_scatter(links, place, buf, first, second, rooms, target):
    def half(region, room, x_first):
        columns = pl.ds(*region)
        firsts, lined, lasts = room

        def line(k):
            return buf.at[:, k, :, columns] if x_first else buf.at[k, :, :, columns]

        yield from direct_scatter(links, place.ring("x" if x_first else "y"), line, firsts, lined, BF16)
        out = target.at[:, :, columns]
        yield from direct_scatter(
            links, place.ring("y" if x_first else "x"), lambda k: lined.at[pl.ds(k, 1)], lasts, out, F32
        )

    return half(first, rooms[:3], False), half(second, rooms[3:], True)


def line_scatter_room(rows, columns):
    low, high = row_part(rows, 0)[1], row_part(rows, 1)[1]
    return [pltpu.VMEM((1, low, columns), BF16), pltpu.VMEM((1, high, columns), BF16)] * 2 + [
        pltpu.VMEM((1, rows, columns), BF16)
    ] * 2


def line_scatter(links, place, buf, room, target):
    rows = buf.shape[1]

    def part(k, half):
        off, size = row_part(rows, half)
        return buf.at[pl.ds(k, 1), pl.ds(off, size), :]

    def view(ref):
        def cut(half):
            off, size = row_part(rows, half)
            return ref.at[:, pl.ds(off, size), :]

        return cut

    low, high, sum_low, sum_high, prev, nxt = room
    yield from ring_scatter(
        links, place.ring("z"), part, (low, high, sum_low, sum_high, view(prev), view(nxt)), target, F32
    )


def line_gather(links, place, buf):
    rows = buf.shape[1]

    def slot(k, half):
        off, size = row_part(rows, half)
        return buf.at[k, pl.ds(off, size)]

    yield from ring_gather(links, place.ring("z"), slot)


def line_swap(links, place, source, target):
    ring = place.ring("z")
    copies = [(source.at[other], target.at[ring.own], ring.device(other)) for other in (ring.next, ring.prev, ring.far)]
    arrived = links.group(copies, target.at[pl.ds(0, 3)])
    target[ring.own] = source[ring.own]
    yield
    arrived()


def small_gather(links, ring, slot, three):
    own = slot(ring.own)
    arrived = links.group([(own, own, ring.device(k)) for k in (ring.next, ring.prev, ring.far)], three)
    yield
    arrived()


def shared_gather(links, place, buf, start, size):
    half = size // 2
    flip = place.core == 1
    columns = pl.ds(pl.multiple_of(start + place.core * half, 128), half)
    first, second = jnp.where(flip, place.y, place.x), jnp.where(flip, place.x, place.y)
    first_next, first_prev, first_far = [lax.rem(first + k, 4) for k in (1, 3, 2)]
    second_next, second_prev, second_far = [lax.rem(second + k, 4) for k in (1, 3, 2)]

    def block(s, f, part=None):
        y, x = jnp.where(flip, f, s), jnp.where(flip, s, f)
        rows = pl.ds(0, 48) if part is None else (pl.ds(0, 32) if part == 0 else pl.ds(32, 16))
        return buf.at[y, x, rows, columns]

    def device(s, f):
        return place.device(x=jnp.where(flip, s, f), y=jnp.where(flip, f, s))

    def send(s, f, to, part=None):
        return links.copy(block(s, f, part), block(s, f, part), to)

    handed = []

    def hands(view):
        pair = links.send_slot(), links.recv_slot()
        links.sent.append(lambda: links.arrived(view, pair[0]))
        handed.append(lambda: links.arrived(view, pair[1]))
        return lambda s, f: links.start(block(s, f), block(s, f), place.other_core(), *pair)

    on_right, on_left = device(second, first_next), device(second, first_prev)
    up, down = device(second_next, first), device(second_prev, first)
    order = (first, first_prev, first_next, first_far)
    ups, downs = [], []

    def line(k):
        ups.append(send(second, order[k], up))
        downs.append(send(second, order[k], down))

    right = send(second, first, on_right)
    left = send(second, first, on_left)
    line(0)
    yield
    right.wait_recv()
    far_low = send(second, first_prev, on_right, 0)
    line(1)
    left.wait_recv()
    far_high = send(second, first_next, on_left, 1)
    line(2)
    hand = hands(buf.at[0, pl.ds(0, 2), :, columns])
    hand(second, first_prev)
    hand(second, first_next)
    yield
    far_low.wait_recv()
    far_high.wait_recv()
    line(3)
    hands(buf.at[0, 0, :, columns])(second, first_far)
    yield
    far = []
    hand = hands(buf.at[pl.ds(0, 2), :, :, columns])
    for k in range(4):
        ups[k].wait_recv()
        if k < 2:
            far.append(send(second_prev, order[k], up))
        hand(second_prev, order[k])
        downs[k].wait_recv()
        if k >= 2:
            far.append(send(second_next, order[k], down))
        hand(second_next, order[k])
    yield
    hand = hands(buf.at[0, :, :, columns])
    for k in range(4):
        far[k].wait_recv()
        hand(second_far, order[k])
    yield
    for wait in handed:
        wait()


def advance(*steps):
    for step in steps:
        next(step, None)


def finish(*steps):
    together(steps)


def dot(left, right):
    return jnp.dot(left, right, preferred_element_type=F32)


def dot_right_t(left, right):
    return lax.dot_general(left, right, LANES, preferred_element_type=F32)


def pack_rows():
    i = lax.broadcasted_iota(jnp.int32, (48, 64), 0)
    k = lax.broadcasted_iota(jnp.int32, (48, 64), 1)
    return (k == lax.div(i, 12) * 16 + lax.rem(i, 12)).astype(BF16)


def spread_rows():
    k = lax.broadcasted_iota(jnp.int32, (64, 48), 0)
    i = lax.broadcasted_iota(jnp.int32, (64, 48), 1)
    return (k == lax.div(i, 12) * 16 + lax.rem(i, 12)).astype(BF16)


def merged(ref):
    rows, columns = ref.shape[0] * ref.shape[1] * ref.shape[2], ref.shape[3]
    return ref[...].reshape(rows, columns)


def mean_square(values):
    return jnp.mean(values * values, axis=-1, keepdims=True)


def norm_back(grad, normed, scale):
    return scale * (grad - normed * jnp.mean(grad * normed, axis=-1, keepdims=True))


def slab_turns(line_ref, turn_ref, s):
    rows = line_ref[s]
    cos_base, sin_base = rows[0:1], rows[1:2]
    cos_off, sin_off = turn_ref[0], turn_ref[1]
    lane = lax.broadcasted_iota(jnp.int32, (SLAB, SLAB), 1)
    sign = jnp.where(lane < 32, -1.0, jnp.where(lane < 64, 1.0, 0.0))
    return cos_base * cos_off - sin_base * sin_off, (sin_base * cos_off + cos_base * sin_off) * sign


def turned(field, cosine, sine):
    lane = lax.broadcasted_iota(jnp.int32, (SLAB, SLAB), 1)
    return field * cosine + jnp.where(lane < 32, pltpu.roll(field, 96, 1), pltpu.roll(field, 32, 1)) * sine


def half_rows(values, k):
    return values[k * SLAB : (k + 1) * SLAB]


def direct_gather(links, place, buf, first, second):
    ring_x, ring_y = place.ring("x"), place.ring("y")
    a, b = pl.ds(*first), pl.ds(*second)

    def spread(ring, view, size):
        return links.group([(view, view, ring.device(k)) for k in (ring.next, ring.prev, ring.far)], size)

    over_x = spread(ring_x, buf.at[place.y, place.x, :, a], buf.at[0, pl.ds(0, 3), :, a])
    over_y = spread(ring_y, buf.at[place.y, place.x, :, b], buf.at[0, pl.ds(0, 3), :, b])
    yield
    over_x()
    over_x = spread(ring_y, buf.at[place.y, :, :, a], buf.at[pl.ds(0, 3), :, :, a])
    over_y()
    over_y = spread(ring_x, buf.at[:, place.x, :, b], buf.at[pl.ds(0, 3), :, :, b])
    yield
    over_x()
    over_y()


def turned_view(buf, flip):
    def view(along, over):
        first, second = (over, along) if flip else (along, over)
        return buf.at[first, second, pl.ds(2 if flip else 0, 2)]

    return view


def slab_gather_half(links, along, over, view):
    three, four = pl.ds(1, 3), pl.ds(0, 4)
    own = view(0, 0)
    over_arrived = links.group(
        [
            (own, view(0, 3), over.device(over.next)),
            (own, view(0, 1), over.device(over.prev)),
            (own, view(0, 2), over.device(over.far)),
        ],
        view(0, three),
    )
    up, down = along.device(along.next), along.device(along.prev)
    lines = [links.recv_slot(), links.recv_slot()]
    links.group([(own, view(3, 0), up), (own, view(1, 0), down)], view(0, pl.ds(0, 2)), lines)
    yield
    over_arrived()
    rest = view(0, three)
    links.group([(rest, view(3, three), up), (rest, view(1, three), down)], view(pl.ds(0, 2), three), lines)
    yield
    low, high = pl.ds(0, 2), pl.ds(2, 2)
    links.arrived(view(3, four), lines[0])
    far = [links.recv_slot()] * 2
    send = links.send_slot()
    links.start(view(3, low), view(2, low), up, send, far[0])
    links.arrived(view(1, four), lines[1])
    links.start(view(1, high), view(2, high), down, send, far[1])
    links.sent.append(lambda: links.arrived(view(0, four), send))
    yield
    links.arrived(view(2, four), far[0])


def slab_gather(links, place, buf):
    ring_x, ring_y = place.ring("x"), place.ring("y")
    return (
        slab_gather_half(links, ring_y, ring_x, turned_view(buf, False)),
        slab_gather_half(links, ring_x, ring_y, turned_view(buf, True)),
    )


def slab_scatter_room():
    many, line = pltpu.VMEM((2, 2, SLAB, SLAB), BF16), pltpu.VMEM((4, 2, SLAB, SLAB), BF16)
    return ([many] * 2 + [line] * 3 + [pltpu.VMEM((3, 2, SLAB, SLAB), BF16)]) * 2


def slab_scatter_half(links, along, over, view, room, target):
    low, high, prev, nxt, lined, lasts = room
    lo, hi, four = pl.ds(0, 2), pl.ds(2, 2), pl.ds(0, 4)
    up, down = along.device(along.next), along.device(along.prev)
    slots = [links.recv_slot() for _ in range(4)]
    links.group(
        [
            (view(2, lo), low, up),
            (view(2, hi), high, down),
            (view(1, hi), prev.at[hi], up),
            (view(3, lo), nxt.at[lo], down),
        ],
        view(lo, four),
        slots,
    )
    yield
    links.arrived(low, slots[0])
    add_into(view(1, lo), [view(1, lo), low], BF16)
    send = links.send_slot()
    links.start(view(1, lo), prev.at[lo], up, send, slots[2])
    links.arrived(high, slots[1])
    add_into(view(3, hi), [view(3, hi), high], BF16)
    links.start(view(3, hi), nxt.at[hi], down, send, slots[3])
    links.sent.append(lambda: links.arrived(view(0, four), send))
    yield
    links.arrived(prev, slots[2])
    links.arrived(nxt, slots[3])
    add_into(lined, [view(0, four), prev, nxt], BF16)
    arrived = links.group(
        [
            (lined.at[1], lasts.at[0], over.device(over.next)),
            (lined.at[3], lasts.at[1], over.device(over.prev)),
            (lined.at[2], lasts.at[2], over.device(over.far)),
        ],
        lasts,
    )
    yield
    arrived()
    add_into(target, [lined.at[0], lasts.at[0], lasts.at[1], lasts.at[2]], F32)


def slab_scatter(links, place, buf, rooms, target):
    ring_x, ring_y = place.ring("x"), place.ring("y")
    return (
        slab_scatter_half(links, ring_y, ring_x, turned_view(buf, False), rooms[:6], target.at[pl.ds(0, 2)]),
        slab_scatter_half(links, ring_x, ring_y, turned_view(buf, True), rooms[6:], target.at[pl.ds(2, 2)]),
    )


def slab_place(at):
    return lax.div(at, 16), lax.rem(lax.div(at, 4), 4), lax.rem(at, 4)


def keys_of(kv_ref, table, s, first, count):
    places = [slab_place(jnp.clip(table[s * 24 + first + k, 0], 0, 63)) for k in range(count)]
    return jnp.concatenate([kv_ref[y, x, z] for y, x, z in places], 0)


def query_positions(table, s, shape, axis):
    return table[s * 24 + 20, 0] + lax.broadcasted_iota(jnp.int32, shape, axis)


def attend_head(j, table, q_ref, kv_ref, top_ref, sum_ref, acc_ref, between):
    def fold(s, first, count, first_key):
        keys = keys_of(kv_ref, table, s, first, count)
        width = count * SLAB
        pos_q = query_positions(table, s, (1, SLAB), 1)
        pos_k = first_key + lax.broadcasted_iota(jnp.int32, (width, 1), 0)
        scores = dot_right_t(keys, q_ref[s, :, pl.ds(j * 128, 128)])
        scores = jnp.where(pos_k <= pos_q, scores, LOW)
        top, total = top_ref[s][0:1], sum_ref[s][0:1]
        new_top = jnp.maximum(top, jnp.max(scores, axis=0, keepdims=True))
        weights = jnp.exp(scores - new_top)
        decay = jnp.exp(top - new_top)
        total = total * decay + jnp.sum(weights, axis=0, keepdims=True)
        sums = lax.dot_general(keys, weights.astype(BF16), (((0,), (0,)), ((), ())), preferred_element_type=F32)
        acc_ref[s] = acc_ref[s] * decay + sums
        top_ref[s] = jnp.broadcast_to(new_top, (8, SLAB))
        sum_ref[s] = jnp.broadcast_to(total, (8, SLAB))

    for s in range(4):
        top_ref[s] = jnp.full((8, SLAB), LOW, F32)
        sum_ref[s] = jnp.zeros((8, SLAB), F32)
        acc_ref[s] = jnp.zeros((SLAB, SLAB), F32)

    def prompt(c, carry):
        for s in range(4):
            fold(s, c * 4, 4, c * 512)
        return carry

    lax.fori_loop(0, 2, prompt, 0)
    between(0)
    lax.fori_loop(2, 4, prompt, 0)
    between(1)
    for s in range(4):
        fold(s, 16, 2, 2048)


def attend_back_head(j, table, q_ref, kv_ref, grad_ref, logs, deltas, dq_ref, terms_ref, pair_ref, between):
    lane = lax.broadcasted_iota(jnp.int32, (SLAB, SLAB), 1)
    for s in range(4):
        grads = grad_ref[j // 2, s].astype(F32)
        if j != 1:
            grads = pltpu.roll(grads, 64, 1)
        pair_ref[s, pl.ds(0, SLAB)] = q_ref[s, :, pl.ds(j * 128, 128)]
        pair_ref[s, pl.ds(SLAB, SLAB)] = jnp.where(lane < 64, 0.0, grads).astype(BF16)
        dq_ref[s] = jnp.zeros((SLAB, SLAB), F32)

    def fold(s, first, count, first_key):
        keys = keys_of(kv_ref, table, s, first, count)
        width = count * SLAB
        pos_q = query_positions(table, s, (1, SLAB), 1)
        pos_k = first_key + lax.broadcasted_iota(jnp.int32, (width, 1), 0)
        pair = pair_ref[s]
        both = dot_right_t(keys, pair)
        weights = jnp.where(pos_k <= pos_q, jnp.exp(both[:, :SLAB] - logs[s]), 0.0)
        slopes = (weights * (both[:, SLAB:] - deltas[s])).astype(BF16)
        terms = dot(jnp.concatenate([slopes, weights.astype(BF16)], 1), pair)
        terms_ref[s, pl.ds(first, count)] = terms.astype(BF16).reshape(count, SLAB, SLAB)
        dq_ref[s] += lax.dot_general(slopes, keys, (((0,), (0,)), ((), ())), preferred_element_type=F32)

    def prompt(c, carry):
        for s in range(4):
            fold(s, c * 4, 4, c * 512)
        return carry

    lax.fori_loop(0, 2, prompt, 0)
    between(0)
    lax.fori_loop(2, 4, prompt, 0)
    between(1)
    for s in range(4):
        fold(s, 16, 2, 2048)
    between(2)


def sum_terms(place, table, terms_ref, part_ref):
    def block(t, carry):
        dy, dx = lax.div(t, 4), lax.rem(t, 4)
        at = lax.rem(dy + place.y, 4) * 16 + lax.rem(dx + place.x, 4) * 4
        for dz in range(4):
            places = [jnp.clip(table[96 + s, at + dz], 0, 18) for s in range(4)]
            total = terms_ref[0, places[0]].astype(F32)
            for s in range(1, 4):
                total = total + terms_ref[s, places[s]].astype(F32)
            part_ref[dy, dx, dz] = total.astype(BF16)
        return carry

    lax.fori_loop(0, 16, block, 0)


def lookups(total, place, meta_ref):
    seg, base = total[2:3], total[3:4]
    lane = lax.broadcasted_iota(jnp.int32, (1, SLAB), 1)
    from_here = lax.rem(lax.div(lane, 16) + 4 - place.y, 4) * 16 + lax.rem(lax.rem(lax.div(lane, 4), 4) + 4 - place.x, 4) * 4
    lane_at = (from_here + lax.rem(lane, 4)).astype(F32)
    own = place.y * 4 + place.x
    n = lax.broadcasted_iota(jnp.int32, (24, 1), 0)
    back_rows = jnp.zeros((8, SLAB), F32)
    back_row = lax.broadcasted_iota(jnp.int32, (8, 1), 0)
    for s in range(4):
        mine = lane == own * 4 + s
        seg_q = jnp.sum(jnp.where(mine, seg, 0.0), axis=1, keepdims=True)
        base_q = jnp.sum(jnp.where(mine, base, 0.0), axis=1, keepdims=True)
        prompt = jnp.where(seg_q >= CONTS + 1.0, CONTS + 1.0, 0.0)
        want = jnp.where(n < 16, prompt, seg_q)
        hit = (seg == want) & (base == n.astype(F32) * SLAB) & (lane < 64)
        places = jnp.max(jnp.where(hit, lane_at, 0.0), axis=1, keepdims=True)
        listed = jnp.where(n == 20, base_q, places)
        meta_ref[pl.ds(s * 24, 24), :] = jnp.broadcast_to(listed, (24, SLAB)).astype(jnp.int32)
        visible = (seg == prompt) | (seg == seg_q)
        places = jnp.where(visible, jnp.minimum(base * (1.0 / SLAB), 17.0), 18.0)
        back_rows = jnp.where(back_row == s, places, back_rows)
    meta_ref[pl.ds(96, 8), :] = back_rows.astype(jnp.int32)


def column_of(gain_ref):
    i = lax.broadcasted_iota(jnp.int32, (12, 12), 0)
    k = lax.broadcasted_iota(jnp.int32, (12, 12), 1)
    return jnp.sum(jnp.where(i == k, gain_ref[...].astype(F32), 0.0), axis=1, keepdims=True)


def plane_columns(z):
    return [((z % 2) * 32 + p * 2 + z // 2) * 48 for p in range(16)]


def own_slab(place, at, seg_ref, pos_ref, base_ref):
    lane = lax.broadcasted_iota(jnp.int32, (1, SLAB), 1)
    high = place.head == 1
    seg = jnp.where(high, seg_ref[1:2], seg_ref[0:1]).astype(F32)
    base = (jnp.where(high, pos_ref[1:2], pos_ref[0:1]) - lane).astype(F32)
    m = lax.broadcasted_iota(jnp.int32, (24, SLAB), 0).astype(F32)
    cosine, sine = [
        jnp.sum(jnp.where(m == base * (1.0 / SLAB), base_ref[k], 0.0), axis=0, keepdims=True) for k in range(2)
    ]
    row = lax.broadcasted_iota(jnp.int32, (8, SLAB), 0)
    here = (lane == at) & (row >= 2)
    facts = jnp.where(here, jnp.where(row == 2, seg, jnp.where(row == 3, base, 0.0)), 0.0)
    return jnp.where(row == 0, cosine, jnp.where(row == 1, sine, facts))


def finish_kernel(
    ff_ref, qkv_ref, og_ref, wq_ref, wk_ref, wv_ref, gate_ref, up_ref, gain1_ref, gain2_ref, out_in, grad_in, down_in,
    out_ref, grad_ref, dgain1_ref, dq_ref, dk_ref, dv_ref, do_ref, dgain2_ref, dgate_ref, dup_ref, down_ref,
):
    out_ref[...] = out_in[...]
    grad_ref[...] = grad_in[...]
    down_ref[...] = down_in[...]
    i = lax.broadcasted_iota(jnp.int32, (12, 12), 0)
    k = lax.broadcasted_iota(jnp.int32, (12, 12), 1)

    def row_of(column):
        return jnp.sum(jnp.where(i == k, column, 0.0), axis=0, keepdims=True)

    gain = column_of(gain1_ref)
    grads = [qkv_ref[z].astype(F32)[:12] for z in range(4)]
    total = jnp.zeros((12, 1), F32)
    for c, w_ref, to_ref in ((384, wq_ref, dq_ref), (0, wk_ref, dk_ref), (64, wv_ref, dv_ref)):
        step = 64 if c == 384 else 128
        grad = jnp.concatenate([grads[z][:, step * j + c : step * j + c + HD] for z in range(4) for j in range(3)], 1)
        total = total + jnp.sum(grad * w_ref[...].astype(F32), axis=1, keepdims=True)
        to_ref[...] = grad * gain
    dgain1_ref[...] = row_of(total)
    do_ref[...] = og_ref[0, pl.ds(0, 12)]

    gain = column_of(gain2_ref)
    total = jnp.zeros((12, 1), F32)
    for k_at, w_ref, to_ref in ((0, gate_ref, dgate_ref), (768, up_ref, dup_ref)):
        pieces = {}
        for z in range(4):
            grad = ff_ref[z, :, pl.ds(k_at, 768)].astype(F32)[:12]
            for p, c in enumerate(plane_columns(z)):
                pieces[c] = grad[:, 48 * p : 48 * p + 48]
        grad = jnp.concatenate([pieces[c] for c in sorted(pieces)], 1)
        total = total + jnp.sum(grad * w_ref[...].astype(F32), axis=1, keepdims=True)
        to_ref[...] = grad * gain
    dgain2_ref[...] = row_of(total)


def layer_kernel(
    tok_ref, cot_hbm, wq_ref, wk_ref, wv_ref, wo_ref, gate_ref, up_ref, down_hbm, gain1_ref, gain2_ref, seg_ref, pos_ref,
    perm_hbm, turn_hbm, base_ref, perm_att_hbm, out_perm_hbm,
    out_ref, in_ref, down_sum_ref, got_ff_ref, got_ref, got_out_ref,
    perm_ref, turn_ref, cot_ref, down_ref, perm_att, out_perm, const_sem, line_ref, descs, meta_ref, table, table_sem,
    for_line, for_line_ff, rows, rows_o, rows_ff, one, cots, wqkv, wo, wff, q_ref, kv0, kv1, kv2,
    tops, sums, accs, heads, att_ref, lse_ref, atts, wo_heads, mid_s, gm_s, two, act, pre, turn_t, part, part_out, sum_z, sum_out,
    to_heads, grads_ref, terms, pairs, kv_own, d_s, qkv_sum, ff_sum,
    og_part, og_sum, og_next, *rest,
):
    send, recv = rest[-2:]
    rooms = list(rest[:-2])

    def take(count):
        out = rooms[:count]
        del rooms[:count]
        return out

    back_room, ff_room, out_room = take(6), take(26), take(6)
    kv_rooms = [take(12) for _ in range(3)]
    qkv_rooms = [take(6) for _ in range(2)]
    in_room, og_line_room, og_room = take(6), take(6), take(6)
    kvs = (kv0, kv1, kv2)

    pairs_in = (
        (perm_hbm, perm_ref), (turn_hbm, turn_ref), (cot_hbm, cot_ref),
        (down_hbm, down_ref), (perm_att_hbm, perm_att), (out_perm_hbm, out_perm),
    )
    loads = [pltpu.make_async_copy(source, target, const_sem.at[n]) for n, (source, target) in enumerate(pairs_in)]
    for load in loads:
        load.start()
    place = Place()
    partners = announce(place)
    links = Links(send, recv)
    own = place.y * 4 + place.x

    line_ref[place.z] = own_slab(place, own * 4 + place.z, seg_ref, pos_ref, base_ref)
    lined = small_gather(links, place.ring("z"), lambda k: line_ref.at[k], line_ref.at[pl.ds(0, 3)])
    gain = column_of(gain1_ref)
    w_q, w_k, w_v = [ref[...].astype(F32) * gain for ref in (wq_ref, wk_ref, wv_ref)]
    none, blank = jnp.zeros((12, HD), F32), jnp.zeros((4, 768), F32)
    for z in range(4):
        pieces, last = [], []
        for j in range(3):
            at = slice(192 * z + 64 * j, 192 * z + 64 * j + 64)
            pieces += [w_k[:, at], w_v[:, at]]
            last.append(w_q[:, at])
        pieces += [*last, none]
        for_line[z] = jnp.concatenate([jnp.concatenate(pieces, 1), blank[:, :640]], 0).astype(BF16)
    loads[0].wait()
    x = dot(tok_ref[...], perm_ref[...])
    one[place.z] = (x * lax.rsqrt(mean_square(x) + EPS)).astype(BF16)
    enter(partners)
    swap = line_swap(links, place, for_line, rows)
    advance(swap, lined)
    rows_o[place.z] = jnp.concatenate([wo_ref[...].astype(F32), blank], 0).astype(BF16)
    o_line = small_gather(links, place.ring("z"), lambda k: rows_o.at[k], rows_o.at[pl.ds(0, 3)])
    advance(o_line)
    ones = line_gather(links, place, one)
    finish(swap)
    advance(ones)
    wqkv[place.y, place.x] = dot(pack_rows(), rows[...].reshape(64, 640)).astype(BF16)
    kv_gather = direct_gather(links, place, wqkv, (0, 256), (256, 128))
    q_gather = shared_gather(links, place, wqkv, 384, 256)
    advance(kv_gather)
    finish(lined, o_line)
    wo[place.y, place.x] = dot(pack_rows(), rows_o[...].reshape(64, 768)).astype(BF16)
    o_gather = shared_gather(links, place, wo, 0, 768)
    descs[place.y, place.x] = line_ref[0] + line_ref[1] + line_ref[2] + line_ref[3]
    desc_x = small_gather(links, place.ring("x"), lambda k: descs.at[place.y, k], descs.at[0, pl.ds(0, 3)])
    desc_y = small_gather(links, place.ring("y"), lambda k: descs.at[k], descs.at[pl.ds(0, 3)])
    advance(desc_x)
    for load in loads[1:]:
        load.wait()
    gain = column_of(gain2_ref)
    for k, ref in enumerate((gate_ref, up_ref)):
        w = ref[...].astype(F32) * gain
        for z in range(4):
            pieces = [w[:, c : c + 48] for c in plane_columns(z)]
            for_line_ff[z, :, pl.ds(768 * k, 768)] = jnp.concatenate([jnp.concatenate(pieces, 1), blank], 0).astype(BF16)
    advance(q_gather)
    advance(o_gather)
    advance(kv_gather)
    finish(desc_x)
    advance(desc_y)
    advance(ones)
    advance(q_gather)
    advance(o_gather)
    ff_swap = line_swap(links, place, for_line_ff, rows_ff)
    cots[place.z] = cot_ref[...]
    cot_gather = line_gather(links, place, cots)
    finish(desc_y)
    total = jnp.zeros((8, SLAB), F32)
    for y in range(4):
        for k in range(4):
            total = total + descs[y, k]
    lookups(total, place, meta_ref)
    table_copy = pltpu.make_async_copy(meta_ref, table, table_sem)
    table_copy.start()
    finish(ones, kv_gather)
    advance(q_gather)
    advance(o_gather)

    lines = one[...].reshape(512, 768)
    gathers = [slab_gather(links, place, kv) for kv in kvs]
    for j in range(3):
        field = dot(lines, wqkv[:, :, :, pl.ds(128 * j, 128)].reshape(768, 128))
        for s in range(4):
            cosine, sine = slab_turns(line_ref, turn_ref, s)
            kvs[j][0, 0, s] = turned(half_rows(field, s), cosine, sine).astype(BF16)
        if j < 2:
            advance(*gathers[j])
    advance(ff_swap, cot_gather)
    advance(q_gather)
    advance(*gathers[0])
    advance(*gathers[2])
    advance(q_gather)
    advance(*gathers[1])
    advance(o_gather)
    advance(*gathers[0])
    finish(q_gather)
    field = dot(lines, wqkv[:, :, :, pl.ds(384, 256)].reshape(768, 256))
    lane = lax.broadcasted_iota(jnp.int32, (SLAB, SLAB), 1)
    for s in range(4):
        cosine, sine = slab_turns(line_ref, turn_ref, s)
        first, last = half_rows(field[:, 0:128], s), half_rows(field[:, 128:256], s)
        for j, query in enumerate((first, pltpu.roll(first, 64, 1), last)):
            query = turned(jnp.where(lane < 64, query * 0.125, 0.0), cosine, sine)
            q_ref[s, :, pl.ds(128 * j, 128)] = query.astype(BF16)
    advance(*gathers[2])
    finish(ff_swap)
    for c in range(0, 1536, 768):
        wff[place.y, place.x, :, pl.ds(c, 768)] = dot(
            pack_rows(), rows_ff[:, :, pl.ds(c, 768)].reshape(64, 768)
        ).astype(BF16)
    wff[place.y, place.x, :, pl.ds(1536, 768)] = down_ref[...]
    table_copy.wait()
    advance(cot_gather)
    advance(*gathers[1])

    lane = lax.broadcasted_iota(jnp.int32, (SLAB, SLAB), 1)
    for s in range(4):
        heads[s, pl.ds(192, 64), :] = jnp.zeros((64, SLAB), F32)
    w_gather = shared_gather(links, place, wff, 0, 2304)
    att_swaps = []
    for j in range(3):
        finish(*gathers[j])

        def between(k, j=j):
            if j == 0 and k == 0:
                links.finish(8)
            if j == 0 and k == 1:
                advance(*gathers[2])
                advance(o_gather)
            if j == 1 and k == 0:
                finish(cot_gather)
                links.finish(8)
            if j == 1 and k == 1:
                advance(o_gather)

        if j == 2:
            advance(w_gather)
        attend_head(j, table, q_ref, kvs[j], tops, sums, accs, between)
        for s in range(4):
            heads[s, pl.ds(64 * j, 64), :] = accs[s, pl.ds(64, 64), :] / sums[s][0:1]
            lse_ref[j, s] = tops[s] + jnp.log(sums[s])
        if j:
            for s in range(4):
                att_ref[j - 1, s] = heads[s, pl.ds(128 * (j - 1), 128), :].T.astype(BF16)
            att_swaps.append(line_swap(links, place, att_ref.at[j - 1], atts.at[j - 1]))
            advance(att_swaps[j - 1])
    advance(w_gather)
    links.finish(20)
    finish(o_gather)
    for z in range(4):
        wo_heads[z] = dot(perm_att[pl.ds(256 * z, 256), :], merged(wo)).astype(BF16)
    finish(*att_swaps)
    advance(w_gather)

    middle = tok_ref[...].astype(F32)
    for z in range(4):
        middle = middle + dot(atts[0, z], wo_heads[z, pl.ds(0, 128)]) + dot(atts[1, z], wo_heads[z, pl.ds(128, 128)])
    mid_s[...] = middle
    middle = mid_s[...]
    scale_two = lax.rsqrt(mean_square(middle) + EPS)
    two[place.z] = dot((middle * scale_two).astype(BF16), perm_ref[...]).astype(BF16)
    two_gather = line_gather(links, place, two)
    advance(two_gather)
    advance(w_gather)
    att = jnp.zeros((SLAB, 1024), F32)
    for z in range(4):
        for t in range(2):
            att = att + dot(atts[t, z], out_perm[pl.ds(256 * z + 128 * t, 128), :])
    att_by_z = att.astype(BF16).T
    advance(two_gather)
    together([w_gather, two_gather])

    def block():
        two_b = two[...].reshape(512, 768)
        cot_b = cots[...].reshape(512, 768)
        gate_w = wff[:, :, :, pl.ds(0, 768)].reshape(768, 768)
        up_w = wff[:, :, :, pl.ds(768, 768)].reshape(768, 768)
        down_w = wff[:, :, :, pl.ds(1536, 768)].reshape(768, 768)
        gate = dot(two_b, gate_w)
        up = dot(two_b, up_w)
        sig = 1.0 / (1.0 + jnp.exp(-gate))
        silu = gate * sig
        act_b = (silu * up).astype(BF16)
        act[...] = act_b
        grad_act = dot_right_t(cot_b, down_w)
        grad_gate = (grad_act * up * (sig * (1.0 + gate * (1.0 - sig)))).astype(BF16)
        grad_up = (grad_act * silu).astype(BF16)
        pre[:, pl.ds(0, 768)] = grad_gate
        pre[:, pl.ds(768, 768)] = grad_up
        back = dot_right_t(grad_gate, gate_w) + dot_right_t(grad_up, up_w)
        part[...] = back.astype(BF16).reshape(4, SLAB, 768)

    def out_block(r, carry):
        at = pl.ds(pl.multiple_of(r * 256, 256), 256)
        down_w = wff[:, :, :, pl.ds(1536, 768)].reshape(768, 768)
        part_out[pl.ds(r * 2, 2)] = dot(act[at, :], down_w).astype(BF16).reshape(2, SLAB, 768)
        return carry

    block()
    links.finish()
    back_sum = line_scatter(links, place, part, back_room, sum_z)
    advance(back_sum)
    lax.fori_loop(0, 2, out_block, 0)
    turn_t[...] = two[...].reshape(512, 768).T

    def first_grads(c, carry):
        at = pl.ds(pl.multiple_of(c * 256, 256), 256)
        wff[:, :, :, at] = dot(turn_t[...], pre[:, at]).astype(BF16).reshape(4, 4, 48, 256)
        return carry

    def last_grads(c, carry):
        at = pl.ds(pl.multiple_of(c * 256, 256), 256)
        to = pl.ds(pl.multiple_of(1536 + c * 256, 256), 256)
        cot_all = cots[:, :, at].reshape(512, 256)
        wff[:, :, :, to] = dot(turn_t[...], cot_all).astype(BF16).reshape(4, 4, 48, 256)
        return carry

    lax.fori_loop(0, 6, first_grads, 0)
    advance(back_sum)
    turn_t[...] = act[...].T
    lax.fori_loop(0, 3, last_grads, 0)
    ff = plane_scatter(links, place, wff, ff_room, ff_sum, False)
    advance(*ff)
    finish(back_sum)
    links.finish(6)

    grad = dot_right_t(sum_z[0].astype(BF16), perm_ref[...])
    middle = mid_s[...]
    scale_two = lax.rsqrt(mean_square(middle) + EPS)
    gm_s[...] = cot_ref[...].astype(F32) + norm_back(grad, middle * scale_two, scale_two)
    low = gm_s[...].astype(BF16)
    heads_swaps = []
    for t in range(2):
        for z in range(4):
            to_heads[t, z] = dot_right_t(low, wo_heads[z, pl.ds(128 * t, 128)]).astype(BF16)
        heads_swaps.append(line_swap(links, place, to_heads.at[t], grads_ref.at[t]))
        advance(heads_swaps[t])
    out_sum = line_scatter(links, place, part_out, out_room, sum_out)
    advance(out_sum)
    turn_t[...] = one[...].reshape(512, 768).T
    og_part[...] = dot(att_by_z, low).astype(BF16).reshape(4, 256, 768)
    for s in range(4):
        terms[s, 18] = jnp.zeros((SLAB, SLAB), BF16)
    finish(heads_swaps[0])

    which = lax.broadcasted_iota(jnp.int32, (8, SLAB), 0)
    at_lane = lax.broadcasted_iota(jnp.int32, (8, SLAB), 1)
    pick = (lax.div(at_lane, HD) == which).astype(F32)

    def deltas_of(j):
        rows = []
        for s in range(4):
            inner = grads_ref[j // 2, s].astype(F32) * att_ref[j // 2, s].astype(F32)
            delta = lax.dot_general(pick, inner, LANES, precision=HIGHEST, preferred_element_type=F32)
            rows.append(jnp.sum(jnp.where(which == j % 2, delta, 0.0), axis=0, keepdims=True))
        return rows

    scatters = []

    def keys_turn(j):
        for s in range(4):
            cosine, sine = slab_turns(line_ref, turn_ref, s)
            d_s[pl.ds(s * SLAB, SLAB), pl.ds(128 * j, 128)] = turned(kv_own[j, s], cosine, -sine).astype(BF16)

    def qkv_grads(columns, first, second, room):
        for c in columns:
            wo[:, :, :, pl.ds(c, 128)] = dot(turn_t[...], d_s[:, pl.ds(c, 128)]).astype(BF16).reshape(4, 4, 48, 128)
        return small_scatter(links, place, wo, first, second, room, qkv_sum)

    og_line = line_scatter(links, place, og_part, og_line_room, og_sum)
    spread = spread_rows()
    for j in range(3):

        def between(k, j=j):
            if j == 0 and k == 0:
                advance(*ff)
                advance(out_sum)
            if j == 1 and k == 0:
                advance(*ff)
                links.finish(8)
            if j == 1 and k == 2:
                advance(*scatters[0])
            if j == 2 and k == 0:
                advance(*ff)
                links.finish(4)
            if j == 2 and k == 1:
                advance(*scatters[0])
            if j == 2 and k == 2:
                advance(*scatters[1])

        if j == 2:
            finish(heads_swaps[1])
        logs = [lse_ref[j, s][0:1] for s in range(4)]
        attend_back_head(j, table, q_ref, kvs[j], grads_ref, logs, deltas_of(j), accs, terms, pairs, between)
        sum_terms(place, table, terms, kvs[j])
        scatters.append(slab_scatter(links, place, kvs[j], kv_rooms[j], kv_own.at[j]))
        advance(*scatters[j])
        for s in range(4):
            cosine, sine = slab_turns(line_ref, turn_ref, s)
            grad = turned(jnp.where(lane < 64, accs[s] * 0.125, 0.0), cosine, -sine)
            to = (pl.ds(s * SLAB, SLAB), pl.ds(384 + 128 * (j // 2), 128))
            if j == 1:
                grad = jnp.where(lane < 64, d_s[to].astype(F32), pltpu.roll(grad, 64, 1))
            d_s[to] = grad.astype(BF16)
        if j == 0:
            finish(out_sum)
            advance(og_line)
            out_ref[...] = (mid_s[...] + sum_out[0]).astype(BF16)
        if j == 1:
            advance(og_line)

    finish(*scatters[0])
    finish(*ff)
    down_sum_ref[...] = ff_sum[0, :, pl.ds(1536, 768)]
    for c in range(0, 1536, 768):
        for_line_ff[:, :, pl.ds(c, 768)] = (
            dot(spread, ff_sum[0, :, pl.ds(c, 768)].astype(BF16)).astype(BF16).reshape(4, 16, 768)
        )
    finish(og_line)
    grads_swap = line_swap(links, place, for_line_ff, got_ff_ref)
    advance(grads_swap)
    keys_turn(0)
    og_next[...] = og_sum[0].astype(BF16).reshape(4, 4, 16, 768)
    links.finish(12)
    advance(*scatters[1])
    advance(*scatters[2])
    finish(*scatters[1])
    keys_turn(1)
    advance(*scatters[2])
    qkv = qkv_grads((0, 128, 384), (0, 256), (384, 128), qkv_rooms[0])
    og = small_scatter(links, place, og_next, (0, 384), (384, 384), og_room, got_out_ref)
    links.finish(12)
    finish(*scatters[2])
    advance(*qkv)
    keys_turn(2)

    def last_block(r, carry):
        at = pl.ds(pl.multiple_of(r * 256, 256), 256)
        part[pl.ds(r * 2, 2)] = dot_right_t(d_s[at, :], merged(wqkv)).astype(BF16).reshape(2, SLAB, 768)
        return carry

    lax.fori_loop(0, 2, last_block, 0)
    in_sum = line_scatter(links, place, part, in_room, sum_z)
    advance(in_sum)
    last_qkv = qkv_grads((256, 512), (256, 128), (512, 128), qkv_rooms[1])
    advance(*last_qkv)
    advance(*og)
    advance(*qkv)
    finish(grads_swap)
    advance(in_sum)
    advance(*last_qkv)
    advance(*og)
    finish(*qkv)
    links.finish(len(links.sent) - 4)
    finish(*last_qkv)
    for_line[...] = dot(spread, qkv_sum[0].astype(BF16)).astype(BF16).reshape(4, 16, 640)
    last = line_swap(links, place, for_line, got_ref)
    advance(last)
    finish(*og)
    finish(in_sum)
    grad = dot_right_t(sum_z[0].astype(BF16), perm_ref[...])
    x = tok_ref[...].astype(F32)
    scale = lax.rsqrt(mean_square(x) + EPS)
    in_ref[...] = gm_s[...] + norm_back(grad, x * scale, scale)
    links.finish()
    finish(last)


SENDS, RECVS = 190, 202
LINE = pltpu.VMEM((4, SLAB, 768), BF16)
KV = pltpu.VMEM((4, 4, 4, SLAB, SLAB), BF16)
OUTS = [
    ((SLAB, 768), BF16),
    ((SLAB, 768), F32),
    ((48, 768), F32),
    ((4, 16, 1536), BF16),
    ((4, 16, 640), BF16),
    ((1, 16, 768), F32),
]
ROOM = (
    [
        pltpu.VMEM((768, 768), BF16),
        pltpu.VMEM((2, SLAB, SLAB), F32),
        pltpu.VMEM((SLAB, 768), BF16),
        pltpu.VMEM((48, 768), BF16),
        pltpu.VMEM((1024, 768), BF16),
        pltpu.VMEM((1024, 1024), BF16),
        pltpu.SemaphoreType.DMA((6,)),
        pltpu.VMEM((4, 8, SLAB), F32),
        pltpu.VMEM((4, 4, 8, SLAB), F32),
        pltpu.VMEM((104, SLAB), jnp.int32),
        pltpu.SMEM((104, SLAB), jnp.int32),
        pltpu.SemaphoreType.DMA,
        pltpu.VMEM((4, 16, 640), BF16),
        pltpu.VMEM((4, 16, 1536), BF16),
        pltpu.VMEM((4, 16, 640), BF16),
        pltpu.VMEM((4, 16, 768), BF16),
        pltpu.VMEM((4, 16, 1536), BF16),
        LINE,
        LINE,
        pltpu.VMEM((4, 4, 48, 640), BF16),
        pltpu.VMEM((4, 4, 48, 768), BF16),
        pltpu.VMEM((4, 4, 48, 2304), BF16),
        pltpu.VMEM((4, SLAB, 384), BF16),
        KV,
        KV,
        KV,
        pltpu.VMEM((4, 8, SLAB), F32),
        pltpu.VMEM((4, 8, SLAB), F32),
        pltpu.VMEM((4, SLAB, SLAB), F32),
        pltpu.VMEM((4, 256, SLAB), F32),
        pltpu.VMEM((2, 4, SLAB, SLAB), BF16),
        pltpu.VMEM((3, 4, 8, SLAB), F32),
        pltpu.VMEM((2, 4, SLAB, SLAB), BF16),
        pltpu.VMEM((4, 256, 768), BF16),
        pltpu.VMEM((SLAB, 768), F32),
        pltpu.VMEM((SLAB, 768), F32),
        LINE,
        pltpu.VMEM((512, 768), BF16),
        pltpu.VMEM((512, 1536), BF16),
        pltpu.VMEM((768, 512), BF16),
        LINE,
        LINE,
        pltpu.VMEM((1, SLAB, 768), F32),
        pltpu.VMEM((1, SLAB, 768), F32),
        pltpu.VMEM((2, 4, SLAB, SLAB), BF16),
        pltpu.VMEM((2, 4, SLAB, SLAB), BF16),
        pltpu.VMEM((4, 19, SLAB, SLAB), BF16),
        pltpu.VMEM((4, 256, SLAB), BF16),
        pltpu.VMEM((3, 4, SLAB, SLAB), F32),
        pltpu.VMEM((512, 640), BF16),
        pltpu.VMEM((1, 48, 640), F32),
        pltpu.VMEM((1, 48, 2304), F32),
        pltpu.VMEM((4, 256, 768), BF16),
        pltpu.VMEM((1, 256, 768), F32),
        pltpu.VMEM((4, 4, 16, 768), BF16),
    ]
    + line_scatter_room(SLAB, 768)
    + plane_scatter_room(48, 2304, False)
    + line_scatter_room(SLAB, 768)
    + slab_scatter_room() * 3
    + small_scatter_room(48, 256, 128)
    + small_scatter_room(48, 128, 128)
    + line_scatter_room(SLAB, 768)
    + line_scatter_room(256, 768)
    + small_scatter_room(16, 384, 384)
)


def per_device(
    tokens, gain_one, w_query, w_key, w_value, w_out, gain_two, w_gate, w_up, w_down, cotangent, segment_ids, positions
):
    gains = (gain_one.reshape(1, 12), gain_two.reshape(1, 12))
    anywhere = pl.BlockSpec(memory_space=pl.ANY)
    output, input_grad, down_grad, got_ff, got_qkv, got_out = pl.pallas_call(
        layer_kernel,
        out_shape=tuple(jax.ShapeDtypeStruct(shape, kind) for shape, kind in OUTS),
        in_specs=[anywhere if k in (1, 8, 13, 14, 16, 17) else VMEM for k in range(18)],
        out_specs=tuple([VMEM] * len(OUTS)),
        scratch_shapes=ROOM
        + [pltpu.SemaphoreType.DMA((SENDS,)), pltpu.SemaphoreType.DMA((RECVS,))],
        compiler_params=pltpu.CompilerParams(collective_id=0, has_side_effects=True, vmem_limit_bytes=62 * MIB),
        name="layer",
    )(
        tokens, cotangent, w_query, w_key, w_value, w_out, w_gate, w_up, w_down, *gains,
        segment_ids.reshape(2, SLAB), positions.reshape(2, SLAB),
        jnp.asarray(TO_PERM, BF16), jnp.asarray(OFFSET_TURNS, F32), jnp.asarray(BASE_TURNS, F32),
        jnp.asarray(ATT_PERM, BF16), jnp.asarray(OUT_PERM, BF16),
    )
    small, square, wide = [jax.ShapeDtypeStruct((rows, columns), F32) for rows, columns in ((1, 12), (12, 768), (12, 3072))]
    output, input_grad, gain_one_grad, dq, dk, dv, do, gain_two_grad, dgate, dup, down_grad = pl.pallas_call(
        finish_kernel,
        out_shape=(*[jax.ShapeDtypeStruct(*OUTS[k]) for k in range(2)], small, square, square, square, square, small, wide, wide,
                   jax.ShapeDtypeStruct(*OUTS[2])),
        in_specs=[VMEM] * 13,
        out_specs=(VMEM,) * 11,
        name="finish",
    )(got_ff, got_qkv, got_out, w_query, w_key, w_value, w_gate, w_up, *gains, output, input_grad, down_grad)
    return (
        output, input_grad, gain_one_grad.reshape(12), dq, dk, dv, do, gain_two_grad.reshape(12), dgate, dup, down_grad
    )


def solution(mesh):
    rows = P(("grp", "blk", "head"), None)
    flat = P(("grp", "blk", "head"))
    weight = P(("blk", "head"), None)
    gain = P(("blk", "head"))
    ids = P(("grp", "blk"))
    in_specs = (rows, gain, weight, weight, weight, weight, gain, weight, weight, weight, rows, ids, ids)
    out_specs = (rows, rows, flat, rows, rows, rows, rows, flat, rows, rows, rows)
    return jax.shard_map(per_device, mesh=mesh, in_specs=in_specs, out_specs=out_specs, check_vma=False)
```
